32 devices in a mesh: batch: 16 (over z, y, x), unit: 2 (over core).
Axes of the slice: x: 2, y: 2, z: 4, core: 2. Of those that a mesh axis runs over, the one named last changes fastest.
Arguments:
- memory: bfloat16 [2, 192, 64, 512], P(None, 'batch'), may hold values from -6 to 6
- targets: bfloat16 [2, 192, 6, 80], P(None, 'batch'), may hold values from -6 to 6
- segments: int32 [2, 192, 6], P(None, 'batch'), may hold values from 0 to 2, never falling along the last dimension, each value on 1 to 3 neighbouring positions
- text_lengths: int32 [2, 192, 3], P(None, 'batch'), may hold values from 1 to 32, 64 in all within a row
- zone_first: int32 [2, 192, 6, 1024], P(None, 'batch', None, 'unit'), may hold values 0 or 1
- zone_second: int32 [2, 192, 6, 1024], P(None, 'batch', None, 'unit'), may hold values 0 or 1
- drop_first: int32 [2, 192, 6, 256], P(None, 'batch'), may hold values 0 or 1
- drop_second: int32 [2, 192, 6, 256], P(None, 'batch'), may hold values 0 or 1
- prenet_first: bfloat16 [80, 256], replicated, may hold values from -0.625 to 0.625
- prenet_second: bfloat16 [256, 256], replicated, may hold values from -0.375 to 0.375
- query_weight: bfloat16 [1024, 128], replicated, may hold values from -0.1875 to 0.1875
- memory_weight: bfloat16 [512, 128], replicated, may hold values from -0.25 to 0.25
- location_conv: bfloat16 [32, 2, 31], replicated, may hold values from -0.75 to 0.75
- location_dense: bfloat16 [32, 128], replicated, may hold values from -1 to 1
- energy_vector: bfloat16 [128], replicated, may hold values from -1.5 to 1.5
- lstm_first: bfloat16 [1792, 4, 1024], P('batch', None, 'unit'), may hold values from -0.125 to 0.125
- bias_first: float32 [4, 1024], P(None, 'unit'), may hold values from -3 to 3
- lstm_second: bfloat16 [2560, 4, 1024], P('batch', None, 'unit'), may hold values from -0.125 to 0.125
- bias_second: float32 [4, 1024], P(None, 'unit'), may hold values from -3 to 3
- frame_weight: bfloat16 [1536, 81], replicated, may hold values from -0.15625 to 0.15625
- frame_bias: float32 [81], replicated, may hold values from -3 to 3
- post_first: bfloat16 [5, 80, 512], P(None, None, 'unit'), may hold values from -0.3125 to 0.3125
- post_middle: bfloat16 [3, 5, 512, 512], P(None, None, 'batch', 'unit'), may hold values from -0.125 to 0.125
- post_last: bfloat16 [5, 512, 80], P(None, 'batch', 'unit'), may hold values from -0.125 to 0.125
- middle_norm: float32 [2, 4, 512], P(None, None, 'unit'), may hold values from 0.1 to 1.9
- last_norm: float32 [2, 80], P(None, 'unit'), may hold values from 0.1 to 1.9
Outputs:
- prenet_first_grad: float32 [80, 256], replicated
- prenet_second_grad: float32 [256, 256], replicated
- query_weight_grad: float32 [1024, 128], replicated
- memory_weight_grad: float32 [512, 128], replicated
- location_conv_grad: float32 [32, 2, 31], replicated
- location_dense_grad: float32 [32, 128], replicated
- energy_vector_grad: float32 [128], replicated
- lstm_first_grad: float32 [1792, 4, 1024], P('batch', None, 'unit')
- bias_first_grad: float32 [4, 1024], P(None, 'unit')
- lstm_second_grad: float32 [2560, 4, 1024], P('batch', None, 'unit')
- bias_second_grad: float32 [4, 1024], P(None, 'unit')
- frame_weight_grad: float32 [1536, 81], replicated
- frame_bias_grad: float32 [81], replicated
- post_first_grad: float32 [5, 80, 512], P(None, None, 'unit')
- post_middle_grad: float32 [3, 5, 512, 512], P(None, None, 'batch', 'unit')
- post_last_grad: float32 [5, 512, 80], P(None, 'batch', 'unit')
- middle_norm_grad: float32 [2, 4, 512], P(None, None, 'unit')
- last_norm_grad: float32 [2, 80], P(None, 'unit')
- memory_grad: float32 [2, 192, 64, 512], P(None, 'batch')
The draws below stay inside these ranges and needn't reach their ends.
Inputs may be any that keep to these rules, and one draw needn't show every extreme that they name: `segments`: each row numbers its frames by utterance in order, never falling; every one of the 3 utterances has 1 to 3 frames. `text_lengths`: the 3 counts of a row sum to 64.
All inputs are finite; a program needn't handle non-finite values. No bound on the sum of `zone_first` or of `zone_second` or of `drop_first` or of `drop_second` on one device may be relied on, other than what follows from the above.
Results may differ from the reference program's by a relative error of at most 0.03.
Values may be sent and summed in bfloat16 or wider, within the bound.
No kernel may reach another device: no remote copies, remote signals or barrier semaphores. Data moves between devices by JAX's collectives and lax.ppermute only.
A program may use at most 256 MiB of HBM per device.

```python
import math
import jax
import jax.numpy as jnp
import numpy as np
from jax import lax

HID = 1024
PRE = 256
ENC = 512
ATT = 128
FILT = 32
MEL = 80
PCH = 512
KW = 31
PKW = 5
STEPS = 6
SEGS = 3
SEG_MOST = 3
TEXT = 64
TEXT_MOST = 32
MICRO = 2
ROWS = 192
IN1 = 1792
IN2 = 2560
FRAME_IN = 1536


def place_ends(entries, stream_key, smallest, high):
    longest = entries.shape.index(max(entries.shape))
    spots = []
    for shift in (0, 1):
        where = [jax.random.randint(jax.random.fold_in(stream_key, axis), (), 0, length) for axis, length in enumerate(entries.shape)]
        where[longest] = (where[longest] + shift) % entries.shape[longest]
        spots.append(tuple(where))
    return entries.at[spots[0]].set(smallest).at[spots[1]].set(high)


def block_levels(rng, dims, cuts, smallest, top_value):
    def one(axis_at, blocks):
        heights = jax.random.uniform(jax.random.fold_in(jax.random.fold_in(rng, 6), axis_at), (blocks,), jnp.float32, smallest / len(cuts), top_value / len(cuts))
        return jnp.repeat(jnp.exp(heights), dims[axis_at] // blocks).reshape((-1,) + (1,) * (len(dims) - axis_at - 1))

    gain = one(*cuts[0])
    for cut in cuts[1:]:
        gain = gain * one(*cut)
    return gain


def profile(count, total, most, slope):
    weights = [(1 << 20) // math.isqrt(grade ** slope) + 1 for grade in range(2, count + 1)]
    surplus, holding = total - most - (count - 1), [1] * (count - 1)
    while surplus > 0:
        free = [i for i in range(count - 1) if holding[i] < most]
        whole, remaining = sum([weights[i] for i in free]), surplus
        for i in free:
            more = min(most - holding[i], max(1, remaining * weights[i] // whole), surplus)
            holding[i] = holding[i] + more
            surplus = surplus - more
    return np.array([most] + holding)


def ragged(key, number_of, total, most, skew):
    if number_of == 2:
        one = jax.random.randint(key, (), max(1, total - most), min(most, total - 1) + 1)
        return jnp.stack([one, total - one])
    lengths = jnp.asarray(profile(number_of, total, most, skew), jnp.int32)
    twos = (number_of - 1) // 2
    source_of, receiver = lengths[1:1 + 2 * twos:2], lengths[2:2 + 2 * twos:2]
    margin = jnp.minimum(source_of - 1, most - receiver)
    moved = jax.random.randint(jax.random.fold_in(key, 1), (twos,), 0, 1 << 20) % (margin + 1)
    lengths = lengths.at[1:1 + 2 * twos:2].set(source_of - moved).at[2:2 + 2 * twos:2].set(receiver + moved)
    return lengths[jax.random.permutation(jax.random.fold_in(key, 2), number_of)]


def scatter_about(stream_key, dims, width, bound, shards=(), kind=jnp.bfloat16):
    factor_of = block_levels(stream_key, dims, shards, -0.22, 0.18) if shards else 1.0
    result = jax.random.normal(stream_key, dims, jnp.float32) * width * factor_of
    return jnp.minimum(jnp.maximum(result, -bound), bound).astype(kind)


def setup_inputs(seed: int = 0) -> dict:
    streams_of = jax.random.split(jax.random.key(seed), 27)
    return {
        "memory": scatter_about(streams_of[0], (MICRO, ROWS, TEXT, ENC), 1.0, 6.0, ((1, 16),)),
        "targets": scatter_about(streams_of[1], (MICRO, ROWS, STEPS, MEL), 1.0, 6.0, ((1, 16),)),
        "segments": jax.vmap(lambda own: jnp.searchsorted(jnp.cumsum(ragged(own, SEGS, STEPS, SEG_MOST, 1)), jnp.arange(STEPS), side="right"))(jax.random.split(streams_of[2], MICRO * ROWS)).reshape((MICRO, ROWS, STEPS)).astype(jnp.int32),
        "text_lengths": jax.vmap(lambda own: ragged(own, SEGS, TEXT, TEXT_MOST, 1))(jax.random.split(streams_of[3], MICRO * ROWS)).reshape((MICRO, ROWS, SEGS)).astype(jnp.int32),
        "zone_first": place_ends((jax.random.randint(streams_of[4], (MICRO, ROWS, STEPS, HID), 0, 10) < 1).astype(jnp.int32), jax.random.fold_in(streams_of[4], 1), 0, 1),
        "zone_second": place_ends((jax.random.randint(streams_of[5], (MICRO, ROWS, STEPS, HID), 0, 10) < 1).astype(jnp.int32), jax.random.fold_in(streams_of[5], 1), 0, 1),
        "drop_first": place_ends((jax.random.randint(streams_of[6], (MICRO, ROWS, STEPS, PRE), 0, 2) < 1).astype(jnp.int32), jax.random.fold_in(streams_of[6], 1), 0, 1),
        "drop_second": place_ends((jax.random.randint(streams_of[7], (MICRO, ROWS, STEPS, PRE), 0, 2) < 1).astype(jnp.int32), jax.random.fold_in(streams_of[7], 1), 0, 1),
        "prenet_first": scatter_about(streams_of[8], (MEL, PRE), MEL ** -0.5, 0.625),
        "prenet_second": scatter_about(streams_of[9], (PRE, PRE), PRE ** -0.5, 0.375),
        "query_weight": scatter_about(streams_of[10], (HID, ATT), HID ** -0.5, 0.1875),
        "memory_weight": scatter_about(streams_of[11], (ENC, ATT), ENC ** -0.5, 0.25),
        "location_conv": scatter_about(streams_of[12], (FILT, 2, KW), (2 * KW) ** -0.5, 0.75),
        "location_dense": scatter_about(streams_of[13], (FILT, ATT), FILT ** -0.5, 1.0),
        "energy_vector": scatter_about(streams_of[14], (ATT,), 0.25, 1.5),
        "lstm_first": scatter_about(streams_of[15], (IN1, 4, HID), IN1 ** -0.5, 0.125, ((0, 16), (2, 2))),
        "bias_first": scatter_about(streams_of[16], (4, HID), 0.5, 3.0, ((1, 2),), jnp.float32),
        "lstm_second": scatter_about(streams_of[17], (IN2, 4, HID), IN2 ** -0.5, 0.125, ((0, 16), (2, 2))),
        "bias_second": scatter_about(streams_of[18], (4, HID), 0.5, 3.0, ((1, 2),), jnp.float32),
        "frame_weight": scatter_about(streams_of[19], (FRAME_IN, MEL + 1), FRAME_IN ** -0.5, 0.15625),
        "frame_bias": scatter_about(streams_of[20], (MEL + 1,), 0.5, 3.0, (), jnp.float32),
        "post_first": scatter_about(streams_of[21], (PKW, MEL, PCH), (PKW * MEL) ** -0.5, 0.3125, ((2, 2),)),
        "post_middle": scatter_about(streams_of[22], (3, PKW, PCH, PCH), (PKW * PCH) ** -0.5, 0.125, ((2, 16), (3, 2))),
        "post_last": scatter_about(streams_of[23], (PKW, PCH, MEL), (PKW * PCH) ** -0.5, 0.125, ((1, 16), (2, 2))),
        "middle_norm": jnp.clip(1.0 + 0.18 * jax.random.normal(streams_of[24], (2, 4, PCH), jnp.float32), 0.1, 1.9),
        "last_norm": jnp.clip(1.0 + 0.18 * jax.random.normal(streams_of[25], (2, MEL), jnp.float32), 0.1, 1.9),
    }


@jax.custom_vjp
def low(v):
    return lax.optimization_barrier(v.astype(jnp.bfloat16)).astype(jnp.float32)

@jax.custom_vjp
def low_back(v):
    return v

def low_keep(v):
    return (low(v), None)

def low_pass(kept, grad):
    return (grad,)

def back_keep(v):
    return (v, None)

def back_low(kept, grad):
    return (low(grad),)
low.defvjp(low_keep, low_pass)
low_back.defvjp(back_keep, back_low)
precise = lax.Precision.HIGHEST
norm_eps = 1e-05

def logistic_unit(values):
    return values * jax.nn.sigmoid(values)

def soft_plus(values):
    return jnp.maximum(values, 0.0) + jnp.log1p(jnp.exp(-jnp.abs(values)))

def frame_tables(segments, text_lengths, text_width):
    step_count = segments.shape[1]
    before = jnp.concatenate([jnp.full_like(segments[:, :1], -1), segments[:, :-1]], axis=1)
    following = jnp.concatenate([segments[:, 1:], jnp.full_like(segments[:, :1], -1)], axis=1)
    carry_on = (segments == before).astype(jnp.float32)
    finished = (segments != following).astype(jnp.float32)
    text_ends = jnp.cumsum(text_lengths, axis=1).astype(jnp.int32)
    positions = jnp.arange(text_width, dtype=jnp.int32)
    text_owner = lax.optimization_barrier(jnp.sum((positions[None, :, None] >= text_ends[:, None, :]).astype(jnp.int32), axis=2)).astype(jnp.int32)
    padded = jnp.pad(segments, ((0, 0), (2, 2)), constant_values=-1)
    tap_masks = jnp.stack([(padded[:, offset:offset + step_count] == segments).astype(jnp.float32) for offset in range(5)])
    return (carry_on, finished, text_owner, tap_masks)

def location_terms(previous_weights, cumulative, conv_kernel, dense_kernel):
    stacked = jnp.stack([previous_weights, cumulative], axis=1)
    reach = conv_kernel.shape[2] // 2
    features = lax.conv_general_dilated(stacked, conv_kernel, (1,), [(reach, reach)], dimension_numbers=('NCH', 'OIH', 'NCH'), precision=precise)
    return jnp.einsum('rft,fa->rta', features, dense_kernel, precision=precise)

def attention_weights(query_in, previous_weights, cumulative, processed, valid, query_weight, conv_kernel, dense_kernel, energy_vector):
    query_term = jnp.dot(query_in, query_weight, precision=precise)
    mixed = jnp.tanh(query_term[:, None, :] + processed + location_terms(previous_weights, cumulative, conv_kernel, dense_kernel))
    energy = jnp.einsum('rta,a->rt', mixed, energy_vector, precision=precise)
    energy = jnp.where(valid, energy, -1000000000.0)
    shifted = jnp.exp(energy - lax.optimization_barrier(jnp.max(energy, axis=1, keepdims=True)))
    return shifted / lax.optimization_barrier(jnp.sum(shifted, axis=1, keepdims=True))

def lstm_cell(gates, cell_prev, state_prev, zoneout):
    input_gate = jax.nn.sigmoid(gates[:, 0])
    forget_gate = jax.nn.sigmoid(gates[:, 1])
    candidate = jnp.tanh(gates[:, 2])
    output_gate = jax.nn.sigmoid(gates[:, 3])
    cell_new = forget_gate * cell_prev + input_gate * candidate
    state_new = output_gate * jnp.tanh(cell_new)
    return (zoneout * state_prev + (1.0 - zoneout) * state_new, zoneout * cell_prev + (1.0 - zoneout) * cell_new)

def post_conv(source, kernel, tap_masks):
    step_count = source.shape[1]
    padded = jnp.pad(source, ((0, 0), (2, 2), (0, 0)))
    summed = jnp.zeros(source.shape[:2] + (kernel.shape[2],), source.dtype)
    for offset in range(5):
        shifted = padded[:, offset:offset + step_count] * tap_masks[offset][:, :, None]
        summed = summed + jnp.einsum('rsc,co->rso', shifted, kernel[offset], precision=precise)
    return summed

def micro_loss(weights, memory, targets, segments, text_lengths, zone_first, zone_second, drop_first, drop_second):
    prenet_first, prenet_second, query_weight, memory_weight, location_conv, location_dense, energy_vector, lstm_first, bias_first, lstm_second, bias_second, frame_weight, frame_bias, post_first, post_middle, post_last, middle_norm, last_norm = weights
    row_count, step_count = segments.shape
    text_width = memory.shape[1]
    hidden_width = lstm_first.shape[2]
    mel_width = targets.shape[2]
    carry_on, finished, text_owner, tap_masks = frame_tables(segments, text_lengths, text_width)
    previous = jnp.concatenate([jnp.zeros_like(targets[:, :1]), targets[:, :-1]], axis=1) * carry_on[:, :, None]
    hidden = low(logistic_unit(jnp.einsum('rsm,mp->rsp', previous, prenet_first, precision=precise)) * drop_first * 2.0)
    prenet_out = low(logistic_unit(jnp.einsum('rsm,mp->rsp', hidden, prenet_second, precision=precise)) * drop_second * 2.0)
    processed = low_back(jnp.einsum('rtc,ca->rta', memory, memory_weight, precision=precise))
    matrix_one = lstm_first.reshape(lstm_first.shape[0], -1)
    matrix_two = lstm_second.reshape(lstm_second.shape[0], -1)
    bias_one = bias_first.reshape(-1)
    bias_two = bias_second.reshape(-1)

    def decode_step(carry, inputs):
        prenet_now, carry_now, zone_one, zone_two, segment_now = inputs
        factor = carry_now[:, None]
        state_one, cell_one, round_one, state_two, cell_two, round_two, context_round, weights_prev, weights_cum = [member * factor for member in carry]
        gates_one = low_back(jnp.dot(jnp.concatenate([prenet_now, context_round, round_one], axis=1), matrix_one, precision=precise) + bias_one)
        state_one, cell_one = lstm_cell(gates_one.reshape(row_count, 4, hidden_width), cell_one, state_one, zone_one)
        round_one = low(state_one)
        valid = text_owner == segment_now[:, None]
        alpha = attention_weights(round_one, weights_prev, weights_cum, processed, valid, query_weight, location_conv, location_dense, energy_vector)
        context_round = low(jnp.einsum('rt,rtc->rc', alpha, memory, precision=precise))
        gates_two = low_back(jnp.dot(jnp.concatenate([round_one, context_round, round_two], axis=1), matrix_two, precision=precise) + bias_two)
        state_two, cell_two = lstm_cell(gates_two.reshape(row_count, 4, hidden_width), cell_two, state_two, zone_two)
        round_two = low(state_two)
        new_carry = (state_one, cell_one, round_one, state_two, cell_two, round_two, context_round, alpha, weights_cum + alpha)
        return (new_carry, jnp.concatenate([round_two, context_round], axis=1))
    number_type = targets.dtype
    zero_state = jnp.zeros((row_count, hidden_width), number_type)
    zero_text = jnp.zeros((row_count, text_width), number_type)
    initial = (zero_state, zero_state, zero_state, zero_state, zero_state, zero_state, jnp.zeros((row_count, memory.shape[2]), number_type), zero_text, zero_text)
    step_inputs = (jnp.transpose(prenet_out, (1, 0, 2)), carry_on.T, jnp.transpose(zone_first, (1, 0, 2)), jnp.transpose(zone_second, (1, 0, 2)), segments.T)
    final_carry, frames = lax.scan(jax.checkpoint(decode_step), initial, step_inputs)
    frame_out = low_back(jnp.einsum('src,co->rso', frames, frame_weight, precision=precise) + frame_bias)
    mel_out = frame_out[:, :, :mel_width]
    stop_logit = frame_out[:, :, mel_width]
    kernels = [post_first, post_middle[0], post_middle[1], post_middle[2], post_last]
    gains = [middle_norm[0, layer] for layer in range(4)] + [last_norm[0]]
    shifts = [middle_norm[1, layer] for layer in range(4)] + [last_norm[1]]
    layer_in = low(mel_out)
    output = None
    for layer in range(5):
        pre_norm = low_back(post_conv(layer_in, kernels[layer], tap_masks))
        mean_now = lax.optimization_barrier(jnp.mean(pre_norm, axis=(0, 1)))
        variance = lax.optimization_barrier(jnp.mean(jnp.square(pre_norm - mean_now), axis=(0, 1)))
        output = (pre_norm - mean_now) * lax.rsqrt(variance + norm_eps) * gains[layer] + shifts[layer]
        if layer < 4:
            layer_in = low(jnp.tanh(output))
    post = mel_out + output
    loss = jnp.sum(lax.optimization_barrier(jnp.mean(jnp.square(mel_out - targets), axis=2)))
    loss = loss + jnp.sum(lax.optimization_barrier(jnp.mean(jnp.square(post - targets), axis=2)))
    loss = loss + jnp.sum(soft_plus(stop_logit) - finished * stop_logit)
    return loss / row_count

def reference(memory, targets, segments, text_lengths, zone_first, zone_second, drop_first, drop_second, prenet_first, prenet_second, query_weight, memory_weight, location_conv, location_dense, energy_vector, lstm_first, bias_first, lstm_second, bias_second, frame_weight, frame_bias, post_first, post_middle, post_last, middle_norm, last_norm):
    weights = tuple((member.astype(jnp.float32) for member in (prenet_first, prenet_second, query_weight, memory_weight, location_conv, location_dense, energy_vector, lstm_first, bias_first, lstm_second, bias_second, frame_weight, frame_bias, post_first, post_middle, post_last, middle_norm, last_norm)))
    totals = jax.tree.map(jnp.zeros_like, weights)
    memory_grads = []
    for micro in range(MICRO):

        def loss_of(weights_in, memory_in, micro=micro):
            return micro_loss(weights_in, memory_in, targets[micro].astype(jnp.float32), segments[micro], text_lengths[micro], zone_first[micro].astype(jnp.float32), zone_second[micro].astype(jnp.float32), drop_first[micro].astype(jnp.float32), drop_second[micro].astype(jnp.float32))
        loss_value, pullback = jax.vjp(loss_of, weights, memory[micro].astype(jnp.float32))
        weight_grads, memory_grad = pullback(jnp.ones_like(loss_value))
        totals = jax.tree.map(jnp.add, totals, weight_grads)
        memory_grads.append(memory_grad)
    return (totals[0], totals[1], totals[2], totals[3], totals[4], totals[5], totals[6], totals[7], totals[8], totals[9], totals[10], totals[11], totals[12], totals[13], totals[14], totals[15], totals[16], totals[17], jnp.stack(memory_grads))
```

```python
import functools

import jax
import jax.numpy as jnp
from jax import lax
from jax.experimental import pallas as pl
from jax.experimental.pallas import tpu as pltpu
from jax.sharding import PartitionSpec as P

precise = lax.Precision.HIGHEST
norm_eps = 1e-05
f32 = jnp.float32
bf16 = jnp.bfloat16
lanes = 128
kernel_vmem = 60 * 1024 * 1024


def split(value):
    high = value.astype(bf16)
    return high, (value - high.astype(f32)).astype(bf16)


def dot(a, b, contract=((1,), (0,))):
    return lax.dot_general(a, b, (contract, ((), ())), preferred_element_type=f32)


def dot_left(exact, value, contract=((1,), (0,))):
    high, low = split(value)
    return dot(exact, high, contract) + dot(exact, low, contract)


def dot_right(value, exact, contract=((1,), (0,))):
    high, low = split(value)
    return dot(high, exact, contract) + dot(low, exact, contract)


def dot_both(a, b, contract=((1,), (0,))):
    a_high, a_low = split(a)
    b_high, b_low = split(b)
    return (
        dot(a_high, b_high, contract) + dot(a_low, b_high, contract) + dot(a_high, b_low, contract)
    )


rows_first = ((0,), (0,))
lanes_both = ((1,), (1,))


def position_hot(position_count, text_width, reverse):
    place = lax.broadcasted_iota(jnp.int32, (position_count, lanes), 0) & (text_width - 1)
    lane = lax.broadcasted_iota(jnp.int32, (position_count, lanes), 1)
    place = (lanes - 1) - place if reverse else place + 1
    return (place == lane).astype(bf16)


def slant(value, text_width):
    blocks = [
        pltpu.roll(value[start : start + text_width], 0, 1, stride=1, stride_axis=0)
        for start in range(0, value.shape[0], text_width)
    ]
    return jnp.concatenate(blocks, axis=0)


def pad_rows(value):
    return jnp.concatenate(
        [value, jnp.zeros((lanes - value.shape[0], value.shape[1]), value.dtype)], axis=0
    )


def unit_spot(chunk, unit, per_half):
    half = (chunk // per_half + unit) % 2
    return pl.multiple_of((half * per_half + chunk % per_half) * lanes, lanes)


def gate_spot(chunk, gate, per_half):
    start = (chunk // per_half) * 4 * per_half + gate * per_half + chunk % per_half
    return pl.multiple_of(start * lanes, lanes)


def forward_kernel(
    unit_ref,
    own_one,
    peer_one,
    own_two,
    peer_two,
    previous_ref,
    drop_one,
    drop_two,
    layer_one,
    layer_two,
    slot_ref,
    zone_one,
    zone_two,
    bias_one,
    bias_two,
    hot_ref,
    memory_ref,
    project_ref,
    query_ref,
    vector_ref,
    conv_ref,
    dense_ref,
    frame_ref,
    frame_bias,
    gates_one,
    gates_two,
    prior_one,
    prior_two,
    round_one,
    round_two,
    context_ref,
    mixed_ref,
    alpha_ref,
    taps_ref,
    prenet_one,
    prenet_two,
    prenet_hidden,
    prenet_out,
    frame_out,
    held_one,
    held_two,
    input_ref,
    prenet_ref,
    processed_ref,
    filter_ref,
    state_one,
    cell_one,
    state_two,
    cell_two,
    sems,
):
    unit = unit_ref[0]
    steps, slots, hidden = round_one.shape
    prenet_width = layer_two.shape[1]
    context_width = context_ref.shape[2]
    half = hidden // 2
    per_half = half // lanes
    position_count = hot_ref.shape[0]
    text_width = position_count // (slots // 4)
    copies_two = [
        pltpu.make_async_copy(own_two, held_two.at[0], sems.at[0]),
        pltpu.make_async_copy(peer_two, held_two.at[1], sems.at[1]),
    ]
    copies_one = [
        pltpu.make_async_copy(own_one, held_one.at[0], sems.at[2]),
        pltpu.make_async_copy(peer_one, held_one.at[1], sems.at[3]),
    ]
    for copy in copies_two + copies_one:
        copy.start()
    for ref in (state_one, cell_one, state_two, cell_two):
        ref[...] = jnp.zeros_like(ref)

    def gates_into(held, depth, bias_ref, out_ref, step):
        def one(block, _):
            side = block // 4
            inputs = input_ref[:, :depth]
            for pair in range(per_half // 2):
                tile = (block % 4) * per_half + 2 * pair
                outside = pl.ds(
                    pl.multiple_of(block * half + 2 * pair * lanes, 2 * lanes), 2 * lanes
                )
                kernel = jnp.concatenate(
                    [held[side, tile, :depth, :], held[side, tile + 1, :depth, :]], axis=1
                )
                out_ref[step, :, outside] = dot(inputs, kernel) + bias_ref[:, outside]
            return 0

        lax.fori_loop(0, 8, one, 0)

    def cell(gates_ref, zone_ref, prior_ref, state, cells, round_ref, step):
        def one(chunk, _):
            spot = pl.ds(pl.multiple_of(chunk * lanes, lanes), lanes)
            values = [
                gates_ref[step, :, pl.ds(gate_spot(chunk, gate, per_half), lanes)]
                for gate in range(4)
            ]
            zone = zone_ref[step, :, spot]
            before = cells[:, spot]
            prior_ref[step, :, spot] = before
            fresh = jax.nn.sigmoid(values[1]) * before + jax.nn.sigmoid(values[0]) * jnp.tanh(
                values[2]
            )
            output = jax.nn.sigmoid(values[3]) * jnp.tanh(fresh)
            now = zone * state[:, spot] + (1.0 - zone) * output
            state[:, spot] = now
            cells[:, spot] = zone * before + (1.0 - zone) * fresh
            round_ref[step, :, pl.ds(unit_spot(chunk, unit, per_half), lanes)] = now.astype(bf16).astype(
                f32
            )
            return 0

        lax.fori_loop(0, 2 * per_half, one, 0)

    def attention(step, location):
        inside = hot_ref[...] > 0.0
        hot = hot_ref[...].astype(bf16)
        query = pad_rows(dot(round_one[step].astype(bf16), query_ref[...].astype(bf16)))
        summed = dot_left(hot, query) + processed_ref[...]
        if location is not None:
            summed = summed + location
        mixed = jnp.tanh(summed)
        mixed_ref[step] = mixed
        energy = dot_right(mixed, vector_ref[...].astype(bf16))
        most = jnp.max(jnp.where(inside, energy, -1000000000.0), axis=0, keepdims=True)
        shifted = jnp.where(inside, jnp.exp(energy - most), 0.0)
        total = jnp.sum(shifted, axis=0, keepdims=True)
        alpha = shifted / jnp.where(total > 0.0, total, 1.0)
        alpha_ref[step] = alpha
        context = dot_right(alpha, memory_ref[...].astype(bf16), rows_first)[:slots]
        context_ref[step] = context.astype(bf16).astype(f32)

    def taps_of(step):
        spread = dot_right(
            alpha_ref[step], position_hot(position_count, text_width, True), rows_first
        )
        taps_ref[step] = slant(dot_left(hot_ref[...].astype(bf16), spread), text_width)

    def second_layer(step, depth):
        input_ref[:, :hidden] = round_one[step].astype(bf16)
        input_ref[:, hidden : hidden + context_width] = context_ref[step].astype(bf16)
        gates_into(held_two, depth, bias_two, gates_two, step)
        cell(gates_two, zone_two, prior_two, state_two, cell_two, round_two, step)

    slot_hot = slot_ref[...].astype(bf16)

    def prenet_layer(source, layer, drops, mixed_out, out):
        mixed = dot(source.astype(bf16), layer[...].astype(bf16))
        mixed_out[...] = mixed
        value = (mixed * jax.nn.sigmoid(mixed) * drops[...] * 2.0).astype(bf16)
        out[...] = value.astype(f32)
        return value

    hidden_value = prenet_layer(previous_ref[...], layer_one, drop_one, prenet_one, prenet_hidden)
    prenet_value = prenet_layer(hidden_value, layer_two, drop_two, prenet_two, prenet_out)
    prenet_slots = dot(slot_hot, prenet_value, rows_first)
    for step in range(steps):
        prenet_ref[step] = prenet_slots[step * slots : (step + 1) * slots]
    processed_ref[...] = dot(memory_ref[...].astype(bf16), project_ref[...].astype(bf16))
    for channel in range(2):
        filter_ref[channel] = dot(
            conv_ref[channel].astype(bf16), dense_ref[...].astype(bf16)
        )

    gates_one[0] = jnp.broadcast_to(bias_one[...], gates_one.shape[1:])
    cell(gates_one, zone_one, prior_one, state_one, cell_one, round_one, 0)
    attention(0, None)
    taps_of(0)
    for copy in copies_two:
        copy.wait()
    second_layer(0, hidden + context_width)
    for copy in copies_one:
        copy.wait()

    def later(step, _):
        input_ref[:, :prenet_width] = prenet_ref[step].astype(bf16)
        input_ref[:, prenet_width : prenet_width + context_width] = context_ref[step - 1].astype(
            bf16
        )
        input_ref[:, prenet_width + context_width : prenet_width + context_width + hidden] = (
            round_one[step - 1].astype(bf16)
        )
        gates_into(
            held_one, prenet_width + context_width + hidden, bias_one, gates_one, step
        )
        cell(gates_one, zone_one, prior_one, state_one, cell_one, round_one, step)
        previous = taps_ref[step - 1]
        summed = jnp.where(step == 2, taps_ref[0] + previous, previous)
        attention(step, dot_both(previous, filter_ref[0]) + dot_both(summed, filter_ref[1]))

        @pl.when(step < steps - 1)
        def _():
            taps_of(step)

        input_ref[:, hidden + context_width :] = round_two[step - 1].astype(bf16)
        second_layer(step, 2 * hidden + context_width)
        return 0

    lax.fori_loop(1, steps, later, 0)
    for step in range(steps):
        values = dot(round_two[step].astype(bf16), frame_ref[:hidden].astype(bf16)) + dot(
            context_ref[step].astype(bf16), frame_ref[hidden:].astype(bf16)
        )
        high = values.astype(bf16)
        rest = values - high.astype(f32)
        middle = rest.astype(bf16)
        low = (rest - middle.astype(f32)).astype(bf16)
        chosen = slot_hot[:, step * slots : (step + 1) * slots]
        picked = (dot(chosen, high) + dot(chosen, middle)) + dot(chosen, low)
        frame_out[...] = (frame_bias[...] if step == 0 else frame_out[...]) + picked


def backward_kernel(
    unit_ref,
    own_one,
    peer_one,
    own_two,
    peer_two,
    gates_one,
    gates_two,
    prior_one,
    prior_two,
    zone_one,
    zone_two,
    hot_ref,
    memory_ref,
    query_ref,
    vector_ref,
    conv_ref,
    dense_ref,
    mixed_ref,
    alpha_ref,
    taps_ref,
    frame_grad,
    frame_weight,
    grads_one,
    grads_two,
    prenet_grad,
    context_grad,
    query_grad,
    processed_grad,
    vector_grad,
    filter_grad,
    held_one,
    held_two,
    back_one,
    back_two,
    state_one,
    cell_one,
    state_two,
    cell_two,
    previous_grad,
    summed_grad,
    from_query,
    frame_ref,
    filter_ref,
    sems,
):
    unit = unit_ref[0]
    steps, slots, prenet_width = prenet_grad.shape
    context_width = context_grad.shape[2]
    hidden = state_one.shape[1]
    half = hidden // 2
    per_half = half // lanes
    position_count = hot_ref.shape[0]
    text_width = position_count // (slots // 4)
    copies_two = [
        pltpu.make_async_copy(own_two, held_two.at[0], sems.at[0]),
        pltpu.make_async_copy(peer_two, held_two.at[1], sems.at[1]),
    ]
    copies_one = [
        pltpu.make_async_copy(own_one, held_one.at[0], sems.at[2]),
        pltpu.make_async_copy(peer_one, held_one.at[1], sems.at[3]),
    ]
    for copy in copies_two + copies_one:
        copy.start()
    for ref in (
        state_one,
        cell_one,
        state_two,
        cell_two,
        back_one,
        back_two,
        previous_grad,
        summed_grad,
        processed_grad,
        vector_grad,
        filter_grad,
    ):
        ref[...] = jnp.zeros_like(ref)

    def cell(gates_ref, prior_ref, zone_ref, state, cells, grads_ref, step, incoming):
        def one(chunk, _):
            spot = pl.ds(pl.multiple_of(chunk * lanes, lanes), lanes)
            places = [pl.ds(gate_spot(chunk, gate, per_half), lanes) for gate in range(4)]
            values = [gates_ref[step, :, place] for place in places]
            zone = zone_ref[step, :, spot]
            keep = 1.0 - zone
            before = prior_ref[step, :, spot]
            gate_in = jax.nn.sigmoid(values[0])
            gate_forget = jax.nn.sigmoid(values[1])
            candidate = jnp.tanh(values[2])
            gate_out = jax.nn.sigmoid(values[3])
            bent = jnp.tanh(gate_forget * before + gate_in * candidate)
            grad_state = incoming(unit_spot(chunk, unit, per_half)) + state[:, spot]
            grad_cell = cells[:, spot]
            grad_new = keep * grad_state
            grad_fresh = grad_new * gate_out * (1.0 - bent * bent) + keep * grad_cell
            state[:, spot] = zone * grad_state
            cells[:, spot] = zone * grad_cell + gate_forget * grad_fresh
            results = (
                grad_fresh * candidate * gate_in * (1.0 - gate_in),
                grad_fresh * before * gate_forget * (1.0 - gate_forget),
                grad_fresh * gate_in * (1.0 - candidate * candidate),
                grad_new * bent * gate_out * (1.0 - gate_out),
            )
            for place, result in zip(places, results):
                grads_ref[step, :, place] = result.astype(bf16).astype(f32)
            return 0

        lax.fori_loop(0, 2 * per_half, one, 0)

    def inputs_back(grads_ref, held, out_ref, step, blocks):
        def one(block, _):
            spot = pl.ds(pl.multiple_of(block * 256, 256), 256)
            total = None
            for tile in range(0, 8 * per_half, 2):
                side, inside = tile // (4 * per_half), tile % (4 * per_half)
                kernel = jnp.concatenate(
                    [held[side, inside, spot, :], held[side, inside + 1, spot, :]], axis=1
                )
                grads = grads_ref[step, :, tile * lanes : (tile + 2) * lanes].astype(bf16)
                product = dot(grads, kernel, lanes_both)
                total = product if total is None else total + product
            out_ref[:, spot] = total
            return 0

        lax.fori_loop(0, blocks, one, 0)

    def attention(step, located):
        inside = hot_ref[...] > 0.0
        hot = hot_ref[...].astype(bf16)
        alpha = alpha_ref[step]
        mixed = mixed_ref[step]
        context_now = pad_rows(context_grad[step])
        weights_grad = jnp.where(
            inside,
            dot_left(memory_ref[...].astype(bf16), context_now, lanes_both)
            + previous_grad[...]
            + summed_grad[...],
            0.0,
        )
        product = alpha * weights_grad
        energy_grad = product - alpha * jnp.sum(product, axis=0, keepdims=True)
        spread = jnp.sum(energy_grad, axis=1, keepdims=True)
        vector_grad[...] += jnp.sum(spread * mixed, axis=0, keepdims=True)
        mixed_grad = spread * vector_ref[...] * (1.0 - mixed * mixed)
        processed_grad[...] += mixed_grad
        high, low = split(mixed_grad)
        query_now = (dot(hot, high, rows_first) + dot(hot, low, rows_first))[:slots]
        query_grad[step] = query_now
        from_query[...] = dot_right(query_now, query_ref[...].astype(bf16), lanes_both)
        if located:
            previous = taps_ref[step - 1]
            summed = jnp.where(step == 2, taps_ref[0] + previous, previous)
            filter_grad[0] += dot_both(previous, mixed_grad, rows_first)
            filter_grad[1] += dot_both(summed, mixed_grad, rows_first)
            place_hot = position_hot(position_count, text_width, False)

            def taps_back(channel):
                taps_grad = slant(
                    dot_both(mixed_grad, filter_ref[channel], lanes_both), text_width
                )
                gathered = dot_right(taps_grad, hot, rows_first)
                return jnp.where(inside, dot_left(place_hot, gathered), 0.0)

            previous_grad[...] = taps_back(0)
            summed_grad[...] += taps_back(1)

    def step_back(step, located):
        cell(
            gates_two,
            prior_two,
            zone_two,
            state_two,
            cell_two,
            grads_two,
            step,
            lambda spot: frame_ref[step, :, pl.ds(spot, lanes)]
            + back_two[:, pl.ds(spot + hidden + context_width, lanes)],
        )
        blocks_two = (hidden + context_width + (hidden if located else 0)) // 256
        inputs_back(grads_two, held_two, back_two, step, blocks_two)
        context_grad[step] = (
            back_two[:, hidden : hidden + context_width]
            + frame_ref[step, :, hidden:]
            + back_one[:, prenet_width : prenet_width + context_width]
        )
        attention(step, located)
        cell(
            gates_one,
            prior_one,
            zone_one,
            state_one,
            cell_one,
            grads_one,
            step,
            lambda spot: back_two[:, pl.ds(spot, lanes)]
            + from_query[:, pl.ds(spot, lanes)]
            + back_one[:, pl.ds(spot + prenet_width + context_width, lanes)],
        )
        blocks_one = (prenet_width + (hidden + context_width if located else 0)) // 256
        inputs_back(grads_one, held_one, back_one, step, blocks_one)
        prenet_grad[step] = back_one[:, :prenet_width]

    for channel in range(2):
        filter_ref[channel] = dot(
            conv_ref[channel].astype(bf16), dense_ref[...].astype(bf16)
        )
    for step in range(steps):
        frame_ref[step] = dot(
            frame_grad[step].astype(bf16), frame_weight[...].astype(bf16), lanes_both
        )
    for copy in copies_two + copies_one:
        copy.wait()

    def later(index, _):
        step_back(steps - 1 - index, True)
        return 0

    lax.fori_loop(0, steps - 1, later, 0)
    step_back(0, False)


def call_forward(unit, weights, small, sizes):
    own_one, peer_one, own_two, peer_two = weights
    steps, slots, hidden, context_width, positions, frame_rows, prenet_width = sizes

    def shape(*dims):
        return jax.ShapeDtypeStruct(dims, f32)

    outs = [
        shape(steps, slots, 4 * hidden),
        shape(steps, slots, 4 * hidden),
        shape(steps, slots, hidden),
        shape(steps, slots, hidden),
        shape(steps, slots, hidden),
        shape(steps, slots, hidden),
        shape(steps, slots, context_width),
        shape(steps, positions, lanes),
        shape(steps, positions, lanes),
        shape(steps - 1, positions, lanes),
        shape(frame_rows, prenet_width),
        shape(frame_rows, prenet_width),
        shape(frame_rows, prenet_width),
        shape(frame_rows, prenet_width),
        shape(frame_rows, lanes),
    ]
    vmem = pl.BlockSpec(memory_space=pltpu.VMEM)
    return pl.pallas_call(
        forward_kernel,
        out_shape=outs,
        in_specs=[pl.BlockSpec(memory_space=pltpu.SMEM)]
        + [pl.BlockSpec(memory_space=pl.ANY)] * 4
        + [vmem] * len(small),
        out_specs=[vmem] * len(outs),
        scratch_shapes=[
            pltpu.VMEM((2,) + own_one.shape, bf16),
            pltpu.VMEM((2,) + own_two.shape, bf16),
            pltpu.VMEM((slots, own_two.shape[1]), bf16),
            pltpu.VMEM((steps, slots, prenet_width), f32),
            pltpu.VMEM((positions, lanes), f32),
            pltpu.VMEM((2, lanes, lanes), f32),
            pltpu.VMEM((slots, hidden), f32),
            pltpu.VMEM((slots, hidden), f32),
            pltpu.VMEM((slots, hidden), f32),
            pltpu.VMEM((slots, hidden), f32),
            pltpu.SemaphoreType.DMA((4,)),
        ],
        compiler_params=pltpu.CompilerParams(vmem_limit_bytes=kernel_vmem),
        name="decoder_forward",
    )(unit, *weights, *small)


def call_backward(unit, weights, small):
    own_one, peer_one, own_two, peer_two = weights
    gates_one = small[0]
    steps, slots, gate_width = gates_one.shape
    hidden = gate_width // 4
    positions, context_width = small[7].shape
    prenet_width = own_one.shape[1] - hidden - context_width

    def shape(dims, kind):
        return jax.ShapeDtypeStruct(dims, kind)

    outs = [
        shape((steps, slots, gate_width), f32),
        shape((steps, slots, gate_width), f32),
        shape((steps, slots, prenet_width), f32),
        shape((steps, slots, context_width), f32),
        shape((steps, slots, lanes), f32),
        shape((positions, lanes), f32),
        shape((1, lanes), f32),
        shape((2, lanes, lanes), f32),
    ]
    vmem = pl.BlockSpec(memory_space=pltpu.VMEM)
    return pl.pallas_call(
        backward_kernel,
        out_shape=outs,
        in_specs=[pl.BlockSpec(memory_space=pltpu.SMEM)]
        + [pl.BlockSpec(memory_space=pl.ANY)] * 4
        + [vmem] * len(small),
        out_specs=[vmem] * len(outs),
        scratch_shapes=[
            pltpu.VMEM((2,) + own_one.shape, bf16),
            pltpu.VMEM((2,) + own_two.shape, bf16),
            pltpu.VMEM((slots, own_one.shape[1]), f32),
            pltpu.VMEM((slots, own_two.shape[1]), f32),
            pltpu.VMEM((slots, hidden), f32),
            pltpu.VMEM((slots, hidden), f32),
            pltpu.VMEM((slots, hidden), f32),
            pltpu.VMEM((slots, hidden), f32),
            pltpu.VMEM((positions, lanes), f32),
            pltpu.VMEM((positions, lanes), f32),
            pltpu.VMEM((slots, hidden), f32),
            pltpu.VMEM((steps, slots, hidden + context_width), f32),
            pltpu.VMEM((2, lanes, lanes), f32),
            pltpu.SemaphoreType.DMA((4,)),
        ],
        compiler_params=pltpu.CompilerParams(vmem_limit_bytes=kernel_vmem),
        name="decoder_backward",
    )(unit, *weights, *small)


def postnet_kernel(
    mel_width,
    loss_scale,
    unit_ref,
    mel_ref,
    target_ref,
    mask_ref,
    first_ref,
    own_ref,
    peer_ref,
    last_ref,
    gain_ref,
    shift_ref,
    inputs_first,
    inputs_later,
    grads_early,
    grads_last,
    norm_grads,
    mel_grad,
    padded,
    padded_mel,
    held,
    normed_early,
    normed_last,
    inverse_ref,
    post_grad,
):
    unit = unit_ref[0]
    count, channels = held.shape
    side = channels // 2
    frames = padded.shape[0] - count
    rows_each = frames // 4
    chunk = 2 * rows_each
    tall = float(count)
    body_rows = slice(2 * rows_each, 2 * rows_each + count)

    for ref in (padded, padded_mel):
        ref[: 2 * rows_each] = jnp.zeros((2 * rows_each, ref.shape[1]), bf16)
        ref[2 * rows_each + count :] = jnp.zeros((2 * rows_each, ref.shape[1]), bf16)

    def piece(source, start, tap, width, lane=None):
        spot = pl.ds(pl.multiple_of(start + tap * rows_each, rows_each), chunk)
        mask = mask_ref[tap, pl.ds(pl.multiple_of(start, rows_each), chunk), :]
        if width < lanes:
            mask = mask[:, :width]
        else:
            mask = jnp.concatenate([mask] * (width // lanes), axis=1)
        value = source[spot, :] if lane is None else source[spot, pl.ds(lane, width)]
        return value * mask

    def chunks(work):
        def one(index, _):
            work(pl.multiple_of(index * chunk, chunk))
            return 0

        lax.fori_loop(0, count // chunk, one, 0)

    def half_spot(which):
        return pl.multiple_of(((which + unit) % 2) * side, side)

    def norm_forward(value, layer, lane, width):
        mean = jnp.sum(value, axis=0, keepdims=True) / tall
        centered = value - mean
        inverse = lax.rsqrt(jnp.sum(centered * centered, axis=0, keepdims=True) / tall + norm_eps)
        inverse_ref[layer, :, pl.ds(lane, width)] = inverse
        return centered * inverse

    def each_lane_block(work):
        def one(index, _):
            work(pl.multiple_of(index * lanes, lanes))
            return 0

        lax.fori_loop(0, channels // lanes, one, 0)

    def activate(layer):
        def block(lane):
            spot = pl.ds(lane, lanes)
            normed = norm_forward(held[:, spot], layer, lane, lanes)
            normed_early[layer, :, spot] = normed
            active = jnp.tanh(
                normed * gain_ref[layer, :, spot] + shift_ref[layer, :, spot]
            ).astype(bf16)
            inputs_later[layer, :, spot] = active
            padded[body_rows, spot] = active

        each_lane_block(block)

    source = mel_ref[...].astype(bf16)
    inputs_first[...] = source
    padded_mel[body_rows] = source

    def first_chunk(start):
        total = None
        for tap in range(5):
            product = dot(piece(padded_mel, start, tap, mel_width), first_ref[tap])
            total = product if total is None else total + product
        held[pl.ds(start, chunk), :] = total

    chunks(first_chunk)
    activate(0)

    def middle(index, _):
        for which, ref in ((0, own_ref), (1, peer_ref)):

            def middle_chunk(start, which=which, ref=ref):
                total = None
                for tap in range(5):
                    product = dot(piece(padded, start, tap, channels), ref[index, tap])
                    total = product if total is None else total + product
                held[pl.ds(start, chunk), pl.ds(half_spot(which), side)] = total

            chunks(middle_chunk)
        activate(index + 1)
        return 0

    lax.fori_loop(0, 3, middle, 0)

    def last_chunk(start):
        total = None
        for tap in range(5):
            product = dot(piece(padded, start, tap, channels), last_ref[tap])
            total = product if total is None else total + product
        normed_last[pl.ds(start, chunk), :] = total

    chunks(last_chunk)
    normed = norm_forward(normed_last[...], 4, 0, mel_width)
    normed_last[...] = normed

    def norm_back(grad, normed, layer, lane, width):
        spot = pl.ds(lane, width)
        shift_grad = jnp.sum(grad, axis=0, keepdims=True)
        gain_grad = jnp.sum(grad * normed, axis=0, keepdims=True)
        norm_grads[0, layer, :, spot] = gain_grad
        norm_grads[1, layer, :, spot] = shift_grad
        return (
            gain_ref[layer, :, spot]
            * inverse_ref[layer, :, spot]
            * (grad - shift_grad / tall - normed * (gain_grad / tall))
        ).astype(bf16)

    output = normed * gain_ref[4, :, :mel_width] + shift_ref[4, :, :mel_width]
    grad = loss_scale * (mel_ref[...] + output - target_ref[...])
    post_grad[...] = grad
    grad_norm = norm_back(grad, normed, 4, 0, mel_width)
    grads_last[...] = grad_norm
    padded_mel[body_rows] = grad_norm

    def last_back(start):
        total = None
        for tap in range(5):
            product = dot(
                piece(padded_mel, start, tap, mel_width), last_ref[4 - tap], lanes_both
            )
            total = product if total is None else total + product
        held[pl.ds(start, chunk), :] = total

    chunks(last_back)

    def deactivate(layer):
        def block(lane):
            spot = pl.ds(lane, lanes)
            normed = normed_early[layer, :, spot]
            active = jnp.tanh(normed * gain_ref[layer, :, spot] + shift_ref[layer, :, spot])
            grad = held[:, spot] * (1.0 - active * active)
            grad_norm = norm_back(grad, normed, layer, lane, lanes)
            grads_early[layer, :, spot] = grad_norm
            padded[body_rows, spot] = grad_norm

        each_lane_block(block)

    def middle_back(back, _):
        index = 2 - back
        deactivate(index + 1)

        def chunk_back(start):
            total = None
            for which, ref in ((0, own_ref), (1, peer_ref)):
                for tap in range(5):
                    product = dot(
                        piece(padded, start, tap, side, half_spot(which)),
                        ref[index, 4 - tap],
                        lanes_both,
                    )
                    total = product if total is None else total + product
            held[pl.ds(start, chunk), :] = total

        chunks(chunk_back)
        return 0

    lax.fori_loop(0, 3, middle_back, 0)
    deactivate(0)

    def first_back(start):
        total = None
        for tap in range(5):
            product = dot(piece(padded, start, tap, channels), first_ref[4 - tap], lanes_both)
            total = product if total is None else total + product
        spot = pl.ds(start, chunk)
        mel_grad[spot, :] = (
            loss_scale * (mel_ref[spot, :] - target_ref[spot, :]) + post_grad[spot, :] + total
        )

    chunks(first_back)


def call_postnet(unit, small, loss_scale, rows_all):
    mel = small[0]
    count, mel_width = mel.shape
    channels = small[3].shape[2]

    def shape(kind, *dims):
        return jax.ShapeDtypeStruct(dims, kind)

    outs = [
        shape(bf16, count, mel_width),
        shape(bf16, 4, count, channels),
        shape(bf16, 4, count, channels),
        shape(bf16, count, mel_width),
        shape(f32, 2, 5, 1, channels),
        shape(f32, count, mel_width),
    ]
    vmem = pl.BlockSpec(memory_space=pltpu.VMEM)
    tall = count + 4 * rows_all
    return pl.pallas_call(
        functools.partial(postnet_kernel, mel_width, loss_scale),
        out_shape=outs,
        in_specs=[pl.BlockSpec(memory_space=pltpu.SMEM)] + [vmem] * len(small),
        out_specs=[vmem] * len(outs),
        scratch_shapes=[
            pltpu.VMEM((tall, channels), bf16),
            pltpu.VMEM((tall, mel_width), bf16),
            pltpu.VMEM((count, channels), f32),
            pltpu.VMEM((4, count, channels), f32),
            pltpu.VMEM((count, mel_width), f32),
            pltpu.VMEM((5, 1, channels), f32),
            pltpu.VMEM((count, mel_width), f32),
        ],
        compiler_params=pltpu.CompilerParams(vmem_limit_bytes=kernel_vmem),
        name="postnet",
    )(unit, *small)


def shifted_frames(source, same):
    steps = source.shape[0]
    padded = jnp.pad(source, ((2, 2), (0, 0), (0, 0)))
    return [
        padded[offset : offset + steps] * same[:, :, offset, None].astype(source.dtype)
        for offset in range(5)
    ]


def by_rows(work, roomy, arrays, summed=False):
    if roomy:
        return work(*arrays)
    parts = arrays[0].shape[1] // 192

    def cut(value):
        value = value.reshape((value.shape[0], parts, -1) + value.shape[2:])
        return jnp.moveaxis(value, 1, 0)

    pieces = tuple(cut(value) for value in arrays)
    if summed:
        first = jax.eval_shape(work, *[value[0] for value in pieces])
        start = jnp.zeros(first.shape, first.dtype)
        return lax.scan(lambda total, now: (total + work(*now), None), start, pieces)[0]
    result = jnp.moveaxis(lax.map(lambda now: work(*now), pieces), 0, 1)
    return result.reshape((result.shape[0], -1) + result.shape[3:])


def post_layer(source, kernel, same):
    wide = jnp.concatenate(shifted_frames(source, same), axis=2)
    return jnp.einsum(
        "src,co->sro", wide, kernel.reshape(-1, kernel.shape[2]), preferred_element_type=f32
    )


def post_layer_back(grad, kernel, same):
    wide = jnp.concatenate(shifted_frames(grad, same), axis=2)
    turned = jnp.transpose(kernel[::-1], (0, 2, 1)).reshape(-1, kernel.shape[1])
    return jnp.einsum("sro,oc->src", wide, turned, preferred_element_type=f32)


def post_kernel_grad(source, grad, same):
    wide = jnp.concatenate(shifted_frames(source, same), axis=2)
    return jnp.einsum("src,sro->co", wide, grad, preferred_element_type=f32)


def on_device(
    memory,
    targets,
    segments,
    text_lengths,
    zone_first,
    zone_second,
    drop_first,
    drop_second,
    prenet_first,
    prenet_second,
    query_weight,
    memory_weight,
    location_conv,
    location_dense,
    energy_vector,
    lstm_first,
    bias_first,
    lstm_second,
    bias_second,
    frame_weight,
    frame_bias,
    post_first,
    post_middle,
    post_last,
    middle_norm,
    last_norm,
):
    micro_count, rows, text_width, memory_width = memory.shape
    frames = segments.shape[2]
    utterances = text_lengths.shape[2]
    mel_width = targets.shape[3]
    hidden = query_weight.shape[0]
    prenet_width = prenet_first.shape[1]
    attention_width = query_weight.shape[1]
    half = lstm_first.shape[2]
    depth_one, depth_two = lstm_first.shape[0], lstm_second.shape[0]
    unit = lax.axis_index("unit")
    place = lax.axis_index("batch")
    batch_size = lax.axis_size("batch")
    total_rows = rows * batch_size
    frame_count = float(total_rows * frames)
    first_unit = unit == 0
    longest = 3
    slots = 4 * rows

    def exchange(value):
        return lax.ppermute(value, "unit", [(0, 1), (1, 0)])

    def ordered(own, peer):
        return jnp.where(first_unit, own, peer), jnp.where(first_unit, peer, own)

    def whole(value, axis):
        return jnp.concatenate(ordered(value, exchange(value)), axis=axis)

    def mine(value):
        return lax.dynamic_index_in_dim(value, unit, 0, keepdims=False)

    def others(value):
        return lax.dynamic_index_in_dim(value, 1 - unit, 0, keepdims=False)

    def gather_tiles(value):
        tiles = jnp.transpose(value.reshape(value.shape[0], -1, lanes), (1, 0, 2))
        return lax.all_gather(tiles, "batch", axis=1, tiled=True)

    own_two = gather_tiles(lstm_second)
    own_one = gather_tiles(lstm_first)
    peer_two = exchange(own_two)
    peer_one = exchange(own_one)
    weights = (own_one, peer_one, own_two, peer_two)
    middle_half = lax.all_gather(post_middle, "batch", axis=2, tiled=True)
    last_half = lax.all_gather(post_last.astype(f32), "batch", axis=1, tiled=True)
    memory_now = mine(memory).reshape(rows * text_width, memory_width)
    segments_now = mine(segments)
    targets_now = mine(targets)
    frame_info = lax.all_gather(
        jnp.concatenate([targets_now, segments_now[:, :, None].astype(bf16)], axis=2).astype(f32),
        "batch",
        axis=0,
        tiled=True,
    )

    same_frames = segments_now[:, :, None] == segments_now[:, None, :]
    earlier = jnp.tril(jnp.ones((frames, frames), jnp.bool_), -1)
    order = jnp.sum((same_frames & earlier[None]).astype(jnp.int32), axis=2)
    slot_of = order * slots + segments_now * rows + jnp.arange(rows, dtype=jnp.int32)[:, None]
    frame_rows = rows * frames
    padding = -frame_rows % 16
    slot_hot = (
        jnp.pad(slot_of.reshape(-1, 1), ((0, padding), (0, 0)), constant_values=-1)
        == jnp.arange(longest * slots, dtype=jnp.int32)[None, :]
    ).astype(bf16)
    slot_hot_frames = slot_hot[:frame_rows]
    carry_on = jnp.pad(
        (segments_now[:, 1:] == segments_now[:, :-1]).astype(f32), ((0, 0), (1, 0))
    )
    finished = jnp.pad(
        (segments_now[:, 1:] != segments_now[:, :-1]).astype(f32),
        ((0, 0), (0, 1)),
        constant_values=1.0,
    )

    def to_slots(value, kind=bf16):
        return lax.dot_general(
            slot_hot_frames,
            value.astype(bf16),
            (((0,), (0,)), ((), ())),
            preferred_element_type=f32,
        ).astype(kind)

    def to_frames(value):
        return jnp.dot(slot_hot, value.astype(bf16), preferred_element_type=f32).astype(bf16)

    def pad_frames(value):
        return jnp.pad(
            value.astype(f32).reshape(frame_rows, -1), ((0, padding), (0, 0))
        )

    previous = pad_frames(
        jnp.pad(targets_now[:, :-1], ((0, 0), (1, 0), (0, 0))).astype(f32)
        * carry_on[:, :, None]
    )
    drops_one = pad_frames(mine(drop_first))
    drops_two = pad_frames(mine(drop_second))

    zones_own = jnp.concatenate([mine(zone_first), mine(zone_second)], axis=2).astype(f32)
    zones_peer = exchange(
        jnp.concatenate([others(zone_first), others(zone_second)], axis=2).astype(f32)
    )
    zones_slots = to_slots(
        jnp.concatenate([zones_own, zones_peer], axis=2).reshape(rows * frames, -1), f32
    ).reshape(longest, slots, 4 * half)
    zone_one = jnp.concatenate(
        [zones_slots[:, :, :half], zones_slots[:, :, 2 * half : 3 * half]], axis=2
    )
    zone_two = jnp.concatenate(
        [zones_slots[:, :, half : 2 * half], zones_slots[:, :, 3 * half :]], axis=2
    )
    biases = jnp.stack([bias_first.reshape(-1), bias_second.reshape(-1)])
    biases = jnp.concatenate([biases, exchange(biases)], axis=1)
    text_ends = jnp.cumsum(mine(text_lengths), axis=1)
    owner = jnp.sum(
        (jnp.arange(text_width, dtype=jnp.int32)[None, :, None] >= text_ends[:, None, :]).astype(
            jnp.int32
        ),
        axis=2,
    )
    owner_slot = owner * rows + jnp.arange(rows, dtype=jnp.int32)[:, None]
    owner_hot = (
        owner_slot.reshape(-1, 1) == jnp.arange(lanes, dtype=jnp.int32)[None, :]
    ).astype(f32)
    conv_float = location_conv.astype(f32)
    dense_float = location_dense.astype(f32)
    reach = location_conv.shape[2] // 2
    taps_first = jnp.transpose(conv_float, (1, 2, 0))
    taps_first = jnp.pad(
        taps_first,
        ((0, 0), (0, lanes - taps_first.shape[1]), (0, lanes - taps_first.shape[2])),
    )
    dense_wide = jnp.pad(dense_float, ((0, lanes - dense_float.shape[0]), (0, 0)))
    taps_forward = jnp.roll(taps_first[:, ::-1], reach, axis=1)
    taps_back = jnp.roll(taps_first, 1 - reach, axis=1)
    frame_wide = jnp.pad(
        frame_weight.astype(f32), ((0, 0), (0, lanes - frame_weight.shape[1]))
    )
    frame_bias_wide = jnp.pad(frame_bias, (0, lanes - frame_bias.shape[0]))[None, :]
    vector_float = energy_vector.astype(f32)
    vector_wide = jnp.broadcast_to(vector_float[:, None], (attention_width, lanes))
    memory_float = memory_now.astype(f32)
    query_float = query_weight.astype(f32)
    unit_array = unit.astype(jnp.int32).reshape(1)

    (
        gates_one,
        gates_two,
        prior_one,
        prior_two,
        round_one,
        round_two,
        contexts,
        mixed_all,
        alphas,
        taps,
        mixed_one,
        mixed_two,
        hidden_round,
        prenet_round,
        frame_out,
    ) = call_forward(
        unit_array,
        weights,
        (
            previous,
            drops_one,
            drops_two,
            prenet_first.astype(f32),
            prenet_second.astype(f32),
            slot_hot.astype(f32),
            zone_one,
            zone_two,
            biases[0:1],
            biases[1:2],
            owner_hot,
            memory_float,
            memory_weight.astype(f32),
            query_float,
            vector_wide,
            taps_forward,
            dense_wide,
            frame_wide,
            frame_bias_wide,
        ),
        (
            longest,
            slots,
            hidden,
            memory_width,
            rows * text_width,
            frame_rows + padding,
            prenet_width,
        ),
    )

    states = to_frames(
        jnp.concatenate([round_one, contexts, round_two], axis=2).reshape(longest * slots, -1)
    )
    frame_in = jnp.concatenate(
        [states[:, hidden + memory_width :], states[:, hidden : hidden + memory_width]], axis=1
    )
    frame_in = frame_in[:frame_rows]
    frame_out = frame_out[:frame_rows]
    mel_own = frame_out[:, :mel_width].reshape(rows, frames, mel_width)
    stop_logit = frame_out[:, mel_width].reshape(rows, frames)
    mel_all = jnp.transpose(
        lax.all_gather(mel_own, "batch", axis=0, tiled=True), (1, 0, 2)
    )
    inputs_own = jnp.concatenate([prenet_round.astype(bf16), states], axis=1)
    roomy = total_rows * frames <= 2048
    if roomy:
        inputs_all = lax.all_gather(inputs_own, "batch", axis=0, tiled=True)

    targets_all = jnp.transpose(frame_info[:, :, :mel_width].astype(f32), (1, 0, 2))
    segments_all = jnp.transpose(frame_info[:, :, mel_width].astype(jnp.int32))
    padded = jnp.pad(segments_all, ((2, 2), (0, 0)), constant_values=-1)
    same = jnp.stack([padded[offset : offset + frames] == segments_all for offset in range(5)])
    same = jnp.moveaxis(same, 0, 2)
    first_full = whole(post_first, 2)
    last_full = whole(last_half, 2).astype(bf16)
    middle_gain = whole(middle_norm, 2)
    last_gain = whole(last_norm, 1)
    loss_scale = 2.0 / (mel_width * total_rows)
    channel_rows = post_middle.shape[2]
    if roomy:
        count = total_rows * frames
        channels = middle_norm.shape[2] * 2
        masks = jnp.broadcast_to(
            jnp.transpose(same, (2, 0, 1)).reshape(5, count, 1).astype(bf16), (5, count, lanes)
        )
        wide_gain = jnp.pad(last_gain, ((0, 0), (0, channels - mel_width)))
        norms = jnp.concatenate([middle_gain, wide_gain[:, None, :]], axis=1)[:, :, None, :]
        (
            inputs_first,
            inputs_later,
            grads_early,
            grads_last,
            norm_grads,
            grad_mel,
        ) = call_postnet(
            unit_array,
            (
                mel_all.reshape(count, mel_width),
                targets_all.reshape(count, mel_width),
                masks,
                first_full,
                middle_half,
                exchange(middle_half),
                last_full,
                norms[0],
                norms[1],
            ),
            loss_scale,
            total_rows,
        )
        gain_grads = [norm_grads[0, layer, 0] for layer in range(5)]
        shift_grads = [norm_grads[1, layer, 0] for layer in range(5)]
        gain_grads[4], shift_grads[4] = gain_grads[4][:mel_width], shift_grads[4][:mel_width]
        kernel_grads = []
        for layer in range(5):
            if layer == 0:
                source = inputs_first
            else:
                source = lax.dynamic_slice_in_dim(
                    inputs_later[layer - 1], place * channel_rows, channel_rows, 1
                )
            grad_norm = grads_early[layer] if layer < 4 else grads_last
            kernel_grads.append(
                post_kernel_grad(
                    source.reshape(frames, total_rows, -1),
                    grad_norm.reshape(frames, total_rows, -1),
                    same,
                ).reshape(5, source.shape[1], grad_norm.shape[1])
            )
        grad_mel = jnp.transpose(
            lax.dynamic_slice_in_dim(
                grad_mel.reshape(frames, total_rows, mel_width), place * rows, rows, 1
            ),
            (1, 0, 2),
        )
    else:
        middle_full = whole(middle_half, 3)
        kernels = [first_full, middle_full[0], middle_full[1], middle_full[2], last_full]
        gains = [middle_gain[0, layer] for layer in range(4)] + [last_gain[0]]
        shifts = [middle_gain[1, layer] for layer in range(4)] + [last_gain[1]]
        layer_in = mel_all.astype(bf16)
        layer_inputs, normed_all, inverses = [], [], []
        output = None
        for layer in range(5):
            layer_inputs.append(layer_in)
            pre_norm = by_rows(
                lambda source, same_now: post_layer(source, kernels[layer], same_now),
                roomy,
                (layer_in, same),
            )
            mean_now = jnp.sum(pre_norm, axis=(0, 1)) / frame_count
            centered = pre_norm - mean_now
            inverse = lax.rsqrt(jnp.sum(centered * centered, axis=(0, 1)) / frame_count + norm_eps)
            normed = centered * inverse
            output = normed * gains[layer] + shifts[layer]
            normed_all.append(normed)
            inverses.append(inverse)
            if layer < 4:
                layer_in = jnp.tanh(output).astype(bf16)
                if not roomy:
                    layer_in, normed_all[layer] = lax.optimization_barrier(
                        (layer_in, normed_all[layer])
                    )

        grad_post = loss_scale * (mel_all + output - targets_all)
        kernel_grads, gain_grads, shift_grads = [None] * 5, [None] * 5, [None] * 5
        grad_output = grad_post
        grad_input = None
        for layer in (4, 3, 2, 1, 0):
            if layer < 4:
                normed_all[layer] = lax.optimization_barrier(normed_all[layer])
                active = jnp.tanh(normed_all[layer] * gains[layer] + shifts[layer])
                grad_output = grad_input * (1.0 - active * active)
            shift_grads[layer] = jnp.sum(grad_output, axis=(0, 1))
            gain_grads[layer] = jnp.sum(grad_output * normed_all[layer], axis=(0, 1))
            grad_norm = (
                gains[layer]
                * inverses[layer]
                * (
                    grad_output
                    - shift_grads[layer] / frame_count
                    - normed_all[layer] * (gain_grads[layer] / frame_count)
                )
            ).astype(bf16)
            grad_input = by_rows(
                lambda grad, same_now: post_layer_back(grad, kernels[layer], same_now),
                roomy,
                (grad_norm, same),
            )
            source = layer_inputs[layer]
            if layer > 0:
                source = lax.dynamic_slice_in_dim(source, place * channel_rows, channel_rows, 2)
            kernel_grads[layer] = by_rows(post_kernel_grad, roomy, (source, grad_norm, same), True)
            kernel_grads[layer] = kernel_grads[layer].reshape(5, source.shape[2], -1)
            if not roomy:
                grad_input, kernel_grads[layer] = lax.optimization_barrier(
                    (grad_input, kernel_grads[layer])
                )
        grad_mel = loss_scale * (mel_all - targets_all) + grad_post + grad_input
        grad_mel = jnp.transpose(
            lax.dynamic_slice_in_dim(grad_mel, place * rows, rows, 1), (1, 0, 2)
        )

    if not roomy:
        inputs_own, grad_mel = lax.optimization_barrier((inputs_own, grad_mel))
        inputs_all = lax.all_gather(inputs_own, "batch", axis=0, tiled=True)

    def add_units(value, axis):
        width = value.shape[axis] // 2
        halves = [
            lax.slice_in_dim(value, start, start + width, axis=axis) for start in (0, width)
        ]
        keep = jnp.where(first_unit, halves[0], halves[1])
        give = jnp.where(first_unit, halves[1], halves[0])
        return keep + exchange(give)

    post_first_grad = add_units(kernel_grads[0], 2)
    post_middle_grad = add_units(jnp.stack(kernel_grads[1:4]), 3)
    post_last_grad = add_units(kernel_grads[4], 2)
    middle_norm_grad = add_units(
        jnp.stack([jnp.stack(gain_grads[:4]), jnp.stack(shift_grads[:4])]), 2
    )
    last_norm_grad = add_units(jnp.stack([gain_grads[4], shift_grads[4]]), 1)

    grad_stop = (jax.nn.sigmoid(stop_logit) - finished) / total_rows
    grad_frame = (
        jnp.concatenate([grad_mel, grad_stop[:, :, None]], axis=2)
        .reshape(rows * frames, mel_width + 1)
        .astype(bf16)
    )
    frame_weight_grad = lax.dot_general(
        frame_in, grad_frame, (((0,), (0,)), ((), ())), preferred_element_type=f32
    )
    frame_bias_grad = jnp.sum(grad_frame.astype(f32), axis=0)
    grad_frame_slots = to_slots(
        jnp.pad(grad_frame, ((0, 0), (0, lanes - mel_width - 1))), f32
    ).reshape(longest, slots, lanes)

    (
        grads_one,
        grads_two,
        prenet_back,
        context_grads,
        query_back,
        processed_back,
        vector_back,
        filter_back,
    ) = call_backward(
        unit_array,
        weights,
        (
            gates_one,
            gates_two,
            prior_one,
            prior_two,
            zone_one,
            zone_two,
            owner_hot,
            memory_float,
            query_float,
            vector_float[None, :],
            taps_back,
            dense_wide,
            mixed_all,
            alphas,
            taps,
            grad_frame_slots,
            frame_wide,
        ),
    )

    both = jnp.concatenate([grads_one, grads_two], axis=2).reshape(longest * slots, -1)
    both = to_frames(both)
    bias_local = jnp.sum(both.astype(f32), axis=0).reshape(2, 2, 4, half)
    bias_low, bias_high = ordered(bias_local[:, 0], bias_local[:, 1])
    both = both.reshape(frame_rows + padding, 2, 2, batch_size, -1)
    both_low, both_high = ordered(both[:, :, 0], both[:, :, 1])
    sent = jnp.transpose(jnp.stack([both_low, both_high], axis=2), (3, 0, 1, 2, 4))
    slice_width = sent.shape[4]
    sent = sent.reshape(batch_size, frame_rows + padding, -1)
    received = lax.all_to_all(sent, "batch", 0, 0, tiled=True)
    segments_rows = segments_all.T
    carried = jnp.pad(
        (segments_rows[:, 1:] == segments_rows[:, :-1]).astype(bf16), ((0, 0), (0, 1))
    ).reshape(batch_size, frame_rows)
    carried = jnp.pad(carried, ((0, 0), (0, padding)))
    after = jnp.pad(received[:, 1:], ((0, 0), (0, 1), (0, 0))) * carried[:, :, None]
    received = received.reshape(batch_size * (frame_rows + padding), -1)
    after = after.reshape(batch_size * (frame_rows + padding), -1)

    def product(start, width, grads):
        return lax.dot_general(
            inputs_all[:, start : start + width],
            grads,
            (((0,), (0,)), ((), ())),
            preferred_element_type=f32,
        )

    pair = 2 * slice_width
    first_part = jnp.concatenate(
        [
            product(0, prenet_width, received[:, :pair]),
            product(prenet_width + hidden, memory_width, after[:, :pair]),
            product(prenet_width, hidden, after[:, :pair]),
        ],
        axis=0,
    )
    second_part = jnp.concatenate(
        [
            product(prenet_width, hidden + memory_width, received[:, pair:]),
            product(prenet_width + hidden + memory_width, hidden, after[:, pair:]),
        ],
        axis=0,
    )
    parts = jnp.concatenate(
        [
            first_part.reshape(batch_size, depth_one, pair),
            second_part.reshape(batch_size, depth_two, pair),
        ],
        axis=1,
    )
    parts = add_units(parts, 2)
    parts = lax.all_to_all(parts, "batch", 0, 0, tiled=True)
    parts = jnp.transpose(parts, (1, 0, 2)).reshape(depth_one + depth_two, 4, half)

    grad_prenet = lax.dot_general(
        slot_hot.astype(f32),
        prenet_back.reshape(longest * slots, prenet_width),
        (((1,), (0,)), ((), ())),
        precision=precise,
    )

    def silu_back(grad, mixed, drops):
        gate = jax.nn.sigmoid(mixed)
        return grad * drops * 2.0 * gate * (1.0 + mixed * (1.0 - gate))

    def exact(a, b, contract):
        return lax.dot_general(
            a.astype(f32), b.astype(f32), (contract, ((), ())), precision=precise
        )

    grad_mixed_two = silu_back(grad_prenet, mixed_two, drops_two)
    prenet_second_grad = exact(hidden_round, grad_mixed_two, ((0,), (0,)))
    grad_hidden = exact(grad_mixed_two, prenet_second, ((1,), (1,)))
    grad_mixed_one = silu_back(grad_hidden, mixed_one, drops_one)
    prenet_first_grad = exact(previous, grad_mixed_one, ((0,), (0,)))

    query_weight_grad = exact(
        round_one.reshape(longest * slots, hidden),
        query_back.reshape(longest * slots, attention_width),
        ((0,), (0,)),
    )
    processed_round = processed_back.astype(bf16)
    memory_weight_grad = lax.dot_general(
        memory_now, processed_round, (((0,), (0,)), ((), ())), preferred_element_type=f32
    )
    memory_grad = lax.dot_general(
        processed_round, memory_weight, (((1,), (1,)), ((), ())), preferred_element_type=f32
    )
    for step in range(longest):
        memory_grad = memory_grad + exact(
            alphas[step][:, :slots], context_grads[step], ((1,), (0,))
        )
    memory_grad = memory_grad.reshape(rows, text_width, memory_width)
    memory_grads = jnp.stack(ordered(memory_grad, exchange(memory_grad)))
    filter_grads = jnp.roll(filter_back, -reach, axis=1)[:, ::-1][:, : location_conv.shape[2]]
    conv_grad = jnp.einsum("cka,fa->fck", filter_grads, dense_float, precision=precise)
    dense_grad = jnp.einsum("cka,fck->fa", filter_grads, conv_float, precision=precise)

    small = lax.psum(
        (
            prenet_first_grad,
            prenet_second_grad,
            query_weight_grad,
            memory_weight_grad,
            conv_grad,
            dense_grad,
            vector_back[0],
            frame_weight_grad,
            frame_bias_grad,
            jnp.stack([bias_low, bias_high]),
        ),
        ("batch", "unit"),
    )
    biases_grad = mine(small[9])
    return (
        small[0],
        small[1],
        small[2],
        small[3],
        small[4],
        small[5],
        small[6],
        parts[:depth_one],
        biases_grad[0],
        parts[depth_one:],
        biases_grad[1],
        small[7],
        small[8],
        post_first_grad,
        post_middle_grad,
        post_last_grad,
        middle_norm_grad,
        last_norm_grad,
        memory_grads,
    )


def solution(mesh):
    in_specs = (
        P(None, "batch", None, None),
        P(None, "batch", None, None),
        P(None, "batch", None),
        P(None, "batch", None),
        P(None, "batch", None, "unit"),
        P(None, "batch", None, "unit"),
        P(None, "batch", None, None),
        P(None, "batch", None, None),
        P(),
        P(),
        P(),
        P(),
        P(),
        P(),
        P(),
        P("batch", None, "unit"),
        P(None, "unit"),
        P("batch", None, "unit"),
        P(None, "unit"),
        P(),
        P(),
        P(None, None, "unit"),
        P(None, None, "batch", "unit"),
        P(None, "batch", "unit"),
        P(None, None, "unit"),
        P(None, "unit"),
    )
    out_specs = (
        P(),
        P(),
        P(),
        P(),
        P(),
        P(),
        P(),
        P("batch", None, "unit"),
        P(None, "unit"),
        P("batch", None, "unit"),
        P(None, "unit"),
        P(),
        P(),
        P(None, None, "unit"),
        P(None, None, "batch", "unit"),
        P(None, "batch", "unit"),
        P(None, None, "unit"),
        P(None, "unit"),
        P(None, "batch", None, None),
    )
    return jax.shard_map(
        on_device, mesh=mesh, in_specs=in_specs, out_specs=out_specs, check_vma=False
    )
```

```python
import functools

import jax
import jax.numpy as jnp
from jax import lax
from jax.experimental import pallas as pl
from jax.experimental.pallas import tpu as pltpu
from jax.sharding import PartitionSpec as P

precise = lax.Precision.HIGHEST
norm_eps = 1e-05
f32 = jnp.float32
bf16 = jnp.bfloat16
lanes = 128
kernel_vmem = 60 * 1024 * 1024


def split(value):
    high = value.astype(bf16)
    return high, (value - high.astype(f32)).astype(bf16)


def dot(a, b, contract=((1,), (0,))):
    return lax.dot_general(a, b, (contract, ((), ())), preferred_element_type=f32)


def dot_left(exact, value, contract=((1,), (0,))):
    high, low = split(value)
    return dot(exact, high, contract) + dot(exact, low, contract)


def dot_right(value, exact, contract=((1,), (0,))):
    high, low = split(value)
    return dot(high, exact, contract) + dot(low, exact, contract)


def dot_both(a, b, contract=((1,), (0,))):
    a_high, a_low = split(a)
    b_high, b_low = split(b)
    return (
        dot(a_high, b_high, contract) + dot(a_low, b_high, contract) + dot(a_high, b_low, contract)
    )


rows_first = ((0,), (0,))
lanes_both = ((1,), (1,))


def position_hot(position_count, text_width, reverse):
    place = lax.broadcasted_iota(jnp.int32, (position_count, lanes), 0) & (text_width - 1)
    lane = lax.broadcasted_iota(jnp.int32, (position_count, lanes), 1)
    place = (lanes - 1) - place if reverse else place + 1
    return (place == lane).astype(bf16)


def slant(value, text_width):
    blocks = [
        pltpu.roll(value[start : start + text_width], 0, 1, stride=1, stride_axis=0)
        for start in range(0, value.shape[0], text_width)
    ]
    return jnp.concatenate(blocks, axis=0)


def pad_rows(value):
    return jnp.concatenate(
        [value, jnp.zeros((lanes - value.shape[0], value.shape[1]), value.dtype)], axis=0
    )


def unit_spot(chunk, unit, per_half):
    half = (chunk // per_half + unit) % 2
    return pl.multiple_of((half * per_half + chunk % per_half) * lanes, lanes)


def gate_spot(chunk, gate, per_half):
    start = (chunk // per_half) * 4 * per_half + gate * per_half + chunk % per_half
    return pl.multiple_of(start * lanes, lanes)


def forward_kernel(
    unit_ref,
    own_one,
    peer_one,
    own_two,
    peer_two,
    previous_ref,
    drop_one,
    drop_two,
    layer_one,
    layer_two,
    slot_ref,
    zone_one,
    zone_two,
    bias_one,
    bias_two,
    hot_ref,
    memory_ref,
    project_ref,
    query_ref,
    vector_ref,
    conv_ref,
    dense_ref,
    frame_ref,
    frame_bias,
    gates_one,
    gates_two,
    prior_one,
    prior_two,
    round_one,
    round_two,
    context_ref,
    mixed_ref,
    alpha_ref,
    taps_ref,
    prenet_one,
    prenet_two,
    prenet_hidden,
    prenet_out,
    frame_out,
    held_one,
    held_two,
    input_ref,
    prenet_ref,
    processed_ref,
    filter_ref,
    state_one,
    cell_one,
    state_two,
    cell_two,
    sems,
):
    unit = unit_ref[0]
    steps, slots, hidden = round_one.shape
    prenet_width = layer_two.shape[1]
    context_width = context_ref.shape[2]
    half = hidden // 2
    per_half = half // lanes
    position_count = hot_ref.shape[0]
    text_width = position_count // (slots // 4)
    copies_two = [
        pltpu.make_async_copy(own_two, held_two.at[0], sems.at[0]),
        pltpu.make_async_copy(peer_two, held_two.at[1], sems.at[1]),
    ]
    copies_one = [
        pltpu.make_async_copy(own_one, held_one.at[0], sems.at[2]),
        pltpu.make_async_copy(peer_one, held_one.at[1], sems.at[3]),
    ]
    for copy in copies_two + copies_one:
        copy.start()
    for ref in (state_one, cell_one, state_two, cell_two):
        ref[...] = jnp.zeros_like(ref)

    def gates_into(held, depth, bias_ref, out_ref, step):
        def one(block, _):
            side = block // 4
            inputs = input_ref[:, :depth]
            for pair in range(per_half // 2):
                tile = (block % 4) * per_half + 2 * pair
                outside = pl.ds(
                    pl.multiple_of(block * half + 2 * pair * lanes, 2 * lanes), 2 * lanes
                )
                kernel = jnp.concatenate(
                    [held[side, tile, :depth, :], held[side, tile + 1, :depth, :]], axis=1
                )
                out_ref[step, :, outside] = dot(inputs, kernel) + bias_ref[:, outside]
            return 0

        lax.fori_loop(0, 8, one, 0)

    def cell(gates_ref, zone_ref, prior_ref, state, cells, round_ref, step):
        def one(chunk, _):
            spot = pl.ds(pl.multiple_of(chunk * lanes, lanes), lanes)
            values = [
                gates_ref[step, :, pl.ds(gate_spot(chunk, gate, per_half), lanes)]
                for gate in range(4)
            ]
            zone = zone_ref[step, :, spot]
            before = cells[:, spot]
            prior_ref[step, :, spot] = before
            fresh = jax.nn.sigmoid(values[1]) * before + jax.nn.sigmoid(values[0]) * jnp.tanh(
                values[2]
            )
            output = jax.nn.sigmoid(values[3]) * jnp.tanh(fresh)
            now = zone * state[:, spot] + (1.0 - zone) * output
            state[:, spot] = now
            cells[:, spot] = zone * before + (1.0 - zone) * fresh
            round_ref[step, :, pl.ds(unit_spot(chunk, unit, per_half), lanes)] = now.astype(bf16).astype(
                f32
            )
            return 0

        lax.fori_loop(0, 2 * per_half, one, 0)

    def attention(step, location):
        inside = hot_ref[...] > 0.0
        hot = hot_ref[...].astype(bf16)
        query = pad_rows(dot(round_one[step].astype(bf16), query_ref[...].astype(bf16)))
        summed = dot_left(hot, query) + processed_ref[...]
        if location is not None:
            summed = summed + location
        mixed = jnp.tanh(summed)
        mixed_ref[step] = mixed
        energy = dot_right(mixed, vector_ref[...].astype(bf16))
        most = jnp.max(jnp.where(inside, energy, -1000000000.0), axis=0, keepdims=True)
        shifted = jnp.where(inside, jnp.exp(energy - most), 0.0)
        total = jnp.sum(shifted, axis=0, keepdims=True)
        alpha = shifted / jnp.where(total > 0.0, total, 1.0)
        alpha_ref[step] = alpha
        context = dot_right(alpha, memory_ref[...].astype(bf16), rows_first)[:slots]
        context_ref[step] = context.astype(bf16).astype(f32)

    def taps_of(step):
        spread = dot_right(
            alpha_ref[step], position_hot(position_count, text_width, True), rows_first
        )
        taps_ref[step] = slant(dot_left(hot_ref[...].astype(bf16), spread), text_width)

    def second_layer(step, depth):
        input_ref[:, :hidden] = round_one[step].astype(bf16)
        input_ref[:, hidden : hidden + context_width] = context_ref[step].astype(bf16)
        gates_into(held_two, depth, bias_two, gates_two, step)
        cell(gates_two, zone_two, prior_two, state_two, cell_two, round_two, step)

    slot_hot = slot_ref[...].astype(bf16)

    def prenet_layer(source, layer, drops, mixed_out, out):
        mixed = dot(source.astype(bf16), layer[...].astype(bf16))
        mixed_out[...] = mixed
        value = (mixed * jax.nn.sigmoid(mixed) * drops[...] * 2.0).astype(bf16)
        out[...] = value.astype(f32)
        return value

    hidden_value = prenet_layer(previous_ref[...], layer_one, drop_one, prenet_one, prenet_hidden)
    prenet_value = prenet_layer(hidden_value, layer_two, drop_two, prenet_two, prenet_out)
    prenet_slots = dot(slot_hot, prenet_value, rows_first)
    for step in range(steps):
        prenet_ref[step] = prenet_slots[step * slots : (step + 1) * slots]
    processed_ref[...] = dot(memory_ref[...].astype(bf16), project_ref[...].astype(bf16))
    for channel in range(2):
        filter_ref[channel] = dot(
            conv_ref[channel].astype(bf16), dense_ref[...].astype(bf16)
        )

    gates_one[0] = jnp.broadcast_to(bias_one[...], gates_one.shape[1:])
    cell(gates_one, zone_one, prior_one, state_one, cell_one, round_one, 0)
    attention(0, None)
    taps_of(0)
    for copy in copies_two:
        copy.wait()
    second_layer(0, hidden + context_width)
    for copy in copies_one:
        copy.wait()

    def later(step, _):
        input_ref[:, :prenet_width] = prenet_ref[step].astype(bf16)
        input_ref[:, prenet_width : prenet_width + context_width] = context_ref[step - 1].astype(
            bf16
        )
        input_ref[:, prenet_width + context_width : prenet_width + context_width + hidden] = (
            round_one[step - 1].astype(bf16)
        )
        gates_into(
            held_one, prenet_width + context_width + hidden, bias_one, gates_one, step
        )
        cell(gates_one, zone_one, prior_one, state_one, cell_one, round_one, step)
        previous = taps_ref[step - 1]
        summed = jnp.where(step == 2, taps_ref[0] + previous, previous)
        attention(step, dot_both(previous, filter_ref[0]) + dot_both(summed, filter_ref[1]))

        @pl.when(step < steps - 1)
        def _():
            taps_of(step)

        input_ref[:, hidden + context_width :] = round_two[step - 1].astype(bf16)
        second_layer(step, 2 * hidden + context_width)
        return 0

    lax.fori_loop(1, steps, later, 0)
    for step in range(steps):
        values = dot(round_two[step].astype(bf16), frame_ref[:hidden].astype(bf16)) + dot(
            context_ref[step].astype(bf16), frame_ref[hidden:].astype(bf16)
        )
        high = values.astype(bf16)
        rest = values - high.astype(f32)
        middle = rest.astype(bf16)
        low = (rest - middle.astype(f32)).astype(bf16)
        chosen = slot_hot[:, step * slots : (step + 1) * slots]
        picked = (dot(chosen, high) + dot(chosen, middle)) + dot(chosen, low)
        frame_out[...] = (frame_bias[...] if step == 0 else frame_out[...]) + picked


def backward_kernel(
    unit_ref,
    own_one,
    peer_one,
    own_two,
    peer_two,
    gates_one,
    gates_two,
    prior_one,
    prior_two,
    zone_one,
    zone_two,
    hot_ref,
    memory_ref,
    query_ref,
    vector_ref,
    conv_ref,
    dense_ref,
    mixed_ref,
    alpha_ref,
    taps_ref,
    frame_grad,
    frame_weight,
    slot_ref,
    sent_ref,
    prenet_grad,
    context_grad,
    query_grad,
    processed_grad,
    vector_grad,
    filter_grad,
    held_one,
    held_two,
    grads_one,
    grads_two,
    back_one,
    back_two,
    state_one,
    cell_one,
    state_two,
    cell_two,
    previous_grad,
    summed_grad,
    from_query,
    frame_ref,
    filter_ref,
    sems,
):
    unit = unit_ref[0]
    steps, slots, prenet_width = prenet_grad.shape
    context_width = context_grad.shape[2]
    hidden = state_one.shape[1]
    half = hidden // 2
    per_half = half // lanes
    position_count = hot_ref.shape[0]
    text_width = position_count // (slots // 4)
    copies_two = [
        pltpu.make_async_copy(own_two, held_two.at[0], sems.at[0]),
        pltpu.make_async_copy(peer_two, held_two.at[1], sems.at[1]),
    ]
    copies_one = [
        pltpu.make_async_copy(own_one, held_one.at[0], sems.at[2]),
        pltpu.make_async_copy(peer_one, held_one.at[1], sems.at[3]),
    ]
    for copy in copies_two + copies_one:
        copy.start()
    for ref in (
        state_one,
        cell_one,
        state_two,
        cell_two,
        back_one,
        back_two,
        previous_grad,
        summed_grad,
        processed_grad,
        vector_grad,
        filter_grad,
    ):
        ref[...] = jnp.zeros_like(ref)

    def cell(gates_ref, prior_ref, zone_ref, state, cells, grads_ref, step, incoming):
        def one(chunk, _):
            spot = pl.ds(pl.multiple_of(chunk * lanes, lanes), lanes)
            places = [pl.ds(gate_spot(chunk, gate, per_half), lanes) for gate in range(4)]
            values = [gates_ref[step, :, place] for place in places]
            zone = zone_ref[step, :, spot]
            keep = 1.0 - zone
            before = prior_ref[step, :, spot]
            gate_in = jax.nn.sigmoid(values[0])
            gate_forget = jax.nn.sigmoid(values[1])
            candidate = jnp.tanh(values[2])
            gate_out = jax.nn.sigmoid(values[3])
            bent = jnp.tanh(gate_forget * before + gate_in * candidate)
            grad_state = incoming(unit_spot(chunk, unit, per_half)) + state[:, spot]
            grad_cell = cells[:, spot]
            grad_new = keep * grad_state
            grad_fresh = grad_new * gate_out * (1.0 - bent * bent) + keep * grad_cell
            state[:, spot] = zone * grad_state
            cells[:, spot] = zone * grad_cell + gate_forget * grad_fresh
            results = (
                grad_fresh * candidate * gate_in * (1.0 - gate_in),
                grad_fresh * before * gate_forget * (1.0 - gate_forget),
                grad_fresh * gate_in * (1.0 - candidate * candidate),
                grad_new * bent * gate_out * (1.0 - gate_out),
            )
            for place, result in zip(places, results):
                grads_ref[step, :, place] = result.astype(bf16)
            return 0

        lax.fori_loop(0, 2 * per_half, one, 0)

    def inputs_back(grads_ref, held, out_ref, step, blocks):
        def one(block, _):
            spot = pl.ds(pl.multiple_of(block * 256, 256), 256)
            total = None
            for tile in range(0, 8 * per_half, 2):
                side, inside = tile // (4 * per_half), tile % (4 * per_half)
                kernel = jnp.concatenate(
                    [held[side, inside, spot, :], held[side, inside + 1, spot, :]], axis=1
                )
                grads = grads_ref[step, :, tile * lanes : (tile + 2) * lanes]
                product = dot(grads, kernel, lanes_both)
                total = product if total is None else total + product
            out_ref[:, spot] = total
            return 0

        lax.fori_loop(0, blocks, one, 0)

    def attention(step, located):
        inside = hot_ref[...] > 0.0
        hot = hot_ref[...].astype(bf16)
        alpha = alpha_ref[step]
        mixed = mixed_ref[step]
        context_now = pad_rows(context_grad[step])
        weights_grad = jnp.where(
            inside,
            dot_left(memory_ref[...].astype(bf16), context_now, lanes_both)
            + previous_grad[...]
            + summed_grad[...],
            0.0,
        )
        product = alpha * weights_grad
        energy_grad = product - alpha * jnp.sum(product, axis=0, keepdims=True)
        spread = jnp.sum(energy_grad, axis=1, keepdims=True)
        vector_grad[...] += jnp.sum(spread * mixed, axis=0, keepdims=True)
        mixed_grad = spread * vector_ref[...] * (1.0 - mixed * mixed)
        processed_grad[...] += mixed_grad
        high, low = split(mixed_grad)
        query_now = (dot(hot, high, rows_first) + dot(hot, low, rows_first))[:slots]
        query_grad[step] = query_now
        from_query[...] = dot_right(query_now, query_ref[...].astype(bf16), lanes_both)
        if located:
            previous = taps_ref[step - 1]
            summed = jnp.where(step == 2, taps_ref[0] + previous, previous)
            filter_grad[0] += dot_both(previous, mixed_grad, rows_first)
            filter_grad[1] += dot_both(summed, mixed_grad, rows_first)
            place_hot = position_hot(position_count, text_width, False)

            def taps_back(channel):
                taps_grad = slant(
                    dot_both(mixed_grad, filter_ref[channel], lanes_both), text_width
                )
                gathered = dot_right(taps_grad, hot, rows_first)
                return jnp.where(inside, dot_left(place_hot, gathered), 0.0)

            previous_grad[...] = taps_back(0)
            summed_grad[...] += taps_back(1)

    def step_back(step, located):
        cell(
            gates_two,
            prior_two,
            zone_two,
            state_two,
            cell_two,
            grads_two,
            step,
            lambda spot: frame_ref[step, :, pl.ds(spot, lanes)]
            + back_two[:, pl.ds(spot + hidden + context_width, lanes)],
        )
        blocks_two = (hidden + context_width + (hidden if located else 0)) // 256
        inputs_back(grads_two, held_two, back_two, step, blocks_two)
        context_grad[step] = (
            back_two[:, hidden : hidden + context_width]
            + frame_ref[step, :, hidden:]
            + back_one[:, prenet_width : prenet_width + context_width]
        )
        attention(step, located)
        cell(
            gates_one,
            prior_one,
            zone_one,
            state_one,
            cell_one,
            grads_one,
            step,
            lambda spot: back_two[:, pl.ds(spot, lanes)]
            + from_query[:, pl.ds(spot, lanes)]
            + back_one[:, pl.ds(spot + prenet_width + context_width, lanes)],
        )
        blocks_one = (prenet_width + (hidden + context_width if located else 0)) // 256
        inputs_back(grads_one, held_one, back_one, step, blocks_one)
        prenet_grad[step] = back_one[:, :prenet_width]

    for channel in range(2):
        filter_ref[channel] = dot(
            conv_ref[channel].astype(bf16), dense_ref[...].astype(bf16)
        )
    for step in range(steps):
        frame_ref[step] = dot(
            frame_grad[step].astype(bf16), frame_weight[...].astype(bf16), lanes_both
        )
    for copy in copies_two + copies_one:
        copy.wait()

    def later(index, _):
        step_back(steps - 1 - index, True)
        return 0

    lax.fori_loop(0, steps - 1, later, 0)
    step_back(0, False)
    slot_hot = slot_ref[...].astype(bf16)

    def tile_out(tile, _):
        for layer, grads_ref in ((0, grads_one), (1, grads_two)):
            for side in range(2):
                place = ((side + unit) % 2) * 4 * half + tile * lanes
                grads = grads_ref[:, :, pl.ds(pl.multiple_of(place, lanes), lanes)]
                chosen = dot(slot_hot, grads.reshape(steps * slots, lanes)).astype(bf16)
                spot = (2 * layer + side) * lanes
                sent_ref[tile, :, spot : spot + lanes] = chosen
        return 0

    lax.fori_loop(0, 4 * per_half, tile_out, 0)


def call_forward(unit, weights, small, sizes):
    own_one, peer_one, own_two, peer_two = weights
    steps, slots, hidden, context_width, positions, frame_rows, prenet_width = sizes

    def shape(*dims):
        return jax.ShapeDtypeStruct(dims, f32)

    outs = [
        shape(steps, slots, 4 * hidden),
        shape(steps, slots, 4 * hidden),
        shape(steps, slots, hidden),
        shape(steps, slots, hidden),
        shape(steps, slots, hidden),
        shape(steps, slots, hidden),
        shape(steps, slots, context_width),
        shape(steps, positions, lanes),
        shape(steps, positions, lanes),
        shape(steps - 1, positions, lanes),
        shape(frame_rows, prenet_width),
        shape(frame_rows, prenet_width),
        shape(frame_rows, prenet_width),
        shape(frame_rows, prenet_width),
        shape(frame_rows, lanes),
    ]
    vmem = pl.BlockSpec(memory_space=pltpu.VMEM)
    return pl.pallas_call(
        forward_kernel,
        out_shape=outs,
        in_specs=[pl.BlockSpec(memory_space=pltpu.SMEM)]
        + [pl.BlockSpec(memory_space=pl.ANY)] * 4
        + [vmem] * len(small),
        out_specs=[vmem] * len(outs),
        scratch_shapes=[
            pltpu.VMEM((2,) + own_one.shape, bf16),
            pltpu.VMEM((2,) + own_two.shape, bf16),
            pltpu.VMEM((slots, own_two.shape[1]), bf16),
            pltpu.VMEM((steps, slots, prenet_width), f32),
            pltpu.VMEM((positions, lanes), f32),
            pltpu.VMEM((2, lanes, lanes), f32),
            pltpu.VMEM((slots, hidden), f32),
            pltpu.VMEM((slots, hidden), f32),
            pltpu.VMEM((slots, hidden), f32),
            pltpu.VMEM((slots, hidden), f32),
            pltpu.SemaphoreType.DMA((4,)),
        ],
        compiler_params=pltpu.CompilerParams(vmem_limit_bytes=kernel_vmem),
        name="decoder_forward",
    )(unit, *weights, *small)


def call_backward(unit, weights, small):
    own_one, peer_one, own_two, peer_two = weights
    gates_one = small[0]
    steps, slots, gate_width = gates_one.shape
    hidden = gate_width // 4
    positions, context_width = small[7].shape
    prenet_width = own_one.shape[1] - hidden - context_width

    def shape(dims, kind):
        return jax.ShapeDtypeStruct(dims, kind)

    outs = [
        shape((gate_width // (2 * lanes), small[-1].shape[0], 4 * lanes), bf16),
        shape((steps, slots, prenet_width), f32),
        shape((steps, slots, context_width), f32),
        shape((steps, slots, lanes), f32),
        shape((positions, lanes), f32),
        shape((1, lanes), f32),
        shape((2, lanes, lanes), f32),
    ]
    vmem = pl.BlockSpec(memory_space=pltpu.VMEM)
    return pl.pallas_call(
        backward_kernel,
        out_shape=outs,
        in_specs=[pl.BlockSpec(memory_space=pltpu.SMEM)]
        + [pl.BlockSpec(memory_space=pl.ANY)] * 4
        + [vmem] * len(small),
        out_specs=[vmem] * len(outs),
        scratch_shapes=[
            pltpu.VMEM((2,) + own_one.shape, bf16),
            pltpu.VMEM((2,) + own_two.shape, bf16),
            pltpu.VMEM((steps, slots, gate_width), bf16),
            pltpu.VMEM((steps, slots, gate_width), bf16),
            pltpu.VMEM((slots, own_one.shape[1]), f32),
            pltpu.VMEM((slots, own_two.shape[1]), f32),
            pltpu.VMEM((slots, hidden), f32),
            pltpu.VMEM((slots, hidden), f32),
            pltpu.VMEM((slots, hidden), f32),
            pltpu.VMEM((slots, hidden), f32),
            pltpu.VMEM((positions, lanes), f32),
            pltpu.VMEM((positions, lanes), f32),
            pltpu.VMEM((slots, hidden), f32),
            pltpu.VMEM((steps, slots, hidden + context_width), f32),
            pltpu.VMEM((2, lanes, lanes), f32),
            pltpu.SemaphoreType.DMA((4,)),
        ],
        compiler_params=pltpu.CompilerParams(vmem_limit_bytes=kernel_vmem),
        name="decoder_backward",
    )(unit, *weights, *small)


def postnet_kernel(
    mel_width,
    loss_scale,
    unit_ref,
    mel_ref,
    target_ref,
    mask_ref,
    first_ref,
    own_ref,
    peer_ref,
    last_ref,
    gain_ref,
    shift_ref,
    inputs_first,
    inputs_later,
    grads_early,
    grads_last,
    norm_grads,
    mel_grad,
    padded,
    padded_mel,
    held,
    normed_early,
    normed_last,
    inverse_ref,
    post_grad,
):
    unit = unit_ref[0]
    count, channels = held.shape
    side = channels // 2
    frames = padded.shape[0] - count
    rows_each = frames // 4
    chunk = 2 * rows_each
    tall = float(count)
    body_rows = slice(2 * rows_each, 2 * rows_each + count)

    for ref in (padded, padded_mel):
        ref[: 2 * rows_each] = jnp.zeros((2 * rows_each, ref.shape[1]), bf16)
        ref[2 * rows_each + count :] = jnp.zeros((2 * rows_each, ref.shape[1]), bf16)

    def piece(source, start, tap, width, lane=None):
        spot = pl.ds(pl.multiple_of(start + tap * rows_each, rows_each), chunk)
        mask = mask_ref[tap, pl.ds(pl.multiple_of(start, rows_each), chunk), :]
        if width < lanes:
            mask = mask[:, :width]
        else:
            mask = jnp.concatenate([mask] * (width // lanes), axis=1)
        value = source[spot, :] if lane is None else source[spot, pl.ds(lane, width)]
        return value * mask

    def chunks(work):
        def one(index, _):
            work(pl.multiple_of(index * chunk, chunk))
            return 0

        lax.fori_loop(0, count // chunk, one, 0)

    def half_spot(which):
        return pl.multiple_of(((which + unit) % 2) * side, side)

    def norm_forward(value, layer, lane, width):
        mean = jnp.sum(value, axis=0, keepdims=True) / tall
        centered = value - mean
        inverse = lax.rsqrt(jnp.sum(centered * centered, axis=0, keepdims=True) / tall + norm_eps)
        inverse_ref[layer, :, pl.ds(lane, width)] = inverse
        return centered * inverse

    def each_lane_block(work):
        def one(index, _):
            work(pl.multiple_of(index * lanes, lanes))
            return 0

        lax.fori_loop(0, channels // lanes, one, 0)

    def activate(layer):
        def block(lane):
            spot = pl.ds(lane, lanes)
            normed = norm_forward(held[:, spot], layer, lane, lanes)
            normed_early[layer, :, spot] = normed
            active = jnp.tanh(
                normed * gain_ref[layer, :, spot] + shift_ref[layer, :, spot]
            ).astype(bf16)
            inputs_later[layer, :, spot] = active
            padded[body_rows, spot] = active

        each_lane_block(block)

    source = mel_ref[...].astype(bf16)
    inputs_first[...] = source
    padded_mel[body_rows] = source

    def first_chunk(start):
        total = None
        for tap in range(5):
            product = dot(piece(padded_mel, start, tap, mel_width), first_ref[tap])
            total = product if total is None else total + product
        held[pl.ds(start, chunk), :] = total

    chunks(first_chunk)
    activate(0)

    def middle(index, _):
        for which, ref in ((0, own_ref), (1, peer_ref)):

            def middle_chunk(start, which=which, ref=ref):
                total = None
                for tap in range(5):
                    product = dot(piece(padded, start, tap, channels), ref[index, tap])
                    total = product if total is None else total + product
                held[pl.ds(start, chunk), pl.ds(half_spot(which), side)] = total

            chunks(middle_chunk)
        activate(index + 1)
        return 0

    lax.fori_loop(0, 3, middle, 0)

    def last_chunk(start):
        total = None
        for tap in range(5):
            product = dot(piece(padded, start, tap, channels), last_ref[tap])
            total = product if total is None else total + product
        normed_last[pl.ds(start, chunk), :] = total

    chunks(last_chunk)
    normed = norm_forward(normed_last[...], 4, 0, mel_width)
    normed_last[...] = normed

    def norm_back(grad, normed, layer, lane, width):
        spot = pl.ds(lane, width)
        shift_grad = jnp.sum(grad, axis=0, keepdims=True)
        gain_grad = jnp.sum(grad * normed, axis=0, keepdims=True)
        norm_grads[0, layer, :, spot] = gain_grad
        norm_grads[1, layer, :, spot] = shift_grad
        return (
            gain_ref[layer, :, spot]
            * inverse_ref[layer, :, spot]
            * (grad - shift_grad / tall - normed * (gain_grad / tall))
        ).astype(bf16)

    output = normed * gain_ref[4, :, :mel_width] + shift_ref[4, :, :mel_width]
    grad = loss_scale * (mel_ref[...] + output - target_ref[...])
    post_grad[...] = grad
    grad_norm = norm_back(grad, normed, 4, 0, mel_width)
    grads_last[...] = grad_norm
    padded_mel[body_rows] = grad_norm

    def last_back(start):
        total = None
        for tap in range(5):
            product = dot(
                piece(padded_mel, start, tap, mel_width), last_ref[4 - tap], lanes_both
            )
            total = product if total is None else total + product
        held[pl.ds(start, chunk), :] = total

    chunks(last_back)

    def deactivate(layer):
        def block(lane):
            spot = pl.ds(lane, lanes)
            normed = normed_early[layer, :, spot]
            active = jnp.tanh(normed * gain_ref[layer, :, spot] + shift_ref[layer, :, spot])
            grad = held[:, spot] * (1.0 - active * active)
            grad_norm = norm_back(grad, normed, layer, lane, lanes)
            grads_early[layer, :, spot] = grad_norm
            padded[body_rows, spot] = grad_norm

        each_lane_block(block)

    def middle_back(back, _):
        index = 2 - back
        deactivate(index + 1)

        def chunk_back(start):
            total = None
            for which, ref in ((0, own_ref), (1, peer_ref)):
                for tap in range(5):
                    product = dot(
                        piece(padded, start, tap, side, half_spot(which)),
                        ref[index, 4 - tap],
                        lanes_both,
                    )
                    total = product if total is None else total + product
            held[pl.ds(start, chunk), :] = total

        chunks(chunk_back)
        return 0

    lax.fori_loop(0, 3, middle_back, 0)
    deactivate(0)

    def first_back(start):
        total = None
        for tap in range(5):
            product = dot(piece(padded, start, tap, channels), first_ref[4 - tap], lanes_both)
            total = product if total is None else total + product
        spot = pl.ds(start, chunk)
        mel_grad[spot, :] = (
            loss_scale * (mel_ref[spot, :] - target_ref[spot, :]) + post_grad[spot, :] + total
        )

    chunks(first_back)


def call_postnet(unit, small, loss_scale, rows_all):
    mel = small[0]
    count, mel_width = mel.shape
    channels = small[3].shape[2]

    def shape(kind, *dims):
        return jax.ShapeDtypeStruct(dims, kind)

    outs = [
        shape(bf16, count, mel_width),
        shape(bf16, 4, count, channels),
        shape(bf16, 4, count, channels),
        shape(bf16, count, mel_width),
        shape(f32, 2, 5, 1, channels),
        shape(f32, count, mel_width),
    ]
    vmem = pl.BlockSpec(memory_space=pltpu.VMEM)
    tall = count + 4 * rows_all
    return pl.pallas_call(
        functools.partial(postnet_kernel, mel_width, loss_scale),
        out_shape=outs,
        in_specs=[pl.BlockSpec(memory_space=pltpu.SMEM)] + [vmem] * len(small),
        out_specs=[vmem] * len(outs),
        scratch_shapes=[
            pltpu.VMEM((tall, channels), bf16),
            pltpu.VMEM((tall, mel_width), bf16),
            pltpu.VMEM((count, channels), f32),
            pltpu.VMEM((4, count, channels), f32),
            pltpu.VMEM((count, mel_width), f32),
            pltpu.VMEM((5, 1, channels), f32),
            pltpu.VMEM((count, mel_width), f32),
        ],
        compiler_params=pltpu.CompilerParams(vmem_limit_bytes=kernel_vmem),
        name="postnet",
    )(unit, *small)


def shifted_frames(source, same):
    steps = source.shape[0]
    padded = jnp.pad(source, ((2, 2), (0, 0), (0, 0)))
    return [
        padded[offset : offset + steps] * same[:, :, offset, None].astype(source.dtype)
        for offset in range(5)
    ]


def by_rows(work, roomy, arrays, summed=False):
    if roomy:
        return work(*arrays)
    parts = arrays[0].shape[1] // 192

    def cut(value):
        value = value.reshape((value.shape[0], parts, -1) + value.shape[2:])
        return jnp.moveaxis(value, 1, 0)

    pieces = tuple(cut(value) for value in arrays)
    if summed:
        first = jax.eval_shape(work, *[value[0] for value in pieces])
        start = jnp.zeros(first.shape, first.dtype)
        return lax.scan(lambda total, now: (total + work(*now), None), start, pieces)[0]
    result = jnp.moveaxis(lax.map(lambda now: work(*now), pieces), 0, 1)
    return result.reshape((result.shape[0], -1) + result.shape[3:])


def post_layer(source, kernel, same):
    wide = jnp.concatenate(shifted_frames(source, same), axis=2)
    return jnp.einsum(
        "src,co->sro", wide, kernel.reshape(-1, kernel.shape[2]), preferred_element_type=f32
    )


def post_layer_back(grad, kernel, same):
    wide = jnp.concatenate(shifted_frames(grad, same), axis=2)
    turned = jnp.transpose(kernel[::-1], (0, 2, 1)).reshape(-1, kernel.shape[1])
    return jnp.einsum("sro,oc->src", wide, turned, preferred_element_type=f32)


def post_kernel_grad(source, grad, same):
    wide = jnp.concatenate(shifted_frames(source, same), axis=2)
    return jnp.einsum("src,sro->co", wide, grad, preferred_element_type=f32)


def on_device(
    memory,
    targets,
    segments,
    text_lengths,
    zone_first,
    zone_second,
    drop_first,
    drop_second,
    prenet_first,
    prenet_second,
    query_weight,
    memory_weight,
    location_conv,
    location_dense,
    energy_vector,
    lstm_first,
    bias_first,
    lstm_second,
    bias_second,
    frame_weight,
    frame_bias,
    post_first,
    post_middle,
    post_last,
    middle_norm,
    last_norm,
):
    micro_count, rows, text_width, memory_width = memory.shape
    frames = segments.shape[2]
    utterances = text_lengths.shape[2]
    mel_width = targets.shape[3]
    hidden = query_weight.shape[0]
    prenet_width = prenet_first.shape[1]
    attention_width = query_weight.shape[1]
    half = lstm_first.shape[2]
    depth_one, depth_two = lstm_first.shape[0], lstm_second.shape[0]
    unit = lax.axis_index("unit")
    place = lax.axis_index("batch")
    batch_size = lax.axis_size("batch")
    total_rows = rows * batch_size
    frame_count = float(total_rows * frames)
    first_unit = unit == 0
    longest = 3
    slots = 4 * rows

    def exchange(value):
        return lax.ppermute(value, "unit", [(0, 1), (1, 0)])

    def ordered(own, peer):
        return jnp.where(first_unit, own, peer), jnp.where(first_unit, peer, own)

    def whole(value, axis):
        return jnp.concatenate(ordered(value, exchange(value)), axis=axis)

    def mine(value):
        return lax.dynamic_index_in_dim(value, unit, 0, keepdims=False)

    def others(value):
        return lax.dynamic_index_in_dim(value, 1 - unit, 0, keepdims=False)

    def swapped(value, bit):
        pairs = [(index, index ^ bit) for index in range(batch_size)]
        other = lax.ppermute(value, "batch", pairs)
        upper = (place & bit) != 0
        return jnp.where(upper, other, value), jnp.where(upper, value, other)

    def gather_rows(value):
        bit = 1
        while bit < batch_size:
            value = jnp.concatenate(swapped(value, bit), axis=0)
            bit *= 2
        return value

    def gather_far_first(value):
        inner, bit, count = value.ndim, batch_size // 2, 0
        while bit:
            value = jnp.stack(swapped(value, bit))
            bit //= 2
            count += 1
        order = tuple(range(count - 1, -1, -1)) + tuple(range(count, count + inner))
        return jnp.transpose(value, order).reshape((batch_size,) + value.shape[count:])

    def gather_tiles(value):
        tiles = jnp.transpose(value.reshape(value.shape[0], -1, lanes), (1, 0, 2))
        return lax.all_gather(tiles, "batch", axis=1, tiled=True)

    own_two = gather_tiles(lstm_second)
    own_one = gather_tiles(lstm_first)
    peer_two = exchange(own_two)
    channel_rows = post_middle.shape[2]
    middle_width = post_middle.shape[3]
    last_rows = jnp.transpose(post_last, (1, 0, 2)).reshape(1, channel_rows, -1)
    post_rows = jnp.concatenate(
        [
            post_middle.reshape(-1, channel_rows, middle_width),
            jnp.pad(last_rows, ((0, 0), (0, 0), (0, middle_width - last_rows.shape[2]))),
        ],
        axis=0,
    )
    post_rows = jnp.transpose(gather_far_first(post_rows), (1, 0, 2, 3)).reshape(
        post_rows.shape[0], -1, middle_width
    )
    middle_half = post_rows[:-1].reshape(post_middle.shape[:2] + (-1, middle_width))
    middle_peer = exchange(middle_half)
    last_half = jnp.transpose(
        post_rows[-1, :, : last_rows.shape[2]].reshape(-1, 5, post_last.shape[2]), (1, 0, 2)
    )
    memory_now = mine(memory).reshape(rows * text_width, memory_width)
    segments_now = mine(segments)
    targets_now = mine(targets)
    frame_info = gather_rows(
        jnp.concatenate([targets_now, segments_now[:, :, None].astype(bf16)], axis=2).astype(f32)
    )

    same_frames = segments_now[:, :, None] == segments_now[:, None, :]
    earlier = jnp.tril(jnp.ones((frames, frames), jnp.bool_), -1)
    order = jnp.sum((same_frames & earlier[None]).astype(jnp.int32), axis=2)
    slot_of = order * slots + segments_now * rows + jnp.arange(rows, dtype=jnp.int32)[:, None]
    frame_rows = rows * frames
    padding = -frame_rows % 16
    slot_hot = (
        jnp.pad(slot_of.reshape(-1, 1), ((0, padding), (0, 0)), constant_values=-1)
        == jnp.arange(longest * slots, dtype=jnp.int32)[None, :]
    ).astype(bf16)
    slot_hot_frames = slot_hot[:frame_rows]
    carry_on = jnp.pad(
        (segments_now[:, 1:] == segments_now[:, :-1]).astype(f32), ((0, 0), (1, 0))
    )
    finished = jnp.pad(
        (segments_now[:, 1:] != segments_now[:, :-1]).astype(f32),
        ((0, 0), (0, 1)),
        constant_values=1.0,
    )

    def to_slots(value, kind=bf16):
        return lax.dot_general(
            slot_hot_frames,
            value.astype(bf16),
            (((0,), (0,)), ((), ())),
            preferred_element_type=f32,
        ).astype(kind)

    def to_frames(value):
        return jnp.dot(slot_hot, value.astype(bf16), preferred_element_type=f32).astype(bf16)

    def pad_frames(value):
        return jnp.pad(
            value.astype(f32).reshape(frame_rows, -1), ((0, padding), (0, 0))
        )

    previous = pad_frames(
        jnp.pad(targets_now[:, :-1], ((0, 0), (1, 0), (0, 0))).astype(f32)
        * carry_on[:, :, None]
    )
    drops_one = pad_frames(mine(drop_first))
    drops_two = pad_frames(mine(drop_second))

    zones_own = jnp.concatenate([mine(zone_first), mine(zone_second)], axis=2).astype(f32)
    zones_peer = exchange(
        jnp.concatenate([others(zone_first), others(zone_second)], axis=2).astype(f32)
    )
    zones_slots = to_slots(
        jnp.concatenate([zones_own, zones_peer], axis=2).reshape(rows * frames, -1), f32
    ).reshape(longest, slots, 4 * half)
    zone_one = jnp.concatenate(
        [zones_slots[:, :, :half], zones_slots[:, :, 2 * half : 3 * half]], axis=2
    )
    zone_two = jnp.concatenate(
        [zones_slots[:, :, half : 2 * half], zones_slots[:, :, 3 * half :]], axis=2
    )
    biases = jnp.stack([bias_first.reshape(-1), bias_second.reshape(-1)])
    biases = jnp.concatenate([biases, exchange(biases)], axis=1)
    text_ends = jnp.cumsum(mine(text_lengths), axis=1)
    owner = jnp.sum(
        (jnp.arange(text_width, dtype=jnp.int32)[None, :, None] >= text_ends[:, None, :]).astype(
            jnp.int32
        ),
        axis=2,
    )
    owner_slot = owner * rows + jnp.arange(rows, dtype=jnp.int32)[:, None]
    owner_hot = (
        owner_slot.reshape(-1, 1) == jnp.arange(lanes, dtype=jnp.int32)[None, :]
    ).astype(f32)
    conv_float = location_conv.astype(f32)
    dense_float = location_dense.astype(f32)
    reach = location_conv.shape[2] // 2
    taps_first = jnp.transpose(conv_float, (1, 2, 0))
    taps_first = jnp.pad(
        taps_first,
        ((0, 0), (0, lanes - taps_first.shape[1]), (0, lanes - taps_first.shape[2])),
    )
    dense_wide = jnp.pad(dense_float, ((0, lanes - dense_float.shape[0]), (0, 0)))
    taps_forward = jnp.roll(taps_first[:, ::-1], reach, axis=1)
    taps_back = jnp.roll(taps_first, 1 - reach, axis=1)
    frame_wide = jnp.pad(
        frame_weight.astype(f32), ((0, 0), (0, lanes - frame_weight.shape[1]))
    )
    frame_bias_wide = jnp.pad(frame_bias, (0, lanes - frame_bias.shape[0]))[None, :]
    vector_float = energy_vector.astype(f32)
    vector_wide = jnp.broadcast_to(vector_float[:, None], (attention_width, lanes))
    memory_float = memory_now.astype(f32)
    query_float = query_weight.astype(f32)
    unit_array = unit.astype(jnp.int32).reshape(1)

    targets_all = jnp.transpose(frame_info[:, :, :mel_width].astype(f32), (1, 0, 2))
    segments_all = jnp.transpose(frame_info[:, :, mel_width].astype(jnp.int32))
    padded = jnp.pad(segments_all, ((2, 2), (0, 0)), constant_values=-1)
    same = jnp.stack([padded[offset : offset + frames] == segments_all for offset in range(5)])
    same = jnp.moveaxis(same, 0, 2)
    first_full = whole(post_first, 2)
    last_full = whole(last_half, 2)
    middle_gain = whole(middle_norm, 2)
    last_gain = whole(last_norm, 1)
    loss_scale = 2.0 / (mel_width * total_rows)
    count = total_rows * frames
    channels = middle_norm.shape[2] * 2
    masks = jnp.broadcast_to(
        jnp.transpose(same, (2, 0, 1)).reshape(5, count, 1).astype(bf16), (5, count, lanes)
    )
    wide_gain = jnp.pad(last_gain, ((0, 0), (0, channels - mel_width)))
    norms = jnp.concatenate([middle_gain, wide_gain[:, None, :]], axis=1)[:, :, None, :]
    forward_small = (
        previous,
        drops_one,
        drops_two,
        prenet_first.astype(f32),
        prenet_second.astype(f32),
        slot_hot.astype(f32),
        zone_one,
        zone_two,
        biases[0:1],
        biases[1:2],
        owner_hot,
        memory_float,
        memory_weight.astype(f32),
        query_float,
        vector_wide,
        taps_forward,
        dense_wide,
        frame_wide,
        frame_bias_wide,
    )
    (
        own_one,
        own_two,
        forward_small,
        taps_back,
        vector_row,
        targets_all,
        masks,
        first_full,
        middle_half,
        middle_peer,
        last_full,
        norms,
    ) = lax.optimization_barrier(
        (
            own_one,
            own_two,
            forward_small,
            taps_back,
            vector_float[None, :],
            targets_all,
            masks,
            first_full,
            middle_half,
            middle_peer,
            last_full,
            norms,
        )
    )
    weights = (own_one, exchange(own_one), own_two, peer_two)
    slot_wide, zone_one, zone_two = forward_small[5], forward_small[6], forward_small[7]
    memory_float, query_float = forward_small[11], forward_small[13]
    dense_wide, frame_wide = forward_small[16], forward_small[17]

    (
        gates_one,
        gates_two,
        prior_one,
        prior_two,
        round_one,
        round_two,
        contexts,
        mixed_all,
        alphas,
        taps,
        mixed_one,
        mixed_two,
        hidden_round,
        prenet_round,
        frame_out,
    ) = call_forward(
        unit_array,
        weights,
        forward_small,
        (
            longest,
            slots,
            hidden,
            memory_width,
            rows * text_width,
            frame_rows + padding,
            prenet_width,
        ),
    )

    states = to_frames(
        jnp.concatenate([round_one, contexts, round_two], axis=2).reshape(longest * slots, -1)
    )
    frame_in = jnp.concatenate(
        [states[:, hidden + memory_width :], states[:, hidden : hidden + memory_width]], axis=1
    )
    frame_in = frame_in[:frame_rows]
    frame_out = frame_out[:frame_rows]
    mel_own = frame_out[:, :mel_width].reshape(rows, frames, mel_width)
    stop_logit = frame_out[:, mel_width].reshape(rows, frames)
    mel_all = jnp.transpose(
        gather_rows(mel_own), (1, 0, 2)
    )
    inputs_own = jnp.concatenate([prenet_round.astype(bf16), states], axis=1)
    roomy = total_rows * frames <= 2048
    if roomy:
        inputs_all = lax.all_gather(inputs_own, "batch", axis=0, tiled=True)

    if roomy:
        (
            inputs_first,
            inputs_later,
            grads_early,
            grads_last,
            norm_grads,
            grad_mel,
        ) = call_postnet(
            unit_array,
            (
                mel_all.reshape(count, mel_width),
                targets_all.reshape(count, mel_width),
                masks,
                first_full,
                middle_half,
                middle_peer,
                last_full,
                norms[0],
                norms[1],
            ),
            loss_scale,
            total_rows,
        )
        gain_grads = [norm_grads[0, layer, 0] for layer in range(5)]
        shift_grads = [norm_grads[1, layer, 0] for layer in range(5)]
        gain_grads[4], shift_grads[4] = gain_grads[4][:mel_width], shift_grads[4][:mel_width]
        kernel_grads = []
        for layer in range(5):
            if layer == 0:
                source = inputs_first
            else:
                source = lax.dynamic_slice_in_dim(
                    inputs_later[layer - 1], place * channel_rows, channel_rows, 1
                )
            grad_norm = grads_early[layer] if layer < 4 else grads_last
            kernel_grads.append(
                post_kernel_grad(
                    source.reshape(frames, total_rows, -1),
                    grad_norm.reshape(frames, total_rows, -1),
                    same,
                ).reshape(5, source.shape[1], grad_norm.shape[1])
            )
        grad_mel = jnp.transpose(
            lax.dynamic_slice_in_dim(
                grad_mel.reshape(frames, total_rows, mel_width), place * rows, rows, 1
            ),
            (1, 0, 2),
        )
    else:
        middle_full = whole(middle_half, 3)
        kernels = [first_full, middle_full[0], middle_full[1], middle_full[2], last_full]
        gains = [middle_gain[0, layer] for layer in range(4)] + [last_gain[0]]
        shifts = [middle_gain[1, layer] for layer in range(4)] + [last_gain[1]]
        layer_in = mel_all.astype(bf16)
        layer_inputs, normed_all, inverses = [], [], []
        output = None
        for layer in range(5):
            layer_inputs.append(layer_in)
            pre_norm = by_rows(
                lambda source, same_now: post_layer(source, kernels[layer], same_now),
                roomy,
                (layer_in, same),
            )
            mean_now = jnp.sum(pre_norm, axis=(0, 1)) / frame_count
            centered = pre_norm - mean_now
            inverse = lax.rsqrt(jnp.sum(centered * centered, axis=(0, 1)) / frame_count + norm_eps)
            normed = centered * inverse
            output = normed * gains[layer] + shifts[layer]
            normed_all.append(normed)
            inverses.append(inverse)
            if layer < 4:
                layer_in = jnp.tanh(output).astype(bf16)
                if not roomy:
                    layer_in, normed_all[layer] = lax.optimization_barrier(
                        (layer_in, normed_all[layer])
                    )

        grad_post = loss_scale * (mel_all + output - targets_all)
        kernel_grads, gain_grads, shift_grads = [None] * 5, [None] * 5, [None] * 5
        grad_output = grad_post
        grad_input = None
        for layer in (4, 3, 2, 1, 0):
            if layer < 4:
                normed_all[layer] = lax.optimization_barrier(normed_all[layer])
                active = jnp.tanh(normed_all[layer] * gains[layer] + shifts[layer])
                grad_output = grad_input * (1.0 - active * active)
            shift_grads[layer] = jnp.sum(grad_output, axis=(0, 1))
            gain_grads[layer] = jnp.sum(grad_output * normed_all[layer], axis=(0, 1))
            grad_norm = (
                gains[layer]
                * inverses[layer]
                * (
                    grad_output
                    - shift_grads[layer] / frame_count
                    - normed_all[layer] * (gain_grads[layer] / frame_count)
                )
            ).astype(bf16)
            grad_input = by_rows(
                lambda grad, same_now: post_layer_back(grad, kernels[layer], same_now),
                roomy,
                (grad_norm, same),
            )
            source = layer_inputs[layer]
            if layer > 0:
                source = lax.dynamic_slice_in_dim(source, place * channel_rows, channel_rows, 2)
            kernel_grads[layer] = by_rows(post_kernel_grad, roomy, (source, grad_norm, same), True)
            kernel_grads[layer] = kernel_grads[layer].reshape(5, source.shape[2], -1)
            if not roomy:
                grad_input, kernel_grads[layer] = lax.optimization_barrier(
                    (grad_input, kernel_grads[layer])
                )
        grad_mel = loss_scale * (mel_all - targets_all) + grad_post + grad_input
        grad_mel = jnp.transpose(
            lax.dynamic_slice_in_dim(grad_mel, place * rows, rows, 1), (1, 0, 2)
        )

    if not roomy:
        inputs_own, grad_mel = lax.optimization_barrier((inputs_own, grad_mel))
        inputs_all = lax.all_gather(inputs_own, "batch", axis=0, tiled=True)

    def add_units(value, axis):
        width = value.shape[axis] // 2
        halves = [
            lax.slice_in_dim(value, start, start + width, axis=axis) for start in (0, width)
        ]
        keep = jnp.where(first_unit, halves[0], halves[1])
        give = jnp.where(first_unit, halves[1], halves[0])
        return keep + exchange(give)

    post_first_grad = add_units(kernel_grads[0], 2)
    post_middle_grad = add_units(jnp.stack(kernel_grads[1:4]), 3)
    post_last_grad = add_units(kernel_grads[4], 2)
    middle_norm_grad = add_units(
        jnp.stack([jnp.stack(gain_grads[:4]), jnp.stack(shift_grads[:4])]), 2
    )
    last_norm_grad = add_units(jnp.stack([gain_grads[4], shift_grads[4]]), 1)

    grad_stop = (jax.nn.sigmoid(stop_logit) - finished) / total_rows
    grad_frame = (
        jnp.concatenate([grad_mel, grad_stop[:, :, None]], axis=2)
        .reshape(rows * frames, mel_width + 1)
        .astype(bf16)
    )
    frame_weight_grad = lax.dot_general(
        frame_in, grad_frame, (((0,), (0,)), ((), ())), preferred_element_type=f32
    )
    frame_bias_grad = jnp.sum(grad_frame.astype(f32), axis=0)
    grad_frame_slots = to_slots(
        jnp.pad(grad_frame, ((0, 0), (0, lanes - mel_width - 1))), f32
    ).reshape(longest, slots, lanes)

    (
        sent,
        prenet_back,
        context_grads,
        query_back,
        processed_back,
        vector_back,
        filter_back,
    ) = call_backward(
        unit_array,
        weights,
        (
            gates_one,
            gates_two,
            prior_one,
            prior_two,
            zone_one,
            zone_two,
            owner_hot,
            memory_float,
            query_float,
            vector_row,
            taps_back,
            dense_wide,
            mixed_all,
            alphas,
            taps,
            grad_frame_slots,
            frame_wide,
            slot_wide,
        ),
    )

    bias_sums = jnp.transpose(
        jnp.sum(sent.astype(f32), axis=1).reshape(-1, 4, lanes), (1, 0, 2)
    ).reshape(-1, lanes)
    slice_width = 2 * hidden // batch_size
    if slice_width != lanes:
        sent = sent.reshape(sent.shape[0], sent.shape[1], 4, -1, slice_width)
        sent = jnp.transpose(sent, (0, 3, 1, 2, 4)).reshape(batch_size, sent.shape[1], -1)
    received = lax.all_to_all(sent, "batch", 0, 0, tiled=True)
    segments_rows = segments_all.T
    carried = jnp.pad(
        (segments_rows[:, 1:] == segments_rows[:, :-1]).astype(bf16), ((0, 0), (0, 1))
    ).reshape(batch_size, frame_rows)
    carried = jnp.pad(carried, ((0, 0), (0, padding)))
    after = jnp.pad(received[:, 1:], ((0, 0), (0, 1), (0, 0))) * carried[:, :, None]
    received = received.reshape(batch_size * (frame_rows + padding), -1)
    after = after.reshape(batch_size * (frame_rows + padding), -1)

    def product(start, width, grads):
        return lax.dot_general(
            inputs_all[:, start : start + width],
            grads,
            (((0,), (0,)), ((), ())),
            preferred_element_type=f32,
        )

    pair = 2 * slice_width
    first_part = jnp.concatenate(
        [
            product(0, prenet_width, received[:, :pair]),
            product(prenet_width + hidden, memory_width, after[:, :pair]),
            product(prenet_width, hidden, after[:, :pair]),
        ],
        axis=0,
    )
    second_part = jnp.concatenate(
        [
            product(prenet_width, hidden + memory_width, received[:, pair:]),
            product(prenet_width + hidden + memory_width, hidden, after[:, pair:]),
        ],
        axis=0,
    )
    parts = jnp.concatenate(
        [
            first_part.reshape(batch_size, depth_one, pair),
            second_part.reshape(batch_size, depth_two, pair),
        ],
        axis=1,
    )
    parts = add_units(parts, 2).astype(bf16)
    parts = lax.all_to_all(parts, "batch", 0, 0, tiled=True).astype(f32)
    parts = jnp.transpose(parts, (1, 0, 2)).reshape(depth_one + depth_two, 4, half)

    grad_prenet = lax.dot_general(
        slot_hot.astype(f32),
        prenet_back.reshape(longest * slots, prenet_width),
        (((1,), (0,)), ((), ())),
        precision=precise,
    )

    def silu_back(grad, mixed, drops):
        gate = jax.nn.sigmoid(mixed)
        return grad * drops * 2.0 * gate * (1.0 + mixed * (1.0 - gate))

    def exact(a, b, contract):
        return lax.dot_general(
            a.astype(f32), b.astype(f32), (contract, ((), ())), precision=precise
        )

    grad_mixed_two = silu_back(grad_prenet, mixed_two, drops_two)
    prenet_second_grad = exact(hidden_round, grad_mixed_two, ((0,), (0,)))
    grad_hidden = exact(grad_mixed_two, prenet_second, ((1,), (1,)))
    grad_mixed_one = silu_back(grad_hidden, mixed_one, drops_one)
    prenet_first_grad = exact(previous, grad_mixed_one, ((0,), (0,)))

    query_weight_grad = exact(
        round_one.reshape(longest * slots, hidden),
        query_back.reshape(longest * slots, attention_width),
        ((0,), (0,)),
    )
    processed_round = processed_back.astype(bf16)
    memory_weight_grad = lax.dot_general(
        memory_now, processed_round, (((0,), (0,)), ((), ())), preferred_element_type=f32
    )
    memory_grad = lax.dot_general(
        processed_round, memory_weight, (((1,), (1,)), ((), ())), preferred_element_type=f32
    )
    for step in range(longest):
        memory_grad = memory_grad + exact(
            alphas[step][:, :slots], context_grads[step], ((1,), (0,))
        )
    memory_grad = memory_grad.reshape(rows, text_width, memory_width)
    memory_grads = jnp.stack(ordered(memory_grad, exchange(memory_grad)))
    filter_grads = jnp.roll(filter_back, -reach, axis=1)[:, ::-1][:, : location_conv.shape[2]]
    conv_grad = jnp.einsum("cka,fa->fck", filter_grads, dense_float, precision=precise)
    dense_grad = jnp.einsum("cka,fck->fa", filter_grads, conv_float, precision=precise)

    def two_columns(value):
        return jnp.concatenate([value[:, :lanes], value[:, lanes:]], axis=0)

    def to_lanes(value):
        return jnp.pad(value, ((0, 0), (0, lanes - value.shape[1])))

    filter_count, _, tap_count = location_conv.shape
    packed = [
        two_columns(prenet_first_grad),
        two_columns(prenet_second_grad),
        query_weight_grad,
        memory_weight_grad,
        to_lanes(frame_weight_grad),
        to_lanes(conv_grad.reshape(filter_count, -1)),
        dense_grad,
        bias_sums,
        vector_back,
        to_lanes(frame_bias_grad[None, :]),
    ]
    heights = [value.shape[0] for value in packed]
    shares = 2 * batch_size
    surplus = -sum(heights) % (8 * shares)
    packed = jnp.concatenate(packed + [jnp.zeros((surplus, lanes), f32)], axis=0)
    packed = add_units(packed, 0).reshape(batch_size, -1, lanes)
    packed = jnp.sum(lax.all_to_all(packed, "batch", 0, 0, tiled=True), axis=0)
    packed = whole(gather_rows(packed), 0)
    small, start = [], 0
    for height in heights:
        small.append(packed[start : start + height])
        start += height

    def from_columns(value):
        tall = value.shape[0] // 2
        return jnp.concatenate([value[:tall], value[tall:]], axis=1)

    biases_grad = small[7].reshape(2, 2, -1)
    biases_grad = jnp.where(first_unit, biases_grad[:, 0], biases_grad[:, 1])
    biases_grad = biases_grad.reshape(2, 4, half)
    small = [
        from_columns(small[0]),
        from_columns(small[1]),
        small[2],
        small[3],
        small[5][:, : 2 * tap_count].reshape(filter_count, 2, tap_count),
        small[6],
        small[8][0],
        small[4][:, : mel_width + 1],
        small[9][0, : mel_width + 1],
    ]
    return (
        small[0],
        small[1],
        small[2],
        small[3],
        small[4],
        small[5],
        small[6],
        parts[:depth_one],
        biases_grad[0],
        parts[depth_one:],
        biases_grad[1],
        small[7],
        small[8],
        post_first_grad,
        post_middle_grad,
        post_last_grad,
        middle_norm_grad,
        last_norm_grad,
        memory_grads,
    )


def solution(mesh):
    in_specs = (
        P(None, "batch", None, None),
        P(None, "batch", None, None),
        P(None, "batch", None),
        P(None, "batch", None),
        P(None, "batch", None, "unit"),
        P(None, "batch", None, "unit"),
        P(None, "batch", None, None),
        P(None, "batch", None, None),
        P(),
        P(),
        P(),
        P(),
        P(),
        P(),
        P(),
        P("batch", None, "unit"),
        P(None, "unit"),
        P("batch", None, "unit"),
        P(None, "unit"),
        P(),
        P(),
        P(None, None, "unit"),
        P(None, None, "batch", "unit"),
        P(None, "batch", "unit"),
        P(None, None, "unit"),
        P(None, "unit"),
    )
    out_specs = (
        P(),
        P(),
        P(),
        P(),
        P(),
        P(),
        P(),
        P("batch", None, "unit"),
        P(None, "unit"),
        P("batch", None, "unit"),
        P(None, "unit"),
        P(),
        P(),
        P(None, None, "unit"),
        P(None, None, "batch", "unit"),
        P(None, "batch", "unit"),
        P(None, None, "unit"),
        P(None, "unit"),
        P(None, "batch", None, None),
    )
    return jax.shard_map(
        on_device, mesh=mesh, in_specs=in_specs, out_specs=out_specs, check_vma=False
    )
```

```python
import functools

import jax
import jax.numpy as jnp
from jax import lax
from jax.experimental import pallas as pl
from jax.experimental.pallas import tpu as pltpu
from jax.sharding import PartitionSpec as P

precise = lax.Precision.HIGHEST
norm_eps = 1e-05
f32 = jnp.float32
bf16 = jnp.bfloat16
lanes = 128
kernel_vmem = 60 * 1024 * 1024


def split(value):
    high = value.astype(bf16)
    return high, (value - high.astype(f32)).astype(bf16)


def dot(a, b, contract=((1,), (0,))):
    return lax.dot_general(a, b, (contract, ((), ())), preferred_element_type=f32)


def dot_left(exact, value, contract=((1,), (0,))):
    high, low = split(value)
    return dot(exact, high, contract) + dot(exact, low, contract)


def dot_right(value, exact, contract=((1,), (0,))):
    high, low = split(value)
    return dot(high, exact, contract) + dot(low, exact, contract)


def dot_both(a, b, contract=((1,), (0,))):
    a_high, a_low = split(a)
    b_high, b_low = split(b)
    return (
        dot(a_high, b_high, contract) + dot(a_low, b_high, contract) + dot(a_high, b_low, contract)
    )


rows_first = ((0,), (0,))
lanes_both = ((1,), (1,))


def position_hot(position_count, text_width, reverse):
    place = lax.broadcasted_iota(jnp.int32, (position_count, lanes), 0) & (text_width - 1)
    lane = lax.broadcasted_iota(jnp.int32, (position_count, lanes), 1)
    place = (lanes - 1) - place if reverse else place + 1
    return (place == lane).astype(bf16)


def slant(value, text_width):
    blocks = [
        pltpu.roll(value[start : start + text_width], 0, 1, stride=1, stride_axis=0)
        for start in range(0, value.shape[0], text_width)
    ]
    return jnp.concatenate(blocks, axis=0)


def pad_rows(value):
    return jnp.concatenate(
        [value, jnp.zeros((lanes - value.shape[0], value.shape[1]), value.dtype)], axis=0
    )


def unit_spot(chunk, unit, per_half):
    half = (chunk // per_half + unit) % 2
    return pl.multiple_of((half * per_half + chunk % per_half) * lanes, lanes)


def gate_spot(chunk, gate, per_half):
    start = (chunk // per_half) * 4 * per_half + gate * per_half + chunk % per_half
    return pl.multiple_of(start * lanes, lanes)


def forward_kernel(
    unit_ref,
    own_one,
    peer_one,
    own_two,
    peer_two,
    previous_ref,
    drop_one,
    drop_two,
    layer_one,
    layer_two,
    slot_ref,
    zone_one,
    zone_two,
    bias_one,
    bias_two,
    hot_ref,
    memory_ref,
    project_ref,
    query_ref,
    vector_ref,
    conv_ref,
    dense_ref,
    frame_ref,
    frame_bias,
    gates_one,
    gates_two,
    prior_one,
    prior_two,
    round_one,
    round_two,
    context_ref,
    mixed_ref,
    alpha_ref,
    taps_ref,
    prenet_one,
    prenet_two,
    prenet_hidden,
    prenet_out,
    frame_out,
    held_one,
    held_two,
    input_ref,
    prenet_ref,
    processed_ref,
    filter_ref,
    state_one,
    cell_one,
    state_two,
    cell_two,
    sems,
):
    unit = unit_ref[0]
    steps, slots, hidden = round_one.shape
    prenet_width = layer_two.shape[1]
    context_width = context_ref.shape[2]
    half = hidden // 2
    per_half = half // lanes
    position_count = hot_ref.shape[0]
    text_width = position_count // (slots // 4)
    copies_two = [
        pltpu.make_async_copy(own_two, held_two.at[0], sems.at[0]),
        pltpu.make_async_copy(peer_two, held_two.at[1], sems.at[1]),
    ]
    copies_one = [
        pltpu.make_async_copy(own_one, held_one.at[0], sems.at[2]),
        pltpu.make_async_copy(peer_one, held_one.at[1], sems.at[3]),
    ]
    for copy in copies_two + copies_one:
        copy.start()
    for ref in (state_one, cell_one, state_two, cell_two):
        ref[...] = jnp.zeros_like(ref)

    def gates_into(held, depth, bias_ref, out_ref, step):
        def one(block, _):
            side = block // 4
            inputs = input_ref[:, :depth]
            for pair in range(per_half // 2):
                tile = (block % 4) * per_half + 2 * pair
                outside = pl.ds(
                    pl.multiple_of(block * half + 2 * pair * lanes, 2 * lanes), 2 * lanes
                )
                kernel = jnp.concatenate(
                    [held[side, tile, :depth, :], held[side, tile + 1, :depth, :]], axis=1
                )
                out_ref[step, :, outside] = dot(inputs, kernel) + bias_ref[:, outside]
            return 0

        lax.fori_loop(0, 8, one, 0)

    def cell(gates_ref, zone_ref, prior_ref, state, cells, round_ref, step):
        def one(chunk, _):
            spot = pl.ds(pl.multiple_of(chunk * lanes, lanes), lanes)
            values = [
                gates_ref[step, :, pl.ds(gate_spot(chunk, gate, per_half), lanes)]
                for gate in range(4)
            ]
            zone = zone_ref[step, :, spot]
            before = cells[:, spot]
            prior_ref[step, :, spot] = before
            fresh = jax.nn.sigmoid(values[1]) * before + jax.nn.sigmoid(values[0]) * jnp.tanh(
                values[2]
            )
            output = jax.nn.sigmoid(values[3]) * jnp.tanh(fresh)
            now = zone * state[:, spot] + (1.0 - zone) * output
            state[:, spot] = now
            cells[:, spot] = zone * before + (1.0 - zone) * fresh
            round_ref[step, :, pl.ds(unit_spot(chunk, unit, per_half), lanes)] = now.astype(bf16).astype(
                f32
            )
            return 0

        lax.fori_loop(0, 2 * per_half, one, 0)

    def attention(step, location):
        inside = hot_ref[...] > 0.0
        hot = hot_ref[...].astype(bf16)
        query = pad_rows(dot(round_one[step].astype(bf16), query_ref[...].astype(bf16)))
        summed = dot_left(hot, query) + processed_ref[...]
        if location is not None:
            summed = summed + location
        mixed = jnp.tanh(summed)
        mixed_ref[step] = mixed
        energy = dot_right(mixed, vector_ref[...].astype(bf16))
        most = jnp.max(jnp.where(inside, energy, -1000000000.0), axis=0, keepdims=True)
        shifted = jnp.where(inside, jnp.exp(energy - most), 0.0)
        total = jnp.sum(shifted, axis=0, keepdims=True)
        alpha = shifted / jnp.where(total > 0.0, total, 1.0)
        alpha_ref[step] = alpha
        context = dot_right(alpha, memory_ref[...].astype(bf16), rows_first)[:slots]
        context_ref[step] = context.astype(bf16).astype(f32)

    def taps_of(step):
        spread = dot_right(
            alpha_ref[step], position_hot(position_count, text_width, True), rows_first
        )
        taps_ref[step] = slant(dot_left(hot_ref[...].astype(bf16), spread), text_width)

    def second_layer(step, depth):
        input_ref[:, :hidden] = round_one[step].astype(bf16)
        input_ref[:, hidden : hidden + context_width] = context_ref[step].astype(bf16)
        gates_into(held_two, depth, bias_two, gates_two, step)
        cell(gates_two, zone_two, prior_two, state_two, cell_two, round_two, step)

    slot_hot = slot_ref[...].astype(bf16)

    def prenet_layer(source, layer, drops, mixed_out, out):
        mixed = dot(source.astype(bf16), layer[...].astype(bf16))
        mixed_out[...] = mixed
        value = (mixed * jax.nn.sigmoid(mixed) * drops[...] * 2.0).astype(bf16)
        out[...] = value.astype(f32)
        return value

    hidden_value = prenet_layer(previous_ref[...], layer_one, drop_one, prenet_one, prenet_hidden)
    prenet_value = prenet_layer(hidden_value, layer_two, drop_two, prenet_two, prenet_out)
    prenet_slots = dot(slot_hot, prenet_value, rows_first)
    for step in range(steps):
        prenet_ref[step] = prenet_slots[step * slots : (step + 1) * slots]
    processed_ref[...] = dot(memory_ref[...].astype(bf16), project_ref[...].astype(bf16))
    for channel in range(2):
        filter_ref[channel] = dot(
            conv_ref[channel].astype(bf16), dense_ref[...].astype(bf16)
        )

    gates_one[0] = jnp.broadcast_to(bias_one[...], gates_one.shape[1:])
    cell(gates_one, zone_one, prior_one, state_one, cell_one, round_one, 0)
    attention(0, None)
    taps_of(0)
    for copy in copies_two:
        copy.wait()
    second_layer(0, hidden + context_width)
    for copy in copies_one:
        copy.wait()

    def later(step, _):
        input_ref[:, :prenet_width] = prenet_ref[step].astype(bf16)
        input_ref[:, prenet_width : prenet_width + context_width] = context_ref[step - 1].astype(
            bf16
        )
        input_ref[:, prenet_width + context_width : prenet_width + context_width + hidden] = (
            round_one[step - 1].astype(bf16)
        )
        gates_into(
            held_one, prenet_width + context_width + hidden, bias_one, gates_one, step
        )
        cell(gates_one, zone_one, prior_one, state_one, cell_one, round_one, step)
        previous = taps_ref[step - 1]
        summed = jnp.where(step == 2, taps_ref[0] + previous, previous)
        attention(step, dot_both(previous, filter_ref[0]) + dot_both(summed, filter_ref[1]))

        @pl.when(step < steps - 1)
        def _():
            taps_of(step)

        input_ref[:, hidden + context_width :] = round_two[step - 1].astype(bf16)
        second_layer(step, 2 * hidden + context_width)
        return 0

    lax.fori_loop(1, steps, later, 0)
    for step in range(steps):
        values = dot(round_two[step].astype(bf16), frame_ref[:hidden].astype(bf16)) + dot(
            context_ref[step].astype(bf16), frame_ref[hidden:].astype(bf16)
        )
        high = values.astype(bf16)
        rest = values - high.astype(f32)
        middle = rest.astype(bf16)
        low = (rest - middle.astype(f32)).astype(bf16)
        chosen = slot_hot[:, step * slots : (step + 1) * slots]
        picked = (dot(chosen, high) + dot(chosen, middle)) + dot(chosen, low)
        frame_out[...] = (frame_bias[...] if step == 0 else frame_out[...]) + picked


def backward_kernel(
    unit_ref,
    own_one,
    peer_one,
    own_two,
    peer_two,
    gates_one,
    gates_two,
    prior_one,
    prior_two,
    zone_one,
    zone_two,
    hot_ref,
    memory_ref,
    query_ref,
    vector_ref,
    conv_ref,
    dense_ref,
    mixed_ref,
    alpha_ref,
    taps_ref,
    frame_grad,
    frame_weight,
    slot_ref,
    sent_ref,
    prenet_grad,
    context_grad,
    query_grad,
    processed_grad,
    vector_grad,
    filter_grad,
    held_one,
    held_two,
    grads_one,
    grads_two,
    back_one,
    back_two,
    state_one,
    cell_one,
    state_two,
    cell_two,
    previous_grad,
    summed_grad,
    from_query,
    frame_ref,
    filter_ref,
    sems,
):
    unit = unit_ref[0]
    steps, slots, prenet_width = prenet_grad.shape
    context_width = context_grad.shape[2]
    hidden = state_one.shape[1]
    half = hidden // 2
    per_half = half // lanes
    position_count = hot_ref.shape[0]
    text_width = position_count // (slots // 4)
    copies_two = [
        pltpu.make_async_copy(own_two, held_two.at[0], sems.at[0]),
        pltpu.make_async_copy(peer_two, held_two.at[1], sems.at[1]),
    ]
    copies_one = [
        pltpu.make_async_copy(own_one, held_one.at[0], sems.at[2]),
        pltpu.make_async_copy(peer_one, held_one.at[1], sems.at[3]),
    ]
    for copy in copies_two + copies_one:
        copy.start()
    for ref in (
        state_one,
        cell_one,
        state_two,
        cell_two,
        back_one,
        back_two,
        previous_grad,
        summed_grad,
        processed_grad,
        vector_grad,
        filter_grad,
    ):
        ref[...] = jnp.zeros_like(ref)

    def cell(gates_ref, prior_ref, zone_ref, state, cells, grads_ref, step, incoming):
        def one(chunk, _):
            spot = pl.ds(pl.multiple_of(chunk * lanes, lanes), lanes)
            places = [pl.ds(gate_spot(chunk, gate, per_half), lanes) for gate in range(4)]
            values = [gates_ref[step, :, place] for place in places]
            zone = zone_ref[step, :, spot]
            keep = 1.0 - zone
            before = prior_ref[step, :, spot]
            gate_in = jax.nn.sigmoid(values[0])
            gate_forget = jax.nn.sigmoid(values[1])
            candidate = jnp.tanh(values[2])
            gate_out = jax.nn.sigmoid(values[3])
            bent = jnp.tanh(gate_forget * before + gate_in * candidate)
            grad_state = incoming(unit_spot(chunk, unit, per_half)) + state[:, spot]
            grad_cell = cells[:, spot]
            grad_new = keep * grad_state
            grad_fresh = grad_new * gate_out * (1.0 - bent * bent) + keep * grad_cell
            state[:, spot] = zone * grad_state
            cells[:, spot] = zone * grad_cell + gate_forget * grad_fresh
            results = (
                grad_fresh * candidate * gate_in * (1.0 - gate_in),
                grad_fresh * before * gate_forget * (1.0 - gate_forget),
                grad_fresh * gate_in * (1.0 - candidate * candidate),
                grad_new * bent * gate_out * (1.0 - gate_out),
            )
            for place, result in zip(places, results):
                grads_ref[step, :, place] = result.astype(bf16)
            return 0

        lax.fori_loop(0, 2 * per_half, one, 0)

    def inputs_back(grads_ref, held, out_ref, step, blocks):
        def one(block, _):
            spot = pl.ds(pl.multiple_of(block * 256, 256), 256)
            total = None
            for tile in range(0, 8 * per_half, 2):
                side, inside = tile // (4 * per_half), tile % (4 * per_half)
                kernel = jnp.concatenate(
                    [held[side, inside, spot, :], held[side, inside + 1, spot, :]], axis=1
                )
                grads = grads_ref[step, :, tile * lanes : (tile + 2) * lanes]
                product = dot(grads, kernel, lanes_both)
                total = product if total is None else total + product
            out_ref[:, spot] = total
            return 0

        lax.fori_loop(0, blocks, one, 0)

    def attention(step, located):
        inside = hot_ref[...] > 0.0
        hot = hot_ref[...].astype(bf16)
        alpha = alpha_ref[step]
        mixed = mixed_ref[step]
        context_now = pad_rows(context_grad[step])
        weights_grad = jnp.where(
            inside,
            dot_left(memory_ref[...].astype(bf16), context_now, lanes_both)
            + previous_grad[...]
            + summed_grad[...],
            0.0,
        )
        product = alpha * weights_grad
        energy_grad = product - alpha * jnp.sum(product, axis=0, keepdims=True)
        spread = jnp.sum(energy_grad, axis=1, keepdims=True)
        vector_grad[...] += jnp.sum(spread * mixed, axis=0, keepdims=True)
        mixed_grad = spread * vector_ref[...] * (1.0 - mixed * mixed)
        processed_grad[...] += mixed_grad
        high, low = split(mixed_grad)
        query_now = (dot(hot, high, rows_first) + dot(hot, low, rows_first))[:slots]
        query_grad[step] = query_now
        from_query[...] = dot_right(query_now, query_ref[...].astype(bf16), lanes_both)
        if located:
            previous = taps_ref[step - 1]
            summed = jnp.where(step == 2, taps_ref[0] + previous, previous)
            filter_grad[0] += dot_both(previous, mixed_grad, rows_first)
            filter_grad[1] += dot_both(summed, mixed_grad, rows_first)
            place_hot = position_hot(position_count, text_width, False)

            def taps_back(channel):
                taps_grad = slant(
                    dot_both(mixed_grad, filter_ref[channel], lanes_both), text_width
                )
                gathered = dot_right(taps_grad, hot, rows_first)
                return jnp.where(inside, dot_left(place_hot, gathered), 0.0)

            previous_grad[...] = taps_back(0)
            summed_grad[...] += taps_back(1)

    def arrived(step, copies):
        @pl.when(step == steps - 1)
        def _():
            for copy in copies:
                copy.wait()

    def step_back(step, located):
        cell(
            gates_two,
            prior_two,
            zone_two,
            state_two,
            cell_two,
            grads_two,
            step,
            lambda spot: frame_ref[step, :, pl.ds(spot, lanes)]
            + back_two[:, pl.ds(spot + hidden + context_width, lanes)],
        )
        blocks_two = (hidden + context_width + (hidden if located else 0)) // 256
        if located:
            arrived(step, copies_two)
        inputs_back(grads_two, held_two, back_two, step, blocks_two)
        context_grad[step] = (
            back_two[:, hidden : hidden + context_width]
            + frame_ref[step, :, hidden:]
            + back_one[:, prenet_width : prenet_width + context_width]
        )
        attention(step, located)
        cell(
            gates_one,
            prior_one,
            zone_one,
            state_one,
            cell_one,
            grads_one,
            step,
            lambda spot: back_two[:, pl.ds(spot, lanes)]
            + from_query[:, pl.ds(spot, lanes)]
            + back_one[:, pl.ds(spot + prenet_width + context_width, lanes)],
        )
        blocks_one = (prenet_width + (hidden + context_width if located else 0)) // 256
        if located:
            arrived(step, copies_one)
        inputs_back(grads_one, held_one, back_one, step, blocks_one)
        prenet_grad[step] = back_one[:, :prenet_width]

    for channel in range(2):
        filter_ref[channel] = dot(
            conv_ref[channel].astype(bf16), dense_ref[...].astype(bf16)
        )
    for step in range(steps):
        frame_ref[step] = dot(
            frame_grad[step].astype(bf16), frame_weight[...].astype(bf16), lanes_both
        )

    def later(index, _):
        step_back(steps - 1 - index, True)
        return 0

    lax.fori_loop(0, steps - 1, later, 0)
    step_back(0, False)
    slot_hot = slot_ref[...].astype(bf16)

    def tile_out(tile, _):
        for layer, grads_ref in ((0, grads_one), (1, grads_two)):
            for side in range(2):
                place = ((side + unit) % 2) * 4 * half + tile * lanes
                grads = grads_ref[:, :, pl.ds(pl.multiple_of(place, lanes), lanes)]
                chosen = dot(slot_hot, grads.reshape(steps * slots, lanes)).astype(bf16)
                spot = (2 * layer + side) * lanes
                sent_ref[tile, :, spot : spot + lanes] = chosen
        return 0

    lax.fori_loop(0, 4 * per_half, tile_out, 0)


def call_forward(unit, weights, small, sizes):
    own_one, peer_one, own_two, peer_two = weights
    steps, slots, hidden, context_width, positions, frame_rows, prenet_width = sizes

    def shape(*dims):
        return jax.ShapeDtypeStruct(dims, f32)

    outs = [
        shape(steps, slots, 4 * hidden),
        shape(steps, slots, 4 * hidden),
        shape(steps, slots, hidden),
        shape(steps, slots, hidden),
        shape(steps, slots, hidden),
        shape(steps, slots, hidden),
        shape(steps, slots, context_width),
        shape(steps, positions, lanes),
        shape(steps, positions, lanes),
        shape(steps - 1, positions, lanes),
        shape(frame_rows, prenet_width),
        shape(frame_rows, prenet_width),
        shape(frame_rows, prenet_width),
        shape(frame_rows, prenet_width),
        shape(frame_rows, lanes),
    ]
    vmem = pl.BlockSpec(memory_space=pltpu.VMEM)
    return pl.pallas_call(
        forward_kernel,
        out_shape=outs,
        in_specs=[pl.BlockSpec(memory_space=pltpu.SMEM)]
        + [pl.BlockSpec(memory_space=pl.ANY)] * 4
        + [vmem] * len(small),
        out_specs=[vmem] * len(outs),
        scratch_shapes=[
            pltpu.VMEM((2,) + own_one.shape, bf16),
            pltpu.VMEM((2,) + own_two.shape, bf16),
            pltpu.VMEM((slots, own_two.shape[1]), bf16),
            pltpu.VMEM((steps, slots, prenet_width), f32),
            pltpu.VMEM((positions, lanes), f32),
            pltpu.VMEM((2, lanes, lanes), f32),
            pltpu.VMEM((slots, hidden), f32),
            pltpu.VMEM((slots, hidden), f32),
            pltpu.VMEM((slots, hidden), f32),
            pltpu.VMEM((slots, hidden), f32),
            pltpu.SemaphoreType.DMA((4,)),
        ],
        compiler_params=pltpu.CompilerParams(vmem_limit_bytes=kernel_vmem),
        name="decoder_forward",
    )(unit, *weights, *small)


def call_backward(unit, weights, small):
    own_one, peer_one, own_two, peer_two = weights
    gates_one = small[0]
    steps, slots, gate_width = gates_one.shape
    hidden = gate_width // 4
    positions, context_width = small[7].shape
    prenet_width = own_one.shape[1] - hidden - context_width

    def shape(dims, kind):
        return jax.ShapeDtypeStruct(dims, kind)

    outs = [
        shape((gate_width // (2 * lanes), small[-1].shape[0], 4 * lanes), bf16),
        shape((steps, slots, prenet_width), f32),
        shape((steps, slots, context_width), f32),
        shape((steps, slots, lanes), f32),
        shape((positions, lanes), f32),
        shape((1, lanes), f32),
        shape((2, lanes, lanes), f32),
    ]
    vmem = pl.BlockSpec(memory_space=pltpu.VMEM)
    return pl.pallas_call(
        backward_kernel,
        out_shape=outs,
        in_specs=[pl.BlockSpec(memory_space=pltpu.SMEM)]
        + [pl.BlockSpec(memory_space=pl.ANY)] * 4
        + [vmem] * len(small),
        out_specs=[vmem] * len(outs),
        scratch_shapes=[
            pltpu.VMEM((2,) + own_one.shape, bf16),
            pltpu.VMEM((2,) + own_two.shape, bf16),
            pltpu.VMEM((steps, slots, gate_width), bf16),
            pltpu.VMEM((steps, slots, gate_width), bf16),
            pltpu.VMEM((slots, own_one.shape[1]), f32),
            pltpu.VMEM((slots, own_two.shape[1]), f32),
            pltpu.VMEM((slots, hidden), f32),
            pltpu.VMEM((slots, hidden), f32),
            pltpu.VMEM((slots, hidden), f32),
            pltpu.VMEM((slots, hidden), f32),
            pltpu.VMEM((positions, lanes), f32),
            pltpu.VMEM((positions, lanes), f32),
            pltpu.VMEM((slots, hidden), f32),
            pltpu.VMEM((steps, slots, hidden + context_width), f32),
            pltpu.VMEM((2, lanes, lanes), f32),
            pltpu.SemaphoreType.DMA((4,)),
        ],
        compiler_params=pltpu.CompilerParams(vmem_limit_bytes=kernel_vmem),
        name="decoder_backward",
    )(unit, *weights, *small)


def postnet_kernel(
    mel_width,
    loss_scale,
    unit_ref,
    mel_ref,
    target_ref,
    mask_ref,
    first_ref,
    own_ref,
    peer_ref,
    last_ref,
    gain_ref,
    shift_ref,
    inputs_first,
    inputs_later,
    grads_early,
    grads_last,
    norm_grads,
    mel_grad,
    padded,
    padded_mel,
    held,
    normed_early,
    normed_last,
    inverse_ref,
    post_grad,
):
    unit = unit_ref[0]
    count, channels = held.shape
    side = channels // 2
    frames = padded.shape[0] - count
    rows_each = frames // 4
    chunk = 2 * rows_each
    tall = float(count)
    body_rows = slice(2 * rows_each, 2 * rows_each + count)

    for ref in (padded, padded_mel):
        ref[: 2 * rows_each] = jnp.zeros((2 * rows_each, ref.shape[1]), bf16)
        ref[2 * rows_each + count :] = jnp.zeros((2 * rows_each, ref.shape[1]), bf16)

    def piece(source, start, tap, width, lane=None):
        spot = pl.ds(pl.multiple_of(start + tap * rows_each, rows_each), chunk)
        mask = mask_ref[tap, pl.ds(pl.multiple_of(start, rows_each), chunk), :]
        if width < lanes:
            mask = mask[:, :width]
        else:
            mask = jnp.concatenate([mask] * (width // lanes), axis=1)
        value = source[spot, :] if lane is None else source[spot, pl.ds(lane, width)]
        return value * mask

    def chunks(work):
        def one(index, _):
            work(pl.multiple_of(index * chunk, chunk))
            return 0

        lax.fori_loop(0, count // chunk, one, 0)

    def half_spot(which):
        return pl.multiple_of(((which + unit) % 2) * side, side)

    def norm_forward(value, layer, lane, width):
        mean = jnp.sum(value, axis=0, keepdims=True) / tall
        centered = value - mean
        inverse = lax.rsqrt(jnp.sum(centered * centered, axis=0, keepdims=True) / tall + norm_eps)
        inverse_ref[layer, :, pl.ds(lane, width)] = inverse
        return centered * inverse

    def each_lane_block(work):
        def one(index, _):
            work(pl.multiple_of(index * lanes, lanes))
            return 0

        lax.fori_loop(0, channels // lanes, one, 0)

    def activate(layer):
        def block(lane):
            spot = pl.ds(lane, lanes)
            normed = norm_forward(held[:, spot], layer, lane, lanes)
            normed_early[layer, :, spot] = normed
            active = jnp.tanh(
                normed * gain_ref[layer, :, spot] + shift_ref[layer, :, spot]
            ).astype(bf16)
            inputs_later[layer, :, spot] = active
            padded[body_rows, spot] = active

        each_lane_block(block)

    source = mel_ref[...].astype(bf16)
    inputs_first[...] = source
    padded_mel[body_rows] = source

    def first_chunk(start):
        total = None
        for tap in range(5):
            product = dot(piece(padded_mel, start, tap, mel_width), first_ref[tap])
            total = product if total is None else total + product
        held[pl.ds(start, chunk), :] = total

    chunks(first_chunk)
    activate(0)

    def middle(index, _):
        for which, ref in ((0, own_ref), (1, peer_ref)):

            def middle_chunk(start, which=which, ref=ref):
                total = None
                for tap in range(5):
                    product = dot(piece(padded, start, tap, channels), ref[index, tap])
                    total = product if total is None else total + product
                held[pl.ds(start, chunk), pl.ds(half_spot(which), side)] = total

            chunks(middle_chunk)
        activate(index + 1)
        return 0

    lax.fori_loop(0, 3, middle, 0)

    def last_chunk(start):
        total = None
        for tap in range(5):
            product = dot(piece(padded, start, tap, channels), last_ref[tap])
            total = product if total is None else total + product
        normed_last[pl.ds(start, chunk), :] = total

    chunks(last_chunk)
    normed = norm_forward(normed_last[...], 4, 0, mel_width)
    normed_last[...] = normed

    def norm_back(grad, normed, layer, lane, width):
        spot = pl.ds(lane, width)
        shift_grad = jnp.sum(grad, axis=0, keepdims=True)
        gain_grad = jnp.sum(grad * normed, axis=0, keepdims=True)
        norm_grads[0, layer, :, spot] = gain_grad
        norm_grads[1, layer, :, spot] = shift_grad
        return (
            gain_ref[layer, :, spot]
            * inverse_ref[layer, :, spot]
            * (grad - shift_grad / tall - normed * (gain_grad / tall))
        ).astype(bf16)

    output = normed * gain_ref[4, :, :mel_width] + shift_ref[4, :, :mel_width]
    grad = loss_scale * (mel_ref[...] + output - target_ref[...])
    post_grad[...] = grad
    grad_norm = norm_back(grad, normed, 4, 0, mel_width)
    grads_last[...] = grad_norm
    padded_mel[body_rows] = grad_norm

    def last_back(start):
        total = None
        for tap in range(5):
            product = dot(
                piece(padded_mel, start, tap, mel_width), last_ref[4 - tap], lanes_both
            )
            total = product if total is None else total + product
        held[pl.ds(start, chunk), :] = total

    chunks(last_back)

    def deactivate(layer):
        def block(lane):
            spot = pl.ds(lane, lanes)
            normed = normed_early[layer, :, spot]
            active = jnp.tanh(normed * gain_ref[layer, :, spot] + shift_ref[layer, :, spot])
            grad = held[:, spot] * (1.0 - active * active)
            grad_norm = norm_back(grad, normed, layer, lane, lanes)
            grads_early[layer, :, spot] = grad_norm
            padded[body_rows, spot] = grad_norm

        each_lane_block(block)

    def middle_back(back, _):
        index = 2 - back
        deactivate(index + 1)

        def chunk_back(start):
            total = None
            for which, ref in ((0, own_ref), (1, peer_ref)):
                for tap in range(5):
                    product = dot(
                        piece(padded, start, tap, side, half_spot(which)),
                        ref[index, 4 - tap],
                        lanes_both,
                    )
                    total = product if total is None else total + product
            held[pl.ds(start, chunk), :] = total

        chunks(chunk_back)
        return 0

    lax.fori_loop(0, 3, middle_back, 0)
    deactivate(0)

    def first_back(start):
        total = None
        for tap in range(5):
            product = dot(piece(padded, start, tap, channels), first_ref[4 - tap], lanes_both)
            total = product if total is None else total + product
        spot = pl.ds(start, chunk)
        mel_grad[spot, :] = (
            loss_scale * (mel_ref[spot, :] - target_ref[spot, :]) + post_grad[spot, :] + total
        )

    chunks(first_back)


def call_postnet(unit, small, loss_scale, rows_all):
    mel = small[0]
    count, mel_width = mel.shape
    channels = small[3].shape[2]

    def shape(kind, *dims):
        return jax.ShapeDtypeStruct(dims, kind)

    outs = [
        shape(bf16, count, mel_width),
        shape(bf16, 4, count, channels),
        shape(bf16, 4, count, channels),
        shape(bf16, count, mel_width),
        shape(f32, 2, 5, 1, channels),
        shape(f32, count, mel_width),
    ]
    vmem = pl.BlockSpec(memory_space=pltpu.VMEM)
    tall = count + 4 * rows_all
    return pl.pallas_call(
        functools.partial(postnet_kernel, mel_width, loss_scale),
        out_shape=outs,
        in_specs=[pl.BlockSpec(memory_space=pltpu.SMEM)] + [vmem] * len(small),
        out_specs=[vmem] * len(outs),
        scratch_shapes=[
            pltpu.VMEM((tall, channels), bf16),
            pltpu.VMEM((tall, mel_width), bf16),
            pltpu.VMEM((count, channels), f32),
            pltpu.VMEM((4, count, channels), f32),
            pltpu.VMEM((count, mel_width), f32),
            pltpu.VMEM((5, 1, channels), f32),
            pltpu.VMEM((count, mel_width), f32),
        ],
        compiler_params=pltpu.CompilerParams(vmem_limit_bytes=kernel_vmem),
        name="postnet",
    )(unit, *small)


def shifted_frames(source, same):
    steps = source.shape[0]
    padded = jnp.pad(source, ((2, 2), (0, 0), (0, 0)))
    return [
        padded[offset : offset + steps] * same[:, :, offset, None].astype(source.dtype)
        for offset in range(5)
    ]


def by_rows(work, roomy, arrays, summed=False):
    if roomy:
        return work(*arrays)
    parts = arrays[0].shape[1] // 192

    def cut(value):
        value = value.reshape((value.shape[0], parts, -1) + value.shape[2:])
        return jnp.moveaxis(value, 1, 0)

    pieces = tuple(cut(value) for value in arrays)
    if summed:
        first = jax.eval_shape(work, *[value[0] for value in pieces])
        start = jnp.zeros(first.shape, first.dtype)
        return lax.scan(lambda total, now: (total + work(*now), None), start, pieces)[0]
    result = jnp.moveaxis(lax.map(lambda now: work(*now), pieces), 0, 1)
    return result.reshape((result.shape[0], -1) + result.shape[3:])


def post_layer(source, kernel, same):
    wide = jnp.concatenate(shifted_frames(source, same), axis=2)
    return jnp.einsum(
        "src,co->sro", wide, kernel.reshape(-1, kernel.shape[2]), preferred_element_type=f32
    )


def post_layer_back(grad, kernel, same):
    wide = jnp.concatenate(shifted_frames(grad, same), axis=2)
    turned = jnp.transpose(kernel[::-1], (0, 2, 1)).reshape(-1, kernel.shape[1])
    return jnp.einsum("sro,oc->src", wide, turned, preferred_element_type=f32)


def post_kernel_grad(source, grad, same):
    wide = jnp.concatenate(shifted_frames(source, same), axis=2)
    return jnp.einsum("src,sro->co", wide, grad, preferred_element_type=f32)


def on_device(
    memory,
    targets,
    segments,
    text_lengths,
    zone_first,
    zone_second,
    drop_first,
    drop_second,
    prenet_first,
    prenet_second,
    query_weight,
    memory_weight,
    location_conv,
    location_dense,
    energy_vector,
    lstm_first,
    bias_first,
    lstm_second,
    bias_second,
    frame_weight,
    frame_bias,
    post_first,
    post_middle,
    post_last,
    middle_norm,
    last_norm,
):
    micro_count, rows, text_width, memory_width = memory.shape
    frames = segments.shape[2]
    utterances = text_lengths.shape[2]
    mel_width = targets.shape[3]
    hidden = query_weight.shape[0]
    prenet_width = prenet_first.shape[1]
    attention_width = query_weight.shape[1]
    half = lstm_first.shape[2]
    depth_one, depth_two = lstm_first.shape[0], lstm_second.shape[0]
    unit = lax.axis_index("unit")
    place = lax.axis_index("batch")
    batch_size = lax.axis_size("batch")
    total_rows = rows * batch_size
    frame_count = float(total_rows * frames)
    first_unit = unit == 0
    longest = 3
    slots = 4 * rows

    def exchange(value):
        return lax.ppermute(value, "unit", [(0, 1), (1, 0)])

    def ordered(own, peer):
        return jnp.where(first_unit, own, peer), jnp.where(first_unit, peer, own)

    def whole(value, axis):
        return jnp.concatenate(ordered(value, exchange(value)), axis=axis)

    def mine(value):
        return lax.dynamic_index_in_dim(value, unit, 0, keepdims=False)

    def others(value):
        return lax.dynamic_index_in_dim(value, 1 - unit, 0, keepdims=False)

    def swapped(value, bit):
        pairs = [(index, index ^ bit) for index in range(batch_size)]
        other = lax.ppermute(value, "batch", pairs)
        upper = (place & bit) != 0
        return jnp.where(upper, other, value), jnp.where(upper, value, other)

    def gather_rows(value):
        bit = 1
        while bit < batch_size:
            value = jnp.concatenate(swapped(value, bit), axis=0)
            bit *= 2
        return value

    def gather_tiles(value):
        tiles = jnp.transpose(value.reshape(value.shape[0], -1, lanes), (1, 0, 2))
        return lax.all_gather(tiles, "batch", axis=1, tiled=True)

    own_two = gather_tiles(lstm_second)
    own_one = gather_tiles(lstm_first)
    peer_two = exchange(own_two)
    channel_rows = post_middle.shape[2]
    middle_width = post_middle.shape[3]
    last_rows = jnp.transpose(post_last, (1, 0, 2)).reshape(1, channel_rows, -1)
    post_rows = jnp.concatenate(
        [
            post_middle.reshape(-1, channel_rows, middle_width),
            jnp.pad(last_rows, ((0, 0), (0, 0), (0, middle_width - last_rows.shape[2]))),
        ],
        axis=0,
    )
    post_rows = lax.all_gather(post_rows, "batch", axis=1, tiled=True)
    middle_half = post_rows[:-1].reshape(post_middle.shape[:2] + (-1, middle_width))
    middle_peer = exchange(middle_half)
    last_half = jnp.transpose(
        post_rows[-1, :, : last_rows.shape[2]].reshape(-1, 5, post_last.shape[2]), (1, 0, 2)
    )
    memory_now = mine(memory).reshape(rows * text_width, memory_width)
    segments_now = mine(segments)
    targets_now = mine(targets)
    frame_info = gather_rows(
        jnp.concatenate([targets_now, segments_now[:, :, None].astype(bf16)], axis=2).astype(f32)
    )

    same_frames = segments_now[:, :, None] == segments_now[:, None, :]
    earlier = jnp.tril(jnp.ones((frames, frames), jnp.bool_), -1)
    order = jnp.sum((same_frames & earlier[None]).astype(jnp.int32), axis=2)
    slot_of = order * slots + segments_now * rows + jnp.arange(rows, dtype=jnp.int32)[:, None]
    frame_rows = rows * frames
    padding = -frame_rows % 16
    slot_hot = (
        jnp.pad(slot_of.reshape(-1, 1), ((0, padding), (0, 0)), constant_values=-1)
        == jnp.arange(longest * slots, dtype=jnp.int32)[None, :]
    ).astype(bf16)
    slot_hot_frames = slot_hot[:frame_rows]
    carry_on = jnp.pad(
        (segments_now[:, 1:] == segments_now[:, :-1]).astype(f32), ((0, 0), (1, 0))
    )
    finished = jnp.pad(
        (segments_now[:, 1:] != segments_now[:, :-1]).astype(f32),
        ((0, 0), (0, 1)),
        constant_values=1.0,
    )

    def to_slots(value, kind=bf16):
        return lax.dot_general(
            slot_hot_frames,
            value.astype(bf16),
            (((0,), (0,)), ((), ())),
            preferred_element_type=f32,
        ).astype(kind)

    def to_frames(value):
        return jnp.dot(slot_hot, value.astype(bf16), preferred_element_type=f32).astype(bf16)

    def pad_frames(value):
        return jnp.pad(
            value.astype(f32).reshape(frame_rows, -1), ((0, padding), (0, 0))
        )

    previous = pad_frames(
        jnp.pad(targets_now[:, :-1], ((0, 0), (1, 0), (0, 0))).astype(f32)
        * carry_on[:, :, None]
    )
    drops_one = pad_frames(mine(drop_first))
    drops_two = pad_frames(mine(drop_second))

    zones_own = jnp.concatenate([mine(zone_first), mine(zone_second)], axis=2).astype(f32)
    zones_peer = exchange(
        jnp.concatenate([others(zone_first), others(zone_second)], axis=2).astype(f32)
    )
    zones_slots = to_slots(
        jnp.concatenate([zones_own, zones_peer], axis=2).reshape(rows * frames, -1), f32
    ).reshape(longest, slots, 4 * half)
    zone_one = jnp.concatenate(
        [zones_slots[:, :, :half], zones_slots[:, :, 2 * half : 3 * half]], axis=2
    )
    zone_two = jnp.concatenate(
        [zones_slots[:, :, half : 2 * half], zones_slots[:, :, 3 * half :]], axis=2
    )
    biases = jnp.stack([bias_first.reshape(-1), bias_second.reshape(-1)])
    biases = jnp.concatenate([biases, exchange(biases)], axis=1)
    text_ends = jnp.cumsum(mine(text_lengths), axis=1)
    owner = jnp.sum(
        (jnp.arange(text_width, dtype=jnp.int32)[None, :, None] >= text_ends[:, None, :]).astype(
            jnp.int32
        ),
        axis=2,
    )
    owner_slot = owner * rows + jnp.arange(rows, dtype=jnp.int32)[:, None]
    owner_hot = (
        owner_slot.reshape(-1, 1) == jnp.arange(lanes, dtype=jnp.int32)[None, :]
    ).astype(f32)
    conv_float = location_conv.astype(f32)
    dense_float = location_dense.astype(f32)
    reach = location_conv.shape[2] // 2
    taps_first = jnp.transpose(conv_float, (1, 2, 0))
    taps_first = jnp.pad(
        taps_first,
        ((0, 0), (0, lanes - taps_first.shape[1]), (0, lanes - taps_first.shape[2])),
    )
    dense_wide = jnp.pad(dense_float, ((0, lanes - dense_float.shape[0]), (0, 0)))
    taps_forward = jnp.roll(taps_first[:, ::-1], reach, axis=1)
    taps_back = jnp.roll(taps_first, 1 - reach, axis=1)
    frame_wide = jnp.pad(
        frame_weight.astype(f32), ((0, 0), (0, lanes - frame_weight.shape[1]))
    )
    frame_bias_wide = jnp.pad(frame_bias, (0, lanes - frame_bias.shape[0]))[None, :]
    vector_float = energy_vector.astype(f32)
    vector_wide = jnp.broadcast_to(vector_float[:, None], (attention_width, lanes))
    memory_float = memory_now.astype(f32)
    query_float = query_weight.astype(f32)
    unit_array = unit.astype(jnp.int32).reshape(1)

    targets_all = jnp.transpose(frame_info[:, :, :mel_width].astype(f32), (1, 0, 2))
    segments_all = jnp.transpose(frame_info[:, :, mel_width].astype(jnp.int32))
    padded = jnp.pad(segments_all, ((2, 2), (0, 0)), constant_values=-1)
    same = jnp.stack([padded[offset : offset + frames] == segments_all for offset in range(5)])
    same = jnp.moveaxis(same, 0, 2)
    first_full = whole(post_first, 2)
    last_full = whole(last_half, 2)
    middle_gain = whole(middle_norm, 2)
    last_gain = whole(last_norm, 1)
    loss_scale = 2.0 / (mel_width * total_rows)
    count = total_rows * frames
    channels = middle_norm.shape[2] * 2
    masks = jnp.broadcast_to(
        jnp.transpose(same, (2, 0, 1)).reshape(5, count, 1).astype(bf16), (5, count, lanes)
    )
    wide_gain = jnp.pad(last_gain, ((0, 0), (0, channels - mel_width)))
    norms = jnp.concatenate([middle_gain, wide_gain[:, None, :]], axis=1)[:, :, None, :]
    forward_small = (
        previous,
        drops_one,
        drops_two,
        prenet_first.astype(f32),
        prenet_second.astype(f32),
        slot_hot.astype(f32),
        zone_one,
        zone_two,
        biases[0:1],
        biases[1:2],
        owner_hot,
        memory_float,
        memory_weight.astype(f32),
        query_float,
        vector_wide,
        taps_forward,
        dense_wide,
        frame_wide,
        frame_bias_wide,
    )
    (
        own_one,
        own_two,
        forward_small,
        taps_back,
        vector_row,
        targets_all,
        masks,
        first_full,
        norms,
    ) = lax.optimization_barrier(
        (
            own_one,
            own_two,
            forward_small,
            taps_back,
            vector_float[None, :],
            targets_all,
            masks,
            first_full,
            norms,
        )
    )
    weights = (own_one, exchange(own_one), own_two, peer_two)
    slot_wide, zone_one, zone_two = forward_small[5], forward_small[6], forward_small[7]
    memory_float, query_float = forward_small[11], forward_small[13]
    dense_wide, frame_wide = forward_small[16], forward_small[17]

    (
        gates_one,
        gates_two,
        prior_one,
        prior_two,
        round_one,
        round_two,
        contexts,
        mixed_all,
        alphas,
        taps,
        mixed_one,
        mixed_two,
        hidden_round,
        prenet_round,
        frame_out,
    ) = call_forward(
        unit_array,
        weights,
        forward_small,
        (
            longest,
            slots,
            hidden,
            memory_width,
            rows * text_width,
            frame_rows + padding,
            prenet_width,
        ),
    )

    states = to_frames(
        jnp.concatenate([round_one, contexts, round_two], axis=2).reshape(longest * slots, -1)
    )
    frame_in = jnp.concatenate(
        [states[:, hidden + memory_width :], states[:, hidden : hidden + memory_width]], axis=1
    )
    frame_in = frame_in[:frame_rows]
    frame_out = frame_out[:frame_rows]
    mel_own = frame_out[:, :mel_width].reshape(rows, frames, mel_width)
    stop_logit = frame_out[:, mel_width].reshape(rows, frames)
    mel_all = jnp.transpose(
        gather_rows(mel_own), (1, 0, 2)
    )
    inputs_own = jnp.concatenate([prenet_round.astype(bf16), states], axis=1)
    roomy = total_rows * frames <= 2048
    if roomy:
        inputs_own, mel_all = lax.optimization_barrier((inputs_own, mel_all))
        inputs_all = lax.all_gather(inputs_own, "batch", axis=0, tiled=True)

    if roomy:
        (
            inputs_first,
            inputs_later,
            grads_early,
            grads_last,
            norm_grads,
            grad_mel,
        ) = call_postnet(
            unit_array,
            (
                mel_all.reshape(count, mel_width),
                targets_all.reshape(count, mel_width),
                masks,
                first_full,
                middle_half,
                middle_peer,
                last_full,
                norms[0],
                norms[1],
            ),
            loss_scale,
            total_rows,
        )
        gain_grads = [norm_grads[0, layer, 0] for layer in range(5)]
        shift_grads = [norm_grads[1, layer, 0] for layer in range(5)]
        gain_grads[4], shift_grads[4] = gain_grads[4][:mel_width], shift_grads[4][:mel_width]
        kernel_grads = []
        for layer in range(5):
            if layer == 0:
                source = inputs_first
            else:
                source = lax.dynamic_slice_in_dim(
                    inputs_later[layer - 1], place * channel_rows, channel_rows, 1
                )
            grad_norm = grads_early[layer] if layer < 4 else grads_last
            kernel_grads.append(
                post_kernel_grad(
                    source.reshape(frames, total_rows, -1),
                    grad_norm.reshape(frames, total_rows, -1),
                    same,
                ).reshape(5, source.shape[1], grad_norm.shape[1])
            )
        grad_mel = jnp.transpose(
            lax.dynamic_slice_in_dim(
                grad_mel.reshape(frames, total_rows, mel_width), place * rows, rows, 1
            ),
            (1, 0, 2),
        )
    else:
        middle_full = whole(middle_half, 3)
        kernels = [first_full, middle_full[0], middle_full[1], middle_full[2], last_full]
        gains = [middle_gain[0, layer] for layer in range(4)] + [last_gain[0]]
        shifts = [middle_gain[1, layer] for layer in range(4)] + [last_gain[1]]
        layer_in = mel_all.astype(bf16)
        layer_inputs, normed_all, inverses = [], [], []
        output = None
        for layer in range(5):
            layer_inputs.append(layer_in)
            pre_norm = by_rows(
                lambda source, same_now: post_layer(source, kernels[layer], same_now),
                roomy,
                (layer_in, same),
            )
            mean_now = jnp.sum(pre_norm, axis=(0, 1)) / frame_count
            centered = pre_norm - mean_now
            inverse = lax.rsqrt(jnp.sum(centered * centered, axis=(0, 1)) / frame_count + norm_eps)
            normed = centered * inverse
            output = normed * gains[layer] + shifts[layer]
            normed_all.append(normed)
            inverses.append(inverse)
            if layer < 4:
                layer_in = jnp.tanh(output).astype(bf16)
                if not roomy:
                    layer_in, normed_all[layer] = lax.optimization_barrier(
                        (layer_in, normed_all[layer])
                    )

        grad_post = loss_scale * (mel_all + output - targets_all)
        kernel_grads, gain_grads, shift_grads = [None] * 5, [None] * 5, [None] * 5
        grad_output = grad_post
        grad_input = None
        for layer in (4, 3, 2, 1, 0):
            if layer < 4:
                normed_all[layer] = lax.optimization_barrier(normed_all[layer])
                active = jnp.tanh(normed_all[layer] * gains[layer] + shifts[layer])
                grad_output = grad_input * (1.0 - active * active)
            shift_grads[layer] = jnp.sum(grad_output, axis=(0, 1))
            gain_grads[layer] = jnp.sum(grad_output * normed_all[layer], axis=(0, 1))
            grad_norm = (
                gains[layer]
                * inverses[layer]
                * (
                    grad_output
                    - shift_grads[layer] / frame_count
                    - normed_all[layer] * (gain_grads[layer] / frame_count)
                )
            ).astype(bf16)
            grad_input = by_rows(
                lambda grad, same_now: post_layer_back(grad, kernels[layer], same_now),
                roomy,
                (grad_norm, same),
            )
            source = layer_inputs[layer]
            if layer > 0:
                source = lax.dynamic_slice_in_dim(source, place * channel_rows, channel_rows, 2)
            kernel_grads[layer] = by_rows(post_kernel_grad, roomy, (source, grad_norm, same), True)
            kernel_grads[layer] = kernel_grads[layer].reshape(5, source.shape[2], -1)
            if not roomy:
                grad_input, kernel_grads[layer] = lax.optimization_barrier(
                    (grad_input, kernel_grads[layer])
                )
        grad_mel = loss_scale * (mel_all - targets_all) + grad_post + grad_input
        grad_mel = jnp.transpose(
            lax.dynamic_slice_in_dim(grad_mel, place * rows, rows, 1), (1, 0, 2)
        )

    if not roomy:
        inputs_own, grad_mel = lax.optimization_barrier((inputs_own, grad_mel))
        inputs_all = lax.all_gather(inputs_own, "batch", axis=0, tiled=True)

    def add_units(value, axis):
        width = value.shape[axis] // 2
        halves = [
            lax.slice_in_dim(value, start, start + width, axis=axis) for start in (0, width)
        ]
        keep = jnp.where(first_unit, halves[0], halves[1])
        give = jnp.where(first_unit, halves[1], halves[0])
        return keep + exchange(give)

    post_first_grad = add_units(kernel_grads[0], 2)
    post_middle_grad = add_units(jnp.stack(kernel_grads[1:4]), 3)
    post_last_grad = add_units(kernel_grads[4], 2)
    middle_norm_grad = add_units(
        jnp.stack([jnp.stack(gain_grads[:4]), jnp.stack(shift_grads[:4])]), 2
    )
    last_norm_grad = add_units(jnp.stack([gain_grads[4], shift_grads[4]]), 1)

    grad_stop = (jax.nn.sigmoid(stop_logit) - finished) / total_rows
    grad_frame = (
        jnp.concatenate([grad_mel, grad_stop[:, :, None]], axis=2)
        .reshape(rows * frames, mel_width + 1)
        .astype(bf16)
    )
    frame_weight_grad = lax.dot_general(
        frame_in, grad_frame, (((0,), (0,)), ((), ())), preferred_element_type=f32
    )
    frame_bias_grad = jnp.sum(grad_frame.astype(f32), axis=0)
    grad_frame_slots = to_slots(
        jnp.pad(grad_frame, ((0, 0), (0, lanes - mel_width - 1))), f32
    ).reshape(longest, slots, lanes)

    (
        sent,
        prenet_back,
        context_grads,
        query_back,
        processed_back,
        vector_back,
        filter_back,
    ) = call_backward(
        unit_array,
        weights,
        (
            gates_one,
            gates_two,
            prior_one,
            prior_two,
            zone_one,
            zone_two,
            owner_hot,
            memory_float,
            query_float,
            vector_row,
            taps_back,
            dense_wide,
            mixed_all,
            alphas,
            taps,
            grad_frame_slots,
            frame_wide,
            slot_wide,
        ),
    )

    bias_sums = jnp.transpose(
        jnp.sum(sent.astype(f32), axis=1).reshape(-1, 4, lanes), (1, 0, 2)
    ).reshape(-1, lanes)
    slice_width = 2 * hidden // batch_size
    if slice_width != lanes:
        sent = sent.reshape(sent.shape[0], sent.shape[1], 4, -1, slice_width)
        sent = jnp.transpose(sent, (0, 3, 1, 2, 4)).reshape(batch_size, sent.shape[1], -1)
    received = lax.all_to_all(sent, "batch", 0, 0, tiled=True)
    grad_prenet = lax.dot_general(
        slot_hot.astype(f32),
        prenet_back.reshape(longest * slots, prenet_width),
        (((1,), (0,)), ((), ())),
        precision=precise,
    )

    def silu_back(grad, mixed, drops):
        gate = jax.nn.sigmoid(mixed)
        return grad * drops * 2.0 * gate * (1.0 + mixed * (1.0 - gate))

    def exact(a, b, contract):
        return lax.dot_general(
            a.astype(f32), b.astype(f32), (contract, ((), ())), precision=precise
        )

    grad_mixed_two = silu_back(grad_prenet, mixed_two, drops_two)
    prenet_second_grad = exact(hidden_round, grad_mixed_two, ((0,), (0,)))
    grad_hidden = exact(grad_mixed_two, prenet_second, ((1,), (1,)))
    grad_mixed_one = silu_back(grad_hidden, mixed_one, drops_one)
    prenet_first_grad = exact(previous, grad_mixed_one, ((0,), (0,)))

    query_weight_grad = exact(
        round_one.reshape(longest * slots, hidden),
        query_back.reshape(longest * slots, attention_width),
        ((0,), (0,)),
    )
    processed_round = processed_back.astype(bf16)
    memory_weight_grad = lax.dot_general(
        memory_now, processed_round, (((0,), (0,)), ((), ())), preferred_element_type=f32
    )
    memory_grad = lax.dot_general(
        processed_round, memory_weight, (((1,), (1,)), ((), ())), preferred_element_type=f32
    )
    for step in range(longest):
        memory_grad = memory_grad + exact(
            alphas[step][:, :slots], context_grads[step], ((1,), (0,))
        )
    memory_grad = memory_grad.reshape(rows, text_width, memory_width)
    memory_grads = jnp.stack(ordered(memory_grad, exchange(memory_grad)))
    filter_grads = jnp.roll(filter_back, -reach, axis=1)[:, ::-1][:, : location_conv.shape[2]]
    conv_grad = jnp.einsum("cka,fa->fck", filter_grads, dense_float, precision=precise)
    dense_grad = jnp.einsum("cka,fck->fa", filter_grads, conv_float, precision=precise)

    def two_columns(value):
        return jnp.concatenate([value[:, :lanes], value[:, lanes:]], axis=0)

    def to_lanes(value):
        return jnp.pad(value, ((0, 0), (0, lanes - value.shape[1])))

    filter_count, _, tap_count = location_conv.shape
    packed = [
        two_columns(prenet_first_grad),
        two_columns(prenet_second_grad),
        query_weight_grad,
        memory_weight_grad,
        to_lanes(frame_weight_grad),
        to_lanes(conv_grad.reshape(filter_count, -1)),
        dense_grad,
        bias_sums,
        vector_back,
        to_lanes(frame_bias_grad[None, :]),
    ]
    heights = [value.shape[0] for value in packed]
    shares = 2 * batch_size
    surplus = -sum(heights) % (8 * shares)
    packed = jnp.concatenate(packed + [jnp.zeros((surplus, lanes), f32)], axis=0)
    packed = add_units(packed, 0).reshape(batch_size, -1, lanes)
    received, packed = lax.optimization_barrier((received, packed))
    shares = jnp.sum(lax.all_to_all(packed, "batch", 0, 0, tiled=True), axis=0)

    segments_rows = segments_all.T
    carried = jnp.pad(
        (segments_rows[:, 1:] == segments_rows[:, :-1]).astype(bf16), ((0, 0), (0, 1))
    ).reshape(batch_size, frame_rows)
    carried = jnp.pad(carried, ((0, 0), (0, padding)))
    after = jnp.pad(received[:, 1:], ((0, 0), (0, 1), (0, 0))) * carried[:, :, None]
    received = received.reshape(batch_size * (frame_rows + padding), -1)
    after = after.reshape(batch_size * (frame_rows + padding), -1)

    def product(start, width, grads):
        return lax.dot_general(
            inputs_all[:, start : start + width],
            grads,
            (((0,), (0,)), ((), ())),
            preferred_element_type=f32,
        )

    pair = 2 * slice_width
    first_part = jnp.concatenate(
        [
            product(0, prenet_width, received[:, :pair]),
            product(prenet_width + hidden, memory_width, after[:, :pair]),
            product(prenet_width, hidden, after[:, :pair]),
        ],
        axis=0,
    )
    second_part = jnp.concatenate(
        [
            product(prenet_width, hidden + memory_width, received[:, pair:]),
            product(prenet_width + hidden + memory_width, hidden, after[:, pair:]),
        ],
        axis=0,
    )
    parts = jnp.concatenate(
        [
            first_part.reshape(batch_size, depth_one, pair),
            second_part.reshape(batch_size, depth_two, pair),
        ],
        axis=1,
    )
    parts = add_units(parts, 2).astype(bf16)
    parts, shares = lax.optimization_barrier((parts, shares))
    parts = lax.all_to_all(parts, "batch", 0, 0, tiled=True).astype(f32)
    parts = jnp.transpose(parts, (1, 0, 2)).reshape(depth_one + depth_two, 4, half)

    packed = lax.all_to_all(
        jnp.broadcast_to(shares[None], (batch_size,) + shares.shape), "batch", 0, 0, tiled=True
    )
    packed = whole(packed.reshape(-1, lanes), 0)
    small, start = [], 0
    for height in heights:
        small.append(packed[start : start + height])
        start += height

    def from_columns(value):
        tall = value.shape[0] // 2
        return jnp.concatenate([value[:tall], value[tall:]], axis=1)

    biases_grad = small[7].reshape(2, 2, -1)
    biases_grad = jnp.where(first_unit, biases_grad[:, 0], biases_grad[:, 1])
    biases_grad = biases_grad.reshape(2, 4, half)
    small = [
        from_columns(small[0]),
        from_columns(small[1]),
        small[2],
        small[3],
        small[5][:, : 2 * tap_count].reshape(filter_count, 2, tap_count),
        small[6],
        small[8][0],
        small[4][:, : mel_width + 1],
        small[9][0, : mel_width + 1],
    ]
    return (
        small[0],
        small[1],
        small[2],
        small[3],
        small[4],
        small[5],
        small[6],
        parts[:depth_one],
        biases_grad[0],
        parts[depth_one:],
        biases_grad[1],
        small[7],
        small[8],
        post_first_grad,
        post_middle_grad,
        post_last_grad,
        middle_norm_grad,
        last_norm_grad,
        memory_grads,
    )


def solution(mesh):
    in_specs = (
        P(None, "batch", None, None),
        P(None, "batch", None, None),
        P(None, "batch", None),
        P(None, "batch", None),
        P(None, "batch", None, "unit"),
        P(None, "batch", None, "unit"),
        P(None, "batch", None, None),
        P(None, "batch", None, None),
        P(),
        P(),
        P(),
        P(),
        P(),
        P(),
        P(),
        P("batch", None, "unit"),
        P(None, "unit"),
        P("batch", None, "unit"),
        P(None, "unit"),
        P(),
        P(),
        P(None, None, "unit"),
        P(None, None, "batch", "unit"),
        P(None, "batch", "unit"),
        P(None, None, "unit"),
        P(None, "unit"),
    )
    out_specs = (
        P(),
        P(),
        P(),
        P(),
        P(),
        P(),
        P(),
        P("batch", None, "unit"),
        P(None, "unit"),
        P("batch", None, "unit"),
        P(None, "unit"),
        P(),
        P(),
        P(None, None, "unit"),
        P(None, None, "batch", "unit"),
        P(None, "batch", "unit"),
        P(None, None, "unit"),
        P(None, "unit"),
        P(None, "batch", None, None),
    )
    return jax.shard_map(
        on_device, mesh=mesh, in_specs=in_specs, out_specs=out_specs, check_vma=False
    )
```

```python
import functools

import jax
import jax.numpy as jnp
from jax import lax
from jax.experimental import pallas as pl
from jax.experimental.pallas import tpu as pltpu
from jax.sharding import PartitionSpec as P

precise = lax.Precision.HIGHEST
norm_eps = 1e-05
f32 = jnp.float32
bf16 = jnp.bfloat16
lanes = 128
kernel_vmem = 60 * 1024 * 1024


def split(value):
    high = value.astype(bf16)
    return high, (value - high.astype(f32)).astype(bf16)


def dot(a, b, contract=((1,), (0,))):
    return lax.dot_general(a, b, (contract, ((), ())), preferred_element_type=f32)


def dot_left(exact, value, contract=((1,), (0,))):
    high, low = split(value)
    return dot(exact, high, contract) + dot(exact, low, contract)


def dot_right(value, exact, contract=((1,), (0,))):
    high, low = split(value)
    return dot(high, exact, contract) + dot(low, exact, contract)


def dot_both(a, b, contract=((1,), (0,))):
    a_high, a_low = split(a)
    b_high, b_low = split(b)
    return (
        dot(a_high, b_high, contract) + dot(a_low, b_high, contract) + dot(a_high, b_low, contract)
    )


rows_first = ((0,), (0,))
lanes_both = ((1,), (1,))


def position_hot(position_count, text_width, reverse):
    place = lax.broadcasted_iota(jnp.int32, (position_count, lanes), 0) & (text_width - 1)
    lane = lax.broadcasted_iota(jnp.int32, (position_count, lanes), 1)
    place = (lanes - 1) - place if reverse else place + 1
    return (place == lane).astype(bf16)


def slant(value, text_width):
    blocks = [
        pltpu.roll(value[start : start + text_width], 0, 1, stride=1, stride_axis=0)
        for start in range(0, value.shape[0], text_width)
    ]
    return jnp.concatenate(blocks, axis=0)


def pad_rows(value):
    return jnp.concatenate(
        [value, jnp.zeros((lanes - value.shape[0], value.shape[1]), value.dtype)], axis=0
    )


def unit_spot(chunk, unit, per_half):
    half = (chunk // per_half + unit) % 2
    return pl.multiple_of((half * per_half + chunk % per_half) * lanes, lanes)


def gate_spot(chunk, gate, per_half):
    start = (chunk // per_half) * 4 * per_half + gate * per_half + chunk % per_half
    return pl.multiple_of(start * lanes, lanes)


def forward_kernel(
    unit_ref,
    own_one,
    peer_one,
    own_two,
    peer_two,
    previous_ref,
    drop_one,
    drop_two,
    layer_one,
    layer_two,
    slot_ref,
    zone_one,
    zone_two,
    bias_one,
    bias_two,
    hot_ref,
    memory_ref,
    project_ref,
    query_ref,
    vector_ref,
    conv_ref,
    dense_ref,
    frame_ref,
    frame_bias,
    gates_one,
    gates_two,
    prior_one,
    prior_two,
    round_one,
    round_two,
    context_ref,
    mixed_ref,
    alpha_ref,
    taps_ref,
    prenet_one,
    prenet_two,
    prenet_hidden,
    prenet_out,
    frame_out,
    held_one,
    held_two,
    input_ref,
    prenet_ref,
    processed_ref,
    filter_ref,
    state_one,
    cell_one,
    state_two,
    cell_two,
    sems,
):
    unit = unit_ref[0]
    steps, slots, hidden = round_one.shape
    prenet_width = layer_two.shape[1]
    context_width = context_ref.shape[2]
    half = hidden // 2
    per_half = half // lanes
    position_count = hot_ref.shape[0]
    text_width = position_count // (slots // 4)
    copies_two = [
        pltpu.make_async_copy(own_two, held_two.at[0], sems.at[0]),
        pltpu.make_async_copy(peer_two, held_two.at[1], sems.at[1]),
    ]
    copies_one = [
        pltpu.make_async_copy(own_one, held_one.at[0], sems.at[2]),
        pltpu.make_async_copy(peer_one, held_one.at[1], sems.at[3]),
    ]
    for copy in copies_two + copies_one:
        copy.start()
    for ref in (state_one, cell_one, state_two, cell_two):
        ref[...] = jnp.zeros_like(ref)

    def gates_into(held, depth, bias_ref, out_ref, step):
        def one(block, _):
            side = block // 4
            inputs = input_ref[:, :depth]
            for pair in range(per_half // 2):
                tile = (block % 4) * per_half + 2 * pair
                outside = pl.ds(
                    pl.multiple_of(block * half + 2 * pair * lanes, 2 * lanes), 2 * lanes
                )
                kernel = jnp.concatenate(
                    [held[side, tile, :depth, :], held[side, tile + 1, :depth, :]], axis=1
                )
                out_ref[step, :, outside] = dot(inputs, kernel) + bias_ref[:, outside]
            return 0

        lax.fori_loop(0, 8, one, 0)

    def cell(gates_ref, zone_ref, prior_ref, state, cells, round_ref, step):
        def one(chunk, _):
            spot = pl.ds(pl.multiple_of(chunk * lanes, lanes), lanes)
            values = [
                gates_ref[step, :, pl.ds(gate_spot(chunk, gate, per_half), lanes)]
                for gate in range(4)
            ]
            zone = zone_ref[step, :, spot]
            before = cells[:, spot]
            prior_ref[step, :, spot] = before
            fresh = jax.nn.sigmoid(values[1]) * before + jax.nn.sigmoid(values[0]) * jnp.tanh(
                values[2]
            )
            output = jax.nn.sigmoid(values[3]) * jnp.tanh(fresh)
            now = zone * state[:, spot] + (1.0 - zone) * output
            state[:, spot] = now
            cells[:, spot] = zone * before + (1.0 - zone) * fresh
            round_ref[step, :, pl.ds(unit_spot(chunk, unit, per_half), lanes)] = now.astype(bf16).astype(
                f32
            )
            return 0

        lax.fori_loop(0, 2 * per_half, one, 0)

    def attention(step, location):
        inside = hot_ref[...] > 0.0
        hot = hot_ref[...].astype(bf16)
        query = pad_rows(dot(round_one[step].astype(bf16), query_ref[...].astype(bf16)))
        summed = dot_left(hot, query) + processed_ref[...]
        if location is not None:
            summed = summed + location
        mixed = jnp.tanh(summed)
        mixed_ref[step] = mixed
        energy = dot_right(mixed, vector_ref[...].astype(bf16))
        most = jnp.max(jnp.where(inside, energy, -1000000000.0), axis=0, keepdims=True)
        shifted = jnp.where(inside, jnp.exp(energy - most), 0.0)
        total = jnp.sum(shifted, axis=0, keepdims=True)
        alpha = shifted / jnp.where(total > 0.0, total, 1.0)
        alpha_ref[step] = alpha
        context = dot_right(alpha, memory_ref[...].astype(bf16), rows_first)[:slots]
        context_ref[step] = context.astype(bf16).astype(f32)

    def taps_of(step):
        spread = dot_right(
            alpha_ref[step], position_hot(position_count, text_width, True), rows_first
        )
        taps_ref[step] = slant(dot_left(hot_ref[...].astype(bf16), spread), text_width)

    def second_layer(step, depth):
        input_ref[:, :hidden] = round_one[step].astype(bf16)
        input_ref[:, hidden : hidden + context_width] = context_ref[step].astype(bf16)
        gates_into(held_two, depth, bias_two, gates_two, step)
        cell(gates_two, zone_two, prior_two, state_two, cell_two, round_two, step)

    slot_hot = slot_ref[...].astype(bf16)

    def prenet_layer(source, layer, drops, mixed_out, out):
        mixed = dot(source.astype(bf16), layer[...].astype(bf16))
        mixed_out[...] = mixed
        value = (mixed * jax.nn.sigmoid(mixed) * drops[...] * 2.0).astype(bf16)
        out[...] = value.astype(f32)
        return value

    hidden_value = prenet_layer(previous_ref[...], layer_one, drop_one, prenet_one, prenet_hidden)
    prenet_value = prenet_layer(hidden_value, layer_two, drop_two, prenet_two, prenet_out)
    prenet_slots = dot(slot_hot, prenet_value, rows_first)
    for step in range(steps):
        prenet_ref[step] = prenet_slots[step * slots : (step + 1) * slots]
    processed_ref[...] = dot(memory_ref[...].astype(bf16), project_ref[...].astype(bf16))
    for channel in range(2):
        filter_ref[channel] = dot(
            conv_ref[channel].astype(bf16), dense_ref[...].astype(bf16)
        )

    gates_one[0] = jnp.broadcast_to(bias_one[...], gates_one.shape[1:])
    cell(gates_one, zone_one, prior_one, state_one, cell_one, round_one, 0)
    attention(0, None)
    taps_of(0)
    for copy in copies_two:
        copy.wait()
    second_layer(0, hidden + context_width)
    for copy in copies_one:
        copy.wait()

    def later(step, _):
        input_ref[:, :prenet_width] = prenet_ref[step].astype(bf16)
        input_ref[:, prenet_width : prenet_width + context_width] = context_ref[step - 1].astype(
            bf16
        )
        input_ref[:, prenet_width + context_width : prenet_width + context_width + hidden] = (
            round_one[step - 1].astype(bf16)
        )
        gates_into(
            held_one, prenet_width + context_width + hidden, bias_one, gates_one, step
        )
        cell(gates_one, zone_one, prior_one, state_one, cell_one, round_one, step)
        previous = taps_ref[step - 1]
        summed = jnp.where(step == 2, taps_ref[0] + previous, previous)
        attention(step, dot_both(previous, filter_ref[0]) + dot_both(summed, filter_ref[1]))

        @pl.when(step < steps - 1)
        def _():
            taps_of(step)

        input_ref[:, hidden + context_width :] = round_two[step - 1].astype(bf16)
        second_layer(step, 2 * hidden + context_width)
        return 0

    lax.fori_loop(1, steps, later, 0)
    for step in range(steps):
        values = dot(round_two[step].astype(bf16), frame_ref[:hidden].astype(bf16)) + dot(
            context_ref[step].astype(bf16), frame_ref[hidden:].astype(bf16)
        )
        high = values.astype(bf16)
        rest = values - high.astype(f32)
        middle = rest.astype(bf16)
        low = (rest - middle.astype(f32)).astype(bf16)
        chosen = slot_hot[:, step * slots : (step + 1) * slots]
        picked = (dot(chosen, high) + dot(chosen, middle)) + dot(chosen, low)
        frame_out[...] = (frame_bias[...] if step == 0 else frame_out[...]) + picked


def backward_kernel(
    unit_ref,
    own_one,
    peer_one,
    own_two,
    peer_two,
    gates_one,
    gates_two,
    prior_one,
    prior_two,
    zone_one,
    zone_two,
    hot_ref,
    memory_ref,
    query_ref,
    vector_ref,
    conv_ref,
    dense_ref,
    mixed_ref,
    alpha_ref,
    taps_ref,
    frame_grad,
    frame_weight,
    slot_ref,
    sent_ref,
    prenet_grad,
    context_grad,
    query_grad,
    processed_grad,
    vector_grad,
    filter_grad,
    held_one,
    held_two,
    grads_one,
    grads_two,
    back_one,
    back_two,
    state_one,
    cell_one,
    state_two,
    cell_two,
    previous_grad,
    summed_grad,
    from_query,
    frame_ref,
    filter_ref,
    sems,
):
    unit = unit_ref[0]
    steps, slots, prenet_width = prenet_grad.shape
    context_width = context_grad.shape[2]
    hidden = state_one.shape[1]
    half = hidden // 2
    per_half = half // lanes
    position_count = hot_ref.shape[0]
    text_width = position_count // (slots // 4)
    copies_two = [
        pltpu.make_async_copy(own_two, held_two.at[0], sems.at[0]),
        pltpu.make_async_copy(peer_two, held_two.at[1], sems.at[1]),
    ]
    copies_one = [
        pltpu.make_async_copy(own_one, held_one.at[0], sems.at[2]),
        pltpu.make_async_copy(peer_one, held_one.at[1], sems.at[3]),
    ]
    for copy in copies_two + copies_one:
        copy.start()
    for ref in (
        state_one,
        cell_one,
        state_two,
        cell_two,
        back_one,
        back_two,
        previous_grad,
        summed_grad,
        processed_grad,
        vector_grad,
        filter_grad,
    ):
        ref[...] = jnp.zeros_like(ref)

    def cell(gates_ref, prior_ref, zone_ref, state, cells, grads_ref, step, incoming):
        def one(chunk, _):
            spot = pl.ds(pl.multiple_of(chunk * lanes, lanes), lanes)
            places = [pl.ds(gate_spot(chunk, gate, per_half), lanes) for gate in range(4)]
            values = [gates_ref[step, :, place] for place in places]
            zone = zone_ref[step, :, spot]
            keep = 1.0 - zone
            before = prior_ref[step, :, spot]
            gate_in = jax.nn.sigmoid(values[0])
            gate_forget = jax.nn.sigmoid(values[1])
            candidate = jnp.tanh(values[2])
            gate_out = jax.nn.sigmoid(values[3])
            bent = jnp.tanh(gate_forget * before + gate_in * candidate)
            grad_state = incoming(unit_spot(chunk, unit, per_half)) + state[:, spot]
            grad_cell = cells[:, spot]
            grad_new = keep * grad_state
            grad_fresh = grad_new * gate_out * (1.0 - bent * bent) + keep * grad_cell
            state[:, spot] = zone * grad_state
            cells[:, spot] = zone * grad_cell + gate_forget * grad_fresh
            results = (
                grad_fresh * candidate * gate_in * (1.0 - gate_in),
                grad_fresh * before * gate_forget * (1.0 - gate_forget),
                grad_fresh * gate_in * (1.0 - candidate * candidate),
                grad_new * bent * gate_out * (1.0 - gate_out),
            )
            for place, result in zip(places, results):
                grads_ref[step, :, place] = result.astype(bf16)
            return 0

        lax.fori_loop(0, 2 * per_half, one, 0)

    def inputs_back(grads_ref, held, out_ref, step, blocks):
        def one(block, _):
            spot = pl.ds(pl.multiple_of(block * 256, 256), 256)
            total = None
            for tile in range(0, 8 * per_half, 2):
                side, inside = tile // (4 * per_half), tile % (4 * per_half)
                kernel = jnp.concatenate(
                    [held[side, inside, spot, :], held[side, inside + 1, spot, :]], axis=1
                )
                grads = grads_ref[step, :, tile * lanes : (tile + 2) * lanes]
                product = dot(grads, kernel, lanes_both)
                total = product if total is None else total + product
            out_ref[:, spot] = total
            return 0

        lax.fori_loop(0, blocks, one, 0)

    def attention(step, located):
        inside = hot_ref[...] > 0.0
        hot = hot_ref[...].astype(bf16)
        alpha = alpha_ref[step]
        mixed = mixed_ref[step]
        context_now = pad_rows(context_grad[step])
        weights_grad = jnp.where(
            inside,
            dot_left(memory_ref[...].astype(bf16), context_now, lanes_both)
            + previous_grad[...]
            + summed_grad[...],
            0.0,
        )
        product = alpha * weights_grad
        energy_grad = product - alpha * jnp.sum(product, axis=0, keepdims=True)
        spread = jnp.sum(energy_grad, axis=1, keepdims=True)
        vector_grad[...] += jnp.sum(spread * mixed, axis=0, keepdims=True)
        mixed_grad = spread * vector_ref[...] * (1.0 - mixed * mixed)
        processed_grad[...] += mixed_grad
        high, low = split(mixed_grad)
        query_now = (dot(hot, high, rows_first) + dot(hot, low, rows_first))[:slots]
        query_grad[step] = query_now
        from_query[...] = dot_right(query_now, query_ref[...].astype(bf16), lanes_both)
        if located:
            previous = taps_ref[step - 1]
            summed = jnp.where(step == 2, taps_ref[0] + previous, previous)
            filter_grad[0] += dot_both(previous, mixed_grad, rows_first)
            filter_grad[1] += dot_both(summed, mixed_grad, rows_first)
            place_hot = position_hot(position_count, text_width, False)

            def taps_back(channel):
                taps_grad = slant(
                    dot_both(mixed_grad, filter_ref[channel], lanes_both), text_width
                )
                gathered = dot_right(taps_grad, hot, rows_first)
                return jnp.where(inside, dot_left(place_hot, gathered), 0.0)

            previous_grad[...] = taps_back(0)
            summed_grad[...] += taps_back(1)

    def arrived(step, copies):
        @pl.when(step == steps - 1)
        def _():
            for copy in copies:
                copy.wait()

    def step_back(step, located):
        cell(
            gates_two,
            prior_two,
            zone_two,
            state_two,
            cell_two,
            grads_two,
            step,
            lambda spot: frame_ref[step, :, pl.ds(spot, lanes)]
            + back_two[:, pl.ds(spot + hidden + context_width, lanes)],
        )
        blocks_two = (hidden + context_width + (hidden if located else 0)) // 256
        if located:
            arrived(step, copies_two)
        inputs_back(grads_two, held_two, back_two, step, blocks_two)
        context_grad[step] = (
            back_two[:, hidden : hidden + context_width]
            + frame_ref[step, :, hidden:]
            + back_one[:, prenet_width : prenet_width + context_width]
        )
        attention(step, located)
        cell(
            gates_one,
            prior_one,
            zone_one,
            state_one,
            cell_one,
            grads_one,
            step,
            lambda spot: back_two[:, pl.ds(spot, lanes)]
            + from_query[:, pl.ds(spot, lanes)]
            + back_one[:, pl.ds(spot + prenet_width + context_width, lanes)],
        )
        blocks_one = (prenet_width + (hidden + context_width if located else 0)) // 256
        if located:
            arrived(step, copies_one)
        inputs_back(grads_one, held_one, back_one, step, blocks_one)
        prenet_grad[step] = back_one[:, :prenet_width]

    for channel in range(2):
        filter_ref[channel] = dot(
            conv_ref[channel].astype(bf16), dense_ref[...].astype(bf16)
        )
    for step in range(steps):
        frame_ref[step] = dot(
            frame_grad[step].astype(bf16), frame_weight[...].astype(bf16), lanes_both
        )

    def later(index, _):
        step_back(steps - 1 - index, True)
        return 0

    lax.fori_loop(0, steps - 1, later, 0)
    step_back(0, False)
    slot_hot = slot_ref[...].astype(bf16)

    def tile_out(tile, _):
        for layer, grads_ref in ((0, grads_one), (1, grads_two)):
            for side in range(2):
                place = ((side + unit) % 2) * 4 * half + tile * lanes
                grads = grads_ref[:, :, pl.ds(pl.multiple_of(place, lanes), lanes)]
                chosen = dot(slot_hot, grads.reshape(steps * slots, lanes)).astype(bf16)
                spot = (2 * layer + side) * lanes
                sent_ref[tile, :, spot : spot + lanes] = chosen
        return 0

    lax.fori_loop(0, 4 * per_half, tile_out, 0)


def call_forward(unit, weights, small, sizes):
    own_one, peer_one, own_two, peer_two = weights
    steps, slots, hidden, context_width, positions, frame_rows, prenet_width = sizes

    def shape(*dims):
        return jax.ShapeDtypeStruct(dims, f32)

    outs = [
        shape(steps, slots, 4 * hidden),
        shape(steps, slots, 4 * hidden),
        shape(steps, slots, hidden),
        shape(steps, slots, hidden),
        shape(steps, slots, hidden),
        shape(steps, slots, hidden),
        shape(steps, slots, context_width),
        shape(steps, positions, lanes),
        shape(steps, positions, lanes),
        shape(steps - 1, positions, lanes),
        shape(frame_rows, prenet_width),
        shape(frame_rows, prenet_width),
        shape(frame_rows, prenet_width),
        shape(frame_rows, prenet_width),
        shape(frame_rows, lanes),
    ]
    vmem = pl.BlockSpec(memory_space=pltpu.VMEM)
    return pl.pallas_call(
        forward_kernel,
        out_shape=outs,
        in_specs=[pl.BlockSpec(memory_space=pltpu.SMEM)]
        + [pl.BlockSpec(memory_space=pl.ANY)] * 4
        + [vmem] * len(small),
        out_specs=[vmem] * len(outs),
        scratch_shapes=[
            pltpu.VMEM((2,) + own_one.shape, bf16),
            pltpu.VMEM((2,) + own_two.shape, bf16),
            pltpu.VMEM((slots, own_two.shape[1]), bf16),
            pltpu.VMEM((steps, slots, prenet_width), f32),
            pltpu.VMEM((positions, lanes), f32),
            pltpu.VMEM((2, lanes, lanes), f32),
            pltpu.VMEM((slots, hidden), f32),
            pltpu.VMEM((slots, hidden), f32),
            pltpu.VMEM((slots, hidden), f32),
            pltpu.VMEM((slots, hidden), f32),
            pltpu.SemaphoreType.DMA((4,)),
        ],
        compiler_params=pltpu.CompilerParams(vmem_limit_bytes=kernel_vmem),
        name="decoder_forward",
    )(unit, *weights, *small)


def call_backward(unit, weights, small):
    own_one, peer_one, own_two, peer_two = weights
    gates_one = small[0]
    steps, slots, gate_width = gates_one.shape
    hidden = gate_width // 4
    positions, context_width = small[7].shape
    prenet_width = own_one.shape[1] - hidden - context_width

    def shape(dims, kind):
        return jax.ShapeDtypeStruct(dims, kind)

    outs = [
        shape((gate_width // (2 * lanes), small[-1].shape[0], 4 * lanes), bf16),
        shape((steps, slots, prenet_width), f32),
        shape((steps, slots, context_width), f32),
        shape((steps, slots, lanes), f32),
        shape((positions, lanes), f32),
        shape((1, lanes), f32),
        shape((2, lanes, lanes), f32),
    ]
    vmem = pl.BlockSpec(memory_space=pltpu.VMEM)
    return pl.pallas_call(
        backward_kernel,
        out_shape=outs,
        in_specs=[pl.BlockSpec(memory_space=pltpu.SMEM)]
        + [pl.BlockSpec(memory_space=pl.ANY)] * 4
        + [vmem] * len(small),
        out_specs=[vmem] * len(outs),
        scratch_shapes=[
            pltpu.VMEM((2,) + own_one.shape, bf16),
            pltpu.VMEM((2,) + own_two.shape, bf16),
            pltpu.VMEM((steps, slots, gate_width), bf16),
            pltpu.VMEM((steps, slots, gate_width), bf16),
            pltpu.VMEM((slots, own_one.shape[1]), f32),
            pltpu.VMEM((slots, own_two.shape[1]), f32),
            pltpu.VMEM((slots, hidden), f32),
            pltpu.VMEM((slots, hidden), f32),
            pltpu.VMEM((slots, hidden), f32),
            pltpu.VMEM((slots, hidden), f32),
            pltpu.VMEM((positions, lanes), f32),
            pltpu.VMEM((positions, lanes), f32),
            pltpu.VMEM((slots, hidden), f32),
            pltpu.VMEM((steps, slots, hidden + context_width), f32),
            pltpu.VMEM((2, lanes, lanes), f32),
            pltpu.SemaphoreType.DMA((4,)),
        ],
        compiler_params=pltpu.CompilerParams(vmem_limit_bytes=kernel_vmem),
        name="decoder_backward",
    )(unit, *weights, *small)


def postnet_kernel(
    mel_width,
    loss_scale,
    unit_ref,
    mel_ref,
    target_ref,
    mask_ref,
    first_ref,
    own_ref,
    peer_ref,
    last_ref,
    gain_ref,
    shift_ref,
    inputs_first,
    inputs_later,
    grads_early,
    grads_last,
    norm_grads,
    mel_grad,
    padded,
    padded_mel,
    held,
    normed_early,
    normed_last,
    inverse_ref,
    post_grad,
):
    unit = unit_ref[0]
    count, channels = held.shape
    side = channels // 2
    frames = padded.shape[0] - count
    rows_each = frames // 4
    chunk = 2 * rows_each
    tall = float(count)
    body_rows = slice(2 * rows_each, 2 * rows_each + count)

    for ref in (padded, padded_mel):
        ref[: 2 * rows_each] = jnp.zeros((2 * rows_each, ref.shape[1]), bf16)
        ref[2 * rows_each + count :] = jnp.zeros((2 * rows_each, ref.shape[1]), bf16)

    def piece(source, start, tap, width, lane=None):
        spot = pl.ds(pl.multiple_of(start + tap * rows_each, rows_each), chunk)
        mask = mask_ref[tap, pl.ds(pl.multiple_of(start, rows_each), chunk), :]
        if width < lanes:
            mask = mask[:, :width]
        else:
            mask = jnp.concatenate([mask] * (width // lanes), axis=1)
        value = source[spot, :] if lane is None else source[spot, pl.ds(lane, width)]
        return value * mask

    def chunks(work):
        def one(index, _):
            work(pl.multiple_of(index * chunk, chunk))
            return 0

        lax.fori_loop(0, count // chunk, one, 0)

    def half_spot(which):
        return pl.multiple_of(((which + unit) % 2) * side, side)

    def norm_forward(value, layer, lane, width):
        mean = jnp.sum(value, axis=0, keepdims=True) / tall
        centered = value - mean
        inverse = lax.rsqrt(jnp.sum(centered * centered, axis=0, keepdims=True) / tall + norm_eps)
        inverse_ref[layer, :, pl.ds(lane, width)] = inverse
        return centered * inverse

    def each_lane_block(work):
        def one(index, _):
            work(pl.multiple_of(index * lanes, lanes))
            return 0

        lax.fori_loop(0, channels // lanes, one, 0)

    def activate(layer):
        def block(lane):
            spot = pl.ds(lane, lanes)
            normed = norm_forward(held[:, spot], layer, lane, lanes)
            normed_early[layer, :, spot] = normed
            active = jnp.tanh(
                normed * gain_ref[layer, :, spot] + shift_ref[layer, :, spot]
            ).astype(bf16)
            inputs_later[layer, :, spot] = active
            padded[body_rows, spot] = active

        each_lane_block(block)

    source = mel_ref[...].astype(bf16)
    inputs_first[...] = source
    padded_mel[body_rows] = source

    def first_chunk(start):
        total = None
        for tap in range(5):
            product = dot(piece(padded_mel, start, tap, mel_width), first_ref[tap])
            total = product if total is None else total + product
        held[pl.ds(start, chunk), :] = total

    chunks(first_chunk)
    activate(0)

    def middle(index, _):
        for which, ref in ((0, own_ref), (1, peer_ref)):

            def middle_chunk(start, which=which, ref=ref):
                total = None
                for tap in range(5):
                    product = dot(piece(padded, start, tap, channels), ref[index * 5 + tap])
                    total = product if total is None else total + product
                held[pl.ds(start, chunk), pl.ds(half_spot(which), side)] = total

            chunks(middle_chunk)
        activate(index + 1)
        return 0

    lax.fori_loop(0, 3, middle, 0)

    def last_chunk(start):
        total = None
        for tap in range(5):
            product = dot(piece(padded, start, tap, channels), last_ref[tap])
            total = product if total is None else total + product
        normed_last[pl.ds(start, chunk), :] = total

    chunks(last_chunk)
    normed = norm_forward(normed_last[...], 4, 0, mel_width)
    normed_last[...] = normed

    def norm_back(grad, normed, layer, lane, width):
        spot = pl.ds(lane, width)
        shift_grad = jnp.sum(grad, axis=0, keepdims=True)
        gain_grad = jnp.sum(grad * normed, axis=0, keepdims=True)
        norm_grads[0, layer, :, spot] = gain_grad
        norm_grads[1, layer, :, spot] = shift_grad
        return (
            gain_ref[layer, :, spot]
            * inverse_ref[layer, :, spot]
            * (grad - shift_grad / tall - normed * (gain_grad / tall))
        ).astype(bf16)

    output = normed * gain_ref[4, :, :mel_width] + shift_ref[4, :, :mel_width]
    grad = loss_scale * (mel_ref[...] + output - target_ref[...])
    post_grad[...] = grad
    grad_norm = norm_back(grad, normed, 4, 0, mel_width)
    grads_last[...] = grad_norm
    padded_mel[body_rows] = grad_norm

    def last_back(start):
        total = None
        for tap in range(5):
            product = dot(
                piece(padded_mel, start, tap, mel_width), last_ref[4 - tap], lanes_both
            )
            total = product if total is None else total + product
        held[pl.ds(start, chunk), :] = total

    chunks(last_back)

    def deactivate(layer):
        def block(lane):
            spot = pl.ds(lane, lanes)
            normed = normed_early[layer, :, spot]
            active = jnp.tanh(normed * gain_ref[layer, :, spot] + shift_ref[layer, :, spot])
            grad = held[:, spot] * (1.0 - active * active)
            grad_norm = norm_back(grad, normed, layer, lane, lanes)
            grads_early[layer, :, spot] = grad_norm
            padded[body_rows, spot] = grad_norm

        each_lane_block(block)

    def middle_back(back, _):
        index = 2 - back
        deactivate(index + 1)

        def chunk_back(start):
            total = None
            for which, ref in ((0, own_ref), (1, peer_ref)):
                for tap in range(5):
                    product = dot(
                        piece(padded, start, tap, side, half_spot(which)),
                        ref[index * 5 + 4 - tap],
                        lanes_both,
                    )
                    total = product if total is None else total + product
            held[pl.ds(start, chunk), :] = total

        chunks(chunk_back)
        return 0

    lax.fori_loop(0, 3, middle_back, 0)
    deactivate(0)

    def first_back(start):
        total = None
        for tap in range(5):
            product = dot(piece(padded, start, tap, channels), first_ref[4 - tap], lanes_both)
            total = product if total is None else total + product
        spot = pl.ds(start, chunk)
        mel_grad[spot, :] = (
            loss_scale * (mel_ref[spot, :] - target_ref[spot, :]) + post_grad[spot, :] + total
        )

    chunks(first_back)


def call_postnet(unit, small, loss_scale, rows_all):
    mel = small[0]
    count, mel_width = mel.shape
    channels = small[3].shape[2]

    def shape(kind, *dims):
        return jax.ShapeDtypeStruct(dims, kind)

    outs = [
        shape(bf16, count, mel_width),
        shape(bf16, 4, count, channels),
        shape(bf16, 4, count, channels),
        shape(bf16, count, mel_width),
        shape(f32, 2, 5, 1, channels),
        shape(f32, count, mel_width),
    ]
    vmem = pl.BlockSpec(memory_space=pltpu.VMEM)
    tall = count + 4 * rows_all
    return pl.pallas_call(
        functools.partial(postnet_kernel, mel_width, loss_scale),
        out_shape=outs,
        in_specs=[pl.BlockSpec(memory_space=pltpu.SMEM)] + [vmem] * len(small),
        out_specs=[vmem] * len(outs),
        scratch_shapes=[
            pltpu.VMEM((tall, channels), bf16),
            pltpu.VMEM((tall, mel_width), bf16),
            pltpu.VMEM((count, channels), f32),
            pltpu.VMEM((4, count, channels), f32),
            pltpu.VMEM((count, mel_width), f32),
            pltpu.VMEM((5, 1, channels), f32),
            pltpu.VMEM((count, mel_width), f32),
        ],
        compiler_params=pltpu.CompilerParams(vmem_limit_bytes=kernel_vmem),
        name="postnet",
    )(unit, *small)


def shifted_frames(source, same):
    steps = source.shape[0]
    padded = jnp.pad(source, ((2, 2), (0, 0), (0, 0)))
    return [
        padded[offset : offset + steps] * same[:, :, offset, None].astype(source.dtype)
        for offset in range(5)
    ]


def by_rows(work, roomy, arrays, summed=False):
    if roomy:
        return work(*arrays)
    parts = arrays[0].shape[1] // 192

    def cut(value):
        value = value.reshape((value.shape[0], parts, -1) + value.shape[2:])
        return jnp.moveaxis(value, 1, 0)

    pieces = tuple(cut(value) for value in arrays)
    if summed:
        first = jax.eval_shape(work, *[value[0] for value in pieces])
        start = jnp.zeros(first.shape, first.dtype)
        return lax.scan(lambda total, now: (total + work(*now), None), start, pieces)[0]
    result = jnp.moveaxis(lax.map(lambda now: work(*now), pieces), 0, 1)
    return result.reshape((result.shape[0], -1) + result.shape[3:])


def post_layer(source, kernel, same):
    wide = jnp.concatenate(shifted_frames(source, same), axis=2)
    return jnp.einsum(
        "src,co->sro", wide, kernel.reshape(-1, kernel.shape[2]), preferred_element_type=f32
    )


def post_layer_back(grad, kernel, same):
    wide = jnp.concatenate(shifted_frames(grad, same), axis=2)
    turned = jnp.transpose(kernel[::-1], (0, 2, 1)).reshape(-1, kernel.shape[1])
    return jnp.einsum("sro,oc->src", wide, turned, preferred_element_type=f32)


def post_kernel_grad(source, grad, same):
    wide = jnp.concatenate(shifted_frames(source, same), axis=2)
    return jnp.einsum("src,sro->co", wide, grad, preferred_element_type=f32)


def on_device(
    memory,
    targets,
    segments,
    text_lengths,
    zone_first,
    zone_second,
    drop_first,
    drop_second,
    prenet_first,
    prenet_second,
    query_weight,
    memory_weight,
    location_conv,
    location_dense,
    energy_vector,
    lstm_first,
    bias_first,
    lstm_second,
    bias_second,
    frame_weight,
    frame_bias,
    post_first,
    post_middle,
    post_last,
    middle_norm,
    last_norm,
):
    micro_count, rows, text_width, memory_width = memory.shape
    frames = segments.shape[2]
    utterances = text_lengths.shape[2]
    mel_width = targets.shape[3]
    hidden = query_weight.shape[0]
    prenet_width = prenet_first.shape[1]
    attention_width = query_weight.shape[1]
    half = lstm_first.shape[2]
    depth_one, depth_two = lstm_first.shape[0], lstm_second.shape[0]
    unit = lax.axis_index("unit")
    place = lax.axis_index("batch")
    batch_size = lax.axis_size("batch")
    total_rows = rows * batch_size
    frame_count = float(total_rows * frames)
    first_unit = unit == 0
    longest = 3
    slots = 4 * rows

    def exchange(value):
        return lax.ppermute(value, "unit", [(0, 1), (1, 0)])

    def ordered(own, peer):
        return jnp.where(first_unit, own, peer), jnp.where(first_unit, peer, own)

    def whole(value, axis):
        return jnp.concatenate(ordered(value, exchange(value)), axis=axis)

    def mine(value):
        return lax.dynamic_index_in_dim(value, unit, 0, keepdims=False)

    def others(value):
        return lax.dynamic_index_in_dim(value, 1 - unit, 0, keepdims=False)

    def swapped(value, bit):
        pairs = [(index, index ^ bit) for index in range(batch_size)]
        other = lax.ppermute(value, "batch", pairs)
        upper = (place & bit) != 0
        return jnp.where(upper, other, value), jnp.where(upper, value, other)

    def add_batch(value):
        bit = 1
        while bit < batch_size:
            upper = (place & bit) != 0
            tall = value.shape[0] // 2
            pairs = [(index, index ^ bit) for index in range(batch_size)]
            give = jnp.where(upper, value[:tall], value[tall:])
            value = jnp.where(upper, value[tall:], value[:tall]) + lax.ppermute(
                give, "batch", pairs
            )
            bit *= 2
        while bit > 1:
            bit //= 2
            value = jnp.concatenate(swapped(value, bit), axis=0)
        return value

    def gather_rows(value):
        bit = 1
        while bit < batch_size:
            value = jnp.concatenate(swapped(value, bit), axis=0)
            bit *= 2
        return value

    def gather_tiles(value):
        tiles = jnp.transpose(value.reshape(value.shape[0], -1, lanes), (1, 0, 2))
        return lax.all_gather(tiles, "batch", axis=1, tiled=True)

    own_two = gather_tiles(lstm_second)
    own_one = gather_tiles(lstm_first)
    peer_two = exchange(own_two)
    channel_rows = post_middle.shape[2]
    middle_width = post_middle.shape[3]
    middle_half = lax.all_gather(
        post_middle.reshape(-1, channel_rows, middle_width), "batch", axis=1, tiled=True
    )
    middle_peer = exchange(middle_half)
    last_half = gather_rows(jnp.transpose(post_last, (1, 0, 2)).reshape(channel_rows, -1))
    last_half = jnp.transpose(
        last_half.reshape(-1, post_last.shape[0], post_last.shape[2]), (1, 0, 2)
    )
    memory_now = mine(memory).reshape(rows * text_width, memory_width)
    segments_now = mine(segments)
    targets_now = mine(targets)
    frame_info = gather_rows(
        jnp.concatenate([targets_now, segments_now[:, :, None].astype(bf16)], axis=2).astype(f32)
    )

    same_frames = segments_now[:, :, None] == segments_now[:, None, :]
    earlier = jnp.tril(jnp.ones((frames, frames), jnp.bool_), -1)
    order = jnp.sum((same_frames & earlier[None]).astype(jnp.int32), axis=2)
    slot_of = order * slots + segments_now * rows + jnp.arange(rows, dtype=jnp.int32)[:, None]
    frame_rows = rows * frames
    padding = -frame_rows % 16
    slot_hot = (
        jnp.pad(slot_of.reshape(-1, 1), ((0, padding), (0, 0)), constant_values=-1)
        == jnp.arange(longest * slots, dtype=jnp.int32)[None, :]
    ).astype(bf16)
    slot_hot_frames = slot_hot[:frame_rows]
    carry_on = jnp.pad(
        (segments_now[:, 1:] == segments_now[:, :-1]).astype(f32), ((0, 0), (1, 0))
    )
    finished = jnp.pad(
        (segments_now[:, 1:] != segments_now[:, :-1]).astype(f32),
        ((0, 0), (0, 1)),
        constant_values=1.0,
    )

    def to_slots(value, kind=bf16):
        return lax.dot_general(
            slot_hot_frames,
            value.astype(bf16),
            (((0,), (0,)), ((), ())),
            preferred_element_type=f32,
        ).astype(kind)

    def to_frames(value):
        return jnp.dot(slot_hot, value.astype(bf16), preferred_element_type=f32).astype(bf16)

    def pad_frames(value):
        return jnp.pad(
            value.astype(f32).reshape(frame_rows, -1), ((0, padding), (0, 0))
        )

    previous = pad_frames(
        jnp.pad(targets_now[:, :-1], ((0, 0), (1, 0), (0, 0))).astype(f32)
        * carry_on[:, :, None]
    )
    drops_one = pad_frames(mine(drop_first))
    drops_two = pad_frames(mine(drop_second))

    zones_own = jnp.concatenate([mine(zone_first), mine(zone_second)], axis=2).astype(f32)
    zones_peer = exchange(
        jnp.concatenate([others(zone_first), others(zone_second)], axis=2).astype(f32)
    )
    zones_slots = to_slots(
        jnp.concatenate([zones_own, zones_peer], axis=2).reshape(rows * frames, -1), f32
    ).reshape(longest, slots, 4 * half)
    zone_one = jnp.concatenate(
        [zones_slots[:, :, :half], zones_slots[:, :, 2 * half : 3 * half]], axis=2
    )
    zone_two = jnp.concatenate(
        [zones_slots[:, :, half : 2 * half], zones_slots[:, :, 3 * half :]], axis=2
    )
    biases = jnp.stack([bias_first.reshape(-1), bias_second.reshape(-1)])
    biases = jnp.concatenate([biases, exchange(biases)], axis=1)
    text_ends = jnp.cumsum(mine(text_lengths), axis=1)
    owner = jnp.sum(
        (jnp.arange(text_width, dtype=jnp.int32)[None, :, None] >= text_ends[:, None, :]).astype(
            jnp.int32
        ),
        axis=2,
    )
    owner_slot = owner * rows + jnp.arange(rows, dtype=jnp.int32)[:, None]
    owner_hot = (
        owner_slot.reshape(-1, 1) == jnp.arange(lanes, dtype=jnp.int32)[None, :]
    ).astype(f32)
    conv_float = location_conv.astype(f32)
    dense_float = location_dense.astype(f32)
    reach = location_conv.shape[2] // 2
    taps_first = jnp.transpose(conv_float, (1, 2, 0))
    taps_first = jnp.pad(
        taps_first,
        ((0, 0), (0, lanes - taps_first.shape[1]), (0, lanes - taps_first.shape[2])),
    )
    dense_wide = jnp.pad(dense_float, ((0, lanes - dense_float.shape[0]), (0, 0)))
    taps_forward = jnp.roll(taps_first[:, ::-1], reach, axis=1)
    taps_back = jnp.roll(taps_first, 1 - reach, axis=1)
    frame_wide = jnp.pad(
        frame_weight.astype(f32), ((0, 0), (0, lanes - frame_weight.shape[1]))
    )
    frame_bias_wide = jnp.pad(frame_bias, (0, lanes - frame_bias.shape[0]))[None, :]
    vector_float = energy_vector.astype(f32)
    vector_wide = jnp.broadcast_to(vector_float[:, None], (attention_width, lanes))
    memory_float = memory_now.astype(f32)
    query_float = query_weight.astype(f32)
    unit_array = unit.astype(jnp.int32).reshape(1)

    targets_all = jnp.transpose(frame_info[:, :, :mel_width].astype(f32), (1, 0, 2))
    segments_all = jnp.transpose(frame_info[:, :, mel_width].astype(jnp.int32))
    padded = jnp.pad(segments_all, ((2, 2), (0, 0)), constant_values=-1)
    same = jnp.stack([padded[offset : offset + frames] == segments_all for offset in range(5)])
    same = jnp.moveaxis(same, 0, 2)
    first_full = whole(post_first, 2)
    last_full = whole(last_half, 2)
    middle_gain = whole(middle_norm, 2)
    last_gain = whole(last_norm, 1)
    loss_scale = 2.0 / (mel_width * total_rows)
    count = total_rows * frames
    channels = middle_norm.shape[2] * 2
    masks = jnp.broadcast_to(
        jnp.transpose(same, (2, 0, 1)).reshape(5, count, 1).astype(bf16), (5, count, lanes)
    )
    wide_gain = jnp.pad(last_gain, ((0, 0), (0, channels - mel_width)))
    norms = jnp.concatenate([middle_gain, wide_gain[:, None, :]], axis=1)[:, :, None, :]
    forward_small = (
        previous,
        drops_one,
        drops_two,
        prenet_first.astype(f32),
        prenet_second.astype(f32),
        slot_hot.astype(f32),
        zone_one,
        zone_two,
        biases[0:1],
        biases[1:2],
        owner_hot,
        memory_float,
        memory_weight.astype(f32),
        query_float,
        vector_wide,
        taps_forward,
        dense_wide,
        frame_wide,
        frame_bias_wide,
    )
    (
        own_one,
        own_two,
        forward_small,
        taps_back,
        vector_row,
        targets_all,
        masks,
        first_full,
        last_full,
        norms,
    ) = lax.optimization_barrier(
        (
            own_one,
            own_two,
            forward_small,
            taps_back,
            vector_float[None, :],
            targets_all,
            masks,
            first_full,
            last_full,
            norms,
        )
    )
    weights = (own_one, exchange(own_one), own_two, peer_two)
    slot_wide, zone_one, zone_two = forward_small[5], forward_small[6], forward_small[7]
    memory_float, query_float = forward_small[11], forward_small[13]
    dense_wide, frame_wide = forward_small[16], forward_small[17]

    (
        gates_one,
        gates_two,
        prior_one,
        prior_two,
        round_one,
        round_two,
        contexts,
        mixed_all,
        alphas,
        taps,
        mixed_one,
        mixed_two,
        hidden_round,
        prenet_round,
        frame_out,
    ) = call_forward(
        unit_array,
        weights,
        forward_small,
        (
            longest,
            slots,
            hidden,
            memory_width,
            rows * text_width,
            frame_rows + padding,
            prenet_width,
        ),
    )

    states = to_frames(
        jnp.concatenate([round_one, contexts, round_two], axis=2).reshape(longest * slots, -1)
    )
    frame_in = jnp.concatenate(
        [states[:, hidden + memory_width :], states[:, hidden : hidden + memory_width]], axis=1
    )
    frame_in = frame_in[:frame_rows]
    frame_out = frame_out[:frame_rows]
    mel_own = frame_out[:, :mel_width].reshape(rows, frames, mel_width)
    stop_logit = frame_out[:, mel_width].reshape(rows, frames)
    mel_all = jnp.transpose(
        gather_rows(mel_own), (1, 0, 2)
    )
    inputs_own = jnp.concatenate([prenet_round.astype(bf16), states], axis=1)
    roomy = total_rows * frames <= 2048
    if roomy:
        inputs_own, mel_all = lax.optimization_barrier((inputs_own, mel_all))
        inputs_all = lax.all_gather(inputs_own, "batch", axis=0, tiled=True)

    if roomy:
        (
            inputs_first,
            inputs_later,
            grads_early,
            grads_last,
            norm_grads,
            grad_mel,
        ) = call_postnet(
            unit_array,
            (
                mel_all.reshape(count, mel_width),
                targets_all.reshape(count, mel_width),
                masks,
                first_full,
                middle_half,
                middle_peer,
                last_full,
                norms[0],
                norms[1],
            ),
            loss_scale,
            total_rows,
        )
        gain_grads = [norm_grads[0, layer, 0] for layer in range(5)]
        shift_grads = [norm_grads[1, layer, 0] for layer in range(5)]
        gain_grads[4], shift_grads[4] = gain_grads[4][:mel_width], shift_grads[4][:mel_width]
        kernel_grads = []
        for layer in range(5):
            if layer == 0:
                source = inputs_first
            else:
                source = lax.dynamic_slice_in_dim(
                    inputs_later[layer - 1], place * channel_rows, channel_rows, 1
                )
            grad_norm = grads_early[layer] if layer < 4 else grads_last
            kernel_grads.append(
                post_kernel_grad(
                    source.reshape(frames, total_rows, -1),
                    grad_norm.reshape(frames, total_rows, -1),
                    same,
                ).reshape(5, source.shape[1], grad_norm.shape[1])
            )
        grad_mel = jnp.transpose(
            lax.dynamic_slice_in_dim(
                grad_mel.reshape(frames, total_rows, mel_width), place * rows, rows, 1
            ),
            (1, 0, 2),
        )
    else:
        middle_full = whole(middle_half, 2).reshape(post_middle.shape[:2] + (channels, channels))
        kernels = [first_full, middle_full[0], middle_full[1], middle_full[2], last_full]
        gains = [middle_gain[0, layer] for layer in range(4)] + [last_gain[0]]
        shifts = [middle_gain[1, layer] for layer in range(4)] + [last_gain[1]]
        layer_in = mel_all.astype(bf16)
        layer_inputs, normed_all, inverses = [], [], []
        output = None
        for layer in range(5):
            layer_inputs.append(layer_in)
            pre_norm = by_rows(
                lambda source, same_now: post_layer(source, kernels[layer], same_now),
                roomy,
                (layer_in, same),
            )
            mean_now = jnp.sum(pre_norm, axis=(0, 1)) / frame_count
            centered = pre_norm - mean_now
            inverse = lax.rsqrt(jnp.sum(centered * centered, axis=(0, 1)) / frame_count + norm_eps)
            normed = centered * inverse
            output = normed * gains[layer] + shifts[layer]
            normed_all.append(normed)
            inverses.append(inverse)
            if layer < 4:
                layer_in = jnp.tanh(output).astype(bf16)
                if not roomy:
                    layer_in, normed_all[layer] = lax.optimization_barrier(
                        (layer_in, normed_all[layer])
                    )

        grad_post = loss_scale * (mel_all + output - targets_all)
        kernel_grads, gain_grads, shift_grads = [None] * 5, [None] * 5, [None] * 5
        grad_output = grad_post
        grad_input = None
        for layer in (4, 3, 2, 1, 0):
            if layer < 4:
                normed_all[layer] = lax.optimization_barrier(normed_all[layer])
                active = jnp.tanh(normed_all[layer] * gains[layer] + shifts[layer])
                grad_output = grad_input * (1.0 - active * active)
            shift_grads[layer] = jnp.sum(grad_output, axis=(0, 1))
            gain_grads[layer] = jnp.sum(grad_output * normed_all[layer], axis=(0, 1))
            grad_norm = (
                gains[layer]
                * inverses[layer]
                * (
                    grad_output
                    - shift_grads[layer] / frame_count
                    - normed_all[layer] * (gain_grads[layer] / frame_count)
                )
            ).astype(bf16)
            grad_input = by_rows(
                lambda grad, same_now: post_layer_back(grad, kernels[layer], same_now),
                roomy,
                (grad_norm, same),
            )
            source = layer_inputs[layer]
            if layer > 0:
                source = lax.dynamic_slice_in_dim(source, place * channel_rows, channel_rows, 2)
            kernel_grads[layer] = by_rows(post_kernel_grad, roomy, (source, grad_norm, same), True)
            kernel_grads[layer] = kernel_grads[layer].reshape(5, source.shape[2], -1)
            if not roomy:
                grad_input, kernel_grads[layer] = lax.optimization_barrier(
                    (grad_input, kernel_grads[layer])
                )
        grad_mel = loss_scale * (mel_all - targets_all) + grad_post + grad_input
        grad_mel = jnp.transpose(
            lax.dynamic_slice_in_dim(grad_mel, place * rows, rows, 1), (1, 0, 2)
        )

    if not roomy:
        inputs_own, grad_mel = lax.optimization_barrier((inputs_own, grad_mel))
        inputs_all = lax.all_gather(inputs_own, "batch", axis=0, tiled=True)

    def add_units(value, axis):
        width = value.shape[axis] // 2
        halves = [
            lax.slice_in_dim(value, start, start + width, axis=axis) for start in (0, width)
        ]
        keep = jnp.where(first_unit, halves[0], halves[1])
        give = jnp.where(first_unit, halves[1], halves[0])
        return keep + exchange(give)

    post_first_grad = add_units(kernel_grads[0], 2)
    post_middle_grad = add_units(jnp.stack(kernel_grads[1:4]), 3)
    post_last_grad = add_units(kernel_grads[4], 2)
    middle_norm_grad = add_units(
        jnp.stack([jnp.stack(gain_grads[:4]), jnp.stack(shift_grads[:4])]), 2
    )
    last_norm_grad = add_units(jnp.stack([gain_grads[4], shift_grads[4]]), 1)

    grad_stop = (jax.nn.sigmoid(stop_logit) - finished) / total_rows
    grad_frame = (
        jnp.concatenate([grad_mel, grad_stop[:, :, None]], axis=2)
        .reshape(rows * frames, mel_width + 1)
        .astype(bf16)
    )
    frame_weight_grad = lax.dot_general(
        frame_in, grad_frame, (((0,), (0,)), ((), ())), preferred_element_type=f32
    )
    frame_bias_grad = jnp.sum(grad_frame.astype(f32), axis=0)
    grad_frame_slots = to_slots(
        jnp.pad(grad_frame, ((0, 0), (0, lanes - mel_width - 1))), f32
    ).reshape(longest, slots, lanes)

    (
        sent,
        prenet_back,
        context_grads,
        query_back,
        processed_back,
        vector_back,
        filter_back,
    ) = call_backward(
        unit_array,
        weights,
        (
            gates_one,
            gates_two,
            prior_one,
            prior_two,
            zone_one,
            zone_two,
            owner_hot,
            memory_float,
            query_float,
            vector_row,
            taps_back,
            dense_wide,
            mixed_all,
            alphas,
            taps,
            grad_frame_slots,
            frame_wide,
            slot_wide,
        ),
    )

    bias_sums = jnp.transpose(
        jnp.sum(sent.astype(f32), axis=1).reshape(-1, 4, lanes), (1, 0, 2)
    ).reshape(-1, lanes)
    slice_width = 2 * hidden // batch_size
    if slice_width != lanes:
        sent = sent.reshape(sent.shape[0], sent.shape[1], 4, -1, slice_width)
        sent = jnp.transpose(sent, (0, 3, 1, 2, 4)).reshape(batch_size, sent.shape[1], -1)
    received = lax.all_to_all(sent, "batch", 0, 0, tiled=True)
    grad_prenet = lax.dot_general(
        slot_hot.astype(f32),
        prenet_back.reshape(longest * slots, prenet_width),
        (((1,), (0,)), ((), ())),
        precision=precise,
    )

    def silu_back(grad, mixed, drops):
        gate = jax.nn.sigmoid(mixed)
        return grad * drops * 2.0 * gate * (1.0 + mixed * (1.0 - gate))

    def exact(a, b, contract):
        return lax.dot_general(
            a.astype(f32), b.astype(f32), (contract, ((), ())), precision=precise
        )

    grad_mixed_two = silu_back(grad_prenet, mixed_two, drops_two)
    prenet_second_grad = exact(hidden_round, grad_mixed_two, ((0,), (0,)))
    grad_hidden = exact(grad_mixed_two, prenet_second, ((1,), (1,)))
    grad_mixed_one = silu_back(grad_hidden, mixed_one, drops_one)
    prenet_first_grad = exact(previous, grad_mixed_one, ((0,), (0,)))

    query_weight_grad = exact(
        round_one.reshape(longest * slots, hidden),
        query_back.reshape(longest * slots, attention_width),
        ((0,), (0,)),
    )
    processed_round = processed_back.astype(bf16)
    memory_weight_grad = lax.dot_general(
        memory_now, processed_round, (((0,), (0,)), ((), ())), preferred_element_type=f32
    )
    memory_grad = lax.dot_general(
        processed_round, memory_weight, (((1,), (1,)), ((), ())), preferred_element_type=f32
    )
    for step in range(longest):
        memory_grad = memory_grad + exact(
            alphas[step][:, :slots], context_grads[step], ((1,), (0,))
        )
    memory_grad = memory_grad.reshape(rows, text_width, memory_width)
    memory_grads = jnp.stack(ordered(memory_grad, exchange(memory_grad)))
    filter_grads = jnp.roll(filter_back, -reach, axis=1)[:, ::-1][:, : location_conv.shape[2]]
    conv_grad = jnp.einsum("cka,fa->fck", filter_grads, dense_float, precision=precise)
    dense_grad = jnp.einsum("cka,fck->fa", filter_grads, conv_float, precision=precise)

    def two_columns(value):
        return jnp.concatenate([value[:, :lanes], value[:, lanes:]], axis=0)

    def to_lanes(value):
        return jnp.pad(value, ((0, 0), (0, lanes - value.shape[1])))

    filter_count, _, tap_count = location_conv.shape
    packed = [
        two_columns(prenet_first_grad),
        two_columns(prenet_second_grad),
        query_weight_grad,
        memory_weight_grad,
        to_lanes(frame_weight_grad),
        to_lanes(conv_grad.reshape(filter_count, -1)),
        dense_grad,
        bias_sums,
        vector_back,
        to_lanes(frame_bias_grad[None, :]),
    ]
    heights = [value.shape[0] for value in packed]
    shares = 2 * batch_size
    surplus = -sum(heights) % (8 * shares)
    packed = jnp.concatenate(packed + [jnp.zeros((surplus, lanes), f32)], axis=0)
    packed = add_units(packed, 0)
    received, packed = lax.optimization_barrier((received, packed))

    segments_rows = segments_all.T
    carried = jnp.pad(
        (segments_rows[:, 1:] == segments_rows[:, :-1]).astype(bf16), ((0, 0), (0, 1))
    ).reshape(batch_size, frame_rows)
    carried = jnp.pad(carried, ((0, 0), (0, padding)))
    after = jnp.pad(received[:, 1:], ((0, 0), (0, 1), (0, 0))) * carried[:, :, None]
    received = received.reshape(batch_size * (frame_rows + padding), -1)
    after = after.reshape(batch_size * (frame_rows + padding), -1)

    def product(start, width, grads):
        return lax.dot_general(
            inputs_all[:, start : start + width],
            grads,
            (((0,), (0,)), ((), ())),
            preferred_element_type=f32,
        )

    pair = 2 * slice_width
    first_part = jnp.concatenate(
        [
            product(0, prenet_width, received[:, :pair]),
            product(prenet_width + hidden, memory_width, after[:, :pair]),
            product(prenet_width, hidden, after[:, :pair]),
        ],
        axis=0,
    )
    second_part = jnp.concatenate(
        [
            product(prenet_width, hidden + memory_width, received[:, pair:]),
            product(prenet_width + hidden + memory_width, hidden, after[:, pair:]),
        ],
        axis=0,
    )
    parts = jnp.concatenate(
        [
            first_part.reshape(batch_size, depth_one, pair),
            second_part.reshape(batch_size, depth_two, pair),
        ],
        axis=1,
    )
    parts = add_units(parts, 2).astype(bf16)
    parts = lax.all_to_all(parts, "batch", 0, 0, tiled=True).astype(f32)
    parts = jnp.transpose(parts, (1, 0, 2)).reshape(depth_one + depth_two, 4, half)

    packed = whole(add_batch(packed), 0)
    small, start = [], 0
    for height in heights:
        small.append(packed[start : start + height])
        start += height

    def from_columns(value):
        tall = value.shape[0] // 2
        return jnp.concatenate([value[:tall], value[tall:]], axis=1)

    biases_grad = small[7].reshape(2, 2, -1)
    biases_grad = jnp.where(first_unit, biases_grad[:, 0], biases_grad[:, 1])
    biases_grad = biases_grad.reshape(2, 4, half)
    small = [
        from_columns(small[0]),
        from_columns(small[1]),
        small[2],
        small[3],
        small[5][:, : 2 * tap_count].reshape(filter_count, 2, tap_count),
        small[6],
        small[8][0],
        small[4][:, : mel_width + 1],
        small[9][0, : mel_width + 1],
    ]
    return (
        small[0],
        small[1],
        small[2],
        small[3],
        small[4],
        small[5],
        small[6],
        parts[:depth_one],
        biases_grad[0],
        parts[depth_one:],
        biases_grad[1],
        small[7],
        small[8],
        post_first_grad,
        post_middle_grad,
        post_last_grad,
        middle_norm_grad,
        last_norm_grad,
        memory_grads,
    )


def solution(mesh):
    in_specs = (
        P(None, "batch", None, None),
        P(None, "batch", None, None),
        P(None, "batch", None),
        P(None, "batch", None),
        P(None, "batch", None, "unit"),
        P(None, "batch", None, "unit"),
        P(None, "batch", None, None),
        P(None, "batch", None, None),
        P(),
        P(),
        P(),
        P(),
        P(),
        P(),
        P(),
        P("batch", None, "unit"),
        P(None, "unit"),
        P("batch", None, "unit"),
        P(None, "unit"),
        P(),
        P(),
        P(None, None, "unit"),
        P(None, None, "batch", "unit"),
        P(None, "batch", "unit"),
        P(None, None, "unit"),
        P(None, "unit"),
    )
    out_specs = (
        P(),
        P(),
        P(),
        P(),
        P(),
        P(),
        P(),
        P("batch", None, "unit"),
        P(None, "unit"),
        P("batch", None, "unit"),
        P(None, "unit"),
        P(),
        P(),
        P(None, None, "unit"),
        P(None, None, "batch", "unit"),
        P(None, "batch", "unit"),
        P(None, None, "unit"),
        P(None, "unit"),
        P(None, "batch", None, None),
    )
    return jax.shard_map(
        on_device, mesh=mesh, in_specs=in_specs, out_specs=out_specs, check_vma=False
    )
```

```python
import functools

import jax
import jax.numpy as jnp
from jax import lax
from jax.experimental import pallas as pl
from jax.experimental.pallas import tpu as pltpu
from jax.sharding import PartitionSpec as P

precise = lax.Precision.HIGHEST
norm_eps = 1e-05
f32 = jnp.float32
bf16 = jnp.bfloat16
lanes = 128
kernel_vmem = 60 * 1024 * 1024


def split(value):
    high = value.astype(bf16)
    return high, (value - high.astype(f32)).astype(bf16)


def dot(a, b, contract=((1,), (0,))):
    return lax.dot_general(a, b, (contract, ((), ())), preferred_element_type=f32)


def dot_left(exact, value, contract=((1,), (0,))):
    high, low = split(value)
    return dot(exact, high, contract) + dot(exact, low, contract)


def dot_right(value, exact, contract=((1,), (0,))):
    high, low = split(value)
    return dot(high, exact, contract) + dot(low, exact, contract)


def dot_both(a, b, contract=((1,), (0,))):
    a_high, a_low = split(a)
    b_high, b_low = split(b)
    return (
        dot(a_high, b_high, contract) + dot(a_low, b_high, contract) + dot(a_high, b_low, contract)
    )


rows_first = ((0,), (0,))
lanes_both = ((1,), (1,))


def position_hot(position_count, text_width, reverse):
    place = lax.broadcasted_iota(jnp.int32, (position_count, lanes), 0) & (text_width - 1)
    lane = lax.broadcasted_iota(jnp.int32, (position_count, lanes), 1)
    place = (lanes - 1) - place if reverse else place + 1
    return (place == lane).astype(bf16)


def slant(value, text_width):
    blocks = [
        pltpu.roll(value[start : start + text_width], 0, 1, stride=1, stride_axis=0)
        for start in range(0, value.shape[0], text_width)
    ]
    return jnp.concatenate(blocks, axis=0)


def pad_rows(value):
    return jnp.concatenate(
        [value, jnp.zeros((lanes - value.shape[0], value.shape[1]), value.dtype)], axis=0
    )


def unit_spot(chunk, unit, per_half):
    half = (chunk // per_half + unit) % 2
    return pl.multiple_of((half * per_half + chunk % per_half) * lanes, lanes)


def gate_spot(chunk, gate, per_half):
    start = (chunk // per_half) * 4 * per_half + gate * per_half + chunk % per_half
    return pl.multiple_of(start * lanes, lanes)


def forward_kernel(
    unit_ref,
    own_one,
    peer_one,
    own_two,
    peer_two,
    previous_ref,
    drop_one,
    drop_two,
    layer_one,
    layer_two,
    slot_ref,
    zone_one,
    zone_two,
    bias_one,
    bias_two,
    hot_ref,
    memory_ref,
    project_ref,
    query_ref,
    vector_ref,
    conv_ref,
    dense_ref,
    frame_ref,
    frame_bias,
    gates_one,
    gates_two,
    prior_one,
    prior_two,
    round_one,
    round_two,
    context_ref,
    mixed_ref,
    alpha_ref,
    taps_ref,
    prenet_one,
    prenet_two,
    prenet_hidden,
    prenet_out,
    frame_out,
    held_one,
    held_two,
    input_ref,
    prenet_ref,
    processed_ref,
    filter_ref,
    state_one,
    cell_one,
    state_two,
    cell_two,
    sems,
):
    unit = unit_ref[0]
    steps, slots, hidden = round_one.shape
    prenet_width = layer_two.shape[1]
    context_width = context_ref.shape[2]
    half = hidden // 2
    per_half = half // lanes
    position_count = hot_ref.shape[0]
    text_width = position_count // (slots // 4)
    copies_two = [
        pltpu.make_async_copy(own_two, held_two.at[0], sems.at[0]),
        pltpu.make_async_copy(peer_two, held_two.at[1], sems.at[1]),
    ]
    copies_one = [
        pltpu.make_async_copy(own_one, held_one.at[0], sems.at[2]),
        pltpu.make_async_copy(peer_one, held_one.at[1], sems.at[3]),
    ]
    for copy in copies_two + copies_one:
        copy.start()
    for ref in (state_one, cell_one, state_two, cell_two):
        ref[...] = jnp.zeros_like(ref)

    def gates_into(held, depth, bias_ref, out_ref, step):
        def one(block, _):
            side = block // 4
            inputs = input_ref[:, :depth]
            for pair in range(per_half // 2):
                tile = (block % 4) * per_half + 2 * pair
                outside = pl.ds(
                    pl.multiple_of(block * half + 2 * pair * lanes, 2 * lanes), 2 * lanes
                )
                kernel = jnp.concatenate(
                    [held[side, tile, :depth, :], held[side, tile + 1, :depth, :]], axis=1
                )
                out_ref[step, :, outside] = dot(inputs, kernel) + bias_ref[:, outside]
            return 0

        lax.fori_loop(0, 8, one, 0)

    def cell(gates_ref, zone_ref, prior_ref, state, cells, round_ref, step):
        def one(chunk, _):
            spot = pl.ds(pl.multiple_of(chunk * lanes, lanes), lanes)
            values = [
                gates_ref[step, :, pl.ds(gate_spot(chunk, gate, per_half), lanes)]
                for gate in range(4)
            ]
            zone = zone_ref[step, :, spot]
            before = cells[:, spot]
            prior_ref[step, :, spot] = before
            fresh = jax.nn.sigmoid(values[1]) * before + jax.nn.sigmoid(values[0]) * jnp.tanh(
                values[2]
            )
            output = jax.nn.sigmoid(values[3]) * jnp.tanh(fresh)
            now = zone * state[:, spot] + (1.0 - zone) * output
            state[:, spot] = now
            cells[:, spot] = zone * before + (1.0 - zone) * fresh
            round_ref[step, :, pl.ds(unit_spot(chunk, unit, per_half), lanes)] = now.astype(bf16).astype(
                f32
            )
            return 0

        lax.fori_loop(0, 2 * per_half, one, 0)

    def attention(step, location):
        inside = hot_ref[...] > 0.0
        hot = hot_ref[...].astype(bf16)
        query = pad_rows(dot(round_one[step].astype(bf16), query_ref[...].astype(bf16)))
        summed = dot_left(hot, query) + processed_ref[...]
        if location is not None:
            summed = summed + location
        mixed = jnp.tanh(summed)
        mixed_ref[step] = mixed
        energy = dot_right(mixed, vector_ref[...].astype(bf16))
        most = jnp.max(jnp.where(inside, energy, -1000000000.0), axis=0, keepdims=True)
        shifted = jnp.where(inside, jnp.exp(energy - most), 0.0)
        total = jnp.sum(shifted, axis=0, keepdims=True)
        alpha = shifted / jnp.where(total > 0.0, total, 1.0)
        alpha_ref[step] = alpha
        context = dot_right(alpha, memory_ref[...].astype(bf16), rows_first)[:slots]
        context_ref[step] = context.astype(bf16).astype(f32)

    def taps_of(step):
        spread = dot_right(
            alpha_ref[step], position_hot(position_count, text_width, True), rows_first
        )
        taps_ref[step] = slant(dot_left(hot_ref[...].astype(bf16), spread), text_width)

    def second_layer(step, depth):
        input_ref[:, :hidden] = round_one[step].astype(bf16)
        input_ref[:, hidden : hidden + context_width] = context_ref[step].astype(bf16)
        gates_into(held_two, depth, bias_two, gates_two, step)
        cell(gates_two, zone_two, prior_two, state_two, cell_two, round_two, step)

    slot_hot = slot_ref[...].astype(bf16)

    def prenet_layer(source, layer, drops, mixed_out, out):
        mixed = dot(source.astype(bf16), layer[...].astype(bf16))
        mixed_out[...] = mixed
        value = (mixed * jax.nn.sigmoid(mixed) * drops[...] * 2.0).astype(bf16)
        out[...] = value.astype(f32)
        return value

    hidden_value = prenet_layer(previous_ref[...], layer_one, drop_one, prenet_one, prenet_hidden)
    prenet_value = prenet_layer(hidden_value, layer_two, drop_two, prenet_two, prenet_out)
    prenet_slots = dot(slot_hot, prenet_value, rows_first)
    for step in range(steps):
        prenet_ref[step] = prenet_slots[step * slots : (step + 1) * slots]
    processed_ref[...] = dot(memory_ref[...].astype(bf16), project_ref[...].astype(bf16))
    for channel in range(2):
        filter_ref[channel] = dot(
            conv_ref[channel].astype(bf16), dense_ref[...].astype(bf16)
        )

    gates_one[0] = jnp.broadcast_to(bias_one[...], gates_one.shape[1:])
    cell(gates_one, zone_one, prior_one, state_one, cell_one, round_one, 0)
    attention(0, None)
    taps_of(0)
    for copy in copies_two:
        copy.wait()
    second_layer(0, hidden + context_width)
    for copy in copies_one:
        copy.wait()

    def later(step, _):
        input_ref[:, :prenet_width] = prenet_ref[step].astype(bf16)
        input_ref[:, prenet_width : prenet_width + context_width] = context_ref[step - 1].astype(
            bf16
        )
        input_ref[:, prenet_width + context_width : prenet_width + context_width + hidden] = (
            round_one[step - 1].astype(bf16)
        )
        gates_into(
            held_one, prenet_width + context_width + hidden, bias_one, gates_one, step
        )
        cell(gates_one, zone_one, prior_one, state_one, cell_one, round_one, step)
        previous = taps_ref[step - 1]
        summed = jnp.where(step == 2, taps_ref[0] + previous, previous)
        attention(step, dot_both(previous, filter_ref[0]) + dot_both(summed, filter_ref[1]))

        @pl.when(step < steps - 1)
        def _():
            taps_of(step)

        input_ref[:, hidden + context_width :] = round_two[step - 1].astype(bf16)
        second_layer(step, 2 * hidden + context_width)
        return 0

    lax.fori_loop(1, steps, later, 0)
    for step in range(steps):
        values = dot(round_two[step].astype(bf16), frame_ref[:hidden].astype(bf16)) + dot(
            context_ref[step].astype(bf16), frame_ref[hidden:].astype(bf16)
        )
        high = values.astype(bf16)
        rest = values - high.astype(f32)
        middle = rest.astype(bf16)
        low = (rest - middle.astype(f32)).astype(bf16)
        chosen = slot_hot[:, step * slots : (step + 1) * slots]
        picked = (dot(chosen, high) + dot(chosen, middle)) + dot(chosen, low)
        frame_out[...] = (frame_bias[...] if step == 0 else frame_out[...]) + picked


def backward_kernel(
    unit_ref,
    own_one,
    peer_one,
    own_two,
    peer_two,
    gates_one,
    gates_two,
    prior_one,
    prior_two,
    zone_one,
    zone_two,
    hot_ref,
    memory_ref,
    query_ref,
    vector_ref,
    conv_ref,
    dense_ref,
    mixed_ref,
    alpha_ref,
    taps_ref,
    frame_grad,
    frame_weight,
    slot_ref,
    sent_ref,
    prenet_grad,
    context_grad,
    query_grad,
    processed_grad,
    vector_grad,
    filter_grad,
    held_one,
    held_two,
    grads_one,
    grads_two,
    back_one,
    back_two,
    state_one,
    cell_one,
    state_two,
    cell_two,
    previous_grad,
    summed_grad,
    from_query,
    frame_ref,
    filter_ref,
    sems,
):
    unit = unit_ref[0]
    steps, slots, prenet_width = prenet_grad.shape
    context_width = context_grad.shape[2]
    hidden = state_one.shape[1]
    half = hidden // 2
    per_half = half // lanes
    position_count = hot_ref.shape[0]
    text_width = position_count // (slots // 4)
    copies_two = [
        pltpu.make_async_copy(own_two, held_two.at[0], sems.at[0]),
        pltpu.make_async_copy(peer_two, held_two.at[1], sems.at[1]),
    ]
    copies_one = [
        pltpu.make_async_copy(own_one, held_one.at[0], sems.at[2]),
        pltpu.make_async_copy(peer_one, held_one.at[1], sems.at[3]),
    ]
    for copy in copies_two + copies_one:
        copy.start()
    for ref in (
        state_one,
        cell_one,
        state_two,
        cell_two,
        back_one,
        back_two,
        previous_grad,
        summed_grad,
        processed_grad,
        vector_grad,
        filter_grad,
    ):
        ref[...] = jnp.zeros_like(ref)

    def cell(gates_ref, prior_ref, zone_ref, state, cells, grads_ref, step, incoming):
        def one(chunk, _):
            spot = pl.ds(pl.multiple_of(chunk * lanes, lanes), lanes)
            places = [pl.ds(gate_spot(chunk, gate, per_half), lanes) for gate in range(4)]
            values = [gates_ref[step, :, place] for place in places]
            zone = zone_ref[step, :, spot]
            keep = 1.0 - zone
            before = prior_ref[step, :, spot]
            gate_in = jax.nn.sigmoid(values[0])
            gate_forget = jax.nn.sigmoid(values[1])
            candidate = jnp.tanh(values[2])
            gate_out = jax.nn.sigmoid(values[3])
            bent = jnp.tanh(gate_forget * before + gate_in * candidate)
            grad_state = incoming(unit_spot(chunk, unit, per_half)) + state[:, spot]
            grad_cell = cells[:, spot]
            grad_new = keep * grad_state
            grad_fresh = grad_new * gate_out * (1.0 - bent * bent) + keep * grad_cell
            state[:, spot] = zone * grad_state
            cells[:, spot] = zone * grad_cell + gate_forget * grad_fresh
            results = (
                grad_fresh * candidate * gate_in * (1.0 - gate_in),
                grad_fresh * before * gate_forget * (1.0 - gate_forget),
                grad_fresh * gate_in * (1.0 - candidate * candidate),
                grad_new * bent * gate_out * (1.0 - gate_out),
            )
            for place, result in zip(places, results):
                grads_ref[step, :, place] = result.astype(bf16)
            return 0

        lax.fori_loop(0, 2 * per_half, one, 0)

    def inputs_back(grads_ref, held, out_ref, step, blocks):
        def one(block, _):
            spot = pl.ds(pl.multiple_of(block * 256, 256), 256)
            total = None
            for tile in range(0, 8 * per_half, 2):
                side, inside = tile // (4 * per_half), tile % (4 * per_half)
                kernel = jnp.concatenate(
                    [held[side, inside, spot, :], held[side, inside + 1, spot, :]], axis=1
                )
                grads = grads_ref[step, :, tile * lanes : (tile + 2) * lanes]
                product = dot(grads, kernel, lanes_both)
                total = product if total is None else total + product
            out_ref[:, spot] = total
            return 0

        lax.fori_loop(0, blocks, one, 0)

    def attention(step, located):
        inside = hot_ref[...] > 0.0
        hot = hot_ref[...].astype(bf16)
        alpha = alpha_ref[step]
        mixed = mixed_ref[step]
        context_now = pad_rows(context_grad[step])
        weights_grad = jnp.where(
            inside,
            dot_left(memory_ref[...].astype(bf16), context_now, lanes_both)
            + previous_grad[...]
            + summed_grad[...],
            0.0,
        )
        product = alpha * weights_grad
        energy_grad = product - alpha * jnp.sum(product, axis=0, keepdims=True)
        spread = jnp.sum(energy_grad, axis=1, keepdims=True)
        vector_grad[...] += jnp.sum(spread * mixed, axis=0, keepdims=True)
        mixed_grad = spread * vector_ref[...] * (1.0 - mixed * mixed)
        processed_grad[...] += mixed_grad
        high, low = split(mixed_grad)
        query_now = (dot(hot, high, rows_first) + dot(hot, low, rows_first))[:slots]
        query_grad[step] = query_now
        from_query[...] = dot_right(query_now, query_ref[...].astype(bf16), lanes_both)
        if located:
            previous = taps_ref[step - 1]
            summed = jnp.where(step == 2, taps_ref[0] + previous, previous)
            filter_grad[0] += dot_both(previous, mixed_grad, rows_first)
            filter_grad[1] += dot_both(summed, mixed_grad, rows_first)
            place_hot = position_hot(position_count, text_width, False)

            def taps_back(channel):
                taps_grad = slant(
                    dot_both(mixed_grad, filter_ref[channel], lanes_both), text_width
                )
                gathered = dot_right(taps_grad, hot, rows_first)
                return jnp.where(inside, dot_left(place_hot, gathered), 0.0)

            previous_grad[...] = taps_back(0)
            summed_grad[...] += taps_back(1)

    def arrived(step, copies):
        @pl.when(step == steps - 1)
        def _():
            for copy in copies:
                copy.wait()

    def step_back(step, located):
        cell(
            gates_two,
            prior_two,
            zone_two,
            state_two,
            cell_two,
            grads_two,
            step,
            lambda spot: frame_ref[step, :, pl.ds(spot, lanes)]
            + back_two[:, pl.ds(spot + hidden + context_width, lanes)],
        )
        blocks_two = (hidden + context_width + (hidden if located else 0)) // 256
        if located:
            arrived(step, copies_two)
        inputs_back(grads_two, held_two, back_two, step, blocks_two)
        context_grad[step] = (
            back_two[:, hidden : hidden + context_width]
            + frame_ref[step, :, hidden:]
            + back_one[:, prenet_width : prenet_width + context_width]
        )
        attention(step, located)
        cell(
            gates_one,
            prior_one,
            zone_one,
            state_one,
            cell_one,
            grads_one,
            step,
            lambda spot: back_two[:, pl.ds(spot, lanes)]
            + from_query[:, pl.ds(spot, lanes)]
            + back_one[:, pl.ds(spot + prenet_width + context_width, lanes)],
        )
        blocks_one = (prenet_width + (hidden + context_width if located else 0)) // 256
        if located:
            arrived(step, copies_one)
        inputs_back(grads_one, held_one, back_one, step, blocks_one)
        prenet_grad[step] = back_one[:, :prenet_width]

    for channel in range(2):
        filter_ref[channel] = dot(
            conv_ref[channel].astype(bf16), dense_ref[...].astype(bf16)
        )
    for step in range(steps):
        frame_ref[step] = dot(
            frame_grad[step].astype(bf16), frame_weight[...].astype(bf16), lanes_both
        )

    def later(index, _):
        step_back(steps - 1 - index, True)
        return 0

    lax.fori_loop(0, steps - 1, later, 0)
    step_back(0, False)
    slot_hot = slot_ref[...].astype(bf16)

    def tile_out(tile, _):
        for layer, grads_ref in ((0, grads_one), (1, grads_two)):
            for side in range(2):
                place = ((side + unit) % 2) * 4 * half + tile * lanes
                grads = grads_ref[:, :, pl.ds(pl.multiple_of(place, lanes), lanes)]
                chosen = dot(slot_hot, grads.reshape(steps * slots, lanes)).astype(bf16)
                spot = (2 * layer + side) * lanes
                sent_ref[tile, :, spot : spot + lanes] = chosen
        return 0

    lax.fori_loop(0, 4 * per_half, tile_out, 0)


def call_forward(unit, weights, small, sizes):
    own_one, peer_one, own_two, peer_two = weights
    steps, slots, hidden, context_width, positions, frame_rows, prenet_width = sizes

    def shape(*dims):
        return jax.ShapeDtypeStruct(dims, f32)

    outs = [
        shape(steps, slots, 4 * hidden),
        shape(steps, slots, 4 * hidden),
        shape(steps, slots, hidden),
        shape(steps, slots, hidden),
        shape(steps, slots, hidden),
        shape(steps, slots, hidden),
        shape(steps, slots, context_width),
        shape(steps, positions, lanes),
        shape(steps, positions, lanes),
        shape(steps - 1, positions, lanes),
        shape(frame_rows, prenet_width),
        shape(frame_rows, prenet_width),
        shape(frame_rows, prenet_width),
        shape(frame_rows, prenet_width),
        shape(frame_rows, lanes),
    ]
    vmem = pl.BlockSpec(memory_space=pltpu.VMEM)
    return pl.pallas_call(
        forward_kernel,
        out_shape=outs,
        in_specs=[pl.BlockSpec(memory_space=pltpu.SMEM)]
        + [pl.BlockSpec(memory_space=pl.ANY)] * 4
        + [vmem] * len(small),
        out_specs=[vmem] * len(outs),
        scratch_shapes=[
            pltpu.VMEM((2,) + own_one.shape, bf16),
            pltpu.VMEM((2,) + own_two.shape, bf16),
            pltpu.VMEM((slots, own_two.shape[1]), bf16),
            pltpu.VMEM((steps, slots, prenet_width), f32),
            pltpu.VMEM((positions, lanes), f32),
            pltpu.VMEM((2, lanes, lanes), f32),
            pltpu.VMEM((slots, hidden), f32),
            pltpu.VMEM((slots, hidden), f32),
            pltpu.VMEM((slots, hidden), f32),
            pltpu.VMEM((slots, hidden), f32),
            pltpu.SemaphoreType.DMA((4,)),
        ],
        compiler_params=pltpu.CompilerParams(vmem_limit_bytes=kernel_vmem),
        name="decoder_forward",
    )(unit, *weights, *small)


def call_backward(unit, weights, small):
    own_one, peer_one, own_two, peer_two = weights
    gates_one = small[0]
    steps, slots, gate_width = gates_one.shape
    hidden = gate_width // 4
    positions, context_width = small[7].shape
    prenet_width = own_one.shape[1] - hidden - context_width

    def shape(dims, kind):
        return jax.ShapeDtypeStruct(dims, kind)

    outs = [
        shape((gate_width // (2 * lanes), small[-1].shape[0], 4 * lanes), bf16),
        shape((steps, slots, prenet_width), f32),
        shape((steps, slots, context_width), f32),
        shape((steps, slots, lanes), f32),
        shape((positions, lanes), f32),
        shape((1, lanes), f32),
        shape((2, lanes, lanes), f32),
    ]
    vmem = pl.BlockSpec(memory_space=pltpu.VMEM)
    return pl.pallas_call(
        backward_kernel,
        out_shape=outs,
        in_specs=[pl.BlockSpec(memory_space=pltpu.SMEM)]
        + [pl.BlockSpec(memory_space=pl.ANY)] * 4
        + [vmem] * len(small),
        out_specs=[vmem] * len(outs),
        scratch_shapes=[
            pltpu.VMEM((2,) + own_one.shape, bf16),
            pltpu.VMEM((2,) + own_two.shape, bf16),
            pltpu.VMEM((steps, slots, gate_width), bf16),
            pltpu.VMEM((steps, slots, gate_width), bf16),
            pltpu.VMEM((slots, own_one.shape[1]), f32),
            pltpu.VMEM((slots, own_two.shape[1]), f32),
            pltpu.VMEM((slots, hidden), f32),
            pltpu.VMEM((slots, hidden), f32),
            pltpu.VMEM((slots, hidden), f32),
            pltpu.VMEM((slots, hidden), f32),
            pltpu.VMEM((positions, lanes), f32),
            pltpu.VMEM((positions, lanes), f32),
            pltpu.VMEM((slots, hidden), f32),
            pltpu.VMEM((steps, slots, hidden + context_width), f32),
            pltpu.VMEM((2, lanes, lanes), f32),
            pltpu.SemaphoreType.DMA((4,)),
        ],
        compiler_params=pltpu.CompilerParams(vmem_limit_bytes=kernel_vmem),
        name="decoder_backward",
    )(unit, *weights, *small)


def postnet_kernel(
    mel_width,
    loss_scale,
    unit_ref,
    mel_ref,
    target_ref,
    mask_ref,
    first_ref,
    own_ref,
    peer_ref,
    last_ref,
    gain_ref,
    shift_ref,
    inputs_first,
    inputs_later,
    grads_early,
    grads_last,
    norm_grads,
    mel_grad,
    padded,
    padded_mel,
    held,
    normed_early,
    normed_last,
    inverse_ref,
    post_grad,
):
    unit = unit_ref[0]
    count, channels = held.shape
    side = channels // 2
    frames = padded.shape[0] - count
    rows_each = frames // 4
    chunk = 2 * rows_each
    tall = float(count)
    body_rows = slice(2 * rows_each, 2 * rows_each + count)

    for ref in (padded, padded_mel):
        ref[: 2 * rows_each] = jnp.zeros((2 * rows_each, ref.shape[1]), bf16)
        ref[2 * rows_each + count :] = jnp.zeros((2 * rows_each, ref.shape[1]), bf16)

    def piece(source, start, tap, width, lane=None):
        spot = pl.ds(pl.multiple_of(start + tap * rows_each, rows_each), chunk)
        mask = mask_ref[tap, pl.ds(pl.multiple_of(start, rows_each), chunk), :]
        if width < lanes:
            mask = mask[:, :width]
        else:
            mask = jnp.concatenate([mask] * (width // lanes), axis=1)
        value = source[spot, :] if lane is None else source[spot, pl.ds(lane, width)]
        return value * mask

    def chunks(work):
        def one(index, _):
            work(pl.multiple_of(index * chunk, chunk))
            return 0

        lax.fori_loop(0, count // chunk, one, 0)

    def half_spot(which):
        return pl.multiple_of(((which + unit) % 2) * side, side)

    def norm_forward(value, layer, lane, width):
        mean = jnp.sum(value, axis=0, keepdims=True) / tall
        centered = value - mean
        inverse = lax.rsqrt(jnp.sum(centered * centered, axis=0, keepdims=True) / tall + norm_eps)
        inverse_ref[layer, :, pl.ds(lane, width)] = inverse
        return centered * inverse

    def each_lane_block(work):
        def one(index, _):
            work(pl.multiple_of(index * lanes, lanes))
            return 0

        lax.fori_loop(0, channels // lanes, one, 0)

    def activate(layer):
        def block(lane):
            spot = pl.ds(lane, lanes)
            normed = norm_forward(held[:, spot], layer, lane, lanes)
            normed_early[layer, :, spot] = normed
            active = jnp.tanh(
                normed * gain_ref[layer, :, spot] + shift_ref[layer, :, spot]
            ).astype(bf16)
            inputs_later[layer, :, spot] = active
            padded[body_rows, spot] = active

        each_lane_block(block)

    source = mel_ref[...].astype(bf16)
    inputs_first[...] = source
    padded_mel[body_rows] = source

    def first_chunk(start):
        total = None
        for tap in range(5):
            product = dot(piece(padded_mel, start, tap, mel_width), first_ref[tap])
            total = product if total is None else total + product
        held[pl.ds(start, chunk), :] = total

    chunks(first_chunk)
    activate(0)

    def middle(index, _):
        for which, ref in ((0, own_ref), (1, peer_ref)):

            def middle_chunk(start, which=which, ref=ref):
                total = None
                for tap in range(5):
                    product = dot(piece(padded, start, tap, channels), ref[index * 5 + tap])
                    total = product if total is None else total + product
                held[pl.ds(start, chunk), pl.ds(half_spot(which), side)] = total

            chunks(middle_chunk)
        activate(index + 1)
        return 0

    lax.fori_loop(0, 3, middle, 0)

    def last_chunk(start):
        total = None
        for tap in range(5):
            product = dot(piece(padded, start, tap, channels), last_ref[tap])
            total = product if total is None else total + product
        normed_last[pl.ds(start, chunk), :] = total

    chunks(last_chunk)
    normed = norm_forward(normed_last[...], 4, 0, mel_width)
    normed_last[...] = normed

    def norm_back(grad, normed, layer, lane, width):
        spot = pl.ds(lane, width)
        shift_grad = jnp.sum(grad, axis=0, keepdims=True)
        gain_grad = jnp.sum(grad * normed, axis=0, keepdims=True)
        norm_grads[0, layer, :, spot] = gain_grad
        norm_grads[1, layer, :, spot] = shift_grad
        return (
            gain_ref[layer, :, spot]
            * inverse_ref[layer, :, spot]
            * (grad - shift_grad / tall - normed * (gain_grad / tall))
        ).astype(bf16)

    output = normed * gain_ref[4, :, :mel_width] + shift_ref[4, :, :mel_width]
    grad = loss_scale * (mel_ref[...] + output - target_ref[...])
    post_grad[...] = grad
    grad_norm = norm_back(grad, normed, 4, 0, mel_width)
    grads_last[...] = grad_norm
    padded_mel[body_rows] = grad_norm

    def last_back(start):
        total = None
        for tap in range(5):
            product = dot(
                piece(padded_mel, start, tap, mel_width), last_ref[4 - tap], lanes_both
            )
            total = product if total is None else total + product
        held[pl.ds(start, chunk), :] = total

    chunks(last_back)

    def deactivate(layer):
        def block(lane):
            spot = pl.ds(lane, lanes)
            normed = normed_early[layer, :, spot]
            active = jnp.tanh(normed * gain_ref[layer, :, spot] + shift_ref[layer, :, spot])
            grad = held[:, spot] * (1.0 - active * active)
            grad_norm = norm_back(grad, normed, layer, lane, lanes)
            grads_early[layer, :, spot] = grad_norm
            padded[body_rows, spot] = grad_norm

        each_lane_block(block)

    def middle_back(back, _):
        index = 2 - back
        deactivate(index + 1)

        def chunk_back(start):
            total = None
            for which, ref in ((0, own_ref), (1, peer_ref)):
                for tap in range(5):
                    product = dot(
                        piece(padded, start, tap, side, half_spot(which)),
                        ref[index * 5 + 4 - tap],
                        lanes_both,
                    )
                    total = product if total is None else total + product
            held[pl.ds(start, chunk), :] = total

        chunks(chunk_back)
        return 0

    lax.fori_loop(0, 3, middle_back, 0)
    deactivate(0)

    def first_back(start):
        total = None
        for tap in range(5):
            product = dot(piece(padded, start, tap, channels), first_ref[4 - tap], lanes_both)
            total = product if total is None else total + product
        spot = pl.ds(start, chunk)
        mel_grad[spot, :] = (
            loss_scale * (mel_ref[spot, :] - target_ref[spot, :]) + post_grad[spot, :] + total
        )

    chunks(first_back)


def call_postnet(unit, small, loss_scale, rows_all):
    mel = small[0]
    count, mel_width = mel.shape
    channels = small[3].shape[2]

    def shape(kind, *dims):
        return jax.ShapeDtypeStruct(dims, kind)

    outs = [
        shape(bf16, count, mel_width),
        shape(bf16, 4, count, channels),
        shape(bf16, 4, count, channels),
        shape(bf16, count, mel_width),
        shape(f32, 2, 5, 1, channels),
        shape(f32, count, mel_width),
    ]
    vmem = pl.BlockSpec(memory_space=pltpu.VMEM)
    tall = count + 4 * rows_all
    return pl.pallas_call(
        functools.partial(postnet_kernel, mel_width, loss_scale),
        out_shape=outs,
        in_specs=[pl.BlockSpec(memory_space=pltpu.SMEM)] + [vmem] * len(small),
        out_specs=[vmem] * len(outs),
        scratch_shapes=[
            pltpu.VMEM((tall, channels), bf16),
            pltpu.VMEM((tall, mel_width), bf16),
            pltpu.VMEM((count, channels), f32),
            pltpu.VMEM((4, count, channels), f32),
            pltpu.VMEM((count, mel_width), f32),
            pltpu.VMEM((5, 1, channels), f32),
            pltpu.VMEM((count, mel_width), f32),
        ],
        compiler_params=pltpu.CompilerParams(vmem_limit_bytes=kernel_vmem),
        name="postnet",
    )(unit, *small)


def shifted_frames(source, same):
    steps = source.shape[0]
    padded = jnp.pad(source, ((2, 2), (0, 0), (0, 0)))
    return [
        padded[offset : offset + steps] * same[:, :, offset, None].astype(source.dtype)
        for offset in range(5)
    ]


def by_rows(work, roomy, arrays, summed=False):
    if roomy:
        return work(*arrays)
    parts = arrays[0].shape[1] // 192

    def cut(value):
        value = value.reshape((value.shape[0], parts, -1) + value.shape[2:])
        return jnp.moveaxis(value, 1, 0)

    pieces = tuple(cut(value) for value in arrays)
    if summed:
        first = jax.eval_shape(work, *[value[0] for value in pieces])
        start = jnp.zeros(first.shape, first.dtype)
        return lax.scan(lambda total, now: (total + work(*now), None), start, pieces)[0]
    result = jnp.moveaxis(lax.map(lambda now: work(*now), pieces), 0, 1)
    return result.reshape((result.shape[0], -1) + result.shape[3:])


def post_layer(source, kernel, same):
    wide = jnp.concatenate(shifted_frames(source, same), axis=2)
    return jnp.einsum(
        "src,co->sro", wide, kernel.reshape(-1, kernel.shape[2]), preferred_element_type=f32
    )


def post_layer_back(grad, kernel, same):
    wide = jnp.concatenate(shifted_frames(grad, same), axis=2)
    turned = jnp.transpose(kernel[::-1], (0, 2, 1)).reshape(-1, kernel.shape[1])
    return jnp.einsum("sro,oc->src", wide, turned, preferred_element_type=f32)


def post_kernel_grad(source, grad, same):
    wide = jnp.concatenate(shifted_frames(source, same), axis=2)
    return jnp.einsum("src,sro->co", wide, grad, preferred_element_type=f32)


def on_device(
    memory,
    targets,
    segments,
    text_lengths,
    zone_first,
    zone_second,
    drop_first,
    drop_second,
    prenet_first,
    prenet_second,
    query_weight,
    memory_weight,
    location_conv,
    location_dense,
    energy_vector,
    lstm_first,
    bias_first,
    lstm_second,
    bias_second,
    frame_weight,
    frame_bias,
    post_first,
    post_middle,
    post_last,
    middle_norm,
    last_norm,
):
    micro_count, rows, text_width, memory_width = memory.shape
    frames = segments.shape[2]
    utterances = text_lengths.shape[2]
    mel_width = targets.shape[3]
    hidden = query_weight.shape[0]
    prenet_width = prenet_first.shape[1]
    attention_width = query_weight.shape[1]
    half = lstm_first.shape[2]
    depth_one, depth_two = lstm_first.shape[0], lstm_second.shape[0]
    unit = lax.axis_index("unit")
    place = lax.axis_index("batch")
    batch_size = lax.axis_size("batch")
    total_rows = rows * batch_size
    frame_count = float(total_rows * frames)
    first_unit = unit == 0
    longest = 3
    slots = 4 * rows

    def exchange(value):
        return lax.ppermute(value, "unit", [(0, 1), (1, 0)])

    def ordered(own, peer):
        return jnp.where(first_unit, own, peer), jnp.where(first_unit, peer, own)

    def whole(value, axis):
        return jnp.concatenate(ordered(value, exchange(value)), axis=axis)

    def mine(value):
        return lax.dynamic_index_in_dim(value, unit, 0, keepdims=False)

    def others(value):
        return lax.dynamic_index_in_dim(value, 1 - unit, 0, keepdims=False)

    def swapped(value, bit):
        pairs = [(index, index ^ bit) for index in range(batch_size)]
        other = lax.ppermute(value, "batch", pairs)
        upper = (place & bit) != 0
        return jnp.where(upper, other, value), jnp.where(upper, value, other)

    def gather_rows(value):
        bit = 1
        while bit < batch_size:
            value = jnp.concatenate(swapped(value, bit), axis=0)
            bit *= 2
        return value

    def gather_tiles(value):
        tiles = jnp.transpose(value.reshape(value.shape[0], -1, lanes), (1, 0, 2))
        return lax.all_gather(tiles, "batch", axis=1, tiled=True)

    own_two = gather_tiles(lstm_second)
    own_one = gather_tiles(lstm_first)
    peer_two = exchange(own_two)
    channel_rows = post_middle.shape[2]
    middle_width = post_middle.shape[3]
    middle_half = lax.all_gather(
        post_middle.reshape(-1, channel_rows, middle_width), "batch", axis=1, tiled=True
    )
    last_half = gather_rows(jnp.transpose(post_last, (1, 0, 2)).reshape(channel_rows, -1))
    last_half = jnp.transpose(
        last_half.reshape(-1, post_last.shape[0], post_last.shape[2]), (1, 0, 2)
    )
    memory_now = mine(memory).reshape(rows * text_width, memory_width)
    segments_now = mine(segments)
    targets_now = mine(targets)
    frame_info = gather_rows(
        jnp.concatenate([targets_now, segments_now[:, :, None].astype(bf16)], axis=2).astype(f32)
    )

    same_frames = segments_now[:, :, None] == segments_now[:, None, :]
    earlier = jnp.tril(jnp.ones((frames, frames), jnp.bool_), -1)
    order = jnp.sum((same_frames & earlier[None]).astype(jnp.int32), axis=2)
    slot_of = order * slots + segments_now * rows + jnp.arange(rows, dtype=jnp.int32)[:, None]
    frame_rows = rows * frames
    padding = -frame_rows % 16
    slot_hot = (
        jnp.pad(slot_of.reshape(-1, 1), ((0, padding), (0, 0)), constant_values=-1)
        == jnp.arange(longest * slots, dtype=jnp.int32)[None, :]
    ).astype(bf16)
    slot_hot_frames = slot_hot[:frame_rows]
    carry_on = jnp.pad(
        (segments_now[:, 1:] == segments_now[:, :-1]).astype(f32), ((0, 0), (1, 0))
    )
    finished = jnp.pad(
        (segments_now[:, 1:] != segments_now[:, :-1]).astype(f32),
        ((0, 0), (0, 1)),
        constant_values=1.0,
    )

    def to_slots(value, kind=bf16):
        return lax.dot_general(
            slot_hot_frames,
            value.astype(bf16),
            (((0,), (0,)), ((), ())),
            preferred_element_type=f32,
        ).astype(kind)

    def to_frames(value):
        return jnp.dot(slot_hot, value.astype(bf16), preferred_element_type=f32).astype(bf16)

    def pad_frames(value):
        return jnp.pad(
            value.astype(f32).reshape(frame_rows, -1), ((0, padding), (0, 0))
        )

    previous = pad_frames(
        jnp.pad(targets_now[:, :-1], ((0, 0), (1, 0), (0, 0))).astype(f32)
        * carry_on[:, :, None]
    )
    drops_one = pad_frames(mine(drop_first))
    drops_two = pad_frames(mine(drop_second))

    zones_own = jnp.concatenate([mine(zone_first), mine(zone_second)], axis=2).astype(f32)
    zones_peer = exchange(
        jnp.concatenate([others(zone_first), others(zone_second)], axis=2).astype(f32)
    )
    zones_slots = to_slots(
        jnp.concatenate([zones_own, zones_peer], axis=2).reshape(rows * frames, -1), f32
    ).reshape(longest, slots, 4 * half)
    zone_one = jnp.concatenate(
        [zones_slots[:, :, :half], zones_slots[:, :, 2 * half : 3 * half]], axis=2
    )
    zone_two = jnp.concatenate(
        [zones_slots[:, :, half : 2 * half], zones_slots[:, :, 3 * half :]], axis=2
    )
    biases = jnp.stack([bias_first.reshape(-1), bias_second.reshape(-1)])
    biases = jnp.concatenate([biases, exchange(biases)], axis=1)
    text_ends = jnp.cumsum(mine(text_lengths), axis=1)
    owner = jnp.sum(
        (jnp.arange(text_width, dtype=jnp.int32)[None, :, None] >= text_ends[:, None, :]).astype(
            jnp.int32
        ),
        axis=2,
    )
    owner_slot = owner * rows + jnp.arange(rows, dtype=jnp.int32)[:, None]
    owner_hot = (
        owner_slot.reshape(-1, 1) == jnp.arange(lanes, dtype=jnp.int32)[None, :]
    ).astype(f32)
    conv_float = location_conv.astype(f32)
    dense_float = location_dense.astype(f32)
    reach = location_conv.shape[2] // 2
    taps_first = jnp.transpose(conv_float, (1, 2, 0))
    taps_first = jnp.pad(
        taps_first,
        ((0, 0), (0, lanes - taps_first.shape[1]), (0, lanes - taps_first.shape[2])),
    )
    dense_wide = jnp.pad(dense_float, ((0, lanes - dense_float.shape[0]), (0, 0)))
    taps_forward = jnp.roll(taps_first[:, ::-1], reach, axis=1)
    taps_back = jnp.roll(taps_first, 1 - reach, axis=1)
    frame_wide = jnp.pad(
        frame_weight.astype(f32), ((0, 0), (0, lanes - frame_weight.shape[1]))
    )
    frame_bias_wide = jnp.pad(frame_bias, (0, lanes - frame_bias.shape[0]))[None, :]
    vector_float = energy_vector.astype(f32)
    vector_wide = jnp.broadcast_to(vector_float[:, None], (attention_width, lanes))
    memory_float = memory_now.astype(f32)
    query_float = query_weight.astype(f32)
    unit_array = unit.astype(jnp.int32).reshape(1)

    targets_all = jnp.transpose(frame_info[:, :, :mel_width].astype(f32), (1, 0, 2))
    segments_all = jnp.transpose(frame_info[:, :, mel_width].astype(jnp.int32))
    padded = jnp.pad(segments_all, ((2, 2), (0, 0)), constant_values=-1)
    same = jnp.stack([padded[offset : offset + frames] == segments_all for offset in range(5)])
    same = jnp.moveaxis(same, 0, 2)
    first_full = whole(post_first, 2)
    last_full = whole(last_half, 2)
    middle_gain = whole(middle_norm, 2)
    last_gain = whole(last_norm, 1)
    loss_scale = 2.0 / (mel_width * total_rows)
    count = total_rows * frames
    channels = middle_norm.shape[2] * 2
    masks = jnp.broadcast_to(
        jnp.transpose(same, (2, 0, 1)).reshape(5, count, 1).astype(bf16), (5, count, lanes)
    )
    wide_gain = jnp.pad(last_gain, ((0, 0), (0, channels - mel_width)))
    norms = jnp.concatenate([middle_gain, wide_gain[:, None, :]], axis=1)[:, :, None, :]
    forward_small = (
        previous,
        drops_one,
        drops_two,
        prenet_first.astype(f32),
        prenet_second.astype(f32),
        slot_hot.astype(f32),
        zone_one,
        zone_two,
        biases[0:1],
        biases[1:2],
        owner_hot,
        memory_float,
        memory_weight.astype(f32),
        query_float,
        vector_wide,
        taps_forward,
        dense_wide,
        frame_wide,
        frame_bias_wide,
    )
    (
        own_one,
        own_two,
        forward_small,
        taps_back,
        vector_row,
        targets_all,
        masks,
        first_full,
        last_full,
        norms,
    ) = lax.optimization_barrier(
        (
            own_one,
            own_two,
            forward_small,
            taps_back,
            vector_float[None, :],
            targets_all,
            masks,
            first_full,
            last_full,
            norms,
        )
    )
    weights = (own_one, exchange(own_one), own_two, peer_two)
    slot_wide, zone_one, zone_two = forward_small[5], forward_small[6], forward_small[7]
    memory_float, query_float = forward_small[11], forward_small[13]
    dense_wide, frame_wide = forward_small[16], forward_small[17]

    (
        gates_one,
        gates_two,
        prior_one,
        prior_two,
        round_one,
        round_two,
        contexts,
        mixed_all,
        alphas,
        taps,
        mixed_one,
        mixed_two,
        hidden_round,
        prenet_round,
        frame_out,
    ) = call_forward(
        unit_array,
        weights,
        forward_small,
        (
            longest,
            slots,
            hidden,
            memory_width,
            rows * text_width,
            frame_rows + padding,
            prenet_width,
        ),
    )

    middle_half = lax.optimization_barrier((middle_half, frame_out))[0]
    middle_peer = exchange(middle_half)
    states = to_frames(
        jnp.concatenate([round_one, contexts, round_two], axis=2).reshape(longest * slots, -1)
    )
    frame_in = jnp.concatenate(
        [states[:, hidden + memory_width :], states[:, hidden : hidden + memory_width]], axis=1
    )
    frame_in = frame_in[:frame_rows]
    frame_out = frame_out[:frame_rows]
    mel_own = frame_out[:, :mel_width].reshape(rows, frames, mel_width)
    stop_logit = frame_out[:, mel_width].reshape(rows, frames)
    mel_all = jnp.transpose(
        gather_rows(mel_own), (1, 0, 2)
    )
    inputs_own = jnp.concatenate([prenet_round.astype(bf16), states], axis=1)
    roomy = total_rows * frames <= 2048
    if roomy:
        inputs_own, mel_all = lax.optimization_barrier((inputs_own, mel_all))
        inputs_all = lax.all_gather(inputs_own, "batch", axis=0, tiled=True)

    if roomy:
        (
            inputs_first,
            inputs_later,
            grads_early,
            grads_last,
            norm_grads,
            grad_mel,
        ) = call_postnet(
            unit_array,
            (
                mel_all.reshape(count, mel_width),
                targets_all.reshape(count, mel_width),
                masks,
                first_full,
                middle_half,
                middle_peer,
                last_full,
                norms[0],
                norms[1],
            ),
            loss_scale,
            total_rows,
        )
        gain_grads = [norm_grads[0, layer, 0] for layer in range(5)]
        shift_grads = [norm_grads[1, layer, 0] for layer in range(5)]
        gain_grads[4], shift_grads[4] = gain_grads[4][:mel_width], shift_grads[4][:mel_width]
        grad_mel = jnp.transpose(
            lax.dynamic_slice_in_dim(
                grad_mel.reshape(frames, total_rows, mel_width), place * rows, rows, 1
            ),
            (1, 0, 2),
        )
    else:
        middle_full = whole(middle_half, 2).reshape(post_middle.shape[:2] + (channels, channels))
        kernels = [first_full, middle_full[0], middle_full[1], middle_full[2], last_full]
        gains = [middle_gain[0, layer] for layer in range(4)] + [last_gain[0]]
        shifts = [middle_gain[1, layer] for layer in range(4)] + [last_gain[1]]
        layer_in = mel_all.astype(bf16)
        layer_inputs, normed_all, inverses = [], [], []
        output = None
        for layer in range(5):
            layer_inputs.append(layer_in)
            pre_norm = by_rows(
                lambda source, same_now: post_layer(source, kernels[layer], same_now),
                roomy,
                (layer_in, same),
            )
            mean_now = jnp.sum(pre_norm, axis=(0, 1)) / frame_count
            centered = pre_norm - mean_now
            inverse = lax.rsqrt(jnp.sum(centered * centered, axis=(0, 1)) / frame_count + norm_eps)
            normed = centered * inverse
            output = normed * gains[layer] + shifts[layer]
            normed_all.append(normed)
            inverses.append(inverse)
            if layer < 4:
                layer_in = jnp.tanh(output).astype(bf16)
                if not roomy:
                    layer_in, normed_all[layer] = lax.optimization_barrier(
                        (layer_in, normed_all[layer])
                    )

        grad_post = loss_scale * (mel_all + output - targets_all)
        kernel_grads, gain_grads, shift_grads = [None] * 5, [None] * 5, [None] * 5
        grad_output = grad_post
        grad_input = None
        for layer in (4, 3, 2, 1, 0):
            if layer < 4:
                normed_all[layer] = lax.optimization_barrier(normed_all[layer])
                active = jnp.tanh(normed_all[layer] * gains[layer] + shifts[layer])
                grad_output = grad_input * (1.0 - active * active)
            shift_grads[layer] = jnp.sum(grad_output, axis=(0, 1))
            gain_grads[layer] = jnp.sum(grad_output * normed_all[layer], axis=(0, 1))
            grad_norm = (
                gains[layer]
                * inverses[layer]
                * (
                    grad_output
                    - shift_grads[layer] / frame_count
                    - normed_all[layer] * (gain_grads[layer] / frame_count)
                )
            ).astype(bf16)
            grad_input = by_rows(
                lambda grad, same_now: post_layer_back(grad, kernels[layer], same_now),
                roomy,
                (grad_norm, same),
            )
            source = layer_inputs[layer]
            if layer > 0:
                source = lax.dynamic_slice_in_dim(source, place * channel_rows, channel_rows, 2)
            kernel_grads[layer] = by_rows(post_kernel_grad, roomy, (source, grad_norm, same), True)
            kernel_grads[layer] = kernel_grads[layer].reshape(5, source.shape[2], -1)
            if not roomy:
                grad_input, kernel_grads[layer] = lax.optimization_barrier(
                    (grad_input, kernel_grads[layer])
                )
        grad_mel = loss_scale * (mel_all - targets_all) + grad_post + grad_input
        grad_mel = jnp.transpose(
            lax.dynamic_slice_in_dim(grad_mel, place * rows, rows, 1), (1, 0, 2)
        )

    if not roomy:
        inputs_own, grad_mel = lax.optimization_barrier((inputs_own, grad_mel))
        inputs_all = lax.all_gather(inputs_own, "batch", axis=0, tiled=True)

    def add_units(value, axis):
        width = value.shape[axis] // 2
        halves = [
            lax.slice_in_dim(value, start, start + width, axis=axis) for start in (0, width)
        ]
        keep = jnp.where(first_unit, halves[0], halves[1])
        give = jnp.where(first_unit, halves[1], halves[0])
        return keep + exchange(give)

    grad_stop = (jax.nn.sigmoid(stop_logit) - finished) / total_rows
    grad_frame = (
        jnp.concatenate([grad_mel, grad_stop[:, :, None]], axis=2)
        .reshape(rows * frames, mel_width + 1)
        .astype(bf16)
    )
    frame_weight_grad = lax.dot_general(
        frame_in, grad_frame, (((0,), (0,)), ((), ())), preferred_element_type=f32
    )
    frame_bias_grad = jnp.sum(grad_frame.astype(f32), axis=0)
    grad_frame_slots = to_slots(
        jnp.pad(grad_frame, ((0, 0), (0, lanes - mel_width - 1))), f32
    ).reshape(longest, slots, lanes)

    (
        sent,
        prenet_back,
        context_grads,
        query_back,
        processed_back,
        vector_back,
        filter_back,
    ) = call_backward(
        unit_array,
        weights,
        (
            gates_one,
            gates_two,
            prior_one,
            prior_two,
            zone_one,
            zone_two,
            owner_hot,
            memory_float,
            query_float,
            vector_row,
            taps_back,
            dense_wide,
            mixed_all,
            alphas,
            taps,
            grad_frame_slots,
            frame_wide,
            slot_wide,
        ),
    )

    bias_sums = jnp.transpose(
        jnp.sum(sent.astype(f32), axis=1).reshape(-1, 4, lanes), (1, 0, 2)
    ).reshape(-1, lanes)
    slice_width = 2 * hidden // batch_size
    if slice_width != lanes:
        sent = sent.reshape(sent.shape[0], sent.shape[1], 4, -1, slice_width)
        sent = jnp.transpose(sent, (0, 3, 1, 2, 4)).reshape(batch_size, sent.shape[1], -1)
    received = lax.all_to_all(sent, "batch", 0, 0, tiled=True)
    grad_prenet = lax.dot_general(
        slot_hot.astype(f32),
        prenet_back.reshape(longest * slots, prenet_width),
        (((1,), (0,)), ((), ())),
        precision=precise,
    )

    def silu_back(grad, mixed, drops):
        gate = jax.nn.sigmoid(mixed)
        return grad * drops * 2.0 * gate * (1.0 + mixed * (1.0 - gate))

    def exact(a, b, contract):
        return lax.dot_general(
            a.astype(f32), b.astype(f32), (contract, ((), ())), precision=precise
        )

    grad_mixed_two = silu_back(grad_prenet, mixed_two, drops_two)
    prenet_second_grad = exact(hidden_round, grad_mixed_two, ((0,), (0,)))
    grad_hidden = exact(grad_mixed_two, prenet_second, ((1,), (1,)))
    grad_mixed_one = silu_back(grad_hidden, mixed_one, drops_one)
    prenet_first_grad = exact(previous, grad_mixed_one, ((0,), (0,)))

    query_weight_grad = exact(
        round_one.reshape(longest * slots, hidden),
        query_back.reshape(longest * slots, attention_width),
        ((0,), (0,)),
    )
    processed_round = processed_back.astype(bf16)
    memory_weight_grad = lax.dot_general(
        memory_now, processed_round, (((0,), (0,)), ((), ())), preferred_element_type=f32
    )
    filter_grads = jnp.roll(filter_back, -reach, axis=1)[:, ::-1][:, : location_conv.shape[2]]
    conv_grad = jnp.einsum("cka,fa->fck", filter_grads, dense_float, precision=precise)
    dense_grad = jnp.einsum("cka,fck->fa", filter_grads, conv_float, precision=precise)

    def two_columns(value):
        return jnp.concatenate([value[:, :lanes], value[:, lanes:]], axis=0)

    def to_lanes(value):
        return jnp.pad(value, ((0, 0), (0, lanes - value.shape[1])))

    filter_count, _, tap_count = location_conv.shape
    packed = [
        two_columns(prenet_first_grad),
        two_columns(prenet_second_grad),
        query_weight_grad,
        memory_weight_grad,
        to_lanes(frame_weight_grad),
        to_lanes(conv_grad.reshape(filter_count, -1)),
        dense_grad,
        bias_sums,
        vector_back,
        to_lanes(frame_bias_grad[None, :]),
    ]
    heights = [value.shape[0] for value in packed]
    shares = 2 * batch_size
    surplus = -sum(heights) % (8 * shares)
    packed = jnp.concatenate(packed + [jnp.zeros((surplus, lanes), f32)], axis=0)
    packed = add_units(packed, 0)
    received, packed = lax.optimization_barrier((received, packed))

    segments_rows = segments_all.T
    carried = jnp.pad(
        (segments_rows[:, 1:] == segments_rows[:, :-1]).astype(bf16), ((0, 0), (0, 1))
    ).reshape(batch_size, frame_rows)
    carried = jnp.pad(carried, ((0, 0), (0, padding)))
    after = jnp.pad(received[:, 1:], ((0, 0), (0, 1), (0, 0))) * carried[:, :, None]
    received = received.reshape(batch_size * (frame_rows + padding), -1)
    after = after.reshape(batch_size * (frame_rows + padding), -1)

    def product(start, width, grads):
        return lax.dot_general(
            inputs_all[:, start : start + width],
            grads,
            (((0,), (0,)), ((), ())),
            preferred_element_type=f32,
        )

    pair = 2 * slice_width
    first_part = jnp.concatenate(
        [
            product(0, prenet_width, received[:, :pair]),
            product(prenet_width + hidden, memory_width, after[:, :pair]),
            product(prenet_width, hidden, after[:, :pair]),
        ],
        axis=0,
    )
    second_part = jnp.concatenate(
        [
            product(prenet_width, hidden + memory_width, received[:, pair:]),
            product(prenet_width + hidden + memory_width, hidden, after[:, pair:]),
        ],
        axis=0,
    )
    parts = jnp.concatenate(
        [
            first_part.reshape(batch_size, depth_one, pair),
            second_part.reshape(batch_size, depth_two, pair),
        ],
        axis=1,
    )
    parts = add_units(parts, 2).astype(bf16)
    depth_both = depth_one + depth_two
    parts = jnp.concatenate(
        [parts, packed.astype(bf16).reshape(batch_size, -1, slice_width)], axis=1
    )
    if roomy:
        (
            parts,
            inputs_first,
            inputs_later,
            grads_early,
            grads_last,
            alphas,
            context_grads,
            processed_round,
        ) = lax.optimization_barrier(
            (
                parts,
                inputs_first,
                inputs_later,
                grads_early,
                grads_last,
                alphas,
                context_grads,
                processed_round,
            )
        )
        kernel_grads = []
        for layer in range(5):
            if layer == 0:
                source = inputs_first
            else:
                source = lax.dynamic_slice_in_dim(
                    inputs_later[layer - 1], place * channel_rows, channel_rows, 1
                )
            grad_norm = grads_early[layer] if layer < 4 else grads_last
            kernel_grads.append(
                post_kernel_grad(
                    source.reshape(frames, total_rows, -1),
                    grad_norm.reshape(frames, total_rows, -1),
                    same,
                ).reshape(5, source.shape[1], grad_norm.shape[1])
            )
    parts = lax.all_to_all(parts, "batch", 0, 0, tiled=True)
    share = jnp.sum(parts[:, depth_both:].astype(f32), axis=0)
    parts = parts[:, :depth_both].astype(f32)
    parts = jnp.transpose(parts, (1, 0, 2)).reshape(depth_both, 4, half)

    memory_grad = lax.dot_general(
        processed_round, memory_weight, (((1,), (1,)), ((), ())), preferred_element_type=f32
    )
    for step in range(longest):
        memory_grad = memory_grad + exact(
            alphas[step][:, :slots], context_grads[step], ((1,), (0,))
        )
    memory_grad = memory_grad.reshape(rows, text_width, memory_width)
    memory_grads = jnp.stack(ordered(memory_grad, exchange(memory_grad)))
    post_first_grad = add_units(kernel_grads[0], 2)
    post_middle_grad = add_units(jnp.stack(kernel_grads[1:4]), 3)
    post_last_grad = add_units(kernel_grads[4], 2)
    middle_norm_grad = add_units(
        jnp.stack([jnp.stack(gain_grads[:4]), jnp.stack(shift_grads[:4])]), 2
    )
    last_norm_grad = add_units(jnp.stack([gain_grads[4], shift_grads[4]]), 1)

    packed = whole(gather_rows(share).reshape(-1, lanes), 0)
    small, start = [], 0
    for height in heights:
        small.append(packed[start : start + height])
        start += height

    def from_columns(value):
        tall = value.shape[0] // 2
        return jnp.concatenate([value[:tall], value[tall:]], axis=1)

    biases_grad = small[7].reshape(2, 2, -1)
    biases_grad = jnp.where(first_unit, biases_grad[:, 0], biases_grad[:, 1])
    biases_grad = biases_grad.reshape(2, 4, half)
    small = [
        from_columns(small[0]),
        from_columns(small[1]),
        small[2],
        small[3],
        small[5][:, : 2 * tap_count].reshape(filter_count, 2, tap_count),
        small[6],
        small[8][0],
        small[4][:, : mel_width + 1],
        small[9][0, : mel_width + 1],
    ]
    return (
        small[0],
        small[1],
        small[2],
        small[3],
        small[4],
        small[5],
        small[6],
        parts[:depth_one],
        biases_grad[0],
        parts[depth_one:],
        biases_grad[1],
        small[7],
        small[8],
        post_first_grad,
        post_middle_grad,
        post_last_grad,
        middle_norm_grad,
        last_norm_grad,
        memory_grads,
    )


def solution(mesh):
    in_specs = (
        P(None, "batch", None, None),
        P(None, "batch", None, None),
        P(None, "batch", None),
        P(None, "batch", None),
        P(None, "batch", None, "unit"),
        P(None, "batch", None, "unit"),
        P(None, "batch", None, None),
        P(None, "batch", None, None),
        P(),
        P(),
        P(),
        P(),
        P(),
        P(),
        P(),
        P("batch", None, "unit"),
        P(None, "unit"),
        P("batch", None, "unit"),
        P(None, "unit"),
        P(),
        P(),
        P(None, None, "unit"),
        P(None, None, "batch", "unit"),
        P(None, "batch", "unit"),
        P(None, None, "unit"),
        P(None, "unit"),
    )
    out_specs = (
        P(),
        P(),
        P(),
        P(),
        P(),
        P(),
        P(),
        P("batch", None, "unit"),
        P(None, "unit"),
        P("batch", None, "unit"),
        P(None, "unit"),
        P(),
        P(),
        P(None, None, "unit"),
        P(None, None, "batch", "unit"),
        P(None, "batch", "unit"),
        P(None, None, "unit"),
        P(None, "unit"),
        P(None, "batch", None, None),
    )
    return jax.shard_map(
        on_device, mesh=mesh, in_specs=in_specs, out_specs=out_specs, check_vma=False
    )
```

```python
import functools

import jax
import jax.numpy as jnp
from jax import lax
from jax.experimental import pallas as pl
from jax.experimental.pallas import tpu as pltpu
from jax.sharding import PartitionSpec as P

precise = lax.Precision.HIGHEST
norm_eps = 1e-05
f32 = jnp.float32
bf16 = jnp.bfloat16
lanes = 128
kernel_vmem = 60 * 1024 * 1024


def split(value):
    high = value.astype(bf16)
    return high, (value - high.astype(f32)).astype(bf16)


def dot(a, b, contract=((1,), (0,))):
    return lax.dot_general(a, b, (contract, ((), ())), preferred_element_type=f32)


def dot_left(exact, value, contract=((1,), (0,))):
    high, low = split(value)
    return dot(exact, high, contract) + dot(exact, low, contract)


def dot_right(value, exact, contract=((1,), (0,))):
    high, low = split(value)
    return dot(high, exact, contract) + dot(low, exact, contract)


def dot_both(a, b, contract=((1,), (0,))):
    a_high, a_low = split(a)
    b_high, b_low = split(b)
    return (
        dot(a_high, b_high, contract) + dot(a_low, b_high, contract) + dot(a_high, b_low, contract)
    )


rows_first = ((0,), (0,))
lanes_both = ((1,), (1,))


def position_hot(position_count, text_width, reverse):
    place = lax.broadcasted_iota(jnp.int32, (position_count, lanes), 0) & (text_width - 1)
    lane = lax.broadcasted_iota(jnp.int32, (position_count, lanes), 1)
    place = (lanes - 1) - place if reverse else place + 1
    return (place == lane).astype(bf16)


def slant(value, text_width):
    blocks = [
        pltpu.roll(value[start : start + text_width], 0, 1, stride=1, stride_axis=0)
        for start in range(0, value.shape[0], text_width)
    ]
    return jnp.concatenate(blocks, axis=0)


def pad_rows(value):
    return jnp.concatenate(
        [value, jnp.zeros((lanes - value.shape[0], value.shape[1]), value.dtype)], axis=0
    )


def unit_spot(chunk, unit, per_half):
    half = (chunk // per_half + unit) % 2
    return pl.multiple_of((half * per_half + chunk % per_half) * lanes, lanes)


def gate_spot(chunk, gate, per_half):
    start = (chunk // per_half) * 4 * per_half + gate * per_half + chunk % per_half
    return pl.multiple_of(start * lanes, lanes)


def forward_kernel(
    unit_ref,
    own_one,
    peer_one,
    own_two,
    peer_two,
    previous_ref,
    drop_one,
    drop_two,
    layer_one,
    layer_two,
    slot_ref,
    zone_one,
    zone_two,
    bias_one,
    bias_two,
    hot_ref,
    memory_ref,
    project_ref,
    query_ref,
    vector_ref,
    conv_ref,
    dense_ref,
    frame_ref,
    frame_bias,
    gates_one,
    gates_two,
    prior_one,
    prior_two,
    round_one,
    round_two,
    context_ref,
    mixed_ref,
    alpha_ref,
    taps_ref,
    prenet_one,
    prenet_two,
    prenet_hidden,
    prenet_out,
    frame_out,
    held_one,
    held_two,
    input_ref,
    prenet_ref,
    processed_ref,
    filter_ref,
    state_one,
    cell_one,
    state_two,
    cell_two,
    sems,
):
    unit = unit_ref[0]
    steps, slots, hidden = round_one.shape
    prenet_width = layer_two.shape[1]
    context_width = context_ref.shape[2]
    half = hidden // 2
    per_half = half // lanes
    position_count = hot_ref.shape[0]
    text_width = position_count // (slots // 4)
    copies_two = [
        pltpu.make_async_copy(own_two, held_two.at[0], sems.at[0]),
        pltpu.make_async_copy(peer_two, held_two.at[1], sems.at[1]),
    ]
    copies_one = [
        pltpu.make_async_copy(own_one, held_one.at[0], sems.at[2]),
        pltpu.make_async_copy(peer_one, held_one.at[1], sems.at[3]),
    ]
    for copy in copies_two + copies_one:
        copy.start()
    for ref in (state_one, cell_one, state_two, cell_two):
        ref[...] = jnp.zeros_like(ref)

    def gates_into(held, depth, bias_ref, out_ref, step):
        def one(block, _):
            side = block // 2
            inputs = input_ref[:, :depth]
            for pair in range(per_half):
                tile = (block % 2) * 2 * per_half + 2 * pair
                outside = pl.ds(
                    pl.multiple_of(block * 2 * half + 2 * pair * lanes, 2 * lanes), 2 * lanes
                )
                kernel = jnp.concatenate(
                    [held[side, tile, :depth, :], held[side, tile + 1, :depth, :]], axis=1
                )
                out_ref[step, :, outside] = dot(inputs, kernel) + bias_ref[:, outside]
            return 0

        lax.fori_loop(0, 4, one, 0)

    def cell(gates_ref, zone_ref, prior_ref, state, cells, round_ref, step):
        def one(chunk, _):
            spot = pl.ds(pl.multiple_of(chunk * lanes, lanes), lanes)
            values = [
                gates_ref[step, :, pl.ds(gate_spot(chunk, gate, per_half), lanes)]
                for gate in range(4)
            ]
            zone = zone_ref[step, :, spot]
            before = cells[:, spot]
            prior_ref[step, :, spot] = before
            fresh = jax.nn.sigmoid(values[1]) * before + jax.nn.sigmoid(values[0]) * jnp.tanh(
                values[2]
            )
            output = jax.nn.sigmoid(values[3]) * jnp.tanh(fresh)
            now = zone * state[:, spot] + (1.0 - zone) * output
            state[:, spot] = now
            cells[:, spot] = zone * before + (1.0 - zone) * fresh
            round_ref[step, :, pl.ds(unit_spot(chunk, unit, per_half), lanes)] = now.astype(bf16).astype(
                f32
            )
            return 0

        lax.fori_loop(0, 2 * per_half, one, 0)

    def attention(step, location):
        inside = hot_ref[...] > 0.0
        hot = hot_ref[...].astype(bf16)
        query = pad_rows(dot(round_one[step].astype(bf16), query_ref[...].astype(bf16)))
        summed = dot_left(hot, query) + processed_ref[...]
        if location is not None:
            summed = summed + location
        mixed = jnp.tanh(summed)
        mixed_ref[step] = mixed
        energy = dot_right(mixed, vector_ref[...].astype(bf16))
        most = jnp.max(jnp.where(inside, energy, -1000000000.0), axis=0, keepdims=True)
        shifted = jnp.where(inside, jnp.exp(energy - most), 0.0)
        total = jnp.sum(shifted, axis=0, keepdims=True)
        alpha = shifted / jnp.where(total > 0.0, total, 1.0)
        alpha_ref[step] = alpha
        context = dot_right(alpha, memory_ref[...].astype(bf16), rows_first)[:slots]
        context_ref[step] = context.astype(bf16).astype(f32)

    def taps_of(step):
        spread = dot_right(
            alpha_ref[step], position_hot(position_count, text_width, True), rows_first
        )
        taps_ref[step] = slant(dot_left(hot_ref[...].astype(bf16), spread), text_width)

    def second_layer(step, depth):
        input_ref[:, :hidden] = round_one[step].astype(bf16)
        input_ref[:, hidden : hidden + context_width] = context_ref[step].astype(bf16)
        gates_into(held_two, depth, bias_two, gates_two, step)
        cell(gates_two, zone_two, prior_two, state_two, cell_two, round_two, step)

    slot_hot = slot_ref[...].astype(bf16)

    def prenet_layer(source, layer, drops, mixed_out, out):
        mixed = dot(source.astype(bf16), layer[...].astype(bf16))
        mixed_out[...] = mixed
        value = (mixed * jax.nn.sigmoid(mixed) * drops[...] * 2.0).astype(bf16)
        out[...] = value.astype(f32)
        return value

    hidden_value = prenet_layer(previous_ref[...], layer_one, drop_one, prenet_one, prenet_hidden)
    prenet_value = prenet_layer(hidden_value, layer_two, drop_two, prenet_two, prenet_out)
    prenet_slots = dot(slot_hot, prenet_value, rows_first)
    for step in range(steps):
        prenet_ref[step] = prenet_slots[step * slots : (step + 1) * slots]
    processed_ref[...] = dot(memory_ref[...].astype(bf16), project_ref[...].astype(bf16))
    for channel in range(2):
        filter_ref[channel] = dot(
            conv_ref[channel].astype(bf16), dense_ref[...].astype(bf16)
        )

    gates_one[0] = jnp.broadcast_to(bias_one[...], gates_one.shape[1:])
    cell(gates_one, zone_one, prior_one, state_one, cell_one, round_one, 0)
    attention(0, None)
    taps_of(0)
    for copy in copies_two:
        copy.wait()
    second_layer(0, hidden + context_width)
    for copy in copies_one:
        copy.wait()

    def later(step, _):
        input_ref[:, :prenet_width] = prenet_ref[step].astype(bf16)
        input_ref[:, prenet_width : prenet_width + context_width] = context_ref[step - 1].astype(
            bf16
        )
        input_ref[:, prenet_width + context_width : prenet_width + context_width + hidden] = (
            round_one[step - 1].astype(bf16)
        )
        gates_into(
            held_one, prenet_width + context_width + hidden, bias_one, gates_one, step
        )
        cell(gates_one, zone_one, prior_one, state_one, cell_one, round_one, step)
        previous = taps_ref[step - 1]
        summed = jnp.where(step == 2, taps_ref[0] + previous, previous)
        attention(step, dot_both(previous, filter_ref[0]) + dot_both(summed, filter_ref[1]))

        @pl.when(step < steps - 1)
        def _():
            taps_of(step)

        input_ref[:, hidden + context_width :] = round_two[step - 1].astype(bf16)
        second_layer(step, 2 * hidden + context_width)
        return 0

    lax.fori_loop(1, steps, later, 0)
    for step in range(steps):
        values = dot(round_two[step].astype(bf16), frame_ref[:hidden].astype(bf16)) + dot(
            context_ref[step].astype(bf16), frame_ref[hidden:].astype(bf16)
        )
        high = values.astype(bf16)
        rest = values - high.astype(f32)
        middle = rest.astype(bf16)
        low = (rest - middle.astype(f32)).astype(bf16)
        chosen = slot_hot[:, step * slots : (step + 1) * slots]
        picked = (dot(chosen, high) + dot(chosen, middle)) + dot(chosen, low)
        frame_out[...] = (frame_bias[...] if step == 0 else frame_out[...]) + picked


def backward_kernel(
    unit_ref,
    own_one,
    peer_one,
    own_two,
    peer_two,
    gates_one,
    gates_two,
    prior_one,
    prior_two,
    zone_one,
    zone_two,
    hot_ref,
    memory_ref,
    query_ref,
    vector_ref,
    conv_ref,
    dense_ref,
    mixed_ref,
    alpha_ref,
    taps_ref,
    frame_grad,
    frame_weight,
    slot_ref,
    sent_ref,
    prenet_grad,
    context_grad,
    query_grad,
    processed_grad,
    vector_grad,
    filter_grad,
    held_one,
    held_two,
    grads_one,
    grads_two,
    back_one,
    back_two,
    state_one,
    cell_one,
    state_two,
    cell_two,
    previous_grad,
    summed_grad,
    from_query,
    frame_ref,
    filter_ref,
    sems,
):
    unit = unit_ref[0]
    steps, slots, prenet_width = prenet_grad.shape
    context_width = context_grad.shape[2]
    hidden = state_one.shape[1]
    half = hidden // 2
    per_half = half // lanes
    position_count = hot_ref.shape[0]
    text_width = position_count // (slots // 4)
    copies_two = [
        pltpu.make_async_copy(own_two, held_two.at[0], sems.at[0]),
        pltpu.make_async_copy(peer_two, held_two.at[1], sems.at[1]),
    ]
    copies_one = [
        pltpu.make_async_copy(own_one, held_one.at[0], sems.at[2]),
        pltpu.make_async_copy(peer_one, held_one.at[1], sems.at[3]),
    ]
    for copy in copies_two + copies_one:
        copy.start()
    for ref in (
        state_one,
        cell_one,
        state_two,
        cell_two,
        back_one,
        back_two,
        previous_grad,
        summed_grad,
        processed_grad,
        vector_grad,
        filter_grad,
    ):
        ref[...] = jnp.zeros_like(ref)

    def cell(gates_ref, prior_ref, zone_ref, state, cells, grads_ref, step, incoming):
        def one(chunk, _):
            spot = pl.ds(pl.multiple_of(chunk * lanes, lanes), lanes)
            places = [pl.ds(gate_spot(chunk, gate, per_half), lanes) for gate in range(4)]
            values = [gates_ref[step, :, place] for place in places]
            zone = zone_ref[step, :, spot]
            keep = 1.0 - zone
            before = prior_ref[step, :, spot]
            gate_in = jax.nn.sigmoid(values[0])
            gate_forget = jax.nn.sigmoid(values[1])
            candidate = jnp.tanh(values[2])
            gate_out = jax.nn.sigmoid(values[3])
            bent = jnp.tanh(gate_forget * before + gate_in * candidate)
            grad_state = incoming(unit_spot(chunk, unit, per_half)) + state[:, spot]
            grad_cell = cells[:, spot]
            grad_new = keep * grad_state
            grad_fresh = grad_new * gate_out * (1.0 - bent * bent) + keep * grad_cell
            state[:, spot] = zone * grad_state
            cells[:, spot] = zone * grad_cell + gate_forget * grad_fresh
            results = (
                grad_fresh * candidate * gate_in * (1.0 - gate_in),
                grad_fresh * before * gate_forget * (1.0 - gate_forget),
                grad_fresh * gate_in * (1.0 - candidate * candidate),
                grad_new * bent * gate_out * (1.0 - gate_out),
            )
            for place, result in zip(places, results):
                grads_ref[step, :, place] = result.astype(bf16)
            return 0

        lax.fori_loop(0, 2 * per_half, one, 0)

    def inputs_back(grads_ref, held, out_ref, step, blocks):
        def one(block, _):
            spot = pl.ds(pl.multiple_of(block * 256, 256), 256)
            totals = [None] * 4
            for tile in range(0, 8 * per_half, 2):
                side, inside = tile // (4 * per_half), tile % (4 * per_half)
                kernel = jnp.concatenate(
                    [held[side, inside, spot, :], held[side, inside + 1, spot, :]], axis=1
                )
                grads = grads_ref[step, :, tile * lanes : (tile + 2) * lanes]
                product = dot(grads, kernel, lanes_both)
                which = tile // 2 % 4
                totals[which] = product if totals[which] is None else totals[which] + product
            out_ref[:, spot] = (totals[0] + totals[1]) + (totals[2] + totals[3])
            return 0

        lax.fori_loop(0, blocks, one, 0)

    def attention(step, located):
        inside = hot_ref[...] > 0.0
        hot = hot_ref[...].astype(bf16)
        alpha = alpha_ref[step]
        mixed = mixed_ref[step]
        context_now = pad_rows(context_grad[step])
        weights_grad = jnp.where(
            inside,
            dot_left(memory_ref[...].astype(bf16), context_now, lanes_both)
            + previous_grad[...]
            + summed_grad[...],
            0.0,
        )
        product = alpha * weights_grad
        energy_grad = product - alpha * jnp.sum(product, axis=0, keepdims=True)
        spread = jnp.sum(energy_grad, axis=1, keepdims=True)
        vector_grad[...] += jnp.sum(spread * mixed, axis=0, keepdims=True)
        mixed_grad = spread * vector_ref[...] * (1.0 - mixed * mixed)
        processed_grad[...] += mixed_grad
        high, low = split(mixed_grad)
        query_now = (dot(hot, high, rows_first) + dot(hot, low, rows_first))[:slots]
        query_grad[step] = query_now
        from_query[...] = dot_right(query_now, query_ref[...].astype(bf16), lanes_both)
        if located:
            previous = taps_ref[step - 1]
            summed = jnp.where(step == 2, taps_ref[0] + previous, previous)
            filter_grad[0] += dot_both(previous, mixed_grad, rows_first)
            filter_grad[1] += dot_both(summed, mixed_grad, rows_first)
            place_hot = position_hot(position_count, text_width, False)

            def taps_back(channel):
                taps_grad = slant(
                    dot_both(mixed_grad, filter_ref[channel], lanes_both), text_width
                )
                gathered = dot_right(taps_grad, hot, rows_first)
                return jnp.where(inside, dot_left(place_hot, gathered), 0.0)

            previous_grad[...] = taps_back(0)
            summed_grad[...] += taps_back(1)

    def arrived(step, copies):
        @pl.when(step == steps - 1)
        def _():
            for copy in copies:
                copy.wait()

    def step_back(step, located):
        cell(
            gates_two,
            prior_two,
            zone_two,
            state_two,
            cell_two,
            grads_two,
            step,
            lambda spot: frame_ref[step, :, pl.ds(spot, lanes)]
            + back_two[:, pl.ds(spot + hidden + context_width, lanes)],
        )
        blocks_two = (hidden + context_width + (hidden if located else 0)) // 256
        if located:
            arrived(step, copies_two)
        inputs_back(grads_two, held_two, back_two, step, blocks_two)
        context_grad[step] = (
            back_two[:, hidden : hidden + context_width]
            + frame_ref[step, :, hidden:]
            + back_one[:, prenet_width : prenet_width + context_width]
        )
        attention(step, located)
        cell(
            gates_one,
            prior_one,
            zone_one,
            state_one,
            cell_one,
            grads_one,
            step,
            lambda spot: back_two[:, pl.ds(spot, lanes)]
            + from_query[:, pl.ds(spot, lanes)]
            + back_one[:, pl.ds(spot + prenet_width + context_width, lanes)],
        )
        blocks_one = (prenet_width + (hidden + context_width if located else 0)) // 256
        if located:
            arrived(step, copies_one)
        inputs_back(grads_one, held_one, back_one, step, blocks_one)
        prenet_grad[step] = back_one[:, :prenet_width]

    for channel in range(2):
        filter_ref[channel] = dot(
            conv_ref[channel].astype(bf16), dense_ref[...].astype(bf16)
        )
    for step in range(steps):
        frame_ref[step] = dot(
            frame_grad[step].astype(bf16), frame_weight[...].astype(bf16), lanes_both
        )

    def later(index, _):
        step_back(steps - 1 - index, True)
        return 0

    lax.fori_loop(0, steps - 1, later, 0)
    step_back(0, False)
    slot_hot = slot_ref[...].astype(bf16)

    def tile_out(tile, _):
        for layer, grads_ref in ((0, grads_one), (1, grads_two)):
            for side in range(2):
                place = ((side + unit) % 2) * 4 * half + tile * lanes
                grads = grads_ref[:, :, pl.ds(pl.multiple_of(place, lanes), lanes)]
                chosen = dot(slot_hot, grads.reshape(steps * slots, lanes)).astype(bf16)
                spot = (2 * layer + side) * lanes
                sent_ref[tile, :, spot : spot + lanes] = chosen
        return 0

    lax.fori_loop(0, 4 * per_half, tile_out, 0)


def call_forward(unit, weights, small, sizes):
    own_one, peer_one, own_two, peer_two = weights
    steps, slots, hidden, context_width, positions, frame_rows, prenet_width = sizes

    def shape(*dims):
        return jax.ShapeDtypeStruct(dims, f32)

    outs = [
        shape(steps, slots, 4 * hidden),
        shape(steps, slots, 4 * hidden),
        shape(steps, slots, hidden),
        shape(steps, slots, hidden),
        shape(steps, slots, hidden),
        shape(steps, slots, hidden),
        shape(steps, slots, context_width),
        shape(steps, positions, lanes),
        shape(steps, positions, lanes),
        shape(steps - 1, positions, lanes),
        shape(frame_rows, prenet_width),
        shape(frame_rows, prenet_width),
        shape(frame_rows, prenet_width),
        shape(frame_rows, prenet_width),
        shape(frame_rows, lanes),
    ]
    vmem = pl.BlockSpec(memory_space=pltpu.VMEM)
    return pl.pallas_call(
        forward_kernel,
        out_shape=outs,
        in_specs=[pl.BlockSpec(memory_space=pltpu.SMEM)]
        + [pl.BlockSpec(memory_space=pl.ANY)] * 4
        + [vmem] * len(small),
        out_specs=[vmem] * len(outs),
        scratch_shapes=[
            pltpu.VMEM((2,) + own_one.shape, bf16),
            pltpu.VMEM((2,) + own_two.shape, bf16),
            pltpu.VMEM((slots, own_two.shape[1]), bf16),
            pltpu.VMEM((steps, slots, prenet_width), f32),
            pltpu.VMEM((positions, lanes), f32),
            pltpu.VMEM((2, lanes, lanes), f32),
            pltpu.VMEM((slots, hidden), f32),
            pltpu.VMEM((slots, hidden), f32),
            pltpu.VMEM((slots, hidden), f32),
            pltpu.VMEM((slots, hidden), f32),
            pltpu.SemaphoreType.DMA((4,)),
        ],
        compiler_params=pltpu.CompilerParams(vmem_limit_bytes=kernel_vmem),
        name="decoder_forward",
    )(unit, *weights, *small)


def call_backward(unit, weights, small):
    own_one, peer_one, own_two, peer_two = weights
    gates_one = small[0]
    steps, slots, gate_width = gates_one.shape
    hidden = gate_width // 4
    positions, context_width = small[7].shape
    prenet_width = own_one.shape[1] - hidden - context_width

    def shape(dims, kind):
        return jax.ShapeDtypeStruct(dims, kind)

    outs = [
        shape((gate_width // (2 * lanes), small[-1].shape[0], 4 * lanes), bf16),
        shape((steps, slots, prenet_width), f32),
        shape((steps, slots, context_width), f32),
        shape((steps, slots, lanes), f32),
        shape((positions, lanes), f32),
        shape((1, lanes), f32),
        shape((2, lanes, lanes), f32),
    ]
    vmem = pl.BlockSpec(memory_space=pltpu.VMEM)
    return pl.pallas_call(
        backward_kernel,
        out_shape=outs,
        in_specs=[pl.BlockSpec(memory_space=pltpu.SMEM)]
        + [pl.BlockSpec(memory_space=pl.ANY)] * 4
        + [vmem] * len(small),
        out_specs=[vmem] * len(outs),
        scratch_shapes=[
            pltpu.VMEM((2,) + own_one.shape, bf16),
            pltpu.VMEM((2,) + own_two.shape, bf16),
            pltpu.VMEM((steps, slots, gate_width), bf16),
            pltpu.VMEM((steps, slots, gate_width), bf16),
            pltpu.VMEM((slots, own_one.shape[1]), f32),
            pltpu.VMEM((slots, own_two.shape[1]), f32),
            pltpu.VMEM((slots, hidden), f32),
            pltpu.VMEM((slots, hidden), f32),
            pltpu.VMEM((slots, hidden), f32),
            pltpu.VMEM((slots, hidden), f32),
            pltpu.VMEM((positions, lanes), f32),
            pltpu.VMEM((positions, lanes), f32),
            pltpu.VMEM((slots, hidden), f32),
            pltpu.VMEM((steps, slots, hidden + context_width), f32),
            pltpu.VMEM((2, lanes, lanes), f32),
            pltpu.SemaphoreType.DMA((4,)),
        ],
        compiler_params=pltpu.CompilerParams(vmem_limit_bytes=kernel_vmem),
        name="decoder_backward",
    )(unit, *weights, *small)


def postnet_kernel(
    mel_width,
    loss_scale,
    unit_ref,
    mel_ref,
    target_ref,
    mask_ref,
    first_ref,
    own_ref,
    peer_ref,
    last_ref,
    gain_ref,
    shift_ref,
    inputs_first,
    inputs_later,
    grads_early,
    grads_last,
    norm_grads,
    mel_grad,
    padded,
    padded_mel,
    held,
    normed_early,
    normed_last,
    inverse_ref,
    post_grad,
):
    unit = unit_ref[0]
    count, channels = held.shape
    side = channels // 2
    frames = padded.shape[0] - count
    rows_each = frames // 4
    chunk = 2 * rows_each
    tall = float(count)
    body_rows = slice(2 * rows_each, 2 * rows_each + count)

    for ref in (padded, padded_mel):
        ref[: 2 * rows_each] = jnp.zeros((2 * rows_each, ref.shape[1]), bf16)
        ref[2 * rows_each + count :] = jnp.zeros((2 * rows_each, ref.shape[1]), bf16)

    def piece(source, start, tap, width, lane=None):
        spot = pl.ds(pl.multiple_of(start + tap * rows_each, rows_each), chunk)
        mask = mask_ref[tap, pl.ds(pl.multiple_of(start, rows_each), chunk), :]
        if width < lanes:
            mask = mask[:, :width]
        else:
            mask = jnp.concatenate([mask] * (width // lanes), axis=1)
        value = source[spot, :] if lane is None else source[spot, pl.ds(lane, width)]
        return value * mask

    def chunks(work):
        def one(index, _):
            work(pl.multiple_of(index * chunk, chunk))
            return 0

        lax.fori_loop(0, count // chunk, one, 0)

    def half_spot(which):
        return pl.multiple_of(((which + unit) % 2) * side, side)

    def norm_forward(value, layer, lane, width):
        mean = jnp.sum(value, axis=0, keepdims=True) / tall
        centered = value - mean
        inverse = lax.rsqrt(jnp.sum(centered * centered, axis=0, keepdims=True) / tall + norm_eps)
        inverse_ref[layer, :, pl.ds(lane, width)] = inverse
        return centered * inverse

    def each_lane_block(work):
        def one(index, _):
            work(pl.multiple_of(index * lanes, lanes))
            return 0

        lax.fori_loop(0, channels // lanes, one, 0)

    def activate(layer):
        def block(lane):
            spot = pl.ds(lane, lanes)
            normed = norm_forward(held[:, spot], layer, lane, lanes)
            normed_early[layer, :, spot] = normed
            active = jnp.tanh(
                normed * gain_ref[layer, :, spot] + shift_ref[layer, :, spot]
            ).astype(bf16)
            inputs_later[layer, :, spot] = active
            padded[body_rows, spot] = active

        each_lane_block(block)

    source = mel_ref[...].astype(bf16)
    inputs_first[...] = source
    padded_mel[body_rows] = source

    def first_chunk(start):
        total = None
        for tap in range(5):
            product = dot(piece(padded_mel, start, tap, mel_width), first_ref[tap])
            total = product if total is None else total + product
        held[pl.ds(start, chunk), :] = total

    chunks(first_chunk)
    activate(0)

    def middle(index, _):
        def middle_chunk(start):
            totals = [None, None]
            for tap in range(5):
                value = piece(padded, start, tap, channels)
                for which, ref in ((0, own_ref), (1, peer_ref)):
                    product = dot(value, ref[index * 5 + tap])
                    totals[which] = product if tap == 0 else totals[which] + product
            for which in range(2):
                held[pl.ds(start, chunk), pl.ds(half_spot(which), side)] = totals[which]

        chunks(middle_chunk)
        activate(index + 1)
        return 0

    lax.fori_loop(0, 3, middle, 0)

    def last_chunk(start):
        total = None
        for tap in range(5):
            product = dot(piece(padded, start, tap, channels), last_ref[tap])
            total = product if total is None else total + product
        normed_last[pl.ds(start, chunk), :] = total

    chunks(last_chunk)
    normed = norm_forward(normed_last[...], 4, 0, mel_width)
    normed_last[...] = normed

    def norm_back(grad, normed, layer, lane, width):
        spot = pl.ds(lane, width)
        shift_grad = jnp.sum(grad, axis=0, keepdims=True)
        gain_grad = jnp.sum(grad * normed, axis=0, keepdims=True)
        norm_grads[0, layer, :, spot] = gain_grad
        norm_grads[1, layer, :, spot] = shift_grad
        return (
            gain_ref[layer, :, spot]
            * inverse_ref[layer, :, spot]
            * (grad - shift_grad / tall - normed * (gain_grad / tall))
        ).astype(bf16)

    output = normed * gain_ref[4, :, :mel_width] + shift_ref[4, :, :mel_width]
    grad = loss_scale * (mel_ref[...] + output - target_ref[...])
    post_grad[...] = grad
    grad_norm = norm_back(grad, normed, 4, 0, mel_width)
    grads_last[...] = grad_norm
    padded_mel[body_rows] = grad_norm

    def last_back(start):
        total = None
        for tap in range(5):
            product = dot(
                piece(padded_mel, start, tap, mel_width), last_ref[4 - tap], lanes_both
            )
            total = product if total is None else total + product
        held[pl.ds(start, chunk), :] = total

    chunks(last_back)

    def deactivate(layer):
        def block(lane):
            spot = pl.ds(lane, lanes)
            normed = normed_early[layer, :, spot]
            active = jnp.tanh(normed * gain_ref[layer, :, spot] + shift_ref[layer, :, spot])
            grad = held[:, spot] * (1.0 - active * active)
            grad_norm = norm_back(grad, normed, layer, lane, lanes)
            grads_early[layer, :, spot] = grad_norm
            padded[body_rows, spot] = grad_norm

        each_lane_block(block)

    def middle_back(back, _):
        index = 2 - back
        deactivate(index + 1)

        def chunk_back(start):
            total = None
            for which, ref in ((0, own_ref), (1, peer_ref)):
                for tap in range(5):
                    product = dot(
                        piece(padded, start, tap, side, half_spot(which)),
                        ref[index * 5 + 4 - tap],
                        lanes_both,
                    )
                    total = product if total is None else total + product
            held[pl.ds(start, chunk), :] = total

        chunks(chunk_back)
        return 0

    lax.fori_loop(0, 3, middle_back, 0)
    deactivate(0)

    def first_back(start):
        total = None
        for tap in range(5):
            product = dot(piece(padded, start, tap, channels), first_ref[4 - tap], lanes_both)
            total = product if total is None else total + product
        spot = pl.ds(start, chunk)
        mel_grad[spot, :] = (
            loss_scale * (mel_ref[spot, :] - target_ref[spot, :]) + post_grad[spot, :] + total
        )

    chunks(first_back)


def call_postnet(unit, small, loss_scale, rows_all):
    mel = small[0]
    count, mel_width = mel.shape
    channels = small[3].shape[2]

    def shape(kind, *dims):
        return jax.ShapeDtypeStruct(dims, kind)

    outs = [
        shape(bf16, count, mel_width),
        shape(bf16, 4, count, channels),
        shape(bf16, 4, count, channels),
        shape(bf16, count, mel_width),
        shape(f32, 2, 5, 1, channels),
        shape(f32, count, mel_width),
    ]
    vmem = pl.BlockSpec(memory_space=pltpu.VMEM)
    tall = count + 4 * rows_all
    return pl.pallas_call(
        functools.partial(postnet_kernel, mel_width, loss_scale),
        out_shape=outs,
        in_specs=[pl.BlockSpec(memory_space=pltpu.SMEM)] + [vmem] * len(small),
        out_specs=[vmem] * len(outs),
        scratch_shapes=[
            pltpu.VMEM((tall, channels), bf16),
            pltpu.VMEM((tall, mel_width), bf16),
            pltpu.VMEM((count, channels), f32),
            pltpu.VMEM((4, count, channels), f32),
            pltpu.VMEM((count, mel_width), f32),
            pltpu.VMEM((5, 1, channels), f32),
            pltpu.VMEM((count, mel_width), f32),
        ],
        compiler_params=pltpu.CompilerParams(vmem_limit_bytes=kernel_vmem),
        name="postnet",
    )(unit, *small)


def shifted_frames(source, same):
    steps = source.shape[0]
    padded = jnp.pad(source, ((2, 2), (0, 0), (0, 0)))
    return [
        padded[offset : offset + steps] * same[:, :, offset, None].astype(source.dtype)
        for offset in range(5)
    ]


def by_rows(work, roomy, arrays, summed=False):
    if roomy:
        return work(*arrays)
    parts = arrays[0].shape[1] // 192

    def cut(value):
        value = value.reshape((value.shape[0], parts, -1) + value.shape[2:])
        return jnp.moveaxis(value, 1, 0)

    pieces = tuple(cut(value) for value in arrays)
    if summed:
        first = jax.eval_shape(work, *[value[0] for value in pieces])
        start = jnp.zeros(first.shape, first.dtype)
        return lax.scan(lambda total, now: (total + work(*now), None), start, pieces)[0]
    result = jnp.moveaxis(lax.map(lambda now: work(*now), pieces), 0, 1)
    return result.reshape((result.shape[0], -1) + result.shape[3:])


def post_layer(source, kernel, same):
    wide = jnp.concatenate(shifted_frames(source, same), axis=2)
    return jnp.einsum(
        "src,co->sro", wide, kernel.reshape(-1, kernel.shape[2]), preferred_element_type=f32
    )


def post_layer_back(grad, kernel, same):
    wide = jnp.concatenate(shifted_frames(grad, same), axis=2)
    turned = jnp.transpose(kernel[::-1], (0, 2, 1)).reshape(-1, kernel.shape[1])
    return jnp.einsum("sro,oc->src", wide, turned, preferred_element_type=f32)


def post_kernel_grad(source, grad, same):
    wide = jnp.concatenate(shifted_frames(source, same), axis=2)
    return jnp.einsum("src,sro->co", wide, grad, preferred_element_type=f32)


def on_device(
    memory,
    targets,
    segments,
    text_lengths,
    zone_first,
    zone_second,
    drop_first,
    drop_second,
    prenet_first,
    prenet_second,
    query_weight,
    memory_weight,
    location_conv,
    location_dense,
    energy_vector,
    lstm_first,
    bias_first,
    lstm_second,
    bias_second,
    frame_weight,
    frame_bias,
    post_first,
    post_middle,
    post_last,
    middle_norm,
    last_norm,
):
    micro_count, rows, text_width, memory_width = memory.shape
    frames = segments.shape[2]
    utterances = text_lengths.shape[2]
    mel_width = targets.shape[3]
    hidden = query_weight.shape[0]
    prenet_width = prenet_first.shape[1]
    attention_width = query_weight.shape[1]
    half = lstm_first.shape[2]
    depth_one, depth_two = lstm_first.shape[0], lstm_second.shape[0]
    unit = lax.axis_index("unit")
    place = lax.axis_index("batch")
    batch_size = lax.axis_size("batch")
    total_rows = rows * batch_size
    frame_count = float(total_rows * frames)
    first_unit = unit == 0
    longest = 3
    slots = 4 * rows

    def exchange(value):
        return lax.ppermute(value, "unit", [(0, 1), (1, 0)])

    def ordered(own, peer):
        return jnp.where(first_unit, own, peer), jnp.where(first_unit, peer, own)

    def whole(value, axis):
        return jnp.concatenate(ordered(value, exchange(value)), axis=axis)

    def mine(value):
        return lax.dynamic_index_in_dim(value, unit, 0, keepdims=False)

    def others(value):
        return lax.dynamic_index_in_dim(value, 1 - unit, 0, keepdims=False)

    def swapped(value, bit):
        pairs = [(index, index ^ bit) for index in range(batch_size)]
        other = lax.ppermute(value, "batch", pairs)
        upper = (place & bit) != 0
        return jnp.where(upper, other, value), jnp.where(upper, value, other)

    def gather_far_first(value):
        inner, bit, count = value.ndim, batch_size // 2, 0
        while bit:
            value = jnp.stack(swapped(value, bit))
            bit //= 2
            count += 1
        order = tuple(range(count - 1, -1, -1)) + tuple(range(count, count + inner))
        return jnp.transpose(value, order).reshape((batch_size,) + value.shape[count:])

    def gather_rows(value):
        bit = 1
        while bit < batch_size:
            value = jnp.concatenate(swapped(value, bit), axis=0)
            bit *= 2
        return value

    def gather_tiles(value):
        tiles = jnp.transpose(value.reshape(value.shape[0], -1, lanes), (1, 0, 2))
        return lax.all_gather(tiles, "batch", axis=1, tiled=True)

    own_two = gather_tiles(lstm_second)
    own_one = gather_tiles(lstm_first)
    peer_two = exchange(own_two)
    channel_rows = post_middle.shape[2]
    middle_width = post_middle.shape[3]
    middle_half = lax.all_gather(
        post_middle.reshape(-1, channel_rows, middle_width), "batch", axis=1, tiled=True
    )
    last_half = gather_rows(jnp.transpose(post_last, (1, 0, 2)).reshape(channel_rows, -1))
    last_half = jnp.transpose(
        last_half.reshape(-1, post_last.shape[0], post_last.shape[2]), (1, 0, 2)
    )
    memory_now = mine(memory).reshape(rows * text_width, memory_width)
    segments_now = mine(segments)
    targets_now = mine(targets)
    frame_info = gather_rows(
        jnp.concatenate([targets_now, segments_now[:, :, None].astype(bf16)], axis=2).astype(f32)
    )

    same_frames = segments_now[:, :, None] == segments_now[:, None, :]
    earlier = jnp.tril(jnp.ones((frames, frames), jnp.bool_), -1)
    order = jnp.sum((same_frames & earlier[None]).astype(jnp.int32), axis=2)
    slot_of = order * slots + segments_now * rows + jnp.arange(rows, dtype=jnp.int32)[:, None]
    frame_rows = rows * frames
    padding = -frame_rows % 16
    slot_hot = (
        jnp.pad(slot_of.reshape(-1, 1), ((0, padding), (0, 0)), constant_values=-1)
        == jnp.arange(longest * slots, dtype=jnp.int32)[None, :]
    ).astype(bf16)
    slot_hot_frames = slot_hot[:frame_rows]
    carry_on = jnp.pad(
        (segments_now[:, 1:] == segments_now[:, :-1]).astype(f32), ((0, 0), (1, 0))
    )
    finished = jnp.pad(
        (segments_now[:, 1:] != segments_now[:, :-1]).astype(f32),
        ((0, 0), (0, 1)),
        constant_values=1.0,
    )

    def to_slots(value, kind=bf16):
        return lax.dot_general(
            slot_hot_frames,
            value.astype(bf16),
            (((0,), (0,)), ((), ())),
            preferred_element_type=f32,
        ).astype(kind)

    def to_frames(value):
        return jnp.dot(slot_hot, value.astype(bf16), preferred_element_type=f32).astype(bf16)

    def pad_frames(value):
        return jnp.pad(
            value.astype(f32).reshape(frame_rows, -1), ((0, padding), (0, 0))
        )

    previous = pad_frames(
        jnp.pad(targets_now[:, :-1], ((0, 0), (1, 0), (0, 0))).astype(f32)
        * carry_on[:, :, None]
    )
    drops_one = pad_frames(mine(drop_first))
    drops_two = pad_frames(mine(drop_second))

    zones_own = jnp.concatenate([mine(zone_first), mine(zone_second)], axis=2).astype(f32)
    zones_peer = exchange(
        jnp.concatenate([others(zone_first), others(zone_second)], axis=2).astype(f32)
    )
    zones_slots = to_slots(
        jnp.concatenate([zones_own, zones_peer], axis=2).reshape(rows * frames, -1), f32
    ).reshape(longest, slots, 4 * half)
    zone_one = jnp.concatenate(
        [zones_slots[:, :, :half], zones_slots[:, :, 2 * half : 3 * half]], axis=2
    )
    zone_two = jnp.concatenate(
        [zones_slots[:, :, half : 2 * half], zones_slots[:, :, 3 * half :]], axis=2
    )
    biases = jnp.stack([bias_first.reshape(-1), bias_second.reshape(-1)])
    biases = jnp.concatenate([biases, exchange(biases)], axis=1)
    text_ends = jnp.cumsum(mine(text_lengths), axis=1)
    owner = jnp.sum(
        (jnp.arange(text_width, dtype=jnp.int32)[None, :, None] >= text_ends[:, None, :]).astype(
            jnp.int32
        ),
        axis=2,
    )
    owner_slot = owner * rows + jnp.arange(rows, dtype=jnp.int32)[:, None]
    owner_hot = (
        owner_slot.reshape(-1, 1) == jnp.arange(lanes, dtype=jnp.int32)[None, :]
    ).astype(f32)
    conv_float = location_conv.astype(f32)
    dense_float = location_dense.astype(f32)
    reach = location_conv.shape[2] // 2
    taps_first = jnp.transpose(conv_float, (1, 2, 0))
    taps_first = jnp.pad(
        taps_first,
        ((0, 0), (0, lanes - taps_first.shape[1]), (0, lanes - taps_first.shape[2])),
    )
    dense_wide = jnp.pad(dense_float, ((0, lanes - dense_float.shape[0]), (0, 0)))
    taps_forward = jnp.roll(taps_first[:, ::-1], reach, axis=1)
    taps_back = jnp.roll(taps_first, 1 - reach, axis=1)
    frame_wide = jnp.pad(
        frame_weight.astype(f32), ((0, 0), (0, lanes - frame_weight.shape[1]))
    )
    frame_bias_wide = jnp.pad(frame_bias, (0, lanes - frame_bias.shape[0]))[None, :]
    vector_float = energy_vector.astype(f32)
    vector_wide = jnp.broadcast_to(vector_float[:, None], (attention_width, lanes))
    memory_float = memory_now.astype(f32)
    query_float = query_weight.astype(f32)
    unit_array = unit.astype(jnp.int32).reshape(1)

    targets_all = jnp.transpose(frame_info[:, :, :mel_width].astype(f32), (1, 0, 2))
    segments_all = jnp.transpose(frame_info[:, :, mel_width].astype(jnp.int32))
    padded = jnp.pad(segments_all, ((2, 2), (0, 0)), constant_values=-1)
    same = jnp.stack([padded[offset : offset + frames] == segments_all for offset in range(5)])
    same = jnp.moveaxis(same, 0, 2)
    first_full = whole(post_first, 2)
    last_full = whole(last_half, 2)
    middle_gain = whole(middle_norm, 2)
    last_gain = whole(last_norm, 1)
    loss_scale = 2.0 / (mel_width * total_rows)
    count = total_rows * frames
    channels = middle_norm.shape[2] * 2
    masks = jnp.broadcast_to(
        jnp.transpose(same, (2, 0, 1)).reshape(5, count, 1).astype(bf16), (5, count, lanes)
    )
    wide_gain = jnp.pad(last_gain, ((0, 0), (0, channels - mel_width)))
    norms = jnp.concatenate([middle_gain, wide_gain[:, None, :]], axis=1)[:, :, None, :]
    forward_small = (
        previous,
        drops_one,
        drops_two,
        prenet_first.astype(f32),
        prenet_second.astype(f32),
        slot_hot.astype(f32),
        zone_one,
        zone_two,
        biases[0:1],
        biases[1:2],
        owner_hot,
        memory_float,
        memory_weight.astype(f32),
        query_float,
        vector_wide,
        taps_forward,
        dense_wide,
        frame_wide,
        frame_bias_wide,
    )
    (
        own_one,
        own_two,
        forward_small,
        taps_back,
        vector_row,
        targets_all,
        masks,
        first_full,
        last_full,
        norms,
    ) = lax.optimization_barrier(
        (
            own_one,
            own_two,
            forward_small,
            taps_back,
            vector_float[None, :],
            targets_all,
            masks,
            first_full,
            last_full,
            norms,
        )
    )
    weights = (own_one, exchange(own_one), own_two, peer_two)
    slot_wide, zone_one, zone_two = forward_small[5], forward_small[6], forward_small[7]
    memory_float, query_float = forward_small[11], forward_small[13]
    dense_wide, frame_wide = forward_small[16], forward_small[17]

    (
        gates_one,
        gates_two,
        prior_one,
        prior_two,
        round_one,
        round_two,
        contexts,
        mixed_all,
        alphas,
        taps,
        mixed_one,
        mixed_two,
        hidden_round,
        prenet_round,
        frame_out,
    ) = call_forward(
        unit_array,
        weights,
        forward_small,
        (
            longest,
            slots,
            hidden,
            memory_width,
            rows * text_width,
            frame_rows + padding,
            prenet_width,
        ),
    )

    middle_half = lax.optimization_barrier((middle_half, frame_out))[0]
    middle_peer = exchange(middle_half)
    states = to_frames(
        jnp.concatenate([round_one, contexts, round_two], axis=2).reshape(longest * slots, -1)
    )
    frame_in = jnp.concatenate(
        [states[:, hidden + memory_width :], states[:, hidden : hidden + memory_width]], axis=1
    )
    frame_in = frame_in[:frame_rows]
    frame_out = frame_out[:frame_rows]
    mel_own = frame_out[:, :mel_width].reshape(rows, frames, mel_width)
    stop_logit = frame_out[:, mel_width].reshape(rows, frames)
    mel_all = jnp.transpose(
        gather_rows(mel_own), (1, 0, 2)
    )
    inputs_own = jnp.concatenate([prenet_round.astype(bf16), states], axis=1)
    roomy = total_rows * frames <= 2048
    if roomy:
        inputs_own, mel_all = lax.optimization_barrier((inputs_own, mel_all))
        inputs_all = lax.all_gather(inputs_own, "batch", axis=0, tiled=True)

    if roomy:
        (
            inputs_first,
            inputs_later,
            grads_early,
            grads_last,
            norm_grads,
            grad_mel,
        ) = call_postnet(
            unit_array,
            (
                mel_all.reshape(count, mel_width),
                targets_all.reshape(count, mel_width),
                masks,
                first_full,
                middle_half,
                middle_peer,
                last_full,
                norms[0],
                norms[1],
            ),
            loss_scale,
            total_rows,
        )
        gain_grads = [norm_grads[0, layer, 0] for layer in range(5)]
        shift_grads = [norm_grads[1, layer, 0] for layer in range(5)]
        gain_grads[4], shift_grads[4] = gain_grads[4][:mel_width], shift_grads[4][:mel_width]
        grad_mel = jnp.transpose(
            lax.dynamic_slice_in_dim(
                grad_mel.reshape(frames, total_rows, mel_width), place * rows, rows, 1
            ),
            (1, 0, 2),
        )
    else:
        middle_full = whole(middle_half, 2).reshape(post_middle.shape[:2] + (channels, channels))
        kernels = [first_full, middle_full[0], middle_full[1], middle_full[2], last_full]
        gains = [middle_gain[0, layer] for layer in range(4)] + [last_gain[0]]
        shifts = [middle_gain[1, layer] for layer in range(4)] + [last_gain[1]]
        layer_in = mel_all.astype(bf16)
        layer_inputs, normed_all, inverses = [], [], []
        output = None
        for layer in range(5):
            layer_inputs.append(layer_in)
            pre_norm = by_rows(
                lambda source, same_now: post_layer(source, kernels[layer], same_now),
                roomy,
                (layer_in, same),
            )
            mean_now = jnp.sum(pre_norm, axis=(0, 1)) / frame_count
            centered = pre_norm - mean_now
            inverse = lax.rsqrt(jnp.sum(centered * centered, axis=(0, 1)) / frame_count + norm_eps)
            normed = centered * inverse
            output = normed * gains[layer] + shifts[layer]
            normed_all.append(normed)
            inverses.append(inverse)
            if layer < 4:
                layer_in = jnp.tanh(output).astype(bf16)
                if not roomy:
                    layer_in, normed_all[layer] = lax.optimization_barrier(
                        (layer_in, normed_all[layer])
                    )

        grad_post = loss_scale * (mel_all + output - targets_all)
        kernel_grads, gain_grads, shift_grads = [None] * 5, [None] * 5, [None] * 5
        grad_output = grad_post
        grad_input = None
        for layer in (4, 3, 2, 1, 0):
            if layer < 4:
                normed_all[layer] = lax.optimization_barrier(normed_all[layer])
                active = jnp.tanh(normed_all[layer] * gains[layer] + shifts[layer])
                grad_output = grad_input * (1.0 - active * active)
            shift_grads[layer] = jnp.sum(grad_output, axis=(0, 1))
            gain_grads[layer] = jnp.sum(grad_output * normed_all[layer], axis=(0, 1))
            grad_norm = (
                gains[layer]
                * inverses[layer]
                * (
                    grad_output
                    - shift_grads[layer] / frame_count
                    - normed_all[layer] * (gain_grads[layer] / frame_count)
                )
            ).astype(bf16)
            grad_input = by_rows(
                lambda grad, same_now: post_layer_back(grad, kernels[layer], same_now),
                roomy,
                (grad_norm, same),
            )
            source = layer_inputs[layer]
            if layer > 0:
                source = lax.dynamic_slice_in_dim(source, place * channel_rows, channel_rows, 2)
            kernel_grads[layer] = by_rows(post_kernel_grad, roomy, (source, grad_norm, same), True)
            kernel_grads[layer] = kernel_grads[layer].reshape(5, source.shape[2], -1)
            if not roomy:
                grad_input, kernel_grads[layer] = lax.optimization_barrier(
                    (grad_input, kernel_grads[layer])
                )
        grad_mel = loss_scale * (mel_all - targets_all) + grad_post + grad_input
        grad_mel = jnp.transpose(
            lax.dynamic_slice_in_dim(grad_mel, place * rows, rows, 1), (1, 0, 2)
        )

    if not roomy:
        inputs_own, grad_mel = lax.optimization_barrier((inputs_own, grad_mel))
        inputs_all = lax.all_gather(inputs_own, "batch", axis=0, tiled=True)

    def add_units(value, axis):
        width = value.shape[axis] // 2
        halves = [
            lax.slice_in_dim(value, start, start + width, axis=axis) for start in (0, width)
        ]
        keep = jnp.where(first_unit, halves[0], halves[1])
        give = jnp.where(first_unit, halves[1], halves[0])
        return keep + exchange(give)

    grad_stop = (jax.nn.sigmoid(stop_logit) - finished) / total_rows
    grad_frame = (
        jnp.concatenate([grad_mel, grad_stop[:, :, None]], axis=2)
        .reshape(rows * frames, mel_width + 1)
        .astype(bf16)
    )
    frame_weight_grad = lax.dot_general(
        frame_in, grad_frame, (((0,), (0,)), ((), ())), preferred_element_type=f32
    )
    frame_bias_grad = jnp.sum(grad_frame.astype(f32), axis=0)[None, :]
    grad_frame_slots = to_slots(
        jnp.pad(grad_frame, ((0, 0), (0, lanes - mel_width - 1))), f32
    ).reshape(longest, slots, lanes)

    (
        sent,
        prenet_back,
        context_grads,
        query_back,
        processed_back,
        vector_back,
        filter_back,
    ) = call_backward(
        unit_array,
        weights,
        (
            gates_one,
            gates_two,
            prior_one,
            prior_two,
            zone_one,
            zone_two,
            owner_hot,
            memory_float,
            query_float,
            vector_row,
            taps_back,
            dense_wide,
            mixed_all,
            alphas,
            taps,
            grad_frame_slots,
            frame_wide,
            slot_wide,
        ),
    )

    bias_sums = jnp.transpose(
        jnp.sum(sent.astype(f32), axis=1).reshape(-1, 4, lanes), (1, 0, 2)
    ).reshape(-1, lanes)
    slice_width = 2 * hidden // batch_size
    if slice_width != lanes:
        sent = sent.reshape(sent.shape[0], sent.shape[1], 4, -1, slice_width)
        sent = jnp.transpose(sent, (0, 3, 1, 2, 4)).reshape(batch_size, sent.shape[1], -1)
    received = lax.all_to_all(sent, "batch", 0, 0, tiled=True)
    grad_prenet = lax.dot_general(
        slot_hot.astype(f32),
        prenet_back.reshape(longest * slots, prenet_width),
        (((1,), (0,)), ((), ())),
        precision=precise,
    )

    def silu_back(grad, mixed, drops):
        gate = jax.nn.sigmoid(mixed)
        return grad * drops * 2.0 * gate * (1.0 + mixed * (1.0 - gate))

    def exact(a, b, contract):
        return lax.dot_general(
            a.astype(f32), b.astype(f32), (contract, ((), ())), precision=precise
        )

    grad_mixed_two = silu_back(grad_prenet, mixed_two, drops_two)
    prenet_second_grad = exact(hidden_round, grad_mixed_two, ((0,), (0,)))
    grad_hidden = exact(grad_mixed_two, prenet_second, ((1,), (1,)))
    grad_mixed_one = silu_back(grad_hidden, mixed_one, drops_one)
    prenet_first_grad = exact(previous, grad_mixed_one, ((0,), (0,)))

    query_weight_grad = exact(
        round_one.reshape(longest * slots, hidden),
        query_back.reshape(longest * slots, attention_width),
        ((0,), (0,)),
    )
    processed_round = processed_back.astype(bf16)
    memory_weight_grad = lax.dot_general(
        memory_now, processed_round, (((0,), (0,)), ((), ())), preferred_element_type=f32
    )
    filter_grads = jnp.roll(filter_back, -reach, axis=1)[:, ::-1][:, : location_conv.shape[2]]
    conv_grad = jnp.einsum("cka,fa->fck", filter_grads, dense_float, precision=precise)
    dense_grad = jnp.einsum("cka,fck->fa", filter_grads, conv_float, precision=precise)

    def two_columns(value):
        return jnp.concatenate([value[:, :lanes], value[:, lanes:]], axis=0)

    def to_lanes(value):
        return jnp.pad(value, ((0, 0), (0, lanes - value.shape[1])))

    filter_count, _, tap_count = location_conv.shape
    packed = [
        two_columns(prenet_first_grad),
        two_columns(prenet_second_grad),
        query_weight_grad,
        memory_weight_grad,
        to_lanes(frame_weight_grad),
        to_lanes(conv_grad.reshape(filter_count, -1)),
        dense_grad,
        bias_sums,
        vector_back,
        to_lanes(frame_bias_grad),
    ]
    heights = [value.shape[0] for value in packed]
    shares = 2 * batch_size
    surplus = -sum(heights) % (8 * shares)
    packed = jnp.concatenate(packed + [jnp.zeros((surplus, lanes), f32)], axis=0)
    packed = add_units(packed, 0)
    received, packed = lax.optimization_barrier((received, packed))

    segments_rows = segments_all.T
    carried = jnp.pad(
        (segments_rows[:, 1:] == segments_rows[:, :-1]).astype(bf16), ((0, 0), (0, 1))
    ).reshape(batch_size, frame_rows)
    carried = jnp.pad(carried, ((0, 0), (0, padding)))
    after = jnp.pad(received[:, 1:], ((0, 0), (0, 1), (0, 0))) * carried[:, :, None]
    received = received.reshape(batch_size * (frame_rows + padding), -1)
    after = after.reshape(batch_size * (frame_rows + padding), -1)

    def product(start, width, grads):
        return lax.dot_general(
            inputs_all[:, start : start + width],
            grads,
            (((0,), (0,)), ((), ())),
            preferred_element_type=f32,
        )

    pair = 2 * slice_width
    first_part = jnp.concatenate(
        [
            product(0, prenet_width, received[:, :pair]),
            product(prenet_width + hidden, memory_width, after[:, :pair]),
            product(prenet_width, hidden, after[:, :pair]),
        ],
        axis=0,
    )
    second_part = jnp.concatenate(
        [
            product(prenet_width, hidden + memory_width, received[:, pair:]),
            product(prenet_width + hidden + memory_width, hidden, after[:, pair:]),
        ],
        axis=0,
    )
    parts = jnp.concatenate(
        [
            first_part.reshape(batch_size, depth_one, pair),
            second_part.reshape(batch_size, depth_two, pair),
        ],
        axis=1,
    )
    parts = add_units(parts, 2).astype(bf16)
    depth_both = depth_one + depth_two
    parts = jnp.concatenate(
        [parts, packed.astype(bf16).reshape(batch_size, -1, slice_width)], axis=1
    )
    if roomy:
        (
            parts,
            inputs_first,
            inputs_later,
            grads_early,
            grads_last,
            alphas,
            context_grads,
            processed_round,
        ) = lax.optimization_barrier(
            (
                parts,
                inputs_first,
                inputs_later,
                grads_early,
                grads_last,
                alphas,
                context_grads,
                processed_round,
            )
        )
        kernel_grads = []
        for layer in range(5):
            if layer == 0:
                source = inputs_first
            else:
                source = lax.dynamic_slice_in_dim(
                    inputs_later[layer - 1], place * channel_rows, channel_rows, 1
                )
            grad_norm = grads_early[layer] if layer < 4 else grads_last
            kernel_grads.append(
                post_kernel_grad(
                    source.reshape(frames, total_rows, -1),
                    grad_norm.reshape(frames, total_rows, -1),
                    same,
                ).reshape(5, source.shape[1], grad_norm.shape[1])
            )
    parts = lax.all_to_all(parts, "batch", 0, 0, tiled=True)
    share = jnp.sum(parts[:, depth_both:].astype(f32), axis=0)
    parts = parts[:, :depth_both].astype(f32)
    parts = jnp.transpose(parts, (1, 0, 2)).reshape(depth_both, 4, half)

    memory_grad = lax.dot_general(
        processed_round, memory_weight, (((1,), (1,)), ((), ())), preferred_element_type=f32
    )
    for step in range(longest):
        memory_grad = memory_grad + exact(
            alphas[step][:, :slots], context_grads[step], ((1,), (0,))
        )
    memory_grad = memory_grad.reshape(rows, text_width, memory_width)
    memory_grads = jnp.stack(ordered(memory_grad, exchange(memory_grad)))
    post_first_grad = add_units(kernel_grads[0], 2)
    post_middle_grad = add_units(jnp.stack(kernel_grads[1:4]), 3)
    post_last_grad = add_units(kernel_grads[4], 2)
    middle_norm_grad = add_units(
        jnp.stack([jnp.stack(gain_grads[:4]), jnp.stack(shift_grads[:4])]), 2
    )
    last_norm_grad = add_units(jnp.stack([gain_grads[4], shift_grads[4]]), 1)

    packed = gather_far_first(share.astype(bf16)).reshape(-1, lanes)
    packed = whole(packed, 0).astype(f32)
    small, start = [], 0
    for height in heights:
        small.append(packed[start : start + height])
        start += height

    def from_columns(value):
        tall = value.shape[0] // 2
        return jnp.concatenate([value[:tall], value[tall:]], axis=1)

    biases_grad = small[7].reshape(2, 2, -1)
    biases_grad = jnp.where(first_unit, biases_grad[:, 0], biases_grad[:, 1])
    biases_grad = biases_grad.reshape(2, 4, half)
    small = [
        from_columns(small[0]),
        from_columns(small[1]),
        small[2],
        small[3],
        small[5][:, : 2 * tap_count].reshape(filter_count, 2, tap_count),
        small[6],
        small[8][0],
        small[4][:, : mel_width + 1],
        small[9][0, : mel_width + 1],
    ]
    return (
        small[0],
        small[1],
        small[2],
        small[3],
        small[4],
        small[5],
        small[6],
        parts[:depth_one],
        biases_grad[0],
        parts[depth_one:],
        biases_grad[1],
        small[7],
        small[8],
        post_first_grad,
        post_middle_grad,
        post_last_grad,
        middle_norm_grad,
        last_norm_grad,
        memory_grads,
    )


def solution(mesh):
    in_specs = (
        P(None, "batch", None, None),
        P(None, "batch", None, None),
        P(None, "batch", None),
        P(None, "batch", None),
        P(None, "batch", None, "unit"),
        P(None, "batch", None, "unit"),
        P(None, "batch", None, None),
        P(None, "batch", None, None),
        P(),
        P(),
        P(),
        P(),
        P(),
        P(),
        P(),
        P("batch", None, "unit"),
        P(None, "unit"),
        P("batch", None, "unit"),
        P(None, "unit"),
        P(),
        P(),
        P(None, None, "unit"),
        P(None, None, "batch", "unit"),
        P(None, "batch", "unit"),
        P(None, None, "unit"),
        P(None, "unit"),
    )
    out_specs = (
        P(),
        P(),
        P(),
        P(),
        P(),
        P(),
        P(),
        P("batch", None, "unit"),
        P(None, "unit"),
        P("batch", None, "unit"),
        P(None, "unit"),
        P(),
        P(),
        P(None, None, "unit"),
        P(None, None, "batch", "unit"),
        P(None, "batch", "unit"),
        P(None, None, "unit"),
        P(None, "unit"),
        P(None, "batch", None, None),
    )
    return jax.shard_map(
        on_device, mesh=mesh, in_specs=in_specs, out_specs=out_specs, check_vma=False
    )
```

```python
import functools

import jax
import jax.numpy as jnp
from jax import lax
from jax.experimental import pallas as pl
from jax.experimental.pallas import tpu as pltpu
from jax.sharding import PartitionSpec as P

precise = lax.Precision.HIGHEST
norm_eps = 1e-05
f32 = jnp.float32
bf16 = jnp.bfloat16
lanes = 128
kernel_vmem = 60 * 1024 * 1024


def split(value):
    high = value.astype(bf16)
    return high, (value - high.astype(f32)).astype(bf16)


def dot(a, b, contract=((1,), (0,))):
    return lax.dot_general(a, b, (contract, ((), ())), preferred_element_type=f32)


def dot_left(exact, value, contract=((1,), (0,))):
    high, low = split(value)
    return dot(exact, high, contract) + dot(exact, low, contract)


def dot_right(value, exact, contract=((1,), (0,))):
    high, low = split(value)
    return dot(high, exact, contract) + dot(low, exact, contract)


def dot_both(a, b, contract=((1,), (0,))):
    a_high, a_low = split(a)
    b_high, b_low = split(b)
    return (
        dot(a_high, b_high, contract) + dot(a_low, b_high, contract) + dot(a_high, b_low, contract)
    )


rows_first = ((0,), (0,))
lanes_both = ((1,), (1,))


def position_hot(position_count, text_width, reverse):
    place = lax.broadcasted_iota(jnp.int32, (position_count, lanes), 0) & (text_width - 1)
    lane = lax.broadcasted_iota(jnp.int32, (position_count, lanes), 1)
    place = (lanes - 1) - place if reverse else place + 1
    return (place == lane).astype(bf16)


def slant(value, text_width):
    blocks = [
        pltpu.roll(value[start : start + text_width], 0, 1, stride=1, stride_axis=0)
        for start in range(0, value.shape[0], text_width)
    ]
    return jnp.concatenate(blocks, axis=0)


def pad_rows(value):
    return jnp.concatenate(
        [value, jnp.zeros((lanes - value.shape[0], value.shape[1]), value.dtype)], axis=0
    )


def unit_spot(chunk, unit, per_half):
    half = (chunk // per_half + unit) % 2
    return pl.multiple_of((half * per_half + chunk % per_half) * lanes, lanes)


def gate_spot(chunk, gate, per_half):
    start = (chunk // per_half) * 4 * per_half + gate * per_half + chunk % per_half
    return pl.multiple_of(start * lanes, lanes)


def weight_copies(refs, held, place, sems, start):
    if len(refs) == 2:
        return [
            pltpu.make_async_copy(ref, held.at[side], sems.at[start + side])
            for side, ref in enumerate(refs)
        ]
    copies = []
    for index, ref in enumerate(refs):
        side, turn, which = index // 4, index // 2 % 2, index % 2
        _, _, _, tiles, rows, _ = ref.shape
        near, last = (1, 2) if turn == 0 else (2, 1)
        bit = (place // last + which) % 2
        for k in range(2):
            for far in range(4):
                device = far * 4 + k * near + bit * last
                spot = pl.ds(pl.multiple_of(device * rows, 16), rows)
                copies.append(
                    pltpu.make_async_copy(
                        ref.at[k, far // 2, far % 2],
                        held.at[side, turn * tiles : (turn + 1) * tiles, spot, :],
                        sems.at[start + len(copies)],
                    )
                )
    return copies


def forward_kernel(
    weight_count,
    unit_ref,
    *refs,
):
    weight_refs, refs = refs[:weight_count], refs[weight_count:]
    forward_body(unit_ref, weight_refs, *refs)


def backward_kernel(
    weight_count,
    unit_ref,
    *refs,
):
    weight_refs, refs = refs[:weight_count], refs[weight_count:]
    backward_body(unit_ref, weight_refs, *refs)


def forward_body(
    unit_ref,
    weight_refs,
    previous_ref,
    drop_one,
    drop_two,
    layer_one,
    layer_two,
    slot_ref,
    zone_one,
    zone_two,
    bias_one,
    bias_two,
    hot_ref,
    memory_ref,
    project_ref,
    query_ref,
    vector_ref,
    conv_ref,
    dense_ref,
    frame_ref,
    frame_bias,
    gates_one,
    gates_two,
    prior_one,
    prior_two,
    round_one,
    round_two,
    context_ref,
    mixed_ref,
    alpha_ref,
    taps_ref,
    prenet_one,
    prenet_two,
    prenet_hidden,
    prenet_out,
    frame_out,
    held_one,
    held_two,
    input_ref,
    prenet_ref,
    processed_ref,
    filter_ref,
    state_one,
    cell_one,
    state_two,
    cell_two,
    sems,
):
    unit = unit_ref[0]
    steps, slots, hidden = round_one.shape
    prenet_width = layer_two.shape[1]
    context_width = context_ref.shape[2]
    half = hidden // 2
    per_half = half // lanes
    position_count = hot_ref.shape[0]
    text_width = position_count // (slots // 4)
    each = len(weight_refs) // 2
    copies_two = weight_copies(weight_refs[each:], held_two, unit_ref[1], sems, 0)
    copies_one = weight_copies(weight_refs[:each], held_one, unit_ref[1], sems, len(copies_two))
    for copy in copies_two + copies_one:
        copy.start()
    for ref in (state_one, cell_one, state_two, cell_two):
        ref[...] = jnp.zeros_like(ref)

    def gates_into(held, depth, bias_ref, out_ref, step):
        def one(block, _):
            side = block // 2
            inputs = input_ref[:, :depth]
            for pair in range(per_half):
                tile = (block % 2) * 2 * per_half + 2 * pair
                outside = pl.ds(
                    pl.multiple_of(block * 2 * half + 2 * pair * lanes, 2 * lanes), 2 * lanes
                )
                kernel = jnp.concatenate(
                    [held[side, tile, :depth, :], held[side, tile + 1, :depth, :]], axis=1
                )
                out_ref[step, :, outside] = dot(inputs, kernel) + bias_ref[:, outside]
            return 0

        lax.fori_loop(0, 4, one, 0)

    def cell(gates_ref, zone_ref, prior_ref, state, cells, round_ref, step):
        def one(chunk, _):
            spot = pl.ds(pl.multiple_of(chunk * lanes, lanes), lanes)
            values = [
                gates_ref[step, :, pl.ds(gate_spot(chunk, gate, per_half), lanes)]
                for gate in range(4)
            ]
            zone = zone_ref[step, :, spot]
            before = cells[:, spot]
            prior_ref[step, :, spot] = before
            fresh = jax.nn.sigmoid(values[1]) * before + jax.nn.sigmoid(values[0]) * jnp.tanh(
                values[2]
            )
            output = jax.nn.sigmoid(values[3]) * jnp.tanh(fresh)
            now = zone * state[:, spot] + (1.0 - zone) * output
            state[:, spot] = now
            cells[:, spot] = zone * before + (1.0 - zone) * fresh
            round_ref[step, :, pl.ds(unit_spot(chunk, unit, per_half), lanes)] = now.astype(bf16).astype(
                f32
            )
            return 0

        lax.fori_loop(0, 2 * per_half, one, 0)

    def attention(step, location):
        inside = hot_ref[...] > 0.0
        hot = hot_ref[...].astype(bf16)
        query = pad_rows(dot(round_one[step].astype(bf16), query_ref[...].astype(bf16)))
        summed = dot_left(hot, query) + processed_ref[...]
        if location is not None:
            summed = summed + location
        mixed = jnp.tanh(summed)
        mixed_ref[step] = mixed
        energy = dot_right(mixed, vector_ref[...].astype(bf16))
        most = jnp.max(jnp.where(inside, energy, -1000000000.0), axis=0, keepdims=True)
        shifted = jnp.where(inside, jnp.exp(energy - most), 0.0)
        total = jnp.sum(shifted, axis=0, keepdims=True)
        alpha = shifted / jnp.where(total > 0.0, total, 1.0)
        alpha_ref[step] = alpha
        context = dot_right(alpha, memory_ref[...].astype(bf16), rows_first)[:slots]
        context_ref[step] = context.astype(bf16).astype(f32)

    def taps_of(step):
        spread = dot_right(
            alpha_ref[step], position_hot(position_count, text_width, True), rows_first
        )
        taps_ref[step] = slant(dot_left(hot_ref[...].astype(bf16), spread), text_width)

    def second_layer(step, depth):
        input_ref[:, :hidden] = round_one[step].astype(bf16)
        input_ref[:, hidden : hidden + context_width] = context_ref[step].astype(bf16)
        gates_into(held_two, depth, bias_two, gates_two, step)
        cell(gates_two, zone_two, prior_two, state_two, cell_two, round_two, step)

    slot_hot = slot_ref[...].astype(bf16)

    def prenet_layer(source, layer, drops, mixed_out, out):
        mixed = dot(source.astype(bf16), layer[...].astype(bf16))
        mixed_out[...] = mixed
        value = (mixed * jax.nn.sigmoid(mixed) * drops[...] * 2.0).astype(bf16)
        out[...] = value.astype(f32)
        return value

    hidden_value = prenet_layer(previous_ref[...], layer_one, drop_one, prenet_one, prenet_hidden)
    prenet_value = prenet_layer(hidden_value, layer_two, drop_two, prenet_two, prenet_out)
    prenet_slots = dot(slot_hot, prenet_value, rows_first)
    for step in range(steps):
        prenet_ref[step] = prenet_slots[step * slots : (step + 1) * slots]
    processed_ref[...] = dot(memory_ref[...].astype(bf16), project_ref[...].astype(bf16))
    for channel in range(2):
        filter_ref[channel] = dot(
            conv_ref[channel].astype(bf16), dense_ref[...].astype(bf16)
        )

    gates_one[0] = jnp.broadcast_to(bias_one[...], gates_one.shape[1:])
    cell(gates_one, zone_one, prior_one, state_one, cell_one, round_one, 0)
    attention(0, None)
    taps_of(0)
    for copy in copies_two:
        copy.wait()
    second_layer(0, hidden + context_width)
    for copy in copies_one:
        copy.wait()

    def later(step, _):
        input_ref[:, :prenet_width] = prenet_ref[step].astype(bf16)
        input_ref[:, prenet_width : prenet_width + context_width] = context_ref[step - 1].astype(
            bf16
        )
        input_ref[:, prenet_width + context_width : prenet_width + context_width + hidden] = (
            round_one[step - 1].astype(bf16)
        )
        gates_into(
            held_one, prenet_width + context_width + hidden, bias_one, gates_one, step
        )
        cell(gates_one, zone_one, prior_one, state_one, cell_one, round_one, step)
        previous = taps_ref[step - 1]
        summed = jnp.where(step == 2, taps_ref[0] + previous, previous)
        attention(step, dot_both(previous, filter_ref[0]) + dot_both(summed, filter_ref[1]))

        @pl.when(step < steps - 1)
        def _():
            taps_of(step)

        input_ref[:, hidden + context_width :] = round_two[step - 1].astype(bf16)
        second_layer(step, 2 * hidden + context_width)
        return 0

    lax.fori_loop(1, steps, later, 0)
    for step in range(steps):
        values = dot(round_two[step].astype(bf16), frame_ref[:hidden].astype(bf16)) + dot(
            context_ref[step].astype(bf16), frame_ref[hidden:].astype(bf16)
        )
        high = values.astype(bf16)
        rest = values - high.astype(f32)
        middle = rest.astype(bf16)
        low = (rest - middle.astype(f32)).astype(bf16)
        chosen = slot_hot[:, step * slots : (step + 1) * slots]
        picked = (dot(chosen, high) + dot(chosen, middle)) + dot(chosen, low)
        frame_out[...] = (frame_bias[...] if step == 0 else frame_out[...]) + picked


def backward_body(
    unit_ref,
    weight_refs,
    gates_one,
    gates_two,
    prior_one,
    prior_two,
    zone_one,
    zone_two,
    hot_ref,
    memory_ref,
    query_ref,
    vector_ref,
    conv_ref,
    dense_ref,
    mixed_ref,
    alpha_ref,
    taps_ref,
    frame_grad,
    frame_weight,
    slot_ref,
    sent_ref,
    prenet_grad,
    context_grad,
    query_grad,
    processed_grad,
    vector_grad,
    filter_grad,
    held_one,
    held_two,
    grads_one,
    grads_two,
    back_one,
    back_two,
    state_one,
    cell_one,
    state_two,
    cell_two,
    previous_grad,
    summed_grad,
    from_query,
    frame_ref,
    filter_ref,
    sems,
):
    unit = unit_ref[0]
    steps, slots, prenet_width = prenet_grad.shape
    context_width = context_grad.shape[2]
    hidden = state_one.shape[1]
    half = hidden // 2
    per_half = half // lanes
    position_count = hot_ref.shape[0]
    text_width = position_count // (slots // 4)
    each = len(weight_refs) // 2
    copies_two = weight_copies(weight_refs[each:], held_two, unit_ref[1], sems, 0)
    copies_one = weight_copies(weight_refs[:each], held_one, unit_ref[1], sems, len(copies_two))
    for copy in copies_two + copies_one:
        copy.start()
    for ref in (
        state_one,
        cell_one,
        state_two,
        cell_two,
        back_one,
        back_two,
        previous_grad,
        summed_grad,
        processed_grad,
        vector_grad,
        filter_grad,
    ):
        ref[...] = jnp.zeros_like(ref)

    def cell(gates_ref, prior_ref, zone_ref, state, cells, grads_ref, step, incoming):
        def one(chunk, _):
            spot = pl.ds(pl.multiple_of(chunk * lanes, lanes), lanes)
            places = [pl.ds(gate_spot(chunk, gate, per_half), lanes) for gate in range(4)]
            values = [gates_ref[step, :, place] for place in places]
            zone = zone_ref[step, :, spot]
            keep = 1.0 - zone
            before = prior_ref[step, :, spot]
            gate_in = jax.nn.sigmoid(values[0])
            gate_forget = jax.nn.sigmoid(values[1])
            candidate = jnp.tanh(values[2])
            gate_out = jax.nn.sigmoid(values[3])
            bent = jnp.tanh(gate_forget * before + gate_in * candidate)
            grad_state = incoming(unit_spot(chunk, unit, per_half)) + state[:, spot]
            grad_cell = cells[:, spot]
            grad_new = keep * grad_state
            grad_fresh = grad_new * gate_out * (1.0 - bent * bent) + keep * grad_cell
            state[:, spot] = zone * grad_state
            cells[:, spot] = zone * grad_cell + gate_forget * grad_fresh
            results = (
                grad_fresh * candidate * gate_in * (1.0 - gate_in),
                grad_fresh * before * gate_forget * (1.0 - gate_forget),
                grad_fresh * gate_in * (1.0 - candidate * candidate),
                grad_new * bent * gate_out * (1.0 - gate_out),
            )
            for place, result in zip(places, results):
                grads_ref[step, :, place] = result.astype(bf16)
            return 0

        lax.fori_loop(0, 2 * per_half, one, 0)

    def inputs_back(grads_ref, held, out_ref, step, blocks):
        def one(block, _):
            spot = pl.ds(pl.multiple_of(block * 256, 256), 256)
            totals = [None] * 4
            for tile in range(0, 8 * per_half, 2):
                side, inside = tile // (4 * per_half), tile % (4 * per_half)
                kernel = jnp.concatenate(
                    [held[side, inside, spot, :], held[side, inside + 1, spot, :]], axis=1
                )
                grads = grads_ref[step, :, tile * lanes : (tile + 2) * lanes]
                product = dot(grads, kernel, lanes_both)
                which = tile // 2 % 4
                totals[which] = product if totals[which] is None else totals[which] + product
            out_ref[:, spot] = (totals[0] + totals[1]) + (totals[2] + totals[3])
            return 0

        lax.fori_loop(0, blocks, one, 0)

    def attention(step, located):
        inside = hot_ref[...] > 0.0
        hot = hot_ref[...].astype(bf16)
        alpha = alpha_ref[step]
        mixed = mixed_ref[step]
        context_now = pad_rows(context_grad[step])
        weights_grad = jnp.where(
            inside,
            dot_left(memory_ref[...].astype(bf16), context_now, lanes_both)
            + previous_grad[...]
            + summed_grad[...],
            0.0,
        )
        product = alpha * weights_grad
        energy_grad = product - alpha * jnp.sum(product, axis=0, keepdims=True)
        spread = jnp.sum(energy_grad, axis=1, keepdims=True)
        vector_grad[...] += jnp.sum(spread * mixed, axis=0, keepdims=True)
        mixed_grad = spread * vector_ref[...] * (1.0 - mixed * mixed)
        processed_grad[...] += mixed_grad
        high, low = split(mixed_grad)
        query_now = (dot(hot, high, rows_first) + dot(hot, low, rows_first))[:slots]
        query_grad[step] = query_now
        from_query[...] = dot_right(query_now, query_ref[...].astype(bf16), lanes_both)
        if located:
            previous = taps_ref[step - 1]
            summed = jnp.where(step == 2, taps_ref[0] + previous, previous)
            filter_grad[0] += dot_both(previous, mixed_grad, rows_first)
            filter_grad[1] += dot_both(summed, mixed_grad, rows_first)
            place_hot = position_hot(position_count, text_width, False)

            def taps_back(channel):
                taps_grad = slant(
                    dot_both(mixed_grad, filter_ref[channel], lanes_both), text_width
                )
                gathered = dot_right(taps_grad, hot, rows_first)
                return jnp.where(inside, dot_left(place_hot, gathered), 0.0)

            previous_grad[...] = taps_back(0)
            summed_grad[...] += taps_back(1)

    def arrived(step, copies):
        @pl.when(step == steps - 1)
        def _():
            for copy in copies:
                copy.wait()

    def step_back(step, located):
        cell(
            gates_two,
            prior_two,
            zone_two,
            state_two,
            cell_two,
            grads_two,
            step,
            lambda spot: frame_ref[step, :, pl.ds(spot, lanes)]
            + back_two[:, pl.ds(spot + hidden + context_width, lanes)],
        )
        blocks_two = (hidden + context_width + (hidden if located else 0)) // 256
        if located:
            arrived(step, copies_two)
        inputs_back(grads_two, held_two, back_two, step, blocks_two)
        context_grad[step] = (
            back_two[:, hidden : hidden + context_width]
            + frame_ref[step, :, hidden:]
            + back_one[:, prenet_width : prenet_width + context_width]
        )
        attention(step, located)
        cell(
            gates_one,
            prior_one,
            zone_one,
            state_one,
            cell_one,
            grads_one,
            step,
            lambda spot: back_two[:, pl.ds(spot, lanes)]
            + from_query[:, pl.ds(spot, lanes)]
            + back_one[:, pl.ds(spot + prenet_width + context_width, lanes)],
        )
        blocks_one = (prenet_width + (hidden + context_width if located else 0)) // 256
        if located:
            arrived(step, copies_one)
        inputs_back(grads_one, held_one, back_one, step, blocks_one)
        prenet_grad[step] = back_one[:, :prenet_width]

    for channel in range(2):
        filter_ref[channel] = dot(
            conv_ref[channel].astype(bf16), dense_ref[...].astype(bf16)
        )
    for step in range(steps):
        frame_ref[step] = dot(
            frame_grad[step].astype(bf16), frame_weight[...].astype(bf16), lanes_both
        )

    def later(index, _):
        step_back(steps - 1 - index, True)
        return 0

    lax.fori_loop(0, steps - 1, later, 0)
    step_back(0, False)
    slot_hot = slot_ref[...].astype(bf16)

    def tile_out(tile, _):
        for layer, grads_ref in ((0, grads_one), (1, grads_two)):
            for side in range(2):
                place = ((side + unit) % 2) * 4 * half + tile * lanes
                grads = grads_ref[:, :, pl.ds(pl.multiple_of(place, lanes), lanes)]
                chosen = dot(slot_hot, grads.reshape(steps * slots, lanes)).astype(bf16)
                spot = (2 * layer + side) * lanes
                sent_ref[tile, :, spot : spot + lanes] = chosen
        return 0

    lax.fori_loop(0, 4 * per_half, tile_out, 0)


def call_forward(unit, weights, small, sizes):
    steps, slots, hidden, context_width, positions, frame_rows, prenet_width = sizes
    tiles = 2 * hidden // lanes
    held_one = (2, tiles, prenet_width + context_width + hidden, lanes)
    held_two = (2, tiles, 2 * hidden + context_width, lanes)

    def shape(*dims):
        return jax.ShapeDtypeStruct(dims, f32)

    outs = [
        shape(steps, slots, 4 * hidden),
        shape(steps, slots, 4 * hidden),
        shape(steps, slots, hidden),
        shape(steps, slots, hidden),
        shape(steps, slots, hidden),
        shape(steps, slots, hidden),
        shape(steps, slots, context_width),
        shape(steps, positions, lanes),
        shape(steps, positions, lanes),
        shape(steps - 1, positions, lanes),
        shape(frame_rows, prenet_width),
        shape(frame_rows, prenet_width),
        shape(frame_rows, prenet_width),
        shape(frame_rows, prenet_width),
        shape(frame_rows, lanes),
    ]
    vmem = pl.BlockSpec(memory_space=pltpu.VMEM)
    return pl.pallas_call(
        functools.partial(forward_kernel, len(weights)),
        out_shape=outs,
        in_specs=[pl.BlockSpec(memory_space=pltpu.SMEM)]
        + [pl.BlockSpec(memory_space=pl.ANY)] * len(weights)
        + [vmem] * len(small),
        out_specs=[vmem] * len(outs),
        scratch_shapes=[
            pltpu.VMEM(held_one, bf16),
            pltpu.VMEM(held_two, bf16),
            pltpu.VMEM((slots, held_two[2]), bf16),
            pltpu.VMEM((steps, slots, prenet_width), f32),
            pltpu.VMEM((positions, lanes), f32),
            pltpu.VMEM((2, lanes, lanes), f32),
            pltpu.VMEM((slots, hidden), f32),
            pltpu.VMEM((slots, hidden), f32),
            pltpu.VMEM((slots, hidden), f32),
            pltpu.VMEM((slots, hidden), f32),
            pltpu.SemaphoreType.DMA((8 * len(weights),)),
        ],
        compiler_params=pltpu.CompilerParams(vmem_limit_bytes=kernel_vmem),
        name="decoder_forward",
    )(unit, *weights, *small)


def call_backward(unit, weights, small, prenet_width):
    gates_one = small[0]
    steps, slots, gate_width = gates_one.shape
    hidden = gate_width // 4
    positions, context_width = small[7].shape
    tiles = 2 * hidden // lanes
    held_one = (2, tiles, prenet_width + context_width + hidden, lanes)
    held_two = (2, tiles, 2 * hidden + context_width, lanes)

    def shape(dims, kind):
        return jax.ShapeDtypeStruct(dims, kind)

    outs = [
        shape((gate_width // (2 * lanes), small[-1].shape[0], 4 * lanes), bf16),
        shape((steps, slots, prenet_width), f32),
        shape((steps, slots, context_width), f32),
        shape((steps, slots, lanes), f32),
        shape((positions, lanes), f32),
        shape((1, lanes), f32),
        shape((2, lanes, lanes), f32),
    ]
    vmem = pl.BlockSpec(memory_space=pltpu.VMEM)
    return pl.pallas_call(
        functools.partial(backward_kernel, len(weights)),
        out_shape=outs,
        in_specs=[pl.BlockSpec(memory_space=pltpu.SMEM)]
        + [pl.BlockSpec(memory_space=pl.ANY)] * len(weights)
        + [vmem] * len(small),
        out_specs=[vmem] * len(outs),
        scratch_shapes=[
            pltpu.VMEM(held_one, bf16),
            pltpu.VMEM(held_two, bf16),
            pltpu.VMEM((steps, slots, gate_width), bf16),
            pltpu.VMEM((steps, slots, gate_width), bf16),
            pltpu.VMEM((slots, held_one[2]), f32),
            pltpu.VMEM((slots, held_two[2]), f32),
            pltpu.VMEM((slots, hidden), f32),
            pltpu.VMEM((slots, hidden), f32),
            pltpu.VMEM((slots, hidden), f32),
            pltpu.VMEM((slots, hidden), f32),
            pltpu.VMEM((positions, lanes), f32),
            pltpu.VMEM((positions, lanes), f32),
            pltpu.VMEM((slots, hidden), f32),
            pltpu.VMEM((steps, slots, hidden + context_width), f32),
            pltpu.VMEM((2, lanes, lanes), f32),
            pltpu.SemaphoreType.DMA((8 * len(weights),)),
        ],
        compiler_params=pltpu.CompilerParams(vmem_limit_bytes=kernel_vmem),
        name="decoder_backward",
    )(unit, *weights, *small)


def postnet_kernel(
    mel_width,
    loss_scale,
    unit_ref,
    mel_ref,
    target_ref,
    mask_ref,
    first_ref,
    own_ref,
    peer_ref,
    last_ref,
    gain_ref,
    shift_ref,
    inputs_first,
    inputs_later,
    grads_early,
    grads_last,
    norm_grads,
    mel_grad,
    padded,
    padded_mel,
    held,
    normed_early,
    normed_last,
    inverse_ref,
    post_grad,
):
    unit = unit_ref[0]
    count, channels = held.shape
    side = channels // 2
    frames = padded.shape[0] - count
    rows_each = frames // 4
    chunk = 2 * rows_each
    tall = float(count)
    body_rows = slice(2 * rows_each, 2 * rows_each + count)

    for ref in (padded, padded_mel):
        ref[: 2 * rows_each] = jnp.zeros((2 * rows_each, ref.shape[1]), bf16)
        ref[2 * rows_each + count :] = jnp.zeros((2 * rows_each, ref.shape[1]), bf16)

    def piece(source, start, tap, width, lane=None):
        spot = pl.ds(pl.multiple_of(start + tap * rows_each, rows_each), chunk)
        mask = mask_ref[tap, pl.ds(pl.multiple_of(start, rows_each), chunk), :]
        if width < lanes:
            mask = mask[:, :width]
        else:
            mask = jnp.concatenate([mask] * (width // lanes), axis=1)
        value = source[spot, :] if lane is None else source[spot, pl.ds(lane, width)]
        return value * mask

    def chunks(work):
        def one(index, _):
            work(pl.multiple_of(index * chunk, chunk))
            return 0

        lax.fori_loop(0, count // chunk, one, 0)

    def half_spot(which):
        return pl.multiple_of(((which + unit) % 2) * side, side)

    def norm_forward(value, layer, lane, width):
        mean = jnp.sum(value, axis=0, keepdims=True) / tall
        centered = value - mean
        inverse = lax.rsqrt(jnp.sum(centered * centered, axis=0, keepdims=True) / tall + norm_eps)
        inverse_ref[layer, :, pl.ds(lane, width)] = inverse
        return centered * inverse

    def each_lane_block(work):
        def one(index, _):
            work(pl.multiple_of(index * lanes, lanes))
            return 0

        lax.fori_loop(0, channels // lanes, one, 0)

    def activate(layer):
        def block(lane):
            spot = pl.ds(lane, lanes)
            normed = norm_forward(held[:, spot], layer, lane, lanes)
            normed_early[layer, :, spot] = normed
            active = jnp.tanh(
                normed * gain_ref[layer, :, spot] + shift_ref[layer, :, spot]
            ).astype(bf16)
            inputs_later[layer, :, spot] = active
            padded[body_rows, spot] = active

        each_lane_block(block)

    source = mel_ref[...].astype(bf16)
    inputs_first[...] = source
    padded_mel[body_rows] = source

    def first_chunk(start):
        total = None
        for tap in range(5):
            product = dot(piece(padded_mel, start, tap, mel_width), first_ref[tap])
            total = product if total is None else total + product
        held[pl.ds(start, chunk), :] = total

    chunks(first_chunk)
    activate(0)

    def middle(index, _):
        def middle_chunk(start):
            totals = [None, None]
            for tap in range(5):
                value = piece(padded, start, tap, channels)
                for which, ref in ((0, own_ref), (1, peer_ref)):
                    product = dot(value, ref[index * 5 + tap])
                    totals[which] = product if tap == 0 else totals[which] + product
            for which in range(2):
                held[pl.ds(start, chunk), pl.ds(half_spot(which), side)] = totals[which]

        chunks(middle_chunk)
        activate(index + 1)
        return 0

    lax.fori_loop(0, 3, middle, 0)

    def last_chunk(start):
        total = None
        for tap in range(5):
            product = dot(piece(padded, start, tap, channels), last_ref[tap])
            total = product if total is None else total + product
        normed_last[pl.ds(start, chunk), :] = total

    chunks(last_chunk)
    normed = norm_forward(normed_last[...], 4, 0, mel_width)
    normed_last[...] = normed

    def norm_back(grad, normed, layer, lane, width):
        spot = pl.ds(lane, width)
        shift_grad = jnp.sum(grad, axis=0, keepdims=True)
        gain_grad = jnp.sum(grad * normed, axis=0, keepdims=True)
        norm_grads[0, layer, :, spot] = gain_grad
        norm_grads[1, layer, :, spot] = shift_grad
        return (
            gain_ref[layer, :, spot]
            * inverse_ref[layer, :, spot]
            * (grad - shift_grad / tall - normed * (gain_grad / tall))
        ).astype(bf16)

    output = normed * gain_ref[4, :, :mel_width] + shift_ref[4, :, :mel_width]
    grad = loss_scale * (mel_ref[...] + output - target_ref[...])
    post_grad[...] = grad
    grad_norm = norm_back(grad, normed, 4, 0, mel_width)
    grads_last[...] = grad_norm
    padded_mel[body_rows] = grad_norm

    def last_back(start):
        total = None
        for tap in range(5):
            product = dot(
                piece(padded_mel, start, tap, mel_width), last_ref[4 - tap], lanes_both
            )
            total = product if total is None else total + product
        held[pl.ds(start, chunk), :] = total

    chunks(last_back)

    def deactivate(layer):
        def block(lane):
            spot = pl.ds(lane, lanes)
            normed = normed_early[layer, :, spot]
            active = jnp.tanh(normed * gain_ref[layer, :, spot] + shift_ref[layer, :, spot])
            grad = held[:, spot] * (1.0 - active * active)
            grad_norm = norm_back(grad, normed, layer, lane, lanes)
            grads_early[layer, :, spot] = grad_norm
            padded[body_rows, spot] = grad_norm

        each_lane_block(block)

    def middle_back(back, _):
        index = 2 - back
        deactivate(index + 1)

        def chunk_back(start):
            total = None
            for which, ref in ((0, own_ref), (1, peer_ref)):
                for tap in range(5):
                    product = dot(
                        piece(padded, start, tap, side, half_spot(which)),
                        ref[index * 5 + 4 - tap],
                        lanes_both,
                    )
                    total = product if total is None else total + product
            held[pl.ds(start, chunk), :] = total

        chunks(chunk_back)
        return 0

    lax.fori_loop(0, 3, middle_back, 0)
    deactivate(0)

    def first_back(start):
        total = None
        for tap in range(5):
            product = dot(piece(padded, start, tap, channels), first_ref[4 - tap], lanes_both)
            total = product if total is None else total + product
        spot = pl.ds(start, chunk)
        mel_grad[spot, :] = (
            loss_scale * (mel_ref[spot, :] - target_ref[spot, :]) + post_grad[spot, :] + total
        )

    chunks(first_back)


def call_postnet(unit, small, loss_scale, rows_all):
    mel = small[0]
    count, mel_width = mel.shape
    channels = small[3].shape[2]

    def shape(kind, *dims):
        return jax.ShapeDtypeStruct(dims, kind)

    outs = [
        shape(bf16, count, mel_width),
        shape(bf16, 4, count, channels),
        shape(bf16, 4, count, channels),
        shape(bf16, count, mel_width),
        shape(f32, 2, 5, 1, channels),
        shape(f32, count, mel_width),
    ]
    vmem = pl.BlockSpec(memory_space=pltpu.VMEM)
    tall = count + 4 * rows_all
    return pl.pallas_call(
        functools.partial(postnet_kernel, mel_width, loss_scale),
        out_shape=outs,
        in_specs=[pl.BlockSpec(memory_space=pltpu.SMEM)] + [vmem] * len(small),
        out_specs=[vmem] * len(outs),
        scratch_shapes=[
            pltpu.VMEM((tall, channels), bf16),
            pltpu.VMEM((tall, mel_width), bf16),
            pltpu.VMEM((count, channels), f32),
            pltpu.VMEM((4, count, channels), f32),
            pltpu.VMEM((count, mel_width), f32),
            pltpu.VMEM((5, 1, channels), f32),
            pltpu.VMEM((count, mel_width), f32),
        ],
        compiler_params=pltpu.CompilerParams(vmem_limit_bytes=kernel_vmem),
        name="postnet",
    )(unit, *small)


def shifted_frames(source, same):
    steps = source.shape[0]
    padded = jnp.pad(source, ((2, 2), (0, 0), (0, 0)))
    return [
        padded[offset : offset + steps] * same[:, :, offset, None].astype(source.dtype)
        for offset in range(5)
    ]


def by_rows(work, roomy, arrays, summed=False):
    if roomy:
        return work(*arrays)
    parts = arrays[0].shape[1] // 192

    def cut(value):
        value = value.reshape((value.shape[0], parts, -1) + value.shape[2:])
        return jnp.moveaxis(value, 1, 0)

    pieces = tuple(cut(value) for value in arrays)
    if summed:
        first = jax.eval_shape(work, *[value[0] for value in pieces])
        start = jnp.zeros(first.shape, first.dtype)
        return lax.scan(lambda total, now: (total + work(*now), None), start, pieces)[0]
    result = jnp.moveaxis(lax.map(lambda now: work(*now), pieces), 0, 1)
    return result.reshape((result.shape[0], -1) + result.shape[3:])


def post_layer(source, kernel, same):
    wide = jnp.concatenate(shifted_frames(source, same), axis=2)
    return jnp.einsum(
        "src,co->sro", wide, kernel.reshape(-1, kernel.shape[2]), preferred_element_type=f32
    )


def post_layer_back(grad, kernel, same):
    wide = jnp.concatenate(shifted_frames(grad, same), axis=2)
    turned = jnp.transpose(kernel[::-1], (0, 2, 1)).reshape(-1, kernel.shape[1])
    return jnp.einsum("sro,oc->src", wide, turned, preferred_element_type=f32)


def post_kernel_grad(source, grad, same):
    wide = jnp.concatenate(shifted_frames(source, same), axis=2)
    return jnp.einsum("src,sro->co", wide, grad, preferred_element_type=f32)


def on_device(
    memory,
    targets,
    segments,
    text_lengths,
    zone_first,
    zone_second,
    drop_first,
    drop_second,
    prenet_first,
    prenet_second,
    query_weight,
    memory_weight,
    location_conv,
    location_dense,
    energy_vector,
    lstm_first,
    bias_first,
    lstm_second,
    bias_second,
    frame_weight,
    frame_bias,
    post_first,
    post_middle,
    post_last,
    middle_norm,
    last_norm,
):
    micro_count, rows, text_width, memory_width = memory.shape
    frames = segments.shape[2]
    utterances = text_lengths.shape[2]
    mel_width = targets.shape[3]
    hidden = query_weight.shape[0]
    prenet_width = prenet_first.shape[1]
    attention_width = query_weight.shape[1]
    half = lstm_first.shape[2]
    depth_one, depth_two = lstm_first.shape[0], lstm_second.shape[0]
    unit = lax.axis_index("unit")
    place = lax.axis_index("batch")
    batch_size = lax.axis_size("batch")
    total_rows = rows * batch_size
    frame_count = float(total_rows * frames)
    first_unit = unit == 0
    longest = 3
    slots = 4 * rows

    def exchange(value):
        return lax.ppermute(value, "unit", [(0, 1), (1, 0)])

    def ordered(own, peer):
        return jnp.where(first_unit, own, peer), jnp.where(first_unit, peer, own)

    def whole(value, axis):
        return jnp.concatenate(ordered(value, exchange(value)), axis=axis)

    def mine(value):
        return lax.dynamic_index_in_dim(value, unit, 0, keepdims=False)

    def others(value):
        return lax.dynamic_index_in_dim(value, 1 - unit, 0, keepdims=False)

    def swapped(value, bit):
        pairs = [(index, index ^ bit) for index in range(batch_size)]
        other = lax.ppermute(value, "batch", pairs)
        upper = (place & bit) != 0
        return jnp.where(upper, other, value), jnp.where(upper, value, other)

    def gather_far_first(value):
        inner, bit, count = value.ndim, batch_size // 2, 0
        while bit:
            value = jnp.stack(swapped(value, bit))
            bit //= 2
            count += 1
        order = tuple(range(count - 1, -1, -1)) + tuple(range(count, count + inner))
        return jnp.transpose(value, order).reshape((batch_size,) + value.shape[count:])

    def gather_rows(value):
        bit = 1
        while bit < batch_size:
            value = jnp.concatenate(swapped(value, bit), axis=0)
            bit *= 2
        return value

    def to_tiles(value):
        return jnp.transpose(value.reshape(value.shape[0], -1, lanes), (1, 0, 2))

    def along_z(value):
        value = jnp.stack(swapped(value, 8))
        return jnp.stack(swapped(value, 4), axis=1)

    def in_plane(value):
        pieces = []
        tall = value.shape[2] // 2
        for turn, (near, last) in enumerate(((1, 2), (2, 1))):
            part = jnp.stack(swapped(value[:, :, turn * tall : (turn + 1) * tall], near))
            pairs = [(index, index ^ last) for index in range(batch_size)]
            pieces += [part, lax.ppermute(part, "batch", pairs)]
        return tuple(pieces)

    crossed = batch_size == 16 and depth_one % 16 == 0 and depth_two % 16 == 0
    if crossed:
        line_two = along_z(to_tiles(lstm_second))
        tiles_one, line_two = lax.optimization_barrier((to_tiles(lstm_first), line_two))
        line_one = along_z(tiles_one)
        own_two = in_plane(line_two)
        own_one = in_plane(line_one)
        peer_two = tuple(exchange(value) for value in own_two)
        post_source = lax.optimization_barrier((post_middle, own_two[-1]))[0]
    else:
        own_two = (lax.all_gather(to_tiles(lstm_second), "batch", axis=1, tiled=True),)
        own_one = (lax.all_gather(to_tiles(lstm_first), "batch", axis=1, tiled=True),)
        peer_two = (exchange(own_two[0]),)
        post_source = post_middle
    channel_rows = post_middle.shape[2]
    middle_width = post_middle.shape[3]
    middle_half = lax.all_gather(
        post_source.reshape(-1, channel_rows, middle_width), "batch", axis=1, tiled=True
    )
    last_half = gather_rows(jnp.transpose(post_last, (1, 0, 2)).reshape(channel_rows, -1))
    last_half = jnp.transpose(
        last_half.reshape(-1, post_last.shape[0], post_last.shape[2]), (1, 0, 2)
    )
    memory_now = mine(memory).reshape(rows * text_width, memory_width)
    segments_now = mine(segments)
    targets_now = mine(targets)
    frame_info = gather_rows(
        jnp.concatenate([targets_now, segments_now[:, :, None].astype(bf16)], axis=2).astype(f32)
    )

    same_frames = segments_now[:, :, None] == segments_now[:, None, :]
    earlier = jnp.tril(jnp.ones((frames, frames), jnp.bool_), -1)
    order = jnp.sum((same_frames & earlier[None]).astype(jnp.int32), axis=2)
    slot_of = order * slots + segments_now * rows + jnp.arange(rows, dtype=jnp.int32)[:, None]
    frame_rows = rows * frames
    padding = -frame_rows % 16
    slot_hot = (
        jnp.pad(slot_of.reshape(-1, 1), ((0, padding), (0, 0)), constant_values=-1)
        == jnp.arange(longest * slots, dtype=jnp.int32)[None, :]
    ).astype(bf16)
    slot_hot_frames = slot_hot[:frame_rows]
    carry_on = jnp.pad(
        (segments_now[:, 1:] == segments_now[:, :-1]).astype(f32), ((0, 0), (1, 0))
    )
    finished = jnp.pad(
        (segments_now[:, 1:] != segments_now[:, :-1]).astype(f32),
        ((0, 0), (0, 1)),
        constant_values=1.0,
    )

    def to_slots(value, kind=bf16):
        return lax.dot_general(
            slot_hot_frames,
            value.astype(bf16),
            (((0,), (0,)), ((), ())),
            preferred_element_type=f32,
        ).astype(kind)

    def to_frames(value):
        return jnp.dot(slot_hot, value.astype(bf16), preferred_element_type=f32).astype(bf16)

    def pad_frames(value):
        return jnp.pad(
            value.astype(f32).reshape(frame_rows, -1), ((0, padding), (0, 0))
        )

    previous = pad_frames(
        jnp.pad(targets_now[:, :-1], ((0, 0), (1, 0), (0, 0))).astype(f32)
        * carry_on[:, :, None]
    )
    drops_one = pad_frames(mine(drop_first))
    drops_two = pad_frames(mine(drop_second))

    zones_own = jnp.concatenate([mine(zone_first), mine(zone_second)], axis=2).astype(f32)
    zones_peer = exchange(
        jnp.concatenate([others(zone_first), others(zone_second)], axis=2).astype(f32)
    )
    zones_slots = to_slots(
        jnp.concatenate([zones_own, zones_peer], axis=2).reshape(rows * frames, -1), f32
    ).reshape(longest, slots, 4 * half)
    zone_one = jnp.concatenate(
        [zones_slots[:, :, :half], zones_slots[:, :, 2 * half : 3 * half]], axis=2
    )
    zone_two = jnp.concatenate(
        [zones_slots[:, :, half : 2 * half], zones_slots[:, :, 3 * half :]], axis=2
    )
    biases = jnp.stack([bias_first.reshape(-1), bias_second.reshape(-1)])
    biases = jnp.concatenate([biases, exchange(biases)], axis=1)
    text_ends = jnp.cumsum(mine(text_lengths), axis=1)
    owner = jnp.sum(
        (jnp.arange(text_width, dtype=jnp.int32)[None, :, None] >= text_ends[:, None, :]).astype(
            jnp.int32
        ),
        axis=2,
    )
    owner_slot = owner * rows + jnp.arange(rows, dtype=jnp.int32)[:, None]
    owner_hot = (
        owner_slot.reshape(-1, 1) == jnp.arange(lanes, dtype=jnp.int32)[None, :]
    ).astype(f32)
    conv_float = location_conv.astype(f32)
    dense_float = location_dense.astype(f32)
    reach = location_conv.shape[2] // 2
    taps_first = jnp.transpose(conv_float, (1, 2, 0))
    taps_first = jnp.pad(
        taps_first,
        ((0, 0), (0, lanes - taps_first.shape[1]), (0, lanes - taps_first.shape[2])),
    )
    dense_wide = jnp.pad(dense_float, ((0, lanes - dense_float.shape[0]), (0, 0)))
    taps_forward = jnp.roll(taps_first[:, ::-1], reach, axis=1)
    taps_back = jnp.roll(taps_first, 1 - reach, axis=1)
    frame_wide = jnp.pad(
        frame_weight.astype(f32), ((0, 0), (0, lanes - frame_weight.shape[1]))
    )
    frame_bias_wide = jnp.pad(frame_bias, (0, lanes - frame_bias.shape[0]))[None, :]
    vector_float = energy_vector.astype(f32)
    vector_wide = jnp.broadcast_to(vector_float[:, None], (attention_width, lanes))
    memory_float = memory_now.astype(f32)
    query_float = query_weight.astype(f32)
    unit_array = jnp.stack([unit, place]).astype(jnp.int32)

    targets_all = jnp.transpose(frame_info[:, :, :mel_width].astype(f32), (1, 0, 2))
    segments_all = jnp.transpose(frame_info[:, :, mel_width].astype(jnp.int32))
    padded = jnp.pad(segments_all, ((2, 2), (0, 0)), constant_values=-1)
    same = jnp.stack([padded[offset : offset + frames] == segments_all for offset in range(5)])
    same = jnp.moveaxis(same, 0, 2)
    first_full = whole(post_first, 2)
    last_full = whole(last_half, 2)
    middle_gain = whole(middle_norm, 2)
    last_gain = whole(last_norm, 1)
    loss_scale = 2.0 / (mel_width * total_rows)
    count = total_rows * frames
    channels = middle_norm.shape[2] * 2
    masks = jnp.broadcast_to(
        jnp.transpose(same, (2, 0, 1)).reshape(5, count, 1).astype(bf16), (5, count, lanes)
    )
    wide_gain = jnp.pad(last_gain, ((0, 0), (0, channels - mel_width)))
    norms = jnp.concatenate([middle_gain, wide_gain[:, None, :]], axis=1)[:, :, None, :]
    forward_small = (
        previous,
        drops_one,
        drops_two,
        prenet_first.astype(f32),
        prenet_second.astype(f32),
        slot_hot.astype(f32),
        zone_one,
        zone_two,
        biases[0:1],
        biases[1:2],
        owner_hot,
        memory_float,
        memory_weight.astype(f32),
        query_float,
        vector_wide,
        taps_forward,
        dense_wide,
        frame_wide,
        frame_bias_wide,
    )
    (
        own_one,
        own_two,
        forward_small,
        taps_back,
        vector_row,
        targets_all,
        masks,
        first_full,
        last_full,
        norms,
    ) = lax.optimization_barrier(
        (
            own_one,
            own_two,
            forward_small,
            taps_back,
            vector_float[None, :],
            targets_all,
            masks,
            first_full,
            last_full,
            norms,
        )
    )
    own_one, peer_two = lax.optimization_barrier((own_one, peer_two))
    peer_one = tuple(exchange(value) for value in own_one)
    weights = own_one + peer_one + own_two + peer_two
    slot_wide, zone_one, zone_two = forward_small[5], forward_small[6], forward_small[7]
    memory_float, query_float = forward_small[11], forward_small[13]
    dense_wide, frame_wide = forward_small[16], forward_small[17]

    (
        gates_one,
        gates_two,
        prior_one,
        prior_two,
        round_one,
        round_two,
        contexts,
        mixed_all,
        alphas,
        taps,
        mixed_one,
        mixed_two,
        hidden_round,
        prenet_round,
        frame_out,
    ) = call_forward(
        unit_array,
        weights,
        forward_small,
        (
            longest,
            slots,
            hidden,
            memory_width,
            rows * text_width,
            frame_rows + padding,
            prenet_width,
        ),
    )

    middle_half = lax.optimization_barrier((middle_half, frame_out))[0]
    middle_peer = exchange(middle_half)
    states = to_frames(
        jnp.concatenate([round_one, contexts, round_two], axis=2).reshape(longest * slots, -1)
    )
    frame_in = jnp.concatenate(
        [states[:, hidden + memory_width :], states[:, hidden : hidden + memory_width]], axis=1
    )
    frame_in = frame_in[:frame_rows]
    frame_out = frame_out[:frame_rows]
    mel_own = frame_out[:, :mel_width].reshape(rows, frames, mel_width)
    stop_logit = frame_out[:, mel_width].reshape(rows, frames)
    mel_all = jnp.transpose(
        gather_rows(mel_own), (1, 0, 2)
    )
    inputs_own = jnp.concatenate([prenet_round.astype(bf16), states], axis=1)
    roomy = total_rows * frames <= 2048
    if roomy:
        inputs_own, mel_all = lax.optimization_barrier((inputs_own, mel_all))
        inputs_all = lax.all_gather(inputs_own, "batch", axis=0, tiled=True)

    if roomy:
        (
            inputs_first,
            inputs_later,
            grads_early,
            grads_last,
            norm_grads,
            grad_mel,
        ) = call_postnet(
            unit_array,
            (
                mel_all.reshape(count, mel_width),
                targets_all.reshape(count, mel_width),
                masks,
                first_full,
                middle_half,
                middle_peer,
                last_full,
                norms[0],
                norms[1],
            ),
            loss_scale,
            total_rows,
        )
        gain_grads = [norm_grads[0, layer, 0] for layer in range(5)]
        shift_grads = [norm_grads[1, layer, 0] for layer in range(5)]
        gain_grads[4], shift_grads[4] = gain_grads[4][:mel_width], shift_grads[4][:mel_width]
        grad_mel = jnp.transpose(
            lax.dynamic_slice_in_dim(
                grad_mel.reshape(frames, total_rows, mel_width), place * rows, rows, 1
            ),
            (1, 0, 2),
        )
    else:
        middle_full = whole(middle_half, 2).reshape(post_middle.shape[:2] + (channels, channels))
        kernels = [first_full, middle_full[0], middle_full[1], middle_full[2], last_full]
        gains = [middle_gain[0, layer] for layer in range(4)] + [last_gain[0]]
        shifts = [middle_gain[1, layer] for layer in range(4)] + [last_gain[1]]
        layer_in = mel_all.astype(bf16)
        layer_inputs, normed_all, inverses = [], [], []
        output = None
        for layer in range(5):
            layer_inputs.append(layer_in)
            pre_norm = by_rows(
                lambda source, same_now: post_layer(source, kernels[layer], same_now),
                roomy,
                (layer_in, same),
            )
            mean_now = jnp.sum(pre_norm, axis=(0, 1)) / frame_count
            centered = pre_norm - mean_now
            inverse = lax.rsqrt(jnp.sum(centered * centered, axis=(0, 1)) / frame_count + norm_eps)
            normed = centered * inverse
            output = normed * gains[layer] + shifts[layer]
            normed_all.append(normed)
            inverses.append(inverse)
            if layer < 4:
                layer_in = jnp.tanh(output).astype(bf16)
                if not roomy:
                    layer_in, normed_all[layer] = lax.optimization_barrier(
                        (layer_in, normed_all[layer])
                    )

        grad_post = loss_scale * (mel_all + output - targets_all)
        kernel_grads, gain_grads, shift_grads = [None] * 5, [None] * 5, [None] * 5
        grad_output = grad_post
        grad_input = None
        for layer in (4, 3, 2, 1, 0):
            if layer < 4:
                normed_all[layer] = lax.optimization_barrier(normed_all[layer])
                active = jnp.tanh(normed_all[layer] * gains[layer] + shifts[layer])
                grad_output = grad_input * (1.0 - active * active)
            shift_grads[layer] = jnp.sum(grad_output, axis=(0, 1))
            gain_grads[layer] = jnp.sum(grad_output * normed_all[layer], axis=(0, 1))
            grad_norm = (
                gains[layer]
                * inverses[layer]
                * (
                    grad_output
                    - shift_grads[layer] / frame_count
                    - normed_all[layer] * (gain_grads[layer] / frame_count)
                )
            ).astype(bf16)
            grad_input = by_rows(
                lambda grad, same_now: post_layer_back(grad, kernels[layer], same_now),
                roomy,
                (grad_norm, same),
            )
            source = layer_inputs[layer]
            if layer > 0:
                source = lax.dynamic_slice_in_dim(source, place * channel_rows, channel_rows, 2)
            kernel_grads[layer] = by_rows(post_kernel_grad, roomy, (source, grad_norm, same), True)
            kernel_grads[layer] = kernel_grads[layer].reshape(5, source.shape[2], -1)
            if not roomy:
                grad_input, kernel_grads[layer] = lax.optimization_barrier(
                    (grad_input, kernel_grads[layer])
                )
        grad_mel = loss_scale * (mel_all - targets_all) + grad_post + grad_input
        grad_mel = jnp.transpose(
            lax.dynamic_slice_in_dim(grad_mel, place * rows, rows, 1), (1, 0, 2)
        )

    if not roomy:
        inputs_own, grad_mel = lax.optimization_barrier((inputs_own, grad_mel))
        inputs_all = lax.all_gather(inputs_own, "batch", axis=0, tiled=True)

    def add_units(value, axis):
        width = value.shape[axis] // 2
        halves = [
            lax.slice_in_dim(value, start, start + width, axis=axis) for start in (0, width)
        ]
        keep = jnp.where(first_unit, halves[0], halves[1])
        give = jnp.where(first_unit, halves[1], halves[0])
        return keep + exchange(give)

    grad_stop = (jax.nn.sigmoid(stop_logit) - finished) / total_rows
    grad_frame = (
        jnp.concatenate([grad_mel, grad_stop[:, :, None]], axis=2)
        .reshape(rows * frames, mel_width + 1)
        .astype(bf16)
    )
    frame_weight_grad = lax.dot_general(
        frame_in, grad_frame, (((0,), (0,)), ((), ())), preferred_element_type=f32
    )
    frame_bias_grad = jnp.sum(grad_frame.astype(f32), axis=0)[None, :]
    grad_frame_slots = to_slots(
        jnp.pad(grad_frame, ((0, 0), (0, lanes - mel_width - 1))), f32
    ).reshape(longest, slots, lanes)

    (
        sent,
        prenet_back,
        context_grads,
        query_back,
        processed_back,
        vector_back,
        filter_back,
    ) = call_backward(
        unit_array,
        weights,
        (
            gates_one,
            gates_two,
            prior_one,
            prior_two,
            zone_one,
            zone_two,
            owner_hot,
            memory_float,
            query_float,
            vector_row,
            taps_back,
            dense_wide,
            mixed_all,
            alphas,
            taps,
            grad_frame_slots,
            frame_wide,
            slot_wide,
        ),
        prenet_width,
    )

    bias_sums = jnp.transpose(
        jnp.sum(sent.astype(f32), axis=1).reshape(-1, 4, lanes), (1, 0, 2)
    ).reshape(-1, lanes)
    slice_width = 2 * hidden // batch_size
    if slice_width != lanes:
        sent = sent.reshape(sent.shape[0], sent.shape[1], 4, -1, slice_width)
        sent = jnp.transpose(sent, (0, 3, 1, 2, 4)).reshape(batch_size, sent.shape[1], -1)
    received = lax.all_to_all(sent, "batch", 0, 0, tiled=True)
    grad_prenet = lax.dot_general(
        slot_hot.astype(f32),
        prenet_back.reshape(longest * slots, prenet_width),
        (((1,), (0,)), ((), ())),
        precision=precise,
    )

    def silu_back(grad, mixed, drops):
        gate = jax.nn.sigmoid(mixed)
        return grad * drops * 2.0 * gate * (1.0 + mixed * (1.0 - gate))

    def exact(a, b, contract):
        return lax.dot_general(
            a.astype(f32), b.astype(f32), (contract, ((), ())), precision=precise
        )

    grad_mixed_two = silu_back(grad_prenet, mixed_two, drops_two)
    prenet_second_grad = exact(hidden_round, grad_mixed_two, ((0,), (0,)))
    grad_hidden = exact(grad_mixed_two, prenet_second, ((1,), (1,)))
    grad_mixed_one = silu_back(grad_hidden, mixed_one, drops_one)
    prenet_first_grad = exact(previous, grad_mixed_one, ((0,), (0,)))

    query_weight_grad = exact(
        round_one.reshape(longest * slots, hidden),
        query_back.reshape(longest * slots, attention_width),
        ((0,), (0,)),
    )
    processed_round = processed_back.astype(bf16)
    memory_weight_grad = lax.dot_general(
        memory_now, processed_round, (((0,), (0,)), ((), ())), preferred_element_type=f32
    )
    filter_grads = jnp.roll(filter_back, -reach, axis=1)[:, ::-1][:, : location_conv.shape[2]]
    conv_grad = jnp.einsum("cka,fa->fck", filter_grads, dense_float, precision=precise)
    dense_grad = jnp.einsum("cka,fck->fa", filter_grads, conv_float, precision=precise)

    def two_columns(value):
        return jnp.concatenate([value[:, :lanes], value[:, lanes:]], axis=0)

    def to_lanes(value):
        return jnp.pad(value, ((0, 0), (0, lanes - value.shape[1])))

    filter_count, _, tap_count = location_conv.shape
    packed = [
        two_columns(prenet_first_grad),
        two_columns(prenet_second_grad),
        query_weight_grad,
        memory_weight_grad,
        to_lanes(frame_weight_grad),
        to_lanes(conv_grad.reshape(filter_count, -1)),
        dense_grad,
        bias_sums,
        vector_back,
        to_lanes(frame_bias_grad),
    ]
    heights = [value.shape[0] for value in packed]
    shares = 2 * batch_size
    surplus = -sum(heights) % (8 * shares)
    packed = jnp.concatenate(packed + [jnp.zeros((surplus, lanes), f32)], axis=0)
    packed = add_units(packed, 0)
    received, packed = lax.optimization_barrier((received, packed))

    segments_rows = segments_all.T
    carried = jnp.pad(
        (segments_rows[:, 1:] == segments_rows[:, :-1]).astype(bf16), ((0, 0), (0, 1))
    ).reshape(batch_size, frame_rows)
    carried = jnp.pad(carried, ((0, 0), (0, padding)))
    after = jnp.pad(received[:, 1:], ((0, 0), (0, 1), (0, 0))) * carried[:, :, None]
    received = received.reshape(batch_size * (frame_rows + padding), -1)
    after = after.reshape(batch_size * (frame_rows + padding), -1)

    def product(start, width, grads):
        return lax.dot_general(
            inputs_all[:, start : start + width],
            grads,
            (((0,), (0,)), ((), ())),
            preferred_element_type=f32,
        )

    pair = 2 * slice_width
    first_part = jnp.concatenate(
        [
            product(0, prenet_width, received[:, :pair]),
            product(prenet_width + hidden, memory_width, after[:, :pair]),
            product(prenet_width, hidden, after[:, :pair]),
        ],
        axis=0,
    )
    second_part = jnp.concatenate(
        [
            product(prenet_width, hidden + memory_width, received[:, pair:]),
            product(prenet_width + hidden + memory_width, hidden, after[:, pair:]),
        ],
        axis=0,
    )
    parts = jnp.concatenate(
        [
            first_part.reshape(batch_size, depth_one, pair),
            second_part.reshape(batch_size, depth_two, pair),
        ],
        axis=1,
    )
    parts = add_units(parts, 2).astype(bf16)
    depth_both = depth_one + depth_two
    parts = jnp.concatenate(
        [parts, packed.astype(bf16).reshape(batch_size, -1, slice_width)], axis=1
    )
    if roomy:
        (
            parts,
            inputs_first,
            inputs_later,
            grads_early,
            grads_last,
            alphas,
            context_grads,
            processed_round,
        ) = lax.optimization_barrier(
            (
                parts,
                inputs_first,
                inputs_later,
                grads_early,
                grads_last,
                alphas,
                context_grads,
                processed_round,
            )
        )
        kernel_grads = []
        for layer in range(5):
            if layer == 0:
                source = inputs_first
            else:
                source = lax.dynamic_slice_in_dim(
                    inputs_later[layer - 1], place * channel_rows, channel_rows, 1
                )
            grad_norm = grads_early[layer] if layer < 4 else grads_last
            kernel_grads.append(
                post_kernel_grad(
                    source.reshape(frames, total_rows, -1),
                    grad_norm.reshape(frames, total_rows, -1),
                    same,
                ).reshape(5, source.shape[1], grad_norm.shape[1])
            )
    parts = lax.all_to_all(parts, "batch", 0, 0, tiled=True)
    share = jnp.sum(parts[:, depth_both:].astype(f32), axis=0)
    parts = parts[:, :depth_both].astype(f32)
    parts = jnp.transpose(parts, (1, 0, 2)).reshape(depth_both, 4, half)

    memory_grad = lax.dot_general(
        processed_round, memory_weight, (((1,), (1,)), ((), ())), preferred_element_type=f32
    )
    for step in range(longest):
        memory_grad = memory_grad + exact(
            alphas[step][:, :slots], context_grads[step], ((1,), (0,))
        )
    memory_grad = memory_grad.reshape(rows, text_width, memory_width)
    memory_grads = jnp.stack(ordered(memory_grad, exchange(memory_grad)))
    post_first_grad = add_units(kernel_grads[0], 2)
    post_middle_grad = add_units(jnp.stack(kernel_grads[1:4]), 3)
    post_last_grad = add_units(kernel_grads[4], 2)
    middle_norm_grad = add_units(
        jnp.stack([jnp.stack(gain_grads[:4]), jnp.stack(shift_grads[:4])]), 2
    )
    last_norm_grad = add_units(jnp.stack([gain_grads[4], shift_grads[4]]), 1)

    packed = gather_far_first(share.astype(bf16)).reshape(-1, lanes)
    packed = whole(packed, 0).astype(f32)
    small, start = [], 0
    for height in heights:
        small.append(packed[start : start + height])
        start += height

    def from_columns(value):
        tall = value.shape[0] // 2
        return jnp.concatenate([value[:tall], value[tall:]], axis=1)

    biases_grad = small[7].reshape(2, 2, -1)
    biases_grad = jnp.where(first_unit, biases_grad[:, 0], biases_grad[:, 1])
    biases_grad = biases_grad.reshape(2, 4, half)
    small = [
        from_columns(small[0]),
        from_columns(small[1]),
        small[2],
        small[3],
        small[5][:, : 2 * tap_count].reshape(filter_count, 2, tap_count),
        small[6],
        small[8][0],
        small[4][:, : mel_width + 1],
        small[9][0, : mel_width + 1],
    ]
    return (
        small[0],
        small[1],
        small[2],
        small[3],
        small[4],
        small[5],
        small[6],
        parts[:depth_one],
        biases_grad[0],
        parts[depth_one:],
        biases_grad[1],
        small[7],
        small[8],
        post_first_grad,
        post_middle_grad,
        post_last_grad,
        middle_norm_grad,
        last_norm_grad,
        memory_grads,
    )


def solution(mesh):
    in_specs = (
        P(None, "batch", None, None),
        P(None, "batch", None, None),
        P(None, "batch", None),
        P(None, "batch", None),
        P(None, "batch", None, "unit"),
        P(None, "batch", None, "unit"),
        P(None, "batch", None, None),
        P(None, "batch", None, None),
        P(),
        P(),
        P(),
        P(),
        P(),
        P(),
        P(),
        P("batch", None, "unit"),
        P(None, "unit"),
        P("batch", None, "unit"),
        P(None, "unit"),
        P(),
        P(),
        P(None, None, "unit"),
        P(None, None, "batch", "unit"),
        P(None, "batch", "unit"),
        P(None, None, "unit"),
        P(None, "unit"),
    )
    out_specs = (
        P(),
        P(),
        P(),
        P(),
        P(),
        P(),
        P(),
        P("batch", None, "unit"),
        P(None, "unit"),
        P("batch", None, "unit"),
        P(None, "unit"),
        P(),
        P(),
        P(None, None, "unit"),
        P(None, None, "batch", "unit"),
        P(None, "batch", "unit"),
        P(None, None, "unit"),
        P(None, "unit"),
        P(None, "batch", None, None),
    )
    return jax.shard_map(
        on_device, mesh=mesh, in_specs=in_specs, out_specs=out_specs, check_vma=False
    )
```

```python
import functools

import jax
import jax.numpy as jnp
from jax import lax
from jax.experimental import pallas as pl
from jax.experimental.pallas import tpu as pltpu
from jax.sharding import PartitionSpec as P

precise = lax.Precision.HIGHEST
norm_eps = 1e-05
f32 = jnp.float32
bf16 = jnp.bfloat16
lanes = 128
kernel_vmem = 60 * 1024 * 1024


def split(value):
    high = value.astype(bf16)
    return high, (value - high.astype(f32)).astype(bf16)


def dot(a, b, contract=((1,), (0,))):
    return lax.dot_general(a, b, (contract, ((), ())), preferred_element_type=f32)


def dot_left(exact, value, contract=((1,), (0,))):
    high, low = split(value)
    return dot(exact, high, contract) + dot(exact, low, contract)


def dot_right(value, exact, contract=((1,), (0,))):
    high, low = split(value)
    return dot(high, exact, contract) + dot(low, exact, contract)


def dot_both(a, b, contract=((1,), (0,))):
    a_high, a_low = split(a)
    b_high, b_low = split(b)
    return (
        dot(a_high, b_high, contract) + dot(a_low, b_high, contract) + dot(a_high, b_low, contract)
    )


rows_first = ((0,), (0,))
lanes_both = ((1,), (1,))


def position_hot(position_count, text_width, reverse):
    place = lax.broadcasted_iota(jnp.int32, (position_count, lanes), 0) & (text_width - 1)
    lane = lax.broadcasted_iota(jnp.int32, (position_count, lanes), 1)
    place = (lanes - 1) - place if reverse else place + 1
    return (place == lane).astype(bf16)


def slant(value, text_width):
    blocks = [
        pltpu.roll(value[start : start + text_width], 0, 1, stride=1, stride_axis=0)
        for start in range(0, value.shape[0], text_width)
    ]
    return jnp.concatenate(blocks, axis=0)


def pad_rows(value):
    return jnp.concatenate(
        [value, jnp.zeros((lanes - value.shape[0], value.shape[1]), value.dtype)], axis=0
    )


def unit_spot(chunk, unit, per_half):
    half = (chunk // per_half + unit) % 2
    return pl.multiple_of((half * per_half + chunk % per_half) * lanes, lanes)


def gate_spot(chunk, gate, per_half):
    start = (chunk // per_half) * 4 * per_half + gate * per_half + chunk % per_half
    return pl.multiple_of(start * lanes, lanes)


def weight_copies(refs, held_one, held_two, sems):
    copies_one, copies_two = [], []

    def copy(copies, source, target):
        count = len(copies_one) + len(copies_two)
        copies.append(pltpu.make_async_copy(source, target, sems.at[count]))

    if len(refs) == 4:
        for side in range(2):
            copy(copies_one, refs[side], held_one.at[side])
            copy(copies_two, refs[2 + side], held_two.at[side])
        return copies_one, copies_two
    devices = refs[0].shape[1]
    rows_one, rows_two = held_one.shape[2] // devices, held_two.shape[2] // devices
    for held, copies, rows, start in (
        (held_two, copies_two, rows_two, rows_one),
        (held_one, copies_one, rows_one, 0),
    ):
        for side in range(2):
            for device in range(devices):
                copy(
                    copies,
                    refs[side].at[:, device, start : start + rows, :],
                    held.at[side, :, device * rows : (device + 1) * rows, :],
                )
    return copies_one, copies_two


def forward_kernel(
    weight_count,
    unit_ref,
    *refs,
):
    weight_refs, refs = refs[:weight_count], refs[weight_count:]
    forward_body(unit_ref, weight_refs, *refs)


def backward_kernel(
    weight_count,
    unit_ref,
    *refs,
):
    weight_refs, refs = refs[:weight_count], refs[weight_count:]
    backward_body(unit_ref, weight_refs, *refs)


def forward_body(
    unit_ref,
    weight_refs,
    previous_ref,
    drop_one,
    drop_two,
    layer_one,
    layer_two,
    slot_ref,
    zone_one,
    zone_two,
    bias_one,
    bias_two,
    hot_ref,
    memory_ref,
    project_ref,
    query_ref,
    vector_ref,
    conv_ref,
    dense_ref,
    frame_ref,
    frame_bias,
    gates_one,
    gates_two,
    prior_one,
    prior_two,
    round_one,
    round_two,
    context_ref,
    mixed_ref,
    alpha_ref,
    taps_ref,
    prenet_one,
    prenet_two,
    prenet_hidden,
    prenet_out,
    frame_out,
    held_one,
    held_two,
    input_ref,
    prenet_ref,
    processed_ref,
    filter_ref,
    state_one,
    cell_one,
    state_two,
    cell_two,
    sems,
):
    unit = unit_ref[0]
    steps, slots, hidden = round_one.shape
    prenet_width = layer_two.shape[1]
    context_width = context_ref.shape[2]
    half = hidden // 2
    per_half = half // lanes
    position_count = hot_ref.shape[0]
    text_width = position_count // (slots // 4)
    copies_one, copies_two = weight_copies(weight_refs, held_one, held_two, sems)
    for copy in copies_two + copies_one:
        copy.start()
    for ref in (state_one, cell_one, state_two, cell_two):
        ref[...] = jnp.zeros_like(ref)

    def gates_into(held, depth, bias_ref, out_ref, step):
        def one(block, _):
            side = block // 2
            inputs = input_ref[:, :depth]
            for pair in range(per_half):
                tile = (block % 2) * 2 * per_half + 2 * pair
                outside = pl.ds(
                    pl.multiple_of(block * 2 * half + 2 * pair * lanes, 2 * lanes), 2 * lanes
                )
                kernel = jnp.concatenate(
                    [held[side, tile, :depth, :], held[side, tile + 1, :depth, :]], axis=1
                )
                out_ref[step, :, outside] = dot(inputs, kernel) + bias_ref[:, outside]
            return 0

        lax.fori_loop(0, 4, one, 0)

    def cell(gates_ref, zone_ref, prior_ref, state, cells, round_ref, step):
        def one(chunk, _):
            spot = pl.ds(pl.multiple_of(chunk * lanes, lanes), lanes)
            values = [
                gates_ref[step, :, pl.ds(gate_spot(chunk, gate, per_half), lanes)]
                for gate in range(4)
            ]
            zone = zone_ref[step, :, spot]
            before = cells[:, spot]
            prior_ref[step, :, spot] = before
            fresh = jax.nn.sigmoid(values[1]) * before + jax.nn.sigmoid(values[0]) * jnp.tanh(
                values[2]
            )
            output = jax.nn.sigmoid(values[3]) * jnp.tanh(fresh)
            now = zone * state[:, spot] + (1.0 - zone) * output
            state[:, spot] = now
            cells[:, spot] = zone * before + (1.0 - zone) * fresh
            round_ref[step, :, pl.ds(unit_spot(chunk, unit, per_half), lanes)] = now.astype(bf16).astype(
                f32
            )
            return 0

        lax.fori_loop(0, 2 * per_half, one, 0)

    def attention(step, location):
        inside = hot_ref[...] > 0.0
        hot = hot_ref[...].astype(bf16)
        query = pad_rows(dot(round_one[step].astype(bf16), query_ref[...].astype(bf16)))
        summed = dot_left(hot, query) + processed_ref[...]
        if location is not None:
            summed = summed + location
        mixed = jnp.tanh(summed)
        mixed_ref[step] = mixed
        energy = dot_right(mixed, vector_ref[...].astype(bf16))
        most = jnp.max(jnp.where(inside, energy, -1000000000.0), axis=0, keepdims=True)
        shifted = jnp.where(inside, jnp.exp(energy - most), 0.0)
        total = jnp.sum(shifted, axis=0, keepdims=True)
        alpha = shifted / jnp.where(total > 0.0, total, 1.0)
        alpha_ref[step] = alpha
        context = dot_right(alpha, memory_ref[...].astype(bf16), rows_first)[:slots]
        context_ref[step] = context.astype(bf16).astype(f32)

    def taps_of(step):
        spread = dot_right(
            alpha_ref[step], position_hot(position_count, text_width, True), rows_first
        )
        taps_ref[step] = slant(dot_left(hot_ref[...].astype(bf16), spread), text_width)

    def second_layer(step, depth):
        input_ref[:, :hidden] = round_one[step].astype(bf16)
        input_ref[:, hidden : hidden + context_width] = context_ref[step].astype(bf16)
        gates_into(held_two, depth, bias_two, gates_two, step)
        cell(gates_two, zone_two, prior_two, state_two, cell_two, round_two, step)

    slot_hot = slot_ref[...].astype(bf16)

    def prenet_layer(source, layer, drops, mixed_out, out):
        mixed = dot(source.astype(bf16), layer[...].astype(bf16))
        mixed_out[...] = mixed
        value = (mixed * jax.nn.sigmoid(mixed) * drops[...] * 2.0).astype(bf16)
        out[...] = value.astype(f32)
        return value

    hidden_value = prenet_layer(previous_ref[...], layer_one, drop_one, prenet_one, prenet_hidden)
    prenet_value = prenet_layer(hidden_value, layer_two, drop_two, prenet_two, prenet_out)
    prenet_slots = dot(slot_hot, prenet_value, rows_first)
    for step in range(steps):
        prenet_ref[step] = prenet_slots[step * slots : (step + 1) * slots]
    processed_ref[...] = dot(memory_ref[...].astype(bf16), project_ref[...].astype(bf16))
    for channel in range(2):
        filter_ref[channel] = dot(
            conv_ref[channel].astype(bf16), dense_ref[...].astype(bf16)
        )

    gates_one[0] = jnp.broadcast_to(bias_one[...], gates_one.shape[1:])
    cell(gates_one, zone_one, prior_one, state_one, cell_one, round_one, 0)
    attention(0, None)
    taps_of(0)
    for copy in copies_two:
        copy.wait()
    second_layer(0, hidden + context_width)
    for copy in copies_one:
        copy.wait()

    def later(step, _):
        input_ref[:, :prenet_width] = prenet_ref[step].astype(bf16)
        input_ref[:, prenet_width : prenet_width + context_width] = context_ref[step - 1].astype(
            bf16
        )
        input_ref[:, prenet_width + context_width : prenet_width + context_width + hidden] = (
            round_one[step - 1].astype(bf16)
        )
        gates_into(
            held_one, prenet_width + context_width + hidden, bias_one, gates_one, step
        )
        cell(gates_one, zone_one, prior_one, state_one, cell_one, round_one, step)
        previous = taps_ref[step - 1]
        summed = jnp.where(step == 2, taps_ref[0] + previous, previous)
        attention(step, dot_both(previous, filter_ref[0]) + dot_both(summed, filter_ref[1]))

        @pl.when(step < steps - 1)
        def _():
            taps_of(step)

        input_ref[:, hidden + context_width :] = round_two[step - 1].astype(bf16)
        second_layer(step, 2 * hidden + context_width)
        return 0

    lax.fori_loop(1, steps, later, 0)
    for step in range(steps):
        values = dot(round_two[step].astype(bf16), frame_ref[:hidden].astype(bf16)) + dot(
            context_ref[step].astype(bf16), frame_ref[hidden:].astype(bf16)
        )
        high = values.astype(bf16)
        rest = values - high.astype(f32)
        middle = rest.astype(bf16)
        low = (rest - middle.astype(f32)).astype(bf16)
        chosen = slot_hot[:, step * slots : (step + 1) * slots]
        picked = (dot(chosen, high) + dot(chosen, middle)) + dot(chosen, low)
        frame_out[...] = (frame_bias[...] if step == 0 else frame_out[...]) + picked


def backward_body(
    unit_ref,
    weight_refs,
    gates_one,
    gates_two,
    prior_one,
    prior_two,
    zone_one,
    zone_two,
    hot_ref,
    memory_ref,
    query_ref,
    vector_ref,
    conv_ref,
    dense_ref,
    mixed_ref,
    alpha_ref,
    taps_ref,
    frame_grad,
    frame_weight,
    slot_ref,
    sent_ref,
    prenet_grad,
    context_grad,
    query_grad,
    processed_grad,
    vector_grad,
    filter_grad,
    held_one,
    held_two,
    grads_one,
    grads_two,
    back_one,
    back_two,
    state_one,
    cell_one,
    state_two,
    cell_two,
    previous_grad,
    summed_grad,
    from_query,
    frame_ref,
    filter_ref,
    sems,
):
    unit = unit_ref[0]
    steps, slots, prenet_width = prenet_grad.shape
    context_width = context_grad.shape[2]
    hidden = state_one.shape[1]
    half = hidden // 2
    per_half = half // lanes
    position_count = hot_ref.shape[0]
    text_width = position_count // (slots // 4)
    copies_one, copies_two = weight_copies(weight_refs, held_one, held_two, sems)
    for copy in copies_two + copies_one:
        copy.start()
    for ref in (
        state_one,
        cell_one,
        state_two,
        cell_two,
        back_one,
        back_two,
        previous_grad,
        summed_grad,
        processed_grad,
        vector_grad,
        filter_grad,
    ):
        ref[...] = jnp.zeros_like(ref)

    def cell(gates_ref, prior_ref, zone_ref, state, cells, grads_ref, step, incoming):
        def one(chunk, _):
            spot = pl.ds(pl.multiple_of(chunk * lanes, lanes), lanes)
            places = [pl.ds(gate_spot(chunk, gate, per_half), lanes) for gate in range(4)]
            values = [gates_ref[step, :, place] for place in places]
            zone = zone_ref[step, :, spot]
            keep = 1.0 - zone
            before = prior_ref[step, :, spot]
            gate_in = jax.nn.sigmoid(values[0])
            gate_forget = jax.nn.sigmoid(values[1])
            candidate = jnp.tanh(values[2])
            gate_out = jax.nn.sigmoid(values[3])
            bent = jnp.tanh(gate_forget * before + gate_in * candidate)
            grad_state = incoming(unit_spot(chunk, unit, per_half)) + state[:, spot]
            grad_cell = cells[:, spot]
            grad_new = keep * grad_state
            grad_fresh = grad_new * gate_out * (1.0 - bent * bent) + keep * grad_cell
            state[:, spot] = zone * grad_state
            cells[:, spot] = zone * grad_cell + gate_forget * grad_fresh
            results = (
                grad_fresh * candidate * gate_in * (1.0 - gate_in),
                grad_fresh * before * gate_forget * (1.0 - gate_forget),
                grad_fresh * gate_in * (1.0 - candidate * candidate),
                grad_new * bent * gate_out * (1.0 - gate_out),
            )
            for place, result in zip(places, results):
                grads_ref[step, :, place] = result.astype(bf16)
            return 0

        lax.fori_loop(0, 2 * per_half, one, 0)

    def inputs_back(grads_ref, held, out_ref, step, blocks):
        def one(block, _):
            spot = pl.ds(pl.multiple_of(block * 256, 256), 256)
            totals = [None] * 4
            for tile in range(0, 8 * per_half, 2):
                side, inside = tile // (4 * per_half), tile % (4 * per_half)
                kernel = jnp.concatenate(
                    [held[side, inside, spot, :], held[side, inside + 1, spot, :]], axis=1
                )
                grads = grads_ref[step, :, tile * lanes : (tile + 2) * lanes]
                product = dot(grads, kernel, lanes_both)
                which = tile // 2 % 4
                totals[which] = product if totals[which] is None else totals[which] + product
            out_ref[:, spot] = (totals[0] + totals[1]) + (totals[2] + totals[3])
            return 0

        lax.fori_loop(0, blocks, one, 0)

    def attention(step, located):
        inside = hot_ref[...] > 0.0
        hot = hot_ref[...].astype(bf16)
        alpha = alpha_ref[step]
        mixed = mixed_ref[step]
        context_now = pad_rows(context_grad[step])
        weights_grad = jnp.where(
            inside,
            dot_left(memory_ref[...].astype(bf16), context_now, lanes_both)
            + previous_grad[...]
            + summed_grad[...],
            0.0,
        )
        product = alpha * weights_grad
        energy_grad = product - alpha * jnp.sum(product, axis=0, keepdims=True)
        spread = jnp.sum(energy_grad, axis=1, keepdims=True)
        vector_grad[...] += jnp.sum(spread * mixed, axis=0, keepdims=True)
        mixed_grad = spread * vector_ref[...] * (1.0 - mixed * mixed)
        processed_grad[...] += mixed_grad
        high, low = split(mixed_grad)
        query_now = (dot(hot, high, rows_first) + dot(hot, low, rows_first))[:slots]
        query_grad[step] = query_now
        from_query[...] = dot_right(query_now, query_ref[...].astype(bf16), lanes_both)
        if located:
            previous = taps_ref[step - 1]
            summed = jnp.where(step == 2, taps_ref[0] + previous, previous)
            filter_grad[0] += dot_both(previous, mixed_grad, rows_first)
            filter_grad[1] += dot_both(summed, mixed_grad, rows_first)
            place_hot = position_hot(position_count, text_width, False)

            def taps_back(channel):
                taps_grad = slant(
                    dot_both(mixed_grad, filter_ref[channel], lanes_both), text_width
                )
                gathered = dot_right(taps_grad, hot, rows_first)
                return jnp.where(inside, dot_left(place_hot, gathered), 0.0)

            previous_grad[...] = taps_back(0)
            summed_grad[...] += taps_back(1)

    def arrived(step, copies):
        @pl.when(step == steps - 1)
        def _():
            for copy in copies:
                copy.wait()

    def step_back(step, located):
        cell(
            gates_two,
            prior_two,
            zone_two,
            state_two,
            cell_two,
            grads_two,
            step,
            lambda spot: frame_ref[step, :, pl.ds(spot, lanes)]
            + back_two[:, pl.ds(spot + hidden + context_width, lanes)],
        )
        blocks_two = (hidden + context_width + (hidden if located else 0)) // 256
        if located:
            arrived(step, copies_two)
        inputs_back(grads_two, held_two, back_two, step, blocks_two)
        context_grad[step] = (
            back_two[:, hidden : hidden + context_width]
            + frame_ref[step, :, hidden:]
            + back_one[:, prenet_width : prenet_width + context_width]
        )
        attention(step, located)
        cell(
            gates_one,
            prior_one,
            zone_one,
            state_one,
            cell_one,
            grads_one,
            step,
            lambda spot: back_two[:, pl.ds(spot, lanes)]
            + from_query[:, pl.ds(spot, lanes)]
            + back_one[:, pl.ds(spot + prenet_width + context_width, lanes)],
        )
        blocks_one = (prenet_width + (hidden + context_width if located else 0)) // 256
        if located:
            arrived(step, copies_one)
        inputs_back(grads_one, held_one, back_one, step, blocks_one)
        prenet_grad[step] = back_one[:, :prenet_width]

    for channel in range(2):
        filter_ref[channel] = dot(
            conv_ref[channel].astype(bf16), dense_ref[...].astype(bf16)
        )
    for step in range(steps):
        frame_ref[step] = dot(
            frame_grad[step].astype(bf16), frame_weight[...].astype(bf16), lanes_both
        )

    def later(index, _):
        step_back(steps - 1 - index, True)
        return 0

    lax.fori_loop(0, steps - 1, later, 0)
    step_back(0, False)
    slot_hot = slot_ref[...].astype(bf16)

    def tile_out(tile, _):
        for layer, grads_ref in ((0, grads_one), (1, grads_two)):
            for side in range(2):
                place = ((side + unit) % 2) * 4 * half + tile * lanes
                grads = grads_ref[:, :, pl.ds(pl.multiple_of(place, lanes), lanes)]
                chosen = dot(slot_hot, grads.reshape(steps * slots, lanes)).astype(bf16)
                spot = (2 * layer + side) * lanes
                sent_ref[tile, :, spot : spot + lanes] = chosen
        return 0

    lax.fori_loop(0, 4 * per_half, tile_out, 0)


def call_forward(unit, weights, small, sizes):
    steps, slots, hidden, context_width, positions, frame_rows, prenet_width = sizes
    tiles = 2 * hidden // lanes
    held_one = (2, tiles, prenet_width + context_width + hidden, lanes)
    held_two = (2, tiles, 2 * hidden + context_width, lanes)

    def shape(*dims):
        return jax.ShapeDtypeStruct(dims, f32)

    outs = [
        shape(steps, slots, 4 * hidden),
        shape(steps, slots, 4 * hidden),
        shape(steps, slots, hidden),
        shape(steps, slots, hidden),
        shape(steps, slots, hidden),
        shape(steps, slots, hidden),
        shape(steps, slots, context_width),
        shape(steps, positions, lanes),
        shape(steps, positions, lanes),
        shape(steps - 1, positions, lanes),
        shape(frame_rows, prenet_width),
        shape(frame_rows, prenet_width),
        shape(frame_rows, prenet_width),
        shape(frame_rows, prenet_width),
        shape(frame_rows, lanes),
    ]
    vmem = pl.BlockSpec(memory_space=pltpu.VMEM)
    return pl.pallas_call(
        functools.partial(forward_kernel, len(weights)),
        out_shape=outs,
        in_specs=[pl.BlockSpec(memory_space=pltpu.SMEM)]
        + [pl.BlockSpec(memory_space=pl.ANY)] * len(weights)
        + [vmem] * len(small),
        out_specs=[vmem] * len(outs),
        scratch_shapes=[
            pltpu.VMEM(held_one, bf16),
            pltpu.VMEM(held_two, bf16),
            pltpu.VMEM((slots, held_two[2]), bf16),
            pltpu.VMEM((steps, slots, prenet_width), f32),
            pltpu.VMEM((positions, lanes), f32),
            pltpu.VMEM((2, lanes, lanes), f32),
            pltpu.VMEM((slots, hidden), f32),
            pltpu.VMEM((slots, hidden), f32),
            pltpu.VMEM((slots, hidden), f32),
            pltpu.VMEM((slots, hidden), f32),
            pltpu.SemaphoreType.DMA((4 if len(weights) == 4 else 4 * weights[0].shape[1],)),
        ],
        compiler_params=pltpu.CompilerParams(vmem_limit_bytes=kernel_vmem),
        name="decoder_forward",
    )(unit, *weights, *small)


def call_backward(unit, weights, small, prenet_width):
    gates_one = small[0]
    steps, slots, gate_width = gates_one.shape
    hidden = gate_width // 4
    positions, context_width = small[7].shape
    tiles = 2 * hidden // lanes
    held_one = (2, tiles, prenet_width + context_width + hidden, lanes)
    held_two = (2, tiles, 2 * hidden + context_width, lanes)

    def shape(dims, kind):
        return jax.ShapeDtypeStruct(dims, kind)

    outs = [
        shape((gate_width // (2 * lanes), small[-1].shape[0], 4 * lanes), bf16),
        shape((steps, slots, prenet_width), f32),
        shape((steps, slots, context_width), f32),
        shape((steps, slots, lanes), f32),
        shape((positions, lanes), f32),
        shape((1, lanes), f32),
        shape((2, lanes, lanes), f32),
    ]
    vmem = pl.BlockSpec(memory_space=pltpu.VMEM)
    return pl.pallas_call(
        functools.partial(backward_kernel, len(weights)),
        out_shape=outs,
        in_specs=[pl.BlockSpec(memory_space=pltpu.SMEM)]
        + [pl.BlockSpec(memory_space=pl.ANY)] * len(weights)
        + [vmem] * len(small),
        out_specs=[vmem] * len(outs),
        scratch_shapes=[
            pltpu.VMEM(held_one, bf16),
            pltpu.VMEM(held_two, bf16),
            pltpu.VMEM((steps, slots, gate_width), bf16),
            pltpu.VMEM((steps, slots, gate_width), bf16),
            pltpu.VMEM((slots, held_one[2]), f32),
            pltpu.VMEM((slots, held_two[2]), f32),
            pltpu.VMEM((slots, hidden), f32),
            pltpu.VMEM((slots, hidden), f32),
            pltpu.VMEM((slots, hidden), f32),
            pltpu.VMEM((slots, hidden), f32),
            pltpu.VMEM((positions, lanes), f32),
            pltpu.VMEM((positions, lanes), f32),
            pltpu.VMEM((slots, hidden), f32),
            pltpu.VMEM((steps, slots, hidden + context_width), f32),
            pltpu.VMEM((2, lanes, lanes), f32),
            pltpu.SemaphoreType.DMA((4 if len(weights) == 4 else 4 * weights[0].shape[1],)),
        ],
        compiler_params=pltpu.CompilerParams(vmem_limit_bytes=kernel_vmem),
        name="decoder_backward",
    )(unit, *weights, *small)


def postnet_kernel(
    mel_width,
    loss_scale,
    unit_ref,
    mel_ref,
    target_ref,
    mask_ref,
    first_ref,
    own_ref,
    peer_ref,
    last_ref,
    gain_ref,
    shift_ref,
    inputs_first,
    inputs_later,
    grads_early,
    grads_last,
    norm_grads,
    mel_grad,
    padded,
    padded_mel,
    held,
    normed_early,
    normed_last,
    inverse_ref,
    post_grad,
):
    unit = unit_ref[0]
    count, channels = held.shape
    side = channels // 2
    frames = padded.shape[0] - count
    rows_each = frames // 4
    chunk = 2 * rows_each
    tall = float(count)
    body_rows = slice(2 * rows_each, 2 * rows_each + count)

    for ref in (padded, padded_mel):
        ref[: 2 * rows_each] = jnp.zeros((2 * rows_each, ref.shape[1]), bf16)
        ref[2 * rows_each + count :] = jnp.zeros((2 * rows_each, ref.shape[1]), bf16)

    def piece(source, start, tap, width, lane=None):
        spot = pl.ds(pl.multiple_of(start + tap * rows_each, rows_each), chunk)
        mask = mask_ref[tap, pl.ds(pl.multiple_of(start, rows_each), chunk), :]
        if width < lanes:
            mask = mask[:, :width]
        else:
            mask = jnp.concatenate([mask] * (width // lanes), axis=1)
        value = source[spot, :] if lane is None else source[spot, pl.ds(lane, width)]
        return value * mask

    def chunks(work):
        def one(index, _):
            work(pl.multiple_of(index * chunk, chunk))
            return 0

        lax.fori_loop(0, count // chunk, one, 0)

    def half_spot(which):
        return pl.multiple_of(((which + unit) % 2) * side, side)

    def norm_forward(value, layer, lane, width):
        mean = jnp.sum(value, axis=0, keepdims=True) / tall
        centered = value - mean
        inverse = lax.rsqrt(jnp.sum(centered * centered, axis=0, keepdims=True) / tall + norm_eps)
        inverse_ref[layer, :, pl.ds(lane, width)] = inverse
        return centered * inverse

    def each_lane_block(work):
        def one(index, _):
            work(pl.multiple_of(index * lanes, lanes))
            return 0

        lax.fori_loop(0, channels // lanes, one, 0)

    def activate(layer):
        def block(lane):
            spot = pl.ds(lane, lanes)
            normed = norm_forward(held[:, spot], layer, lane, lanes)
            normed_early[layer, :, spot] = normed
            active = jnp.tanh(
                normed * gain_ref[layer, :, spot] + shift_ref[layer, :, spot]
            ).astype(bf16)
            inputs_later[layer, :, spot] = active
            padded[body_rows, spot] = active

        each_lane_block(block)

    source = mel_ref[...].astype(bf16)
    inputs_first[...] = source
    padded_mel[body_rows] = source

    def first_chunk(start):
        total = None
        for tap in range(5):
            product = dot(piece(padded_mel, start, tap, mel_width), first_ref[tap])
            total = product if total is None else total + product
        held[pl.ds(start, chunk), :] = total

    chunks(first_chunk)
    activate(0)

    def middle(index, _):
        def middle_chunk(start):
            totals = [None, None]
            for tap in range(5):
                value = piece(padded, start, tap, channels)
                for which, ref in ((0, own_ref), (1, peer_ref)):
                    product = dot(value, ref[index * 5 + tap])
                    totals[which] = product if tap == 0 else totals[which] + product
            for which in range(2):
                held[pl.ds(start, chunk), pl.ds(half_spot(which), side)] = totals[which]

        chunks(middle_chunk)
        activate(index + 1)
        return 0

    lax.fori_loop(0, 3, middle, 0)

    def last_chunk(start):
        total = None
        for tap in range(5):
            product = dot(piece(padded, start, tap, channels), last_ref[tap])
            total = product if total is None else total + product
        normed_last[pl.ds(start, chunk), :] = total

    chunks(last_chunk)
    normed = norm_forward(normed_last[...], 4, 0, mel_width)
    normed_last[...] = normed

    def norm_back(grad, normed, layer, lane, width):
        spot = pl.ds(lane, width)
        shift_grad = jnp.sum(grad, axis=0, keepdims=True)
        gain_grad = jnp.sum(grad * normed, axis=0, keepdims=True)
        norm_grads[0, layer, :, spot] = gain_grad
        norm_grads[1, layer, :, spot] = shift_grad
        return (
            gain_ref[layer, :, spot]
            * inverse_ref[layer, :, spot]
            * (grad - shift_grad / tall - normed * (gain_grad / tall))
        ).astype(bf16)

    output = normed * gain_ref[4, :, :mel_width] + shift_ref[4, :, :mel_width]
    grad = loss_scale * (mel_ref[...] + output - target_ref[...])
    post_grad[...] = grad
    grad_norm = norm_back(grad, normed, 4, 0, mel_width)
    grads_last[...] = grad_norm
    padded_mel[body_rows] = grad_norm

    def last_back(start):
        total = None
        for tap in range(5):
            product = dot(
                piece(padded_mel, start, tap, mel_width), last_ref[4 - tap], lanes_both
            )
            total = product if total is None else total + product
        held[pl.ds(start, chunk), :] = total

    chunks(last_back)

    def deactivate(layer):
        def block(lane):
            spot = pl.ds(lane, lanes)
            normed = normed_early[layer, :, spot]
            active = jnp.tanh(normed * gain_ref[layer, :, spot] + shift_ref[layer, :, spot])
            grad = held[:, spot] * (1.0 - active * active)
            grad_norm = norm_back(grad, normed, layer, lane, lanes)
            grads_early[layer, :, spot] = grad_norm
            padded[body_rows, spot] = grad_norm

        each_lane_block(block)

    def middle_back(back, _):
        index = 2 - back
        deactivate(index + 1)

        def chunk_back(start):
            total = None
            for which, ref in ((0, own_ref), (1, peer_ref)):
                for tap in range(5):
                    product = dot(
                        piece(padded, start, tap, side, half_spot(which)),
                        ref[index * 5 + 4 - tap],
                        lanes_both,
                    )
                    total = product if total is None else total + product
            held[pl.ds(start, chunk), :] = total

        chunks(chunk_back)
        return 0

    lax.fori_loop(0, 3, middle_back, 0)
    deactivate(0)

    def first_back(start):
        total = None
        for tap in range(5):
            product = dot(piece(padded, start, tap, channels), first_ref[4 - tap], lanes_both)
            total = product if total is None else total + product
        spot = pl.ds(start, chunk)
        mel_grad[spot, :] = (
            loss_scale * (mel_ref[spot, :] - target_ref[spot, :]) + post_grad[spot, :] + total
        )

    chunks(first_back)


def call_postnet(unit, small, loss_scale, rows_all):
    mel = small[0]
    count, mel_width = mel.shape
    channels = small[3].shape[2]

    def shape(kind, *dims):
        return jax.ShapeDtypeStruct(dims, kind)

    outs = [
        shape(bf16, count, mel_width),
        shape(bf16, 4, count, channels),
        shape(bf16, 4, count, channels),
        shape(bf16, count, mel_width),
        shape(f32, 2, 5, 1, channels),
        shape(f32, count, mel_width),
    ]
    vmem = pl.BlockSpec(memory_space=pltpu.VMEM)
    tall = count + 4 * rows_all
    return pl.pallas_call(
        functools.partial(postnet_kernel, mel_width, loss_scale),
        out_shape=outs,
        in_specs=[pl.BlockSpec(memory_space=pltpu.SMEM)] + [vmem] * len(small),
        out_specs=[vmem] * len(outs),
        scratch_shapes=[
            pltpu.VMEM((tall, channels), bf16),
            pltpu.VMEM((tall, mel_width), bf16),
            pltpu.VMEM((count, channels), f32),
            pltpu.VMEM((4, count, channels), f32),
            pltpu.VMEM((count, mel_width), f32),
            pltpu.VMEM((5, 1, channels), f32),
            pltpu.VMEM((count, mel_width), f32),
        ],
        compiler_params=pltpu.CompilerParams(vmem_limit_bytes=kernel_vmem),
        name="postnet",
    )(unit, *small)


def shifted_frames(source, same):
    steps = source.shape[0]
    padded = jnp.pad(source, ((2, 2), (0, 0), (0, 0)))
    return [
        padded[offset : offset + steps] * same[:, :, offset, None].astype(source.dtype)
        for offset in range(5)
    ]


def by_rows(work, roomy, arrays, summed=False):
    if roomy:
        return work(*arrays)
    parts = arrays[0].shape[1] // 192

    def cut(value):
        value = value.reshape((value.shape[0], parts, -1) + value.shape[2:])
        return jnp.moveaxis(value, 1, 0)

    pieces = tuple(cut(value) for value in arrays)
    if summed:
        first = jax.eval_shape(work, *[value[0] for value in pieces])
        start = jnp.zeros(first.shape, first.dtype)
        return lax.scan(lambda total, now: (total + work(*now), None), start, pieces)[0]
    result = jnp.moveaxis(lax.map(lambda now: work(*now), pieces), 0, 1)
    return result.reshape((result.shape[0], -1) + result.shape[3:])


def post_layer(source, kernel, same):
    wide = jnp.concatenate(shifted_frames(source, same), axis=2)
    return jnp.einsum(
        "src,co->sro", wide, kernel.reshape(-1, kernel.shape[2]), preferred_element_type=f32
    )


def post_layer_back(grad, kernel, same):
    wide = jnp.concatenate(shifted_frames(grad, same), axis=2)
    turned = jnp.transpose(kernel[::-1], (0, 2, 1)).reshape(-1, kernel.shape[1])
    return jnp.einsum("sro,oc->src", wide, turned, preferred_element_type=f32)


def post_kernel_grad(source, grad, same):
    wide = jnp.concatenate(shifted_frames(source, same), axis=2)
    return jnp.einsum("src,sro->co", wide, grad, preferred_element_type=f32)


def on_device(
    memory,
    targets,
    segments,
    text_lengths,
    zone_first,
    zone_second,
    drop_first,
    drop_second,
    prenet_first,
    prenet_second,
    query_weight,
    memory_weight,
    location_conv,
    location_dense,
    energy_vector,
    lstm_first,
    bias_first,
    lstm_second,
    bias_second,
    frame_weight,
    frame_bias,
    post_first,
    post_middle,
    post_last,
    middle_norm,
    last_norm,
):
    micro_count, rows, text_width, memory_width = memory.shape
    frames = segments.shape[2]
    utterances = text_lengths.shape[2]
    mel_width = targets.shape[3]
    hidden = query_weight.shape[0]
    prenet_width = prenet_first.shape[1]
    attention_width = query_weight.shape[1]
    half = lstm_first.shape[2]
    depth_one, depth_two = lstm_first.shape[0], lstm_second.shape[0]
    unit = lax.axis_index("unit")
    place = lax.axis_index("batch")
    batch_size = lax.axis_size("batch")
    total_rows = rows * batch_size
    frame_count = float(total_rows * frames)
    first_unit = unit == 0
    longest = 3
    slots = 4 * rows

    def exchange(value):
        return lax.ppermute(value, "unit", [(0, 1), (1, 0)])

    def ordered(own, peer):
        return jnp.where(first_unit, own, peer), jnp.where(first_unit, peer, own)

    def whole(value, axis):
        return jnp.concatenate(ordered(value, exchange(value)), axis=axis)

    def mine(value):
        return lax.dynamic_index_in_dim(value, unit, 0, keepdims=False)

    def others(value):
        return lax.dynamic_index_in_dim(value, 1 - unit, 0, keepdims=False)

    def swapped(value, bit):
        pairs = [(index, index ^ bit) for index in range(batch_size)]
        other = lax.ppermute(value, "batch", pairs)
        upper = (place & bit) != 0
        return jnp.where(upper, other, value), jnp.where(upper, value, other)

    def gather_far_first(value):
        inner, bit, count = value.ndim, batch_size // 2, 0
        while bit:
            value = jnp.stack(swapped(value, bit))
            bit //= 2
            count += 1
        order = tuple(range(count - 1, -1, -1)) + tuple(range(count, count + inner))
        return jnp.transpose(value, order).reshape((batch_size,) + value.shape[count:])

    def gather_rows(value):
        bit = 1
        while bit < batch_size:
            value = jnp.concatenate(swapped(value, bit), axis=0)
            bit *= 2
        return value

    def to_tiles(value):
        return jnp.transpose(value.reshape(value.shape[0], -1, lanes), (1, 0, 2))

    together = depth_one % 16 == 0 and depth_two % 16 == 0

    def gathered(value):
        return lax.all_gather(value, "batch", axis=1, tiled=True)

    if together:
        both = jnp.concatenate([to_tiles(lstm_first), to_tiles(lstm_second)], axis=1)
        own = (gathered(both).reshape(both.shape[0], batch_size, both.shape[1], lanes),)
    else:
        own = (gathered(to_tiles(lstm_first)), gathered(to_tiles(lstm_second)))
    channel_rows = post_middle.shape[2]
    middle_width = post_middle.shape[3]
    middle_half = lax.all_gather(
        post_middle.reshape(-1, channel_rows, middle_width), "batch", axis=1, tiled=True
    )
    last_half = gather_rows(jnp.transpose(post_last, (1, 0, 2)).reshape(channel_rows, -1))
    last_half = jnp.transpose(
        last_half.reshape(-1, post_last.shape[0], post_last.shape[2]), (1, 0, 2)
    )
    memory_now = mine(memory).reshape(rows * text_width, memory_width)
    segments_now = mine(segments)
    targets_now = mine(targets)
    frame_info = gather_rows(
        jnp.concatenate([targets_now, segments_now[:, :, None].astype(bf16)], axis=2).astype(f32)
    )

    same_frames = segments_now[:, :, None] == segments_now[:, None, :]
    earlier = jnp.tril(jnp.ones((frames, frames), jnp.bool_), -1)
    order = jnp.sum((same_frames & earlier[None]).astype(jnp.int32), axis=2)
    slot_of = order * slots + segments_now * rows + jnp.arange(rows, dtype=jnp.int32)[:, None]
    frame_rows = rows * frames
    padding = -frame_rows % 16
    slot_hot = (
        jnp.pad(slot_of.reshape(-1, 1), ((0, padding), (0, 0)), constant_values=-1)
        == jnp.arange(longest * slots, dtype=jnp.int32)[None, :]
    ).astype(bf16)
    slot_hot_frames = slot_hot[:frame_rows]
    carry_on = jnp.pad(
        (segments_now[:, 1:] == segments_now[:, :-1]).astype(f32), ((0, 0), (1, 0))
    )
    finished = jnp.pad(
        (segments_now[:, 1:] != segments_now[:, :-1]).astype(f32),
        ((0, 0), (0, 1)),
        constant_values=1.0,
    )

    def to_slots(value, kind=bf16):
        return lax.dot_general(
            slot_hot_frames,
            value.astype(bf16),
            (((0,), (0,)), ((), ())),
            preferred_element_type=f32,
        ).astype(kind)

    def to_frames(value):
        return jnp.dot(slot_hot, value.astype(bf16), preferred_element_type=f32).astype(bf16)

    def pad_frames(value):
        return jnp.pad(
            value.astype(f32).reshape(frame_rows, -1), ((0, padding), (0, 0))
        )

    previous = pad_frames(
        jnp.pad(targets_now[:, :-1], ((0, 0), (1, 0), (0, 0))).astype(f32)
        * carry_on[:, :, None]
    )
    drops_one = pad_frames(mine(drop_first))
    drops_two = pad_frames(mine(drop_second))

    zones_own = jnp.concatenate([mine(zone_first), mine(zone_second)], axis=2).astype(f32)
    zones_peer = exchange(
        jnp.concatenate([others(zone_first), others(zone_second)], axis=2).astype(f32)
    )
    zones_slots = to_slots(
        jnp.concatenate([zones_own, zones_peer], axis=2).reshape(rows * frames, -1), f32
    ).reshape(longest, slots, 4 * half)
    zone_one = jnp.concatenate(
        [zones_slots[:, :, :half], zones_slots[:, :, 2 * half : 3 * half]], axis=2
    )
    zone_two = jnp.concatenate(
        [zones_slots[:, :, half : 2 * half], zones_slots[:, :, 3 * half :]], axis=2
    )
    biases = jnp.stack([bias_first.reshape(-1), bias_second.reshape(-1)])
    biases = jnp.concatenate([biases, exchange(biases)], axis=1)
    text_ends = jnp.cumsum(mine(text_lengths), axis=1)
    owner = jnp.sum(
        (jnp.arange(text_width, dtype=jnp.int32)[None, :, None] >= text_ends[:, None, :]).astype(
            jnp.int32
        ),
        axis=2,
    )
    owner_slot = owner * rows + jnp.arange(rows, dtype=jnp.int32)[:, None]
    owner_hot = (
        owner_slot.reshape(-1, 1) == jnp.arange(lanes, dtype=jnp.int32)[None, :]
    ).astype(f32)
    conv_float = location_conv.astype(f32)
    dense_float = location_dense.astype(f32)
    reach = location_conv.shape[2] // 2
    taps_first = jnp.transpose(conv_float, (1, 2, 0))
    taps_first = jnp.pad(
        taps_first,
        ((0, 0), (0, lanes - taps_first.shape[1]), (0, lanes - taps_first.shape[2])),
    )
    dense_wide = jnp.pad(dense_float, ((0, lanes - dense_float.shape[0]), (0, 0)))
    taps_forward = jnp.roll(taps_first[:, ::-1], reach, axis=1)
    taps_back = jnp.roll(taps_first, 1 - reach, axis=1)
    frame_wide = jnp.pad(
        frame_weight.astype(f32), ((0, 0), (0, lanes - frame_weight.shape[1]))
    )
    frame_bias_wide = jnp.pad(frame_bias, (0, lanes - frame_bias.shape[0]))[None, :]
    vector_float = energy_vector.astype(f32)
    vector_wide = jnp.broadcast_to(vector_float[:, None], (attention_width, lanes))
    memory_float = memory_now.astype(f32)
    query_float = query_weight.astype(f32)
    unit_array = unit.astype(jnp.int32).reshape(1)

    targets_all = jnp.transpose(frame_info[:, :, :mel_width].astype(f32), (1, 0, 2))
    segments_all = jnp.transpose(frame_info[:, :, mel_width].astype(jnp.int32))
    padded = jnp.pad(segments_all, ((2, 2), (0, 0)), constant_values=-1)
    same = jnp.stack([padded[offset : offset + frames] == segments_all for offset in range(5)])
    same = jnp.moveaxis(same, 0, 2)
    first_full = whole(post_first, 2)
    last_full = whole(last_half, 2)
    middle_gain = whole(middle_norm, 2)
    last_gain = whole(last_norm, 1)
    loss_scale = 2.0 / (mel_width * total_rows)
    count = total_rows * frames
    channels = middle_norm.shape[2] * 2
    masks = jnp.broadcast_to(
        jnp.transpose(same, (2, 0, 1)).reshape(5, count, 1).astype(bf16), (5, count, lanes)
    )
    wide_gain = jnp.pad(last_gain, ((0, 0), (0, channels - mel_width)))
    norms = jnp.concatenate([middle_gain, wide_gain[:, None, :]], axis=1)[:, :, None, :]
    forward_small = (
        previous,
        drops_one,
        drops_two,
        prenet_first.astype(f32),
        prenet_second.astype(f32),
        slot_hot.astype(f32),
        zone_one,
        zone_two,
        biases[0:1],
        biases[1:2],
        owner_hot,
        memory_float,
        memory_weight.astype(f32),
        query_float,
        vector_wide,
        taps_forward,
        dense_wide,
        frame_wide,
        frame_bias_wide,
    )
    (
        own,
        forward_small,
        taps_back,
        vector_row,
        targets_all,
        masks,
        first_full,
        last_full,
        norms,
    ) = lax.optimization_barrier(
        (
            own,
            forward_small,
            taps_back,
            vector_float[None, :],
            targets_all,
            masks,
            first_full,
            last_full,
            norms,
        )
    )
    weights = sum(((value, exchange(value)) for value in own), ())
    slot_wide, zone_one, zone_two = forward_small[5], forward_small[6], forward_small[7]
    memory_float, query_float = forward_small[11], forward_small[13]
    dense_wide, frame_wide = forward_small[16], forward_small[17]

    (
        gates_one,
        gates_two,
        prior_one,
        prior_two,
        round_one,
        round_two,
        contexts,
        mixed_all,
        alphas,
        taps,
        mixed_one,
        mixed_two,
        hidden_round,
        prenet_round,
        frame_out,
    ) = call_forward(
        unit_array,
        weights,
        forward_small,
        (
            longest,
            slots,
            hidden,
            memory_width,
            rows * text_width,
            frame_rows + padding,
            prenet_width,
        ),
    )

    middle_half = lax.optimization_barrier((middle_half, frame_out))[0]
    middle_peer = exchange(middle_half)
    states = to_frames(
        jnp.concatenate([round_one, contexts, round_two], axis=2).reshape(longest * slots, -1)
    )
    frame_in = jnp.concatenate(
        [states[:, hidden + memory_width :], states[:, hidden : hidden + memory_width]], axis=1
    )
    frame_in = frame_in[:frame_rows]
    frame_out = frame_out[:frame_rows]
    mel_own = frame_out[:, :mel_width].reshape(rows, frames, mel_width)
    stop_logit = frame_out[:, mel_width].reshape(rows, frames)
    mel_all = jnp.transpose(
        gather_rows(mel_own), (1, 0, 2)
    )
    inputs_own = jnp.concatenate([prenet_round.astype(bf16), states], axis=1)
    roomy = total_rows * frames <= 2048
    if roomy:
        inputs_own, mel_all = lax.optimization_barrier((inputs_own, mel_all))
        inputs_all = lax.all_gather(inputs_own, "batch", axis=0, tiled=True)

    if roomy:
        (
            inputs_first,
            inputs_later,
            grads_early,
            grads_last,
            norm_grads,
            grad_mel,
        ) = call_postnet(
            unit_array,
            (
                mel_all.reshape(count, mel_width),
                targets_all.reshape(count, mel_width),
                masks,
                first_full,
                middle_half,
                middle_peer,
                last_full,
                norms[0],
                norms[1],
            ),
            loss_scale,
            total_rows,
        )
        gain_grads = [norm_grads[0, layer, 0] for layer in range(5)]
        shift_grads = [norm_grads[1, layer, 0] for layer in range(5)]
        gain_grads[4], shift_grads[4] = gain_grads[4][:mel_width], shift_grads[4][:mel_width]
        grad_mel = jnp.transpose(
            lax.dynamic_slice_in_dim(
                grad_mel.reshape(frames, total_rows, mel_width), place * rows, rows, 1
            ),
            (1, 0, 2),
        )
    else:
        middle_full = whole(middle_half, 2).reshape(post_middle.shape[:2] + (channels, channels))
        kernels = [first_full, middle_full[0], middle_full[1], middle_full[2], last_full]
        gains = [middle_gain[0, layer] for layer in range(4)] + [last_gain[0]]
        shifts = [middle_gain[1, layer] for layer in range(4)] + [last_gain[1]]
        layer_in = mel_all.astype(bf16)
        layer_inputs, normed_all, inverses = [], [], []
        output = None
        for layer in range(5):
            layer_inputs.append(layer_in)
            pre_norm = by_rows(
                lambda source, same_now: post_layer(source, kernels[layer], same_now),
                roomy,
                (layer_in, same),
            )
            mean_now = jnp.sum(pre_norm, axis=(0, 1)) / frame_count
            centered = pre_norm - mean_now
            inverse = lax.rsqrt(jnp.sum(centered * centered, axis=(0, 1)) / frame_count + norm_eps)
            normed = centered * inverse
            output = normed * gains[layer] + shifts[layer]
            normed_all.append(normed)
            inverses.append(inverse)
            if layer < 4:
                layer_in = jnp.tanh(output).astype(bf16)
                if not roomy:
                    layer_in, normed_all[layer] = lax.optimization_barrier(
                        (layer_in, normed_all[layer])
                    )

        grad_post = loss_scale * (mel_all + output - targets_all)
        kernel_grads, gain_grads, shift_grads = [None] * 5, [None] * 5, [None] * 5
        grad_output = grad_post
        grad_input = None
        for layer in (4, 3, 2, 1, 0):
            if layer < 4:
                normed_all[layer] = lax.optimization_barrier(normed_all[layer])
                active = jnp.tanh(normed_all[layer] * gains[layer] + shifts[layer])
                grad_output = grad_input * (1.0 - active * active)
            shift_grads[layer] = jnp.sum(grad_output, axis=(0, 1))
            gain_grads[layer] = jnp.sum(grad_output * normed_all[layer], axis=(0, 1))
            grad_norm = (
                gains[layer]
                * inverses[layer]
                * (
                    grad_output
                    - shift_grads[layer] / frame_count
                    - normed_all[layer] * (gain_grads[layer] / frame_count)
                )
            ).astype(bf16)
            grad_input = by_rows(
                lambda grad, same_now: post_layer_back(grad, kernels[layer], same_now),
                roomy,
                (grad_norm, same),
            )
            source = layer_inputs[layer]
            if layer > 0:
                source = lax.dynamic_slice_in_dim(source, place * channel_rows, channel_rows, 2)
            kernel_grads[layer] = by_rows(post_kernel_grad, roomy, (source, grad_norm, same), True)
            kernel_grads[layer] = kernel_grads[layer].reshape(5, source.shape[2], -1)
            if not roomy:
                grad_input, kernel_grads[layer] = lax.optimization_barrier(
                    (grad_input, kernel_grads[layer])
                )
        grad_mel = loss_scale * (mel_all - targets_all) + grad_post + grad_input
        grad_mel = jnp.transpose(
            lax.dynamic_slice_in_dim(grad_mel, place * rows, rows, 1), (1, 0, 2)
        )

    if not roomy:
        inputs_own, grad_mel = lax.optimization_barrier((inputs_own, grad_mel))
        inputs_all = lax.all_gather(inputs_own, "batch", axis=0, tiled=True)

    def add_units(value, axis):
        width = value.shape[axis] // 2
        halves = [
            lax.slice_in_dim(value, start, start + width, axis=axis) for start in (0, width)
        ]
        keep = jnp.where(first_unit, halves[0], halves[1])
        give = jnp.where(first_unit, halves[1], halves[0])
        return keep + exchange(give)

    grad_stop = (jax.nn.sigmoid(stop_logit) - finished) / total_rows
    grad_frame = (
        jnp.concatenate([grad_mel, grad_stop[:, :, None]], axis=2)
        .reshape(rows * frames, mel_width + 1)
        .astype(bf16)
    )
    frame_weight_grad = lax.dot_general(
        frame_in, grad_frame, (((0,), (0,)), ((), ())), preferred_element_type=f32
    )
    frame_bias_grad = jnp.sum(grad_frame.astype(f32), axis=0)[None, :]
    grad_frame_slots = to_slots(
        jnp.pad(grad_frame, ((0, 0), (0, lanes - mel_width - 1))), f32
    ).reshape(longest, slots, lanes)

    (
        sent,
        prenet_back,
        context_grads,
        query_back,
        processed_back,
        vector_back,
        filter_back,
    ) = call_backward(
        unit_array,
        weights,
        (
            gates_one,
            gates_two,
            prior_one,
            prior_two,
            zone_one,
            zone_two,
            owner_hot,
            memory_float,
            query_float,
            vector_row,
            taps_back,
            dense_wide,
            mixed_all,
            alphas,
            taps,
            grad_frame_slots,
            frame_wide,
            slot_wide,
        ),
        prenet_width,
    )

    bias_sums = jnp.transpose(
        jnp.sum(sent.astype(f32), axis=1).reshape(-1, 4, lanes), (1, 0, 2)
    ).reshape(-1, lanes)
    slice_width = 2 * hidden // batch_size
    if slice_width != lanes:
        sent = sent.reshape(sent.shape[0], sent.shape[1], 4, -1, slice_width)
        sent = jnp.transpose(sent, (0, 3, 1, 2, 4)).reshape(batch_size, sent.shape[1], -1)
    received = lax.all_to_all(sent, "batch", 0, 0, tiled=True)
    grad_prenet = lax.dot_general(
        slot_hot.astype(f32),
        prenet_back.reshape(longest * slots, prenet_width),
        (((1,), (0,)), ((), ())),
        precision=precise,
    )

    def silu_back(grad, mixed, drops):
        gate = jax.nn.sigmoid(mixed)
        return grad * drops * 2.0 * gate * (1.0 + mixed * (1.0 - gate))

    def exact(a, b, contract):
        return lax.dot_general(
            a.astype(f32), b.astype(f32), (contract, ((), ())), precision=precise
        )

    grad_mixed_two = silu_back(grad_prenet, mixed_two, drops_two)
    prenet_second_grad = exact(hidden_round, grad_mixed_two, ((0,), (0,)))
    grad_hidden = exact(grad_mixed_two, prenet_second, ((1,), (1,)))
    grad_mixed_one = silu_back(grad_hidden, mixed_one, drops_one)
    prenet_first_grad = exact(previous, grad_mixed_one, ((0,), (0,)))

    query_weight_grad = exact(
        round_one.reshape(longest * slots, hidden),
        query_back.reshape(longest * slots, attention_width),
        ((0,), (0,)),
    )
    processed_round = processed_back.astype(bf16)
    memory_weight_grad = lax.dot_general(
        memory_now, processed_round, (((0,), (0,)), ((), ())), preferred_element_type=f32
    )
    filter_grads = jnp.roll(filter_back, -reach, axis=1)[:, ::-1][:, : location_conv.shape[2]]
    conv_grad = jnp.einsum("cka,fa->fck", filter_grads, dense_float, precision=precise)
    dense_grad = jnp.einsum("cka,fck->fa", filter_grads, conv_float, precision=precise)

    def two_columns(value):
        return jnp.concatenate([value[:, :lanes], value[:, lanes:]], axis=0)

    def to_lanes(value):
        return jnp.pad(value, ((0, 0), (0, lanes - value.shape[1])))

    filter_count, _, tap_count = location_conv.shape
    packed = [
        two_columns(prenet_first_grad),
        two_columns(prenet_second_grad),
        query_weight_grad,
        memory_weight_grad,
        to_lanes(frame_weight_grad),
        to_lanes(conv_grad.reshape(filter_count, -1)),
        dense_grad,
        bias_sums,
        vector_back,
        to_lanes(frame_bias_grad),
    ]
    heights = [value.shape[0] for value in packed]
    shares = 2 * batch_size
    surplus = -sum(heights) % (8 * shares)
    packed = jnp.concatenate(packed + [jnp.zeros((surplus, lanes), f32)], axis=0)
    packed = add_units(packed, 0)
    received, packed = lax.optimization_barrier((received, packed))

    segments_rows = segments_all.T
    carried = jnp.pad(
        (segments_rows[:, 1:] == segments_rows[:, :-1]).astype(bf16), ((0, 0), (0, 1))
    ).reshape(batch_size, frame_rows)
    carried = jnp.pad(carried, ((0, 0), (0, padding)))
    after = jnp.pad(received[:, 1:], ((0, 0), (0, 1), (0, 0))) * carried[:, :, None]
    received = received.reshape(batch_size * (frame_rows + padding), -1)
    after = after.reshape(batch_size * (frame_rows + padding), -1)

    def product(start, width, grads):
        return lax.dot_general(
            inputs_all[:, start : start + width],
            grads,
            (((0,), (0,)), ((), ())),
            preferred_element_type=f32,
        )

    pair = 2 * slice_width
    first_part = jnp.concatenate(
        [
            product(0, prenet_width, received[:, :pair]),
            product(prenet_width + hidden, memory_width, after[:, :pair]),
            product(prenet_width, hidden, after[:, :pair]),
        ],
        axis=0,
    )
    second_part = jnp.concatenate(
        [
            product(prenet_width, hidden + memory_width, received[:, pair:]),
            product(prenet_width + hidden + memory_width, hidden, after[:, pair:]),
        ],
        axis=0,
    )
    parts = jnp.concatenate(
        [
            first_part.reshape(batch_size, depth_one, pair),
            second_part.reshape(batch_size, depth_two, pair),
        ],
        axis=1,
    )
    parts = add_units(parts, 2).astype(bf16)
    depth_both = depth_one + depth_two
    parts = jnp.concatenate(
        [parts, packed.astype(bf16).reshape(batch_size, -1, slice_width)], axis=1
    )
    if roomy:
        (
            parts,
            inputs_first,
            inputs_later,
            grads_early,
            grads_last,
            alphas,
            context_grads,
            processed_round,
        ) = lax.optimization_barrier(
            (
                parts,
                inputs_first,
                inputs_later,
                grads_early,
                grads_last,
                alphas,
                context_grads,
                processed_round,
            )
        )
        kernel_grads = []
        for layer in range(5):
            if layer == 0:
                source = inputs_first
            else:
                source = lax.dynamic_slice_in_dim(
                    inputs_later[layer - 1], place * channel_rows, channel_rows, 1
                )
            grad_norm = grads_early[layer] if layer < 4 else grads_last
            kernel_grads.append(
                post_kernel_grad(
                    source.reshape(frames, total_rows, -1),
                    grad_norm.reshape(frames, total_rows, -1),
                    same,
                ).reshape(5, source.shape[1], grad_norm.shape[1])
            )
    parts = lax.all_to_all(parts, "batch", 0, 0, tiled=True)
    share = jnp.sum(parts[:, depth_both:].astype(f32), axis=0)
    parts = parts[:, :depth_both].astype(f32)
    parts = jnp.transpose(parts, (1, 0, 2)).reshape(depth_both, 4, half)

    memory_grad = lax.dot_general(
        processed_round, memory_weight, (((1,), (1,)), ((), ())), preferred_element_type=f32
    )
    for step in range(longest):
        memory_grad = memory_grad + exact(
            alphas[step][:, :slots], context_grads[step], ((1,), (0,))
        )
    memory_grad = memory_grad.reshape(rows, text_width, memory_width)
    memory_grads = jnp.stack(ordered(memory_grad, exchange(memory_grad)))
    post_first_grad = add_units(kernel_grads[0], 2)
    post_middle_grad = add_units(jnp.stack(kernel_grads[1:4]), 3)
    post_last_grad = add_units(kernel_grads[4], 2)
    middle_norm_grad = add_units(
        jnp.stack([jnp.stack(gain_grads[:4]), jnp.stack(shift_grads[:4])]), 2
    )
    last_norm_grad = add_units(jnp.stack([gain_grads[4], shift_grads[4]]), 1)

    packed = gather_far_first(share.astype(bf16)).reshape(-1, lanes)
    packed = whole(packed, 0).astype(f32)
    small, start = [], 0
    for height in heights:
        small.append(packed[start : start + height])
        start += height

    def from_columns(value):
        tall = value.shape[0] // 2
        return jnp.concatenate([value[:tall], value[tall:]], axis=1)

    biases_grad = small[7].reshape(2, 2, -1)
    biases_grad = jnp.where(first_unit, biases_grad[:, 0], biases_grad[:, 1])
    biases_grad = biases_grad.reshape(2, 4, half)
    small = [
        from_columns(small[0]),
        from_columns(small[1]),
        small[2],
        small[3],
        small[5][:, : 2 * tap_count].reshape(filter_count, 2, tap_count),
        small[6],
        small[8][0],
        small[4][:, : mel_width + 1],
        small[9][0, : mel_width + 1],
    ]
    return (
        small[0],
        small[1],
        small[2],
        small[3],
        small[4],
        small[5],
        small[6],
        parts[:depth_one],
        biases_grad[0],
        parts[depth_one:],
        biases_grad[1],
        small[7],
        small[8],
        post_first_grad,
        post_middle_grad,
        post_last_grad,
        middle_norm_grad,
        last_norm_grad,
        memory_grads,
    )


def solution(mesh):
    in_specs = (
        P(None, "batch", None, None),
        P(None, "batch", None, None),
        P(None, "batch", None),
        P(None, "batch", None),
        P(None, "batch", None, "unit"),
        P(None, "batch", None, "unit"),
        P(None, "batch", None, None),
        P(None, "batch", None, None),
        P(),
        P(),
        P(),
        P(),
        P(),
        P(),
        P(),
        P("batch", None, "unit"),
        P(None, "unit"),
        P("batch", None, "unit"),
        P(None, "unit"),
        P(),
        P(),
        P(None, None, "unit"),
        P(None, None, "batch", "unit"),
        P(None, "batch", "unit"),
        P(None, None, "unit"),
        P(None, "unit"),
    )
    out_specs = (
        P(),
        P(),
        P(),
        P(),
        P(),
        P(),
        P(),
        P("batch", None, "unit"),
        P(None, "unit"),
        P("batch", None, "unit"),
        P(None, "unit"),
        P(),
        P(),
        P(None, None, "unit"),
        P(None, None, "batch", "unit"),
        P(None, "batch", "unit"),
        P(None, None, "unit"),
        P(None, "unit"),
        P(None, "batch", None, None),
    )
    return jax.shard_map(
        on_device, mesh=mesh, in_specs=in_specs, out_specs=out_specs, check_vma=False
    )
```

```python
import functools

import jax
import jax.numpy as jnp
from jax import lax
from jax.experimental import pallas as pl
from jax.experimental.pallas import tpu as pltpu
from jax.sharding import PartitionSpec as P

precise = lax.Precision.HIGHEST
norm_eps = 1e-05
f32 = jnp.float32
bf16 = jnp.bfloat16
lanes = 128
kernel_vmem = 60 * 1024 * 1024


def split(value):
    high = value.astype(bf16)
    return high, (value - high.astype(f32)).astype(bf16)


def dot(a, b, contract=((1,), (0,))):
    return lax.dot_general(a, b, (contract, ((), ())), preferred_element_type=f32)


def dot_left(exact, value, contract=((1,), (0,))):
    high, low = split(value)
    return dot(exact, high, contract) + dot(exact, low, contract)


def dot_right(value, exact, contract=((1,), (0,))):
    high, low = split(value)
    return dot(high, exact, contract) + dot(low, exact, contract)


def dot_both(a, b, contract=((1,), (0,))):
    a_high, a_low = split(a)
    b_high, b_low = split(b)
    return (
        dot(a_high, b_high, contract) + dot(a_low, b_high, contract) + dot(a_high, b_low, contract)
    )


rows_first = ((0,), (0,))
lanes_both = ((1,), (1,))


def position_hot(position_count, text_width, reverse):
    place = lax.broadcasted_iota(jnp.int32, (position_count, lanes), 0) & (text_width - 1)
    lane = lax.broadcasted_iota(jnp.int32, (position_count, lanes), 1)
    place = (lanes - 1) - place if reverse else place + 1
    return (place == lane).astype(bf16)


def slant(value, text_width):
    blocks = [
        pltpu.roll(value[start : start + text_width], 0, 1, stride=1, stride_axis=0)
        for start in range(0, value.shape[0], text_width)
    ]
    return jnp.concatenate(blocks, axis=0)


def pad_rows(value):
    return jnp.concatenate(
        [value, jnp.zeros((lanes - value.shape[0], value.shape[1]), value.dtype)], axis=0
    )


def unit_spot(chunk, unit, per_half):
    half = (chunk // per_half + unit) % 2
    return pl.multiple_of((half * per_half + chunk % per_half) * lanes, lanes)


def gate_spot(chunk, gate, per_half):
    start = (chunk // per_half) * 4 * per_half + gate * per_half + chunk % per_half
    return pl.multiple_of(start * lanes, lanes)


def weight_copies(refs, held_one, held_two, sems):
    copies_one, copies_two = [], []

    def copy(copies, source, target):
        count = len(copies_one) + len(copies_two)
        copies.append(pltpu.make_async_copy(source, target, sems.at[count]))

    if len(refs) == 4:
        for side in range(2):
            copy(copies_one, refs[side], held_one.at[side])
            copy(copies_two, refs[2 + side], held_two.at[side])
        return copies_one, copies_two
    devices = refs[0].shape[1]
    rows_one, rows_two = held_one.shape[2] // devices, held_two.shape[2] // devices
    for held, copies, rows, start in (
        (held_two, copies_two, rows_two, rows_one),
        (held_one, copies_one, rows_one, 0),
    ):
        for side in range(2):
            for device in range(devices):
                copy(
                    copies,
                    refs[side].at[:, device, start : start + rows, :],
                    held.at[side, :, device * rows : (device + 1) * rows, :],
                )
    return copies_one, copies_two


def forward_kernel(
    weight_count,
    unit_ref,
    *refs,
):
    weight_refs, refs = refs[:weight_count], refs[weight_count:]
    forward_body(unit_ref, weight_refs, *refs)


def backward_kernel(
    weight_count,
    unit_ref,
    *refs,
):
    weight_refs, refs = refs[:weight_count], refs[weight_count:]
    backward_body(unit_ref, weight_refs, *refs)


def forward_body(
    unit_ref,
    weight_refs,
    previous_ref,
    drop_one,
    drop_two,
    layer_one,
    layer_two,
    slot_ref,
    zone_one,
    zone_two,
    bias_one,
    bias_two,
    hot_ref,
    memory_ref,
    project_ref,
    query_ref,
    vector_ref,
    conv_ref,
    dense_ref,
    frame_ref,
    frame_bias,
    gates_one,
    gates_two,
    prior_one,
    prior_two,
    round_one,
    round_two,
    context_ref,
    mixed_ref,
    alpha_ref,
    taps_ref,
    prenet_one,
    prenet_two,
    prenet_hidden,
    prenet_out,
    frame_out,
    held_one,
    held_two,
    input_ref,
    prenet_ref,
    processed_ref,
    filter_ref,
    state_one,
    cell_one,
    state_two,
    cell_two,
    sems,
):
    unit = unit_ref[0]
    steps, slots, hidden = round_one.shape
    prenet_width = layer_two.shape[1]
    context_width = context_ref.shape[2]
    half = hidden // 2
    per_half = half // lanes
    position_count = hot_ref.shape[0]
    text_width = position_count // (slots // 4)
    copies_one, copies_two = weight_copies(weight_refs, held_one, held_two, sems)
    for copy in copies_two + copies_one:
        copy.start()
    for ref in (state_one, cell_one, state_two, cell_two):
        ref[...] = jnp.zeros_like(ref)

    def gates_into(held, depth, bias_ref, out_ref, step):
        def one(block, _):
            side = block // 2
            inputs = input_ref[:, :depth]
            for pair in range(per_half):
                tile = (block % 2) * 2 * per_half + 2 * pair
                outside = pl.ds(
                    pl.multiple_of(block * 2 * half + 2 * pair * lanes, 2 * lanes), 2 * lanes
                )
                kernel = jnp.concatenate(
                    [held[side, tile, :depth, :], held[side, tile + 1, :depth, :]], axis=1
                )
                out_ref[step, :, outside] = dot(inputs, kernel) + bias_ref[:, outside]
            return 0

        lax.fori_loop(0, 4, one, 0)

    def cell(gates_ref, zone_ref, prior_ref, state, cells, round_ref, step):
        def one(chunk, _):
            spot = pl.ds(pl.multiple_of(chunk * lanes, lanes), lanes)
            values = [
                gates_ref[step, :, pl.ds(gate_spot(chunk, gate, per_half), lanes)]
                for gate in range(4)
            ]
            zone = zone_ref[step, :, spot]
            before = cells[:, spot]
            prior_ref[step, :, spot] = before
            fresh = jax.nn.sigmoid(values[1]) * before + jax.nn.sigmoid(values[0]) * jnp.tanh(
                values[2]
            )
            output = jax.nn.sigmoid(values[3]) * jnp.tanh(fresh)
            now = zone * state[:, spot] + (1.0 - zone) * output
            state[:, spot] = now
            cells[:, spot] = zone * before + (1.0 - zone) * fresh
            round_ref[step, :, pl.ds(unit_spot(chunk, unit, per_half), lanes)] = now.astype(bf16).astype(
                f32
            )
            return 0

        lax.fori_loop(0, 2 * per_half, one, 0)

    def attention(step, location):
        inside = hot_ref[...] > 0.0
        hot = hot_ref[...].astype(bf16)
        query = pad_rows(dot(round_one[step].astype(bf16), query_ref[...].astype(bf16)))
        summed = dot_left(hot, query) + processed_ref[...]
        if location is not None:
            summed = summed + location
        mixed = jnp.tanh(summed)
        mixed_ref[step] = mixed
        energy = dot_right(mixed, vector_ref[...].astype(bf16))
        most = jnp.max(jnp.where(inside, energy, -1000000000.0), axis=0, keepdims=True)
        shifted = jnp.where(inside, jnp.exp(energy - most), 0.0)
        total = jnp.sum(shifted, axis=0, keepdims=True)
        alpha = shifted / jnp.where(total > 0.0, total, 1.0)
        alpha_ref[step] = alpha
        context = dot_right(alpha, memory_ref[...].astype(bf16), rows_first)[:slots]
        context_ref[step] = context.astype(bf16).astype(f32)

    def taps_of(step):
        spread = dot_right(
            alpha_ref[step], position_hot(position_count, text_width, True), rows_first
        )
        taps_ref[step] = slant(dot_left(hot_ref[...].astype(bf16), spread), text_width)

    def second_layer(step, depth):
        input_ref[:, :hidden] = round_one[step].astype(bf16)
        input_ref[:, hidden : hidden + context_width] = context_ref[step].astype(bf16)
        gates_into(held_two, depth, bias_two, gates_two, step)
        cell(gates_two, zone_two, prior_two, state_two, cell_two, round_two, step)

    slot_hot = slot_ref[...].astype(bf16)

    def prenet_layer(source, layer, drops, mixed_out, out):
        mixed = dot(source.astype(bf16), layer[...].astype(bf16))
        mixed_out[...] = mixed
        value = (mixed * jax.nn.sigmoid(mixed) * drops[...] * 2.0).astype(bf16)
        out[...] = value.astype(f32)
        return value

    hidden_value = prenet_layer(previous_ref[...], layer_one, drop_one, prenet_one, prenet_hidden)
    prenet_value = prenet_layer(hidden_value, layer_two, drop_two, prenet_two, prenet_out)
    prenet_slots = dot(slot_hot, prenet_value, rows_first)
    for step in range(steps):
        prenet_ref[step] = prenet_slots[step * slots : (step + 1) * slots]
    processed_ref[...] = dot(memory_ref[...].astype(bf16), project_ref[...].astype(bf16))
    for channel in range(2):
        filter_ref[channel] = dot(
            conv_ref[channel].astype(bf16), dense_ref[...].astype(bf16)
        )

    gates_one[0] = jnp.broadcast_to(bias_one[...], gates_one.shape[1:])
    cell(gates_one, zone_one, prior_one, state_one, cell_one, round_one, 0)
    attention(0, None)
    taps_of(0)
    for copy in copies_two:
        copy.wait()
    second_layer(0, hidden + context_width)
    for copy in copies_one:
        copy.wait()

    def later(step, _):
        input_ref[:, :prenet_width] = prenet_ref[step].astype(bf16)
        input_ref[:, prenet_width : prenet_width + context_width] = context_ref[step - 1].astype(
            bf16
        )
        input_ref[:, prenet_width + context_width : prenet_width + context_width + hidden] = (
            round_one[step - 1].astype(bf16)
        )
        gates_into(
            held_one, prenet_width + context_width + hidden, bias_one, gates_one, step
        )
        cell(gates_one, zone_one, prior_one, state_one, cell_one, round_one, step)
        previous = taps_ref[step - 1]
        summed = jnp.where(step == 2, taps_ref[0] + previous, previous)
        attention(step, dot_both(previous, filter_ref[0]) + dot_both(summed, filter_ref[1]))

        @pl.when(step < steps - 1)
        def _():
            taps_of(step)

        input_ref[:, hidden + context_width :] = round_two[step - 1].astype(bf16)
        second_layer(step, 2 * hidden + context_width)
        return 0

    lax.fori_loop(1, steps, later, 0)
    for step in range(steps):
        values = dot(round_two[step].astype(bf16), frame_ref[:hidden].astype(bf16)) + dot(
            context_ref[step].astype(bf16), frame_ref[hidden:].astype(bf16)
        )
        high = values.astype(bf16)
        rest = values - high.astype(f32)
        middle = rest.astype(bf16)
        low = (rest - middle.astype(f32)).astype(bf16)
        chosen = slot_hot[:, step * slots : (step + 1) * slots]
        picked = (dot(chosen, high) + dot(chosen, middle)) + dot(chosen, low)
        frame_out[...] = (frame_bias[...] if step == 0 else frame_out[...]) + picked


def backward_body(
    unit_ref,
    weight_refs,
    gates_one,
    gates_two,
    prior_one,
    prior_two,
    zone_one,
    zone_two,
    hot_ref,
    memory_ref,
    query_ref,
    vector_ref,
    conv_ref,
    dense_ref,
    mixed_ref,
    alpha_ref,
    taps_ref,
    frame_grad,
    frame_weight,
    slot_ref,
    sent_ref,
    prenet_grad,
    context_grad,
    query_grad,
    processed_grad,
    vector_grad,
    filter_grad,
    held_one,
    held_two,
    grads_one,
    grads_two,
    back_one,
    back_two,
    state_one,
    cell_one,
    state_two,
    cell_two,
    previous_grad,
    summed_grad,
    from_query,
    frame_ref,
    filter_ref,
    sems,
):
    unit = unit_ref[0]
    steps, slots, prenet_width = prenet_grad.shape
    context_width = context_grad.shape[2]
    hidden = state_one.shape[1]
    half = hidden // 2
    per_half = half // lanes
    position_count = hot_ref.shape[0]
    text_width = position_count // (slots // 4)
    copies_one, copies_two = weight_copies(weight_refs, held_one, held_two, sems)
    for copy in copies_two + copies_one:
        copy.start()
    for ref in (
        state_one,
        cell_one,
        state_two,
        cell_two,
        back_one,
        back_two,
        previous_grad,
        summed_grad,
        processed_grad,
        vector_grad,
        filter_grad,
    ):
        ref[...] = jnp.zeros_like(ref)

    def cell(gates_ref, prior_ref, zone_ref, state, cells, grads_ref, step, incoming):
        def one(chunk, _):
            spot = pl.ds(pl.multiple_of(chunk * lanes, lanes), lanes)
            places = [pl.ds(gate_spot(chunk, gate, per_half), lanes) for gate in range(4)]
            values = [gates_ref[step, :, place] for place in places]
            zone = zone_ref[step, :, spot]
            keep = 1.0 - zone
            before = prior_ref[step, :, spot]
            gate_in = jax.nn.sigmoid(values[0])
            gate_forget = jax.nn.sigmoid(values[1])
            candidate = jnp.tanh(values[2])
            gate_out = jax.nn.sigmoid(values[3])
            bent = jnp.tanh(gate_forget * before + gate_in * candidate)
            grad_state = incoming(unit_spot(chunk, unit, per_half)) + state[:, spot]
            grad_cell = cells[:, spot]
            grad_new = keep * grad_state
            grad_fresh = grad_new * gate_out * (1.0 - bent * bent) + keep * grad_cell
            state[:, spot] = zone * grad_state
            cells[:, spot] = zone * grad_cell + gate_forget * grad_fresh
            results = (
                grad_fresh * candidate * gate_in * (1.0 - gate_in),
                grad_fresh * before * gate_forget * (1.0 - gate_forget),
                grad_fresh * gate_in * (1.0 - candidate * candidate),
                grad_new * bent * gate_out * (1.0 - gate_out),
            )
            for place, result in zip(places, results):
                grads_ref[step, :, place] = result.astype(bf16)
            return 0

        lax.fori_loop(0, 2 * per_half, one, 0)

    def inputs_back(grads_ref, held, out_ref, step, blocks):
        def one(block, _):
            spot = pl.ds(pl.multiple_of(block * 256, 256), 256)
            totals = [None] * 4
            for tile in range(0, 8 * per_half, 2):
                side, inside = tile // (4 * per_half), tile % (4 * per_half)
                kernel = jnp.concatenate(
                    [held[side, inside, spot, :], held[side, inside + 1, spot, :]], axis=1
                )
                grads = grads_ref[step, :, tile * lanes : (tile + 2) * lanes]
                product = dot(grads, kernel, lanes_both)
                which = tile // 2 % 4
                totals[which] = product if totals[which] is None else totals[which] + product
            out_ref[:, spot] = (totals[0] + totals[1]) + (totals[2] + totals[3])
            return 0

        lax.fori_loop(0, blocks, one, 0)

    def attention(step, located):
        inside = hot_ref[...] > 0.0
        hot = hot_ref[...].astype(bf16)
        alpha = alpha_ref[step]
        mixed = mixed_ref[step]
        context_now = pad_rows(context_grad[step])
        weights_grad = jnp.where(
            inside,
            dot_left(memory_ref[...].astype(bf16), context_now, lanes_both)
            + previous_grad[...]
            + summed_grad[...],
            0.0,
        )
        product = alpha * weights_grad
        energy_grad = product - alpha * jnp.sum(product, axis=0, keepdims=True)
        spread = jnp.sum(energy_grad, axis=1, keepdims=True)
        vector_grad[...] += jnp.sum(spread * mixed, axis=0, keepdims=True)
        mixed_grad = spread * vector_ref[...] * (1.0 - mixed * mixed)
        processed_grad[...] += mixed_grad
        high, low = split(mixed_grad)
        query_now = (dot(hot, high, rows_first) + dot(hot, low, rows_first))[:slots]
        query_grad[step] = query_now
        from_query[...] = dot_right(query_now, query_ref[...].astype(bf16), lanes_both)
        if located:
            previous = taps_ref[step - 1]
            summed = jnp.where(step == 2, taps_ref[0] + previous, previous)
            filter_grad[0] += dot_both(previous, mixed_grad, rows_first)
            filter_grad[1] += dot_both(summed, mixed_grad, rows_first)
            place_hot = position_hot(position_count, text_width, False)

            def taps_back(channel):
                taps_grad = slant(
                    dot_both(mixed_grad, filter_ref[channel], lanes_both), text_width
                )
                gathered = dot_right(taps_grad, hot, rows_first)
                return jnp.where(inside, dot_left(place_hot, gathered), 0.0)

            previous_grad[...] = taps_back(0)
            summed_grad[...] += taps_back(1)

    def arrived(step, copies):
        @pl.when(step == steps - 1)
        def _():
            for copy in copies:
                copy.wait()

    def step_back(step, located):
        cell(
            gates_two,
            prior_two,
            zone_two,
            state_two,
            cell_two,
            grads_two,
            step,
            lambda spot: frame_ref[step, :, pl.ds(spot, lanes)]
            + back_two[:, pl.ds(spot + hidden + context_width, lanes)],
        )
        blocks_two = (hidden + context_width + (hidden if located else 0)) // 256
        if located:
            arrived(step, copies_two)
        inputs_back(grads_two, held_two, back_two, step, blocks_two)
        context_grad[step] = (
            back_two[:, hidden : hidden + context_width]
            + frame_ref[step, :, hidden:]
            + back_one[:, prenet_width : prenet_width + context_width]
        )
        attention(step, located)
        cell(
            gates_one,
            prior_one,
            zone_one,
            state_one,
            cell_one,
            grads_one,
            step,
            lambda spot: back_two[:, pl.ds(spot, lanes)]
            + from_query[:, pl.ds(spot, lanes)]
            + back_one[:, pl.ds(spot + prenet_width + context_width, lanes)],
        )
        blocks_one = (prenet_width + (hidden + context_width if located else 0)) // 256
        if located:
            arrived(step, copies_one)
        inputs_back(grads_one, held_one, back_one, step, blocks_one)
        prenet_grad[step] = back_one[:, :prenet_width]

    for channel in range(2):
        filter_ref[channel] = dot(
            conv_ref[channel].astype(bf16), dense_ref[...].astype(bf16)
        )
    for step in range(steps):
        frame_ref[step] = dot(
            frame_grad[step].astype(bf16), frame_weight[...].astype(bf16), lanes_both
        )

    def later(index, _):
        step_back(steps - 1 - index, True)
        return 0

    lax.fori_loop(0, steps - 1, later, 0)
    step_back(0, False)
    slot_hot = slot_ref[...].astype(bf16)

    def tile_out(tile, _):
        for layer, grads_ref in ((0, grads_one), (1, grads_two)):
            for side in range(2):
                place = ((side + unit) % 2) * 4 * half + tile * lanes
                grads = grads_ref[:, :, pl.ds(pl.multiple_of(place, lanes), lanes)]
                chosen = dot(slot_hot, grads.reshape(steps * slots, lanes)).astype(bf16)
                spot = (2 * layer + side) * lanes
                sent_ref[tile, :, spot : spot + lanes] = chosen
        return 0

    lax.fori_loop(0, 4 * per_half, tile_out, 0)


def call_forward(unit, weights, small, sizes):
    steps, slots, hidden, context_width, positions, frame_rows, prenet_width = sizes
    tiles = 2 * hidden // lanes
    held_one = (2, tiles, prenet_width + context_width + hidden, lanes)
    held_two = (2, tiles, 2 * hidden + context_width, lanes)

    def shape(*dims):
        return jax.ShapeDtypeStruct(dims, f32)

    outs = [
        shape(steps, slots, 4 * hidden),
        shape(steps, slots, 4 * hidden),
        shape(steps, slots, hidden),
        shape(steps, slots, hidden),
        shape(steps, slots, hidden),
        shape(steps, slots, hidden),
        shape(steps, slots, context_width),
        shape(steps, positions, lanes),
        shape(steps, positions, lanes),
        shape(steps - 1, positions, lanes),
        shape(frame_rows, prenet_width),
        shape(frame_rows, prenet_width),
        shape(frame_rows, prenet_width),
        shape(frame_rows, prenet_width),
        shape(frame_rows, lanes),
    ]
    vmem = pl.BlockSpec(memory_space=pltpu.VMEM)
    return pl.pallas_call(
        functools.partial(forward_kernel, len(weights)),
        out_shape=outs,
        in_specs=[pl.BlockSpec(memory_space=pltpu.SMEM)]
        + [pl.BlockSpec(memory_space=pl.ANY)] * len(weights)
        + [vmem] * len(small),
        out_specs=[vmem] * len(outs),
        scratch_shapes=[
            pltpu.VMEM(held_one, bf16),
            pltpu.VMEM(held_two, bf16),
            pltpu.VMEM((slots, held_two[2]), bf16),
            pltpu.VMEM((steps, slots, prenet_width), f32),
            pltpu.VMEM((positions, lanes), f32),
            pltpu.VMEM((2, lanes, lanes), f32),
            pltpu.VMEM((slots, hidden), f32),
            pltpu.VMEM((slots, hidden), f32),
            pltpu.VMEM((slots, hidden), f32),
            pltpu.VMEM((slots, hidden), f32),
            pltpu.SemaphoreType.DMA((4 if len(weights) == 4 else 4 * weights[0].shape[1],)),
        ],
        compiler_params=pltpu.CompilerParams(vmem_limit_bytes=kernel_vmem),
        name="decoder_forward",
    )(unit, *weights, *small)


def call_backward(unit, weights, small, prenet_width):
    gates_one = small[0]
    steps, slots, gate_width = gates_one.shape
    hidden = gate_width // 4
    positions, context_width = small[7].shape
    tiles = 2 * hidden // lanes
    held_one = (2, tiles, prenet_width + context_width + hidden, lanes)
    held_two = (2, tiles, 2 * hidden + context_width, lanes)

    def shape(dims, kind):
        return jax.ShapeDtypeStruct(dims, kind)

    outs = [
        shape((gate_width // (2 * lanes), small[-1].shape[0], 4 * lanes), bf16),
        shape((steps, slots, prenet_width), f32),
        shape((steps, slots, context_width), f32),
        shape((steps, slots, lanes), f32),
        shape((positions, lanes), f32),
        shape((1, lanes), f32),
        shape((2, lanes, lanes), f32),
    ]
    vmem = pl.BlockSpec(memory_space=pltpu.VMEM)
    return pl.pallas_call(
        functools.partial(backward_kernel, len(weights)),
        out_shape=outs,
        in_specs=[pl.BlockSpec(memory_space=pltpu.SMEM)]
        + [pl.BlockSpec(memory_space=pl.ANY)] * len(weights)
        + [vmem] * len(small),
        out_specs=[vmem] * len(outs),
        scratch_shapes=[
            pltpu.VMEM(held_one, bf16),
            pltpu.VMEM(held_two, bf16),
            pltpu.VMEM((steps, slots, gate_width), bf16),
            pltpu.VMEM((steps, slots, gate_width), bf16),
            pltpu.VMEM((slots, held_one[2]), f32),
            pltpu.VMEM((slots, held_two[2]), f32),
            pltpu.VMEM((slots, hidden), f32),
            pltpu.VMEM((slots, hidden), f32),
            pltpu.VMEM((slots, hidden), f32),
            pltpu.VMEM((slots, hidden), f32),
            pltpu.VMEM((positions, lanes), f32),
            pltpu.VMEM((positions, lanes), f32),
            pltpu.VMEM((slots, hidden), f32),
            pltpu.VMEM((steps, slots, hidden + context_width), f32),
            pltpu.VMEM((2, lanes, lanes), f32),
            pltpu.SemaphoreType.DMA((4 if len(weights) == 4 else 4 * weights[0].shape[1],)),
        ],
        compiler_params=pltpu.CompilerParams(vmem_limit_bytes=kernel_vmem),
        name="decoder_backward",
    )(unit, *weights, *small)


def postnet_kernel(
    mel_width,
    loss_scale,
    unit_ref,
    mel_ref,
    target_ref,
    mask_ref,
    first_ref,
    own_ref,
    peer_ref,
    last_ref,
    gain_ref,
    shift_ref,
    inputs_first,
    inputs_later,
    grads_early,
    grads_last,
    norm_grads,
    mel_grad,
    padded,
    padded_mel,
    held,
    normed_early,
    normed_last,
    inverse_ref,
    post_grad,
):
    unit = unit_ref[0]
    count, channels = held.shape
    side = channels // 2
    frames = padded.shape[0] - count
    rows_each = frames // 4
    chunk = 2 * rows_each
    tall = float(count)
    body_rows = slice(2 * rows_each, 2 * rows_each + count)

    for ref in (padded, padded_mel):
        ref[: 2 * rows_each] = jnp.zeros((2 * rows_each, ref.shape[1]), bf16)
        ref[2 * rows_each + count :] = jnp.zeros((2 * rows_each, ref.shape[1]), bf16)

    def piece(source, start, tap, width, lane=None):
        spot = pl.ds(pl.multiple_of(start + tap * rows_each, rows_each), chunk)
        mask = mask_ref[tap, pl.ds(pl.multiple_of(start, rows_each), chunk), :]
        if width < lanes:
            mask = mask[:, :width]
        else:
            mask = jnp.concatenate([mask] * (width // lanes), axis=1)
        value = source[spot, :] if lane is None else source[spot, pl.ds(lane, width)]
        return value * mask

    def chunks(work):
        def one(index, _):
            work(pl.multiple_of(index * chunk, chunk))
            return 0

        lax.fori_loop(0, count // chunk, one, 0)

    def half_spot(which):
        return pl.multiple_of(((which + unit) % 2) * side, side)

    def norm_forward(value, layer, lane, width):
        mean = jnp.sum(value, axis=0, keepdims=True) / tall
        centered = value - mean
        inverse = lax.rsqrt(jnp.sum(centered * centered, axis=0, keepdims=True) / tall + norm_eps)
        inverse_ref[layer, :, pl.ds(lane, width)] = inverse
        return centered * inverse

    def each_lane_block(work):
        def one(index, _):
            work(pl.multiple_of(index * lanes, lanes))
            return 0

        lax.fori_loop(0, channels // lanes, one, 0)

    def activate(layer):
        def block(lane):
            spot = pl.ds(lane, lanes)
            normed = norm_forward(held[:, spot], layer, lane, lanes)
            normed_early[layer, :, spot] = normed
            active = jnp.tanh(
                normed * gain_ref[layer, :, spot] + shift_ref[layer, :, spot]
            ).astype(bf16)
            inputs_later[layer, :, spot] = active
            padded[body_rows, spot] = active

        each_lane_block(block)

    source = mel_ref[...].astype(bf16)
    inputs_first[...] = source
    padded_mel[body_rows] = source

    def first_chunk(start):
        total = None
        for tap in range(5):
            product = dot(piece(padded_mel, start, tap, mel_width), first_ref[tap])
            total = product if total is None else total + product
        held[pl.ds(start, chunk), :] = total

    chunks(first_chunk)
    activate(0)

    def middle(index, _):
        def middle_chunk(start):
            totals = [None, None]
            for tap in range(5):
                value = piece(padded, start, tap, channels)
                for which, ref in ((0, own_ref), (1, peer_ref)):
                    product = dot(value, ref[index * 5 + tap])
                    totals[which] = product if tap == 0 else totals[which] + product
            for which in range(2):
                held[pl.ds(start, chunk), pl.ds(half_spot(which), side)] = totals[which]

        chunks(middle_chunk)
        activate(index + 1)
        return 0

    lax.fori_loop(0, 3, middle, 0)

    def last_chunk(start):
        total = None
        for tap in range(5):
            product = dot(piece(padded, start, tap, channels), last_ref[tap])
            total = product if total is None else total + product
        normed_last[pl.ds(start, chunk), :] = total

    chunks(last_chunk)
    normed = norm_forward(normed_last[...], 4, 0, mel_width)
    normed_last[...] = normed

    def norm_back(grad, normed, layer, lane, width):
        spot = pl.ds(lane, width)
        shift_grad = jnp.sum(grad, axis=0, keepdims=True)
        gain_grad = jnp.sum(grad * normed, axis=0, keepdims=True)
        norm_grads[0, layer, :, spot] = gain_grad
        norm_grads[1, layer, :, spot] = shift_grad
        return (
            gain_ref[layer, :, spot]
            * inverse_ref[layer, :, spot]
            * (grad - shift_grad / tall - normed * (gain_grad / tall))
        ).astype(bf16)

    output = normed * gain_ref[4, :, :mel_width] + shift_ref[4, :, :mel_width]
    grad = loss_scale * (mel_ref[...] + output - target_ref[...])
    post_grad[...] = grad
    grad_norm = norm_back(grad, normed, 4, 0, mel_width)
    grads_last[...] = grad_norm
    padded_mel[body_rows] = grad_norm

    def last_back(start):
        total = None
        for tap in range(5):
            product = dot(
                piece(padded_mel, start, tap, mel_width), last_ref[4 - tap], lanes_both
            )
            total = product if total is None else total + product
        held[pl.ds(start, chunk), :] = total

    chunks(last_back)

    def deactivate(layer):
        def block(lane):
            spot = pl.ds(lane, lanes)
            normed = normed_early[layer, :, spot]
            active = jnp.tanh(normed * gain_ref[layer, :, spot] + shift_ref[layer, :, spot])
            grad = held[:, spot] * (1.0 - active * active)
            grad_norm = norm_back(grad, normed, layer, lane, lanes)
            grads_early[layer, :, spot] = grad_norm
            padded[body_rows, spot] = grad_norm

        each_lane_block(block)

    def middle_back(back, _):
        index = 2 - back
        deactivate(index + 1)

        def chunk_back(start):
            total = None
            for which, ref in ((0, own_ref), (1, peer_ref)):
                for tap in range(5):
                    product = dot(
                        piece(padded, start, tap, side, half_spot(which)),
                        ref[index * 5 + 4 - tap],
                        lanes_both,
                    )
                    total = product if total is None else total + product
            held[pl.ds(start, chunk), :] = total

        chunks(chunk_back)
        return 0

    lax.fori_loop(0, 3, middle_back, 0)
    deactivate(0)

    def first_back(start):
        total = None
        for tap in range(5):
            product = dot(piece(padded, start, tap, channels), first_ref[4 - tap], lanes_both)
            total = product if total is None else total + product
        spot = pl.ds(start, chunk)
        mel_grad[spot, :] = (
            loss_scale * (mel_ref[spot, :] - target_ref[spot, :]) + post_grad[spot, :] + total
        )

    chunks(first_back)


def call_postnet(unit, small, loss_scale, rows_all):
    mel = small[0]
    count, mel_width = mel.shape
    channels = small[3].shape[2]

    def shape(kind, *dims):
        return jax.ShapeDtypeStruct(dims, kind)

    outs = [
        shape(bf16, count, mel_width),
        shape(bf16, 4, count, channels),
        shape(bf16, 4, count, channels),
        shape(bf16, count, mel_width),
        shape(f32, 2, 5, 1, channels),
        shape(f32, count, mel_width),
    ]
    vmem = pl.BlockSpec(memory_space=pltpu.VMEM)
    tall = count + 4 * rows_all
    return pl.pallas_call(
        functools.partial(postnet_kernel, mel_width, loss_scale),
        out_shape=outs,
        in_specs=[pl.BlockSpec(memory_space=pltpu.SMEM)] + [vmem] * len(small),
        out_specs=[vmem] * len(outs),
        scratch_shapes=[
            pltpu.VMEM((tall, channels), bf16),
            pltpu.VMEM((tall, mel_width), bf16),
            pltpu.VMEM((count, channels), f32),
            pltpu.VMEM((4, count, channels), f32),
            pltpu.VMEM((count, mel_width), f32),
            pltpu.VMEM((5, 1, channels), f32),
            pltpu.VMEM((count, mel_width), f32),
        ],
        compiler_params=pltpu.CompilerParams(vmem_limit_bytes=kernel_vmem),
        name="postnet",
    )(unit, *small)


def shifted_frames(source, same):
    steps = source.shape[0]
    padded = jnp.pad(source, ((2, 2), (0, 0), (0, 0)))
    return [
        padded[offset : offset + steps] * same[:, :, offset, None].astype(source.dtype)
        for offset in range(5)
    ]


def by_rows(work, roomy, arrays, summed=False):
    if roomy:
        return work(*arrays)
    parts = arrays[0].shape[1] // 192

    def cut(value):
        value = value.reshape((value.shape[0], parts, -1) + value.shape[2:])
        return jnp.moveaxis(value, 1, 0)

    pieces = tuple(cut(value) for value in arrays)
    if summed:
        first = jax.eval_shape(work, *[value[0] for value in pieces])
        start = jnp.zeros(first.shape, first.dtype)
        return lax.scan(lambda total, now: (total + work(*now), None), start, pieces)[0]
    result = jnp.moveaxis(lax.map(lambda now: work(*now), pieces), 0, 1)
    return result.reshape((result.shape[0], -1) + result.shape[3:])


def post_layer(source, kernel, same):
    wide = jnp.concatenate(shifted_frames(source, same), axis=2)
    return jnp.einsum(
        "src,co->sro", wide, kernel.reshape(-1, kernel.shape[2]), preferred_element_type=f32
    )


def post_layer_back(grad, kernel, same):
    wide = jnp.concatenate(shifted_frames(grad, same), axis=2)
    turned = jnp.transpose(kernel[::-1], (0, 2, 1)).reshape(-1, kernel.shape[1])
    return jnp.einsum("sro,oc->src", wide, turned, preferred_element_type=f32)


def post_kernel_grad(source, grad, same):
    wide = jnp.concatenate(shifted_frames(source, same), axis=2)
    return jnp.einsum("src,sro->co", wide, grad, preferred_element_type=f32)


def on_device(
    memory,
    targets,
    segments,
    text_lengths,
    zone_first,
    zone_second,
    drop_first,
    drop_second,
    prenet_first,
    prenet_second,
    query_weight,
    memory_weight,
    location_conv,
    location_dense,
    energy_vector,
    lstm_first,
    bias_first,
    lstm_second,
    bias_second,
    frame_weight,
    frame_bias,
    post_first,
    post_middle,
    post_last,
    middle_norm,
    last_norm,
):
    micro_count, rows, text_width, memory_width = memory.shape
    frames = segments.shape[2]
    utterances = text_lengths.shape[2]
    mel_width = targets.shape[3]
    hidden = query_weight.shape[0]
    prenet_width = prenet_first.shape[1]
    attention_width = query_weight.shape[1]
    half = lstm_first.shape[2]
    depth_one, depth_two = lstm_first.shape[0], lstm_second.shape[0]
    unit = lax.axis_index("unit")
    place = lax.axis_index("batch")
    batch_size = lax.axis_size("batch")
    total_rows = rows * batch_size
    frame_count = float(total_rows * frames)
    first_unit = unit == 0
    longest = 3
    slots = 4 * rows

    def exchange(value):
        return lax.ppermute(value, "unit", [(0, 1), (1, 0)])

    def ordered(own, peer):
        return jnp.where(first_unit, own, peer), jnp.where(first_unit, peer, own)

    def whole(value, axis):
        return jnp.concatenate(ordered(value, exchange(value)), axis=axis)

    def mine(value):
        return lax.dynamic_index_in_dim(value, unit, 0, keepdims=False)

    def others(value):
        return lax.dynamic_index_in_dim(value, 1 - unit, 0, keepdims=False)

    def swapped(value, bit):
        pairs = [(index, index ^ bit) for index in range(batch_size)]
        other = lax.ppermute(value, "batch", pairs)
        upper = (place & bit) != 0
        return jnp.where(upper, other, value), jnp.where(upper, value, other)

    def gather_far_first(value):
        inner, bit, count = value.ndim, batch_size // 2, 0
        while bit:
            value = jnp.stack(swapped(value, bit))
            bit //= 2
            count += 1
        order = tuple(range(count - 1, -1, -1)) + tuple(range(count, count + inner))
        return jnp.transpose(value, order).reshape((batch_size,) + value.shape[count:])

    def gather_rows(value):
        return gather_far_first(value).reshape((-1,) + value.shape[1:])

    def to_tiles(value):
        return jnp.transpose(value.reshape(value.shape[0], -1, lanes), (1, 0, 2))

    together = depth_one % 16 == 0 and depth_two % 16 == 0

    def gathered(value):
        return lax.all_gather(value, "batch", axis=1, tiled=True)

    if together:
        both = jnp.concatenate([to_tiles(lstm_first), to_tiles(lstm_second)], axis=1)
        own = (gathered(both).reshape(both.shape[0], batch_size, both.shape[1], lanes),)
    else:
        own = (gathered(to_tiles(lstm_first)), gathered(to_tiles(lstm_second)))
    channel_rows = post_middle.shape[2]
    middle_width = post_middle.shape[3]
    middle_half = lax.all_gather(
        post_middle.reshape(-1, channel_rows, middle_width), "batch", axis=1, tiled=True
    )
    last_half = gather_rows(jnp.transpose(post_last, (1, 0, 2)).reshape(channel_rows, -1))
    last_half = jnp.transpose(
        last_half.reshape(-1, post_last.shape[0], post_last.shape[2]), (1, 0, 2)
    )
    memory_now = mine(memory).reshape(rows * text_width, memory_width)
    segments_now = mine(segments)
    targets_now = mine(targets)
    frame_info = gather_rows(
        jnp.concatenate([targets_now, segments_now[:, :, None].astype(bf16)], axis=2)
    )

    same_frames = segments_now[:, :, None] == segments_now[:, None, :]
    earlier = jnp.tril(jnp.ones((frames, frames), jnp.bool_), -1)
    order = jnp.sum((same_frames & earlier[None]).astype(jnp.int32), axis=2)
    slot_of = order * slots + segments_now * rows + jnp.arange(rows, dtype=jnp.int32)[:, None]
    frame_rows = rows * frames
    padding = -frame_rows % 16
    slot_hot = (
        jnp.pad(slot_of.reshape(-1, 1), ((0, padding), (0, 0)), constant_values=-1)
        == jnp.arange(longest * slots, dtype=jnp.int32)[None, :]
    ).astype(bf16)
    slot_hot_frames = slot_hot[:frame_rows]
    carry_on = jnp.pad(
        (segments_now[:, 1:] == segments_now[:, :-1]).astype(f32), ((0, 0), (1, 0))
    )
    finished = jnp.pad(
        (segments_now[:, 1:] != segments_now[:, :-1]).astype(f32),
        ((0, 0), (0, 1)),
        constant_values=1.0,
    )

    def to_slots(value, kind=bf16):
        return lax.dot_general(
            slot_hot_frames,
            value.astype(bf16),
            (((0,), (0,)), ((), ())),
            preferred_element_type=f32,
        ).astype(kind)

    def to_frames(value):
        return jnp.dot(slot_hot, value.astype(bf16), preferred_element_type=f32).astype(bf16)

    def pad_frames(value):
        return jnp.pad(
            value.astype(f32).reshape(frame_rows, -1), ((0, padding), (0, 0))
        )

    previous = pad_frames(
        jnp.pad(targets_now[:, :-1], ((0, 0), (1, 0), (0, 0))).astype(f32)
        * carry_on[:, :, None]
    )
    drops_one = pad_frames(mine(drop_first))
    drops_two = pad_frames(mine(drop_second))

    zones_own = jnp.concatenate([mine(zone_first), mine(zone_second)], axis=2).astype(f32)
    zones_peer = exchange(
        jnp.concatenate([others(zone_first), others(zone_second)], axis=2).astype(f32)
    )
    zones_slots = to_slots(
        jnp.concatenate([zones_own, zones_peer], axis=2).reshape(rows * frames, -1), f32
    ).reshape(longest, slots, 4 * half)
    zone_one = jnp.concatenate(
        [zones_slots[:, :, :half], zones_slots[:, :, 2 * half : 3 * half]], axis=2
    )
    zone_two = jnp.concatenate(
        [zones_slots[:, :, half : 2 * half], zones_slots[:, :, 3 * half :]], axis=2
    )
    biases = jnp.stack([bias_first.reshape(-1), bias_second.reshape(-1)])
    biases = jnp.concatenate([biases, exchange(biases)], axis=1)
    text_ends = jnp.cumsum(mine(text_lengths), axis=1)
    owner = jnp.sum(
        (jnp.arange(text_width, dtype=jnp.int32)[None, :, None] >= text_ends[:, None, :]).astype(
            jnp.int32
        ),
        axis=2,
    )
    owner_slot = owner * rows + jnp.arange(rows, dtype=jnp.int32)[:, None]
    owner_hot = (
        owner_slot.reshape(-1, 1) == jnp.arange(lanes, dtype=jnp.int32)[None, :]
    ).astype(f32)
    conv_float = location_conv.astype(f32)
    dense_float = location_dense.astype(f32)
    reach = location_conv.shape[2] // 2
    taps_first = jnp.transpose(conv_float, (1, 2, 0))
    taps_first = jnp.pad(
        taps_first,
        ((0, 0), (0, lanes - taps_first.shape[1]), (0, lanes - taps_first.shape[2])),
    )
    dense_wide = jnp.pad(dense_float, ((0, lanes - dense_float.shape[0]), (0, 0)))
    taps_forward = jnp.roll(taps_first[:, ::-1], reach, axis=1)
    taps_back = jnp.roll(taps_first, 1 - reach, axis=1)
    frame_wide = jnp.pad(
        frame_weight.astype(f32), ((0, 0), (0, lanes - frame_weight.shape[1]))
    )
    frame_bias_wide = jnp.pad(frame_bias, (0, lanes - frame_bias.shape[0]))[None, :]
    vector_float = energy_vector.astype(f32)
    vector_wide = jnp.broadcast_to(vector_float[:, None], (attention_width, lanes))
    memory_float = memory_now.astype(f32)
    query_float = query_weight.astype(f32)
    unit_array = unit.astype(jnp.int32).reshape(1)

    targets_all = jnp.transpose(frame_info[:, :, :mel_width].astype(f32), (1, 0, 2))
    segments_all = jnp.transpose(frame_info[:, :, mel_width].astype(jnp.int32))
    padded = jnp.pad(segments_all, ((2, 2), (0, 0)), constant_values=-1)
    same = jnp.stack([padded[offset : offset + frames] == segments_all for offset in range(5)])
    same = jnp.moveaxis(same, 0, 2)
    first_full = whole(post_first, 2)
    last_full = whole(last_half, 2)
    middle_gain = whole(middle_norm, 2)
    last_gain = whole(last_norm, 1)
    loss_scale = 2.0 / (mel_width * total_rows)
    count = total_rows * frames
    channels = middle_norm.shape[2] * 2
    masks = jnp.broadcast_to(
        jnp.transpose(same, (2, 0, 1)).reshape(5, count, 1).astype(bf16), (5, count, lanes)
    )
    wide_gain = jnp.pad(last_gain, ((0, 0), (0, channels - mel_width)))
    norms = jnp.concatenate([middle_gain, wide_gain[:, None, :]], axis=1)[:, :, None, :]
    forward_small = (
        previous,
        drops_one,
        drops_two,
        prenet_first.astype(f32),
        prenet_second.astype(f32),
        slot_hot.astype(f32),
        zone_one,
        zone_two,
        biases[0:1],
        biases[1:2],
        owner_hot,
        memory_float,
        memory_weight.astype(f32),
        query_float,
        vector_wide,
        taps_forward,
        dense_wide,
        frame_wide,
        frame_bias_wide,
    )
    (
        own,
        forward_small,
        taps_back,
        vector_row,
        targets_all,
        masks,
        first_full,
        last_full,
        norms,
    ) = lax.optimization_barrier(
        (
            own,
            forward_small,
            taps_back,
            vector_float[None, :],
            targets_all,
            masks,
            first_full,
            last_full,
            norms,
        )
    )
    weights = sum(((value, exchange(value)) for value in own), ())
    slot_wide, zone_one, zone_two = forward_small[5], forward_small[6], forward_small[7]
    memory_float, query_float = forward_small[11], forward_small[13]
    dense_wide, frame_wide = forward_small[16], forward_small[17]

    (
        gates_one,
        gates_two,
        prior_one,
        prior_two,
        round_one,
        round_two,
        contexts,
        mixed_all,
        alphas,
        taps,
        mixed_one,
        mixed_two,
        hidden_round,
        prenet_round,
        frame_out,
    ) = call_forward(
        unit_array,
        weights,
        forward_small,
        (
            longest,
            slots,
            hidden,
            memory_width,
            rows * text_width,
            frame_rows + padding,
            prenet_width,
        ),
    )

    middle_half = lax.optimization_barrier((middle_half, frame_out))[0]
    middle_peer = exchange(middle_half)
    states = to_frames(
        jnp.concatenate([round_one, contexts, round_two], axis=2).reshape(longest * slots, -1)
    )
    frame_in = jnp.concatenate(
        [states[:, hidden + memory_width :], states[:, hidden : hidden + memory_width]], axis=1
    )
    frame_in = frame_in[:frame_rows]
    frame_out = frame_out[:frame_rows]
    mel_own = frame_out[:, :mel_width].reshape(rows, frames, mel_width)
    stop_logit = frame_out[:, mel_width].reshape(rows, frames)
    mel_all = jnp.transpose(
        gather_rows(mel_own), (1, 0, 2)
    )
    inputs_own = jnp.concatenate([prenet_round.astype(bf16), states], axis=1)
    roomy = total_rows * frames <= 2048
    if roomy:
        inputs_own, mel_all = lax.optimization_barrier((inputs_own, mel_all))
        inputs_all = lax.all_gather(inputs_own, "batch", axis=0, tiled=True)

    if roomy:
        (
            inputs_first,
            inputs_later,
            grads_early,
            grads_last,
            norm_grads,
            grad_mel,
        ) = call_postnet(
            unit_array,
            (
                mel_all.reshape(count, mel_width),
                targets_all.reshape(count, mel_width),
                masks,
                first_full,
                middle_half,
                middle_peer,
                last_full,
                norms[0],
                norms[1],
            ),
            loss_scale,
            total_rows,
        )
        gain_grads = [norm_grads[0, layer, 0] for layer in range(5)]
        shift_grads = [norm_grads[1, layer, 0] for layer in range(5)]
        gain_grads[4], shift_grads[4] = gain_grads[4][:mel_width], shift_grads[4][:mel_width]
        grad_mel = jnp.transpose(
            lax.dynamic_slice_in_dim(
                grad_mel.reshape(frames, total_rows, mel_width), place * rows, rows, 1
            ),
            (1, 0, 2),
        )
    else:
        middle_full = whole(middle_half, 2).reshape(post_middle.shape[:2] + (channels, channels))
        kernels = [first_full, middle_full[0], middle_full[1], middle_full[2], last_full]
        gains = [middle_gain[0, layer] for layer in range(4)] + [last_gain[0]]
        shifts = [middle_gain[1, layer] for layer in range(4)] + [last_gain[1]]
        layer_in = mel_all.astype(bf16)
        layer_inputs, normed_all, inverses = [], [], []
        output = None
        for layer in range(5):
            layer_inputs.append(layer_in)
            pre_norm = by_rows(
                lambda source, same_now: post_layer(source, kernels[layer], same_now),
                roomy,
                (layer_in, same),
            )
            mean_now = jnp.sum(pre_norm, axis=(0, 1)) / frame_count
            centered = pre_norm - mean_now
            inverse = lax.rsqrt(jnp.sum(centered * centered, axis=(0, 1)) / frame_count + norm_eps)
            normed = centered * inverse
            output = normed * gains[layer] + shifts[layer]
            normed_all.append(normed)
            inverses.append(inverse)
            if layer < 4:
                layer_in = jnp.tanh(output).astype(bf16)
                if not roomy:
                    layer_in, normed_all[layer] = lax.optimization_barrier(
                        (layer_in, normed_all[layer])
                    )

        grad_post = loss_scale * (mel_all + output - targets_all)
        kernel_grads, gain_grads, shift_grads = [None] * 5, [None] * 5, [None] * 5
        grad_output = grad_post
        grad_input = None
        for layer in (4, 3, 2, 1, 0):
            if layer < 4:
                normed_all[layer] = lax.optimization_barrier(normed_all[layer])
                active = jnp.tanh(normed_all[layer] * gains[layer] + shifts[layer])
                grad_output = grad_input * (1.0 - active * active)
            shift_grads[layer] = jnp.sum(grad_output, axis=(0, 1))
            gain_grads[layer] = jnp.sum(grad_output * normed_all[layer], axis=(0, 1))
            grad_norm = (
                gains[layer]
                * inverses[layer]
                * (
                    grad_output
                    - shift_grads[layer] / frame_count
                    - normed_all[layer] * (gain_grads[layer] / frame_count)
                )
            ).astype(bf16)
            grad_input = by_rows(
                lambda grad, same_now: post_layer_back(grad, kernels[layer], same_now),
                roomy,
                (grad_norm, same),
            )
            source = layer_inputs[layer]
            if layer > 0:
                source = lax.dynamic_slice_in_dim(source, place * channel_rows, channel_rows, 2)
            kernel_grads[layer] = by_rows(post_kernel_grad, roomy, (source, grad_norm, same), True)
            kernel_grads[layer] = kernel_grads[layer].reshape(5, source.shape[2], -1)
            if not roomy:
                grad_input, kernel_grads[layer] = lax.optimization_barrier(
                    (grad_input, kernel_grads[layer])
                )
        grad_mel = loss_scale * (mel_all - targets_all) + grad_post + grad_input
        grad_mel = jnp.transpose(
            lax.dynamic_slice_in_dim(grad_mel, place * rows, rows, 1), (1, 0, 2)
        )

    if not roomy:
        inputs_own, grad_mel = lax.optimization_barrier((inputs_own, grad_mel))
        inputs_all = lax.all_gather(inputs_own, "batch", axis=0, tiled=True)

    def add_units(value, axis):
        width = value.shape[axis] // 2
        halves = [
            lax.slice_in_dim(value, start, start + width, axis=axis) for start in (0, width)
        ]
        keep = jnp.where(first_unit, halves[0], halves[1])
        give = jnp.where(first_unit, halves[1], halves[0])
        return keep + exchange(give)

    grad_stop = (jax.nn.sigmoid(stop_logit) - finished) / total_rows
    grad_frame = (
        jnp.concatenate([grad_mel, grad_stop[:, :, None]], axis=2)
        .reshape(rows * frames, mel_width + 1)
        .astype(bf16)
    )
    frame_weight_grad = lax.dot_general(
        frame_in, grad_frame, (((0,), (0,)), ((), ())), preferred_element_type=f32
    )
    frame_bias_grad = jnp.sum(grad_frame.astype(f32), axis=0)[None, :]
    grad_frame_slots = to_slots(
        jnp.pad(grad_frame, ((0, 0), (0, lanes - mel_width - 1))), f32
    ).reshape(longest, slots, lanes)

    (
        sent,
        prenet_back,
        context_grads,
        query_back,
        processed_back,
        vector_back,
        filter_back,
    ) = call_backward(
        unit_array,
        weights,
        (
            gates_one,
            gates_two,
            prior_one,
            prior_two,
            zone_one,
            zone_two,
            owner_hot,
            memory_float,
            query_float,
            vector_row,
            taps_back,
            dense_wide,
            mixed_all,
            alphas,
            taps,
            grad_frame_slots,
            frame_wide,
            slot_wide,
        ),
        prenet_width,
    )

    bias_sums = jnp.transpose(
        jnp.sum(sent.astype(f32), axis=1).reshape(-1, 4, lanes), (1, 0, 2)
    ).reshape(-1, lanes)
    slice_width = 2 * hidden // batch_size
    if slice_width != lanes:
        sent = sent.reshape(sent.shape[0], sent.shape[1], 4, -1, slice_width)
        sent = jnp.transpose(sent, (0, 3, 1, 2, 4)).reshape(batch_size, sent.shape[1], -1)
    received = lax.all_to_all(sent, "batch", 0, 0, tiled=True)
    grad_prenet = lax.dot_general(
        slot_hot.astype(f32),
        prenet_back.reshape(longest * slots, prenet_width),
        (((1,), (0,)), ((), ())),
        precision=precise,
    )

    def silu_back(grad, mixed, drops):
        gate = jax.nn.sigmoid(mixed)
        return grad * drops * 2.0 * gate * (1.0 + mixed * (1.0 - gate))

    def exact(a, b, contract):
        return lax.dot_general(
            a.astype(f32), b.astype(f32), (contract, ((), ())), precision=precise
        )

    grad_mixed_two = silu_back(grad_prenet, mixed_two, drops_two)
    prenet_second_grad = exact(hidden_round, grad_mixed_two, ((0,), (0,)))
    grad_hidden = exact(grad_mixed_two, prenet_second, ((1,), (1,)))
    grad_mixed_one = silu_back(grad_hidden, mixed_one, drops_one)
    prenet_first_grad = exact(previous, grad_mixed_one, ((0,), (0,)))

    query_weight_grad = exact(
        round_one.reshape(longest * slots, hidden),
        query_back.reshape(longest * slots, attention_width),
        ((0,), (0,)),
    )
    processed_round = processed_back.astype(bf16)
    memory_weight_grad = lax.dot_general(
        memory_now, processed_round, (((0,), (0,)), ((), ())), preferred_element_type=f32
    )
    filter_grads = jnp.roll(filter_back, -reach, axis=1)[:, ::-1][:, : location_conv.shape[2]]
    conv_grad = jnp.einsum("cka,fa->fck", filter_grads, dense_float, precision=precise)
    dense_grad = jnp.einsum("cka,fck->fa", filter_grads, conv_float, precision=precise)

    def two_columns(value):
        return jnp.concatenate([value[:, :lanes], value[:, lanes:]], axis=0)

    def to_lanes(value):
        return jnp.pad(value, ((0, 0), (0, lanes - value.shape[1])))

    filter_count, _, tap_count = location_conv.shape
    packed = [
        two_columns(prenet_first_grad),
        two_columns(prenet_second_grad),
        query_weight_grad,
        memory_weight_grad,
        to_lanes(frame_weight_grad),
        to_lanes(conv_grad.reshape(filter_count, -1)),
        dense_grad,
        bias_sums,
        vector_back,
        to_lanes(frame_bias_grad),
    ]
    heights = [value.shape[0] for value in packed]
    shares = 2 * batch_size
    surplus = -sum(heights) % (8 * shares)
    packed = jnp.concatenate(packed + [jnp.zeros((surplus, lanes), f32)], axis=0)
    packed = add_units(packed, 0)
    received, packed = lax.optimization_barrier((received, packed))

    segments_rows = segments_all.T
    carried = jnp.pad(
        (segments_rows[:, 1:] == segments_rows[:, :-1]).astype(bf16), ((0, 0), (0, 1))
    ).reshape(batch_size, frame_rows)
    carried = jnp.pad(carried, ((0, 0), (0, padding)))
    after = jnp.pad(received[:, 1:], ((0, 0), (0, 1), (0, 0))) * carried[:, :, None]
    received = received.reshape(batch_size * (frame_rows + padding), -1)
    after = after.reshape(batch_size * (frame_rows + padding), -1)

    def product(start, width, grads):
        return lax.dot_general(
            inputs_all[:, start : start + width],
            grads,
            (((0,), (0,)), ((), ())),
            preferred_element_type=f32,
        )

    pair = 2 * slice_width
    first_part = jnp.concatenate(
        [
            product(0, prenet_width, received[:, :pair]),
            product(prenet_width + hidden, memory_width, after[:, :pair]),
            product(prenet_width, hidden, after[:, :pair]),
        ],
        axis=0,
    )
    second_part = jnp.concatenate(
        [
            product(prenet_width, hidden + memory_width, received[:, pair:]),
            product(prenet_width + hidden + memory_width, hidden, after[:, pair:]),
        ],
        axis=0,
    )
    parts = jnp.concatenate(
        [
            first_part.reshape(batch_size, depth_one, pair),
            second_part.reshape(batch_size, depth_two, pair),
        ],
        axis=1,
    )
    parts = add_units(parts, 2).astype(bf16)
    depth_both = depth_one + depth_two
    parts = jnp.concatenate(
        [parts, packed.astype(bf16).reshape(batch_size, -1, slice_width)], axis=1
    )
    if roomy:
        (
            parts,
            inputs_first,
            inputs_later,
            grads_early,
            grads_last,
            alphas,
            context_grads,
            processed_round,
        ) = lax.optimization_barrier(
            (
                parts,
                inputs_first,
                inputs_later,
                grads_early,
                grads_last,
                alphas,
                context_grads,
                processed_round,
            )
        )
        kernel_grads = []
        for layer in range(5):
            if layer == 0:
                source = inputs_first
            else:
                source = lax.dynamic_slice_in_dim(
                    inputs_later[layer - 1], place * channel_rows, channel_rows, 1
                )
            grad_norm = grads_early[layer] if layer < 4 else grads_last
            kernel_grads.append(
                post_kernel_grad(
                    source.reshape(frames, total_rows, -1),
                    grad_norm.reshape(frames, total_rows, -1),
                    same,
                ).reshape(5, source.shape[1], grad_norm.shape[1])
            )
    parts = lax.all_to_all(parts, "batch", 0, 0, tiled=True)
    share = jnp.sum(parts[:, depth_both:].astype(f32), axis=0)
    parts = parts[:, :depth_both].astype(f32)
    parts = jnp.transpose(parts, (1, 0, 2)).reshape(depth_both, 4, half)

    memory_grad = lax.dot_general(
        processed_round, memory_weight, (((1,), (1,)), ((), ())), preferred_element_type=f32
    )
    for step in range(longest):
        memory_grad = memory_grad + exact(
            alphas[step][:, :slots], context_grads[step], ((1,), (0,))
        )
    memory_grad = memory_grad.reshape(rows, text_width, memory_width)
    memory_grads = jnp.stack(ordered(memory_grad, exchange(memory_grad)))
    post_first_grad = add_units(kernel_grads[0], 2)
    post_middle_grad = add_units(jnp.stack(kernel_grads[1:4]), 3)
    post_last_grad = add_units(kernel_grads[4], 2)
    middle_norm_grad = add_units(
        jnp.stack([jnp.stack(gain_grads[:4]), jnp.stack(shift_grads[:4])]), 2
    )
    last_norm_grad = add_units(jnp.stack([gain_grads[4], shift_grads[4]]), 1)

    packed = gather_far_first(share.astype(bf16)).reshape(-1, lanes)
    packed = whole(packed, 0).astype(f32)
    small, start = [], 0
    for height in heights:
        small.append(packed[start : start + height])
        start += height

    def from_columns(value):
        tall = value.shape[0] // 2
        return jnp.concatenate([value[:tall], value[tall:]], axis=1)

    biases_grad = small[7].reshape(2, 2, -1)
    biases_grad = jnp.where(first_unit, biases_grad[:, 0], biases_grad[:, 1])
    biases_grad = biases_grad.reshape(2, 4, half)
    small = [
        from_columns(small[0]),
        from_columns(small[1]),
        small[2],
        small[3],
        small[5][:, : 2 * tap_count].reshape(filter_count, 2, tap_count),
        small[6],
        small[8][0],
        small[4][:, : mel_width + 1],
        small[9][0, : mel_width + 1],
    ]
    return (
        small[0],
        small[1],
        small[2],
        small[3],
        small[4],
        small[5],
        small[6],
        parts[:depth_one],
        biases_grad[0],
        parts[depth_one:],
        biases_grad[1],
        small[7],
        small[8],
        post_first_grad,
        post_middle_grad,
        post_last_grad,
        middle_norm_grad,
        last_norm_grad,
        memory_grads,
    )


def solution(mesh):
    in_specs = (
        P(None, "batch", None, None),
        P(None, "batch", None, None),
        P(None, "batch", None),
        P(None, "batch", None),
        P(None, "batch", None, "unit"),
        P(None, "batch", None, "unit"),
        P(None, "batch", None, None),
        P(None, "batch", None, None),
        P(),
        P(),
        P(),
        P(),
        P(),
        P(),
        P(),
        P("batch", None, "unit"),
        P(None, "unit"),
        P("batch", None, "unit"),
        P(None, "unit"),
        P(),
        P(),
        P(None, None, "unit"),
        P(None, None, "batch", "unit"),
        P(None, "batch", "unit"),
        P(None, None, "unit"),
        P(None, "unit"),
    )
    out_specs = (
        P(),
        P(),
        P(),
        P(),
        P(),
        P(),
        P(),
        P("batch", None, "unit"),
        P(None, "unit"),
        P("batch", None, "unit"),
        P(None, "unit"),
        P(),
        P(),
        P(None, None, "unit"),
        P(None, None, "batch", "unit"),
        P(None, "batch", "unit"),
        P(None, None, "unit"),
        P(None, "unit"),
        P(None, "batch", None, None),
    )
    return jax.shard_map(
        on_device, mesh=mesh, in_specs=in_specs, out_specs=out_specs, check_vma=False
    )
```
